32 devices in a mesh: dp: 8 (over z, x), tensor: 4 (over y, core).
Axes of the slice: x: 2, y: 2, z: 4, core: 2. Of those that a mesh axis runs over, the one named last changes fastest.
Arguments:
- tokens: bfloat16 [8192, 768], P('dp'), may hold values from -6 to 6
- cotangent: bfloat16 [8192, 768], P('dp'), may hold values from -6 to 6
- clip_lengths: int32 [16, 8], P('dp'), may hold values from 0 to 496, as said below
- key_mask: int32 [8192], P('dp'), may hold values 0 or 1
- rel_buckets: int32 [1023], replicated, may hold values from 0 to 319
- attention_weights: float32 [4, 768, 768], P(None, 'dp', 'tensor'), may hold values from -0.8660254 to 0.8660254
- attention_first: float32 [4, 768, 768], P(None, 'dp', 'tensor'), may hold values from -7.6293945e-05 to 7.6293945e-05
- attention_second: float32 [4, 768, 768], P(None, 'dp', 'tensor'), may hold values from 2.8822156e-11 to 1.15288626e-10
- feedforward_weights: float32 [2, 768, 3072], P(None, 'dp', 'tensor'), may hold values from -0.21875 to 0.21875
- feedforward_first: float32 [2, 768, 3072], P(None, 'dp', 'tensor'), may hold values from -7.6293945e-05 to 7.6293945e-05
- feedforward_second: float32 [2, 768, 3072], P(None, 'dp', 'tensor'), may hold values from 2.8822156e-11 to 1.15288626e-10
- small_params: float32 [13198], replicated, may hold values from -2.8 to 2.8, as said below
- small_first: float32 [13198], replicated, may hold values from -9.1552734e-05 to 9.1552734e-05
- small_second: float32 [13198], replicated, may hold values from 6.499114e-11 to 2.5996455e-10
Outputs:
- global_norm: float32 [], replicated
- attention_moment: float32 [4, 768, 768], P(None, 'dp', 'tensor')
- attention_square: float32 [4, 768, 768], P(None, 'dp', 'tensor')
- attention_master: float32 [4, 768, 768], P(None, 'dp', 'tensor')
- attention_copy: bfloat16 [4, 768, 768], P(None, 'dp', 'tensor')
- feedforward_moment: float32 [2, 768, 3072], P(None, 'dp', 'tensor')
- feedforward_square: float32 [2, 768, 3072], P(None, 'dp', 'tensor')
- feedforward_master: float32 [2, 768, 3072], P(None, 'dp', 'tensor')
- feedforward_copy: bfloat16 [2, 768, 3072], P(None, 'dp', 'tensor')
- small_moment: float32 [13198], replicated
- small_square: float32 [13198], replicated
- small_master: float32 [13198], replicated
- block_output: bfloat16 [8192, 768], P('dp')
- tokens_grad: bfloat16 [8192, 768], P('dp')
The draws below stay inside these ranges and needn't reach their ends.
Inputs may be any that keep to these rules, and one draw needn't show every extreme that they name: `clip_lengths`: each row sums to at most 512; a row holds either one clip of 496 patches with one short remainder or up to five clips of at most 96; every draw has a clip of 496. `small_params`: norm gains are positive.
All inputs are finite; a program needn't handle non-finite values. No bound on the sum of `key_mask` on one device may be relied on, other than what follows from the above.
Results may differ from the reference program's by a relative error of at most 0.011.
Values may be sent and summed in bfloat16 or wider, within the bound.
A program may use at most 128 MiB of HBM per device.

```python
import math
import jax
import jax.numpy as jnp
from jax import lax

MODEL_WIDTH = 768
H = 12
HD = 64
FF = 3072
NB = 320
BUCKET_SLOTS = 512
CLIPS = 8
STEP = 5
LONG_CLIP = 496
SHORT_CLIP = 96
BUCKETS = 16
TOKENS = 8192
NSMALL = 13198


def draw_clip_lengths(key, part):
    key = jax.random.fold_in(key, 11)
    key_long, key_forced, key_short, key_rest = jax.random.split(key, 4)
    long_rows = jax.random.randint(key_long, (BUCKETS,), 0, 4) == 0
    forced = jax.random.randint(key_forced, (), 0, BUCKETS)
    long_rows = long_rows | (jnp.arange(BUCKETS) == forced)
    slot_index = jnp.arange(CLIPS)
    short_rows = jax.random.randint(key_short, (BUCKETS, CLIPS), SHORT_CLIP // 2, SHORT_CLIP + 1)
    short_rows = jnp.where(slot_index[None, :] < 5, short_rows, 0)
    remainder = jax.random.randint(key_rest, (BUCKETS,), 1, BUCKET_SLOTS - LONG_CLIP + 1)
    long_values = jnp.where(slot_index[None, :] == 0, LONG_CLIP, jnp.where(slot_index[None, :] == 1, remainder[:, None], 0))
    return jnp.where(long_rows[:, None], long_values, short_rows).astype(jnp.int32)


def draw_attention_weights(key, part):
    key = jax.random.fold_in(key, 23)
    normal_part = jnp.clip(jax.random.normal(key, (4, MODEL_WIDTH, MODEL_WIDTH), jnp.float32), -6.0, 6.0)
    factor = jnp.where(jnp.arange(4) == 3, 4.0, 1.0) / jnp.sqrt(jnp.float32(MODEL_WIDTH))
    return normal_part * factor[:, None, None]


def draw_small_params(key, part):
    key = jax.random.fold_in(key, 37)
    key_jitter, key_scale = jax.random.split(key)
    jitter = jnp.clip(jax.random.normal(key_jitter, (NSMALL,), jnp.float32), -4.0, 4.0)
    position = jnp.arange(NSMALL)
    column = (position % MODEL_WIDTH).astype(jnp.float32) / MODEL_WIDTH
    rising = 0.6 * jnp.exp(column * jnp.log(3.0)) * (1.0 + 0.1 * jitter)
    is_gain = (position < 4 * MODEL_WIDTH) & (position // MODEL_WIDTH % 2 == 0)
    base_end = 8 * MODEL_WIDTH + FF
    table_end = base_end + NB * H
    gate_end = table_end + 2 * HD
    offset_end = gate_end + 2
    scales = jnp.exp(jax.random.uniform(key_scale, (NSMALL,), jnp.float32, jnp.log(0.5), jnp.log(2.0)))
    values = jnp.where(position < base_end, 0.3 * jitter, 0.0)
    values = jnp.where(is_gain, rising, values)
    values = jnp.where((position >= base_end) & (position < table_end), 0.7 * jitter, values)
    values = jnp.where((position >= table_end) & (position < gate_end), 0.125 * jitter, values)
    values = jnp.where((position >= gate_end) & (position < offset_end), 0.5 * jitter, values)
    values = jnp.where(position >= offset_end, scales, values)
    return values


def touch_ends(array, stream_key, smallest, top_value):
    longest = array.shape.index(max(array.shape))
    spots = []
    for shift in (0, 1):
        where = [jax.random.randint(jax.random.fold_in(stream_key, axis), (), 0, length) for axis, length in enumerate(array.shape)]
        where[longest] = (where[longest] + shift) % array.shape[longest]
        spots.append(tuple(where))
    return array.at[spots[0]].set(smallest).at[spots[1]].set(top_value)


def levels(key, shape, cuts, smallest, top_value):
    level = 1.0
    for axis_at, parts in cuts:
        heights = jax.random.uniform(jax.random.fold_in(jax.random.fold_in(key, 6), axis_at), (parts,), jnp.float32, smallest / len(cuts), top_value / len(cuts))
        level = level * jnp.repeat(jnp.exp(heights), shape[axis_at] // parts).reshape((-1,) + (1,) * (len(shape) - 1 - axis_at))
    return level


def bell_draw(stream_key, shape, spread, reach, cuts=(), kind=jnp.bfloat16):
    values = spread * jax.random.normal(stream_key, shape, jnp.float32)
    if cuts:
        values = values * levels(stream_key, shape, cuts, -0.22, 0.18)
    return jnp.clip(values, -reach, reach).astype(kind)


def setup_inputs(seed: int = 0) -> dict:
    splits = jax.random.split(jax.random.key(seed), 15)
    return {
        "tokens": bell_draw(splits[0], (TOKENS, MODEL_WIDTH), 1.0, 6.0, ((0, 8),)),
        "cotangent": bell_draw(splits[1], (TOKENS, MODEL_WIDTH), 1.0, 6.0, ((0, 8),)),
        "clip_lengths": draw_clip_lengths(jax.random.fold_in(splits[14], 71), 0),
        "key_mask": touch_ends((jax.random.randint(splits[3], (TOKENS,), 0, 8) < 7).astype(jnp.int32), jax.random.fold_in(splits[3], 1), 0, 1),
        "rel_buckets": touch_ends(jax.random.randint(splits[4], (2 * BUCKET_SLOTS - 1,), 0, NB), jax.random.fold_in(splits[4], 1), 0, NB - 1).astype(jnp.int32),
        "attention_weights": draw_attention_weights(jax.random.fold_in(splits[14], 71), 0),
        "attention_first": bell_draw(splits[6], (4, MODEL_WIDTH, MODEL_WIDTH), (0.014 / (4 * MODEL_WIDTH * MODEL_WIDTH + 2 * MODEL_WIDTH * FF) ** 0.5), 7.62939453125e-05, ((1, 8), (2, 4)), jnp.float32),
        "attention_second": jnp.clip(jnp.exp(math.log(1.1528862586818178e-10) - 1.3862944 * jax.random.uniform(splits[7], (4, MODEL_WIDTH, MODEL_WIDTH), jnp.float32) ** levels(splits[7], (4, MODEL_WIDTH, MODEL_WIDTH), ((1, 8), (2, 4)), -0.2, 0.2)), 2.8822156467045446e-11, 1.1528862586818178e-10),
        "feedforward_weights": bell_draw(splits[8], (2, MODEL_WIDTH, FF), MODEL_WIDTH ** -0.5, 0.21875, ((1, 8), (2, 4)), jnp.float32),
        "feedforward_first": bell_draw(splits[9], (2, MODEL_WIDTH, FF), (0.014 / (4 * MODEL_WIDTH * MODEL_WIDTH + 2 * MODEL_WIDTH * FF) ** 0.5), 7.62939453125e-05, ((1, 8), (2, 4)), jnp.float32),
        "feedforward_second": jnp.clip(jnp.exp(math.log(1.1528862586818178e-10) - 1.3862944 * jax.random.uniform(splits[10], (2, MODEL_WIDTH, FF), jnp.float32) ** levels(splits[10], (2, MODEL_WIDTH, FF), ((1, 8), (2, 4)), -0.2, 0.2)), 2.8822156467045446e-11, 1.1528862586818178e-10),
        "small_params": draw_small_params(jax.random.fold_in(splits[14], 71), 0),
        "small_first": bell_draw(splits[12], (NSMALL,), (0.017 / (4 * MODEL_WIDTH * MODEL_WIDTH + 2 * MODEL_WIDTH * FF) ** 0.5), 9.1552734375e-05, (), jnp.float32),
        "small_second": jnp.clip(jnp.exp(jax.random.uniform(splits[13], (NSMALL,), jnp.float32, math.log(6.499113747171492e-11), math.log(2.599645498868597e-10))), 6.499113747171492e-11, 2.599645498868597e-10),
    }


FULL_PRECISION = lax.Precision.HIGHEST
DEEP_ALPHA = 24.0 ** 0.25
NORM_EPSILON = 1e-05
MASK_VALUE = -1e+30
BETA_FIRST = 0.9
BETA_SECOND = 0.98
RATE_MATRIX = 0.03
RATE_SMALL = 0.5
WEIGHT_DECAY = 0.01
ADAM_EPSILON = 1e-08
CLIP_LIMIT = 0.1

@jax.custom_vjp
def low(v):
    return lax.optimization_barrier(v.astype(jnp.bfloat16)).astype(jnp.float32)

@jax.custom_vjp
def low_back(v):
    return v

def low_keep(v):
    return (low(v), None)

def low_pass(kept, grad):
    return (grad,)

def back_keep(v):
    return (v, None)

def back_low(kept, grad):
    return (low(grad),)
low.defvjp(low_keep, low_pass)
low_back.defvjp(back_keep, back_low)

def rounded_pair(values):
    return low_back(low(values))

def matmul(left, right):
    return jnp.dot(left, right, precision=FULL_PRECISION, preferred_element_type=jnp.float32)

def layer_norm(values, norm_gain, norm_shift):
    row_mean = lax.optimization_barrier(jnp.mean(values, axis=-1, keepdims=True))
    centred = values - row_mean
    variance = lax.optimization_barrier(jnp.mean(centred * centred, axis=-1, keepdims=True))
    return centred * lax.rsqrt(variance + NORM_EPSILON) * norm_gain + norm_shift

def split_small(vector):
    widths = [MODEL_WIDTH] * 8 + [FF, NB * H, HD * 2, 2, H]
    pieces = []
    offset = 0
    for extent in widths:
        pieces.append(vector[offset:offset + extent])
        offset += extent
    return pieces

def allowed_mask(lengths_row, keep_row):
    positions = jnp.arange(BUCKET_SLOTS, dtype=jnp.int32)
    clip_ends = jnp.cumsum(lengths_row).astype(jnp.int32)
    segment = lax.optimization_barrier(jnp.sum((positions[:, None] >= clip_ends[None, :]).astype(jnp.int32), axis=1))
    live_keys = (keep_row == 1) & (segment < CLIPS)
    same_clip = segment[:, None] == segment[None, :]
    return same_clip & (live_keys[None, :] | (positions[:, None] == positions[None, :]))

def residual_block(inputs, attention_matrices, forward_matrices, small_values, allowed, rel_buckets):
    gain_one, shift_one, gain_two, shift_two, bias_query, bias_value, bias_output, bias_down, bias_up, rel_table, gate_matrix, gate_offset, gate_scale = split_small(small_values)
    query_weight = low(attention_matrices[0])
    key_weight = low(attention_matrices[1])
    value_weight = low(attention_matrices[2])
    output_weight = low(attention_matrices[3])
    up_weight = low(forward_matrices[0])
    down_weight = low(forward_matrices[1])
    heads_of_query = rounded_pair(matmul(inputs, query_weight) + bias_query).reshape(BUCKET_SLOTS, H, HD)
    heads_of_key = rounded_pair(matmul(inputs, key_weight)).reshape(BUCKET_SLOTS, H, HD)
    heads_of_value = rounded_pair(matmul(inputs, value_weight) + bias_value).reshape(BUCKET_SLOTS, H, HD)
    head_inputs = inputs.reshape(BUCKET_SLOTS, H, HD)
    linear = jnp.einsum('lhd,dk->hlk', head_inputs, gate_matrix.reshape(HD, 2), precision=FULL_PRECISION) + gate_offset
    sigmoid = jax.nn.sigmoid(linear)
    gate = sigmoid[..., 0] * (sigmoid[..., 1] * gate_scale[:, None] - 1.0) + 2.0
    positions = jnp.arange(BUCKET_SLOTS, dtype=jnp.int32)
    offsets = rel_buckets[positions[None, :] - positions[:, None] + BUCKET_SLOTS - 1]
    relative = jnp.transpose(rel_table.reshape(NB, H)[offsets], (2, 0, 1))
    attention_logits = jnp.einsum('zjx,ojx->jzo', heads_of_query, heads_of_key, precision=FULL_PRECISION) * 0.125
    attention_logits = attention_logits + gate[:, :, None] * relative
    scores = low_back(jnp.where(allowed[None], attention_logits, MASK_VALUE))
    attention_probabilities = low(jax.nn.softmax(scores, axis=-1))
    attended_values = rounded_pair(jnp.einsum('gej,jgn->egn', attention_probabilities, heads_of_value, precision=FULL_PRECISION).reshape(BUCKET_SLOTS, MODEL_WIDTH))
    attention = low_back(matmul(attended_values, output_weight.T) + bias_output)
    normed = layer_norm(DEEP_ALPHA * inputs + attention, gain_one, shift_one)
    up_pre = low_back(matmul(low(normed), up_weight) + bias_up)
    activated = low(jax.nn.gelu(up_pre, approximate=False))
    feedforward = low_back(matmul(activated, down_weight.T) + bias_down)
    return layer_norm(DEEP_ALPHA * normed + feedforward, gain_two, shift_two)

def adam_step(weights, moment, second, gradient, step_rate, decay_rate):
    moment_new = BETA_FIRST * moment + (1.0 - BETA_FIRST) * gradient
    second_new = BETA_SECOND * second + (1.0 - BETA_SECOND) * gradient * gradient
    moment_hat = moment_new / (1.0 - BETA_FIRST ** STEP)
    second_hat = second_new / (1.0 - BETA_SECOND ** STEP)
    master = weights - step_rate * (moment_hat / (jnp.sqrt(second_hat) + ADAM_EPSILON) + decay_rate * weights)
    return (moment_new, second_new, master)

def reference(tokens, cotangent, clip_lengths, key_mask, rel_buckets, attention_weights, attention_first, attention_second, feedforward_weights, feedforward_first, feedforward_second, small_params, small_first, small_second):
    inputs = tokens.astype(jnp.float32).reshape(BUCKETS, BUCKET_SLOTS, MODEL_WIDTH)
    upstream = cotangent.astype(jnp.float32).reshape(BUCKETS, BUCKET_SLOTS, MODEL_WIDTH)
    keep_rows = key_mask.reshape(BUCKETS, BUCKET_SLOTS)

    def one_bucket(totals, bucket_item):
        bucket_in, bucket_up, lengths_row, keep_row = bucket_item
        allowed = allowed_mask(lengths_row, keep_row)

        def forward(values_in, attention_matrices, forward_matrices, small_values):
            return residual_block(values_in, attention_matrices, forward_matrices, small_values, allowed, rel_buckets)
        result, pullback = jax.vjp(forward, bucket_in, attention_weights, feedforward_weights, small_params)
        grad_in, grad_attention, grad_forward, grad_small = pullback(bucket_up)
        totals = (totals[0] + grad_attention, totals[1] + grad_forward, totals[2] + grad_small)
        return (totals, (result, grad_in))
    start_totals = (jnp.zeros((4, MODEL_WIDTH, MODEL_WIDTH), jnp.float32), jnp.zeros((2, MODEL_WIDTH, FF), jnp.float32), jnp.zeros((NSMALL,), jnp.float32))
    totals, (results, grads_in) = lax.scan(one_bucket, start_totals, (inputs, upstream, clip_lengths, keep_rows))
    grad_attention, grad_forward, grad_small = totals
    squares = jnp.sum(grad_attention * grad_attention) + jnp.sum(grad_forward * grad_forward)
    squares = squares + jnp.sum(grad_small * grad_small)
    global_norm = jnp.sqrt(squares)
    factor = CLIP_LIMIT / jnp.maximum(global_norm, CLIP_LIMIT)
    attention_moment, attention_square, attention_master = adam_step(attention_weights, attention_first, attention_second, factor * grad_attention, RATE_MATRIX, WEIGHT_DECAY)
    feedforward_moment, feedforward_square, feedforward_master = adam_step(feedforward_weights, feedforward_first, feedforward_second, factor * grad_forward, RATE_MATRIX, WEIGHT_DECAY)
    small_moment, small_square, small_master = adam_step(small_params, small_first, small_second, factor * grad_small, RATE_SMALL, 0.0)
    block_output = results.reshape(TOKENS, MODEL_WIDTH).astype(jnp.bfloat16)
    tokens_grad = grads_in.reshape(TOKENS, MODEL_WIDTH).astype(jnp.bfloat16)
    return (global_norm, attention_moment, attention_square, attention_master, attention_master.astype(jnp.bfloat16), feedforward_moment, feedforward_square, feedforward_master, feedforward_master.astype(jnp.bfloat16), small_moment, small_square, small_master, block_output, tokens_grad)
```

```python
from functools import partial
from types import SimpleNamespace

import jax
import jax.numpy as jnp
from jax import lax
from jax.experimental import pallas as pl
from jax.experimental.pallas import tpu as pltpu
from jax.sharding import PartitionSpec as P

MODEL_WIDTH = 768
H = 12
HD = 64
FF = 3072
NB = 320
BUCKET_SLOTS = 512
CLIPS = 8
STEP = 5


FULL_PRECISION = lax.Precision.HIGHEST
DEEP_ALPHA = 24.0**0.25
NORM_EPSILON = 1e-05
MASK_VALUE = -1e30
BETA_FIRST = 0.9
BETA_SECOND = 0.98
RATE_MATRIX = 0.03
RATE_SMALL = 0.5
WEIGHT_DECAY = 0.01
ADAM_EPSILON = 1e-08
CLIP_LIMIT = 0.1


def layer_norm(values, norm_gain, norm_shift):
    row_mean = jnp.mean(values, axis=-1, keepdims=True)
    centred = values - row_mean
    variance = jnp.mean(centred * centred, axis=-1, keepdims=True)
    return centred * lax.rsqrt(variance + NORM_EPSILON) * norm_gain + norm_shift


def gelu_exact(values):
    return jax.nn.gelu(values, approximate=False)


def split_small(vector):
    widths = [MODEL_WIDTH] * 8 + [FF, NB * H, HD * 2, 2, H]
    pieces = []
    offset = 0
    for extent in widths:
        pieces.append(vector[offset : offset + extent])
        offset += extent
    return pieces


def allowed_mask(lengths_row, keep_row):
    positions = jnp.arange(BUCKET_SLOTS, dtype=jnp.int32)
    clip_ends = jnp.cumsum(lengths_row)
    segment = jnp.sum((positions[:, None] >= clip_ends[None, :]).astype(jnp.int32), axis=1)
    live_keys = (keep_row == 1) & (segment < CLIPS)
    same_clip = segment[:, None] == segment[None, :]
    return same_clip & (live_keys[None, :] | (positions[:, None] == positions[None, :]))


def band_matrix(diagonals):
    head_count = diagonals.shape[0]
    length = (diagonals.shape[1] + 1) // 2
    padded = jnp.concatenate([diagonals, jnp.zeros((head_count, 1), diagonals.dtype)], axis=1)
    repeated = jnp.tile(padded, (1, length))
    folded = repeated[:, : length * (2 * length - 1)].reshape(head_count, length, 2 * length - 1)
    return folded[:, :, length - 1 :]


def position_terms(head_inputs, gate_matrix, gate_offset, scale_local, table_local, rel_buckets):
    linear = (
        jnp.einsum(
            "blhd,dk->bhlk", head_inputs, gate_matrix.reshape(HD, 2), precision=FULL_PRECISION
        )
        + gate_offset
    )
    sigmoid = jax.nn.sigmoid(linear)
    gate = sigmoid[..., 0] * (sigmoid[..., 1] * scale_local[None, :, None] - 1.0) + 2.0
    onehot = (rel_buckets[:, None] == jnp.arange(NB, dtype=jnp.int32)[None, :]).astype(jnp.float32)
    per_offset = jnp.dot(
        onehot, table_local, precision=FULL_PRECISION, preferred_element_type=jnp.float32
    )
    toeplitz = band_matrix(per_offset.T)
    return gate[..., None] * toeplitz[None]


def adam_step(weights, moment, second, gradient, step_rate, decay_rate):
    moment_new = BETA_FIRST * moment + (1.0 - BETA_FIRST) * gradient
    second_new = BETA_SECOND * second + (1.0 - BETA_SECOND) * gradient * gradient
    moment_hat = moment_new / (1.0 - BETA_FIRST**STEP)
    second_hat = second_new / (1.0 - BETA_SECOND**STEP)
    master = weights - step_rate * (
        moment_hat / (jnp.sqrt(second_hat) + ADAM_EPSILON) + decay_rate * weights
    )
    return (moment_new, second_new, master)


def placed(total_length, piece, start):
    return lax.dynamic_update_slice_in_dim(jnp.zeros((total_length,), jnp.float32), piece, start, 0)


def column_sum(values):
    return jnp.sum(values.astype(jnp.float32), axis=0)


def general_body(
    tokens,
    cotangent,
    clip_lengths,
    key_mask,
    rel_buckets,
    attention_weights,
    attention_first,
    attention_second,
    feedforward_weights,
    feedforward_first,
    feedforward_second,
    small_params,
    small_first,
    small_second,
):
    gathered_attention, gathered_forward = (
        lax.all_gather(attention_weights.astype(jnp.bfloat16), "dp", axis=1, tiled=True),
        lax.all_gather(feedforward_weights.astype(jnp.bfloat16), "dp", axis=1, tiled=True),
    )
    query_weight = gathered_attention[0]
    key_weight = gathered_attention[1]
    value_weight = gathered_attention[2]
    output_weight = gathered_attention[3]
    up_weight = gathered_forward[0]
    down_weight = gathered_forward[1]
    head_cols = query_weight.shape[1]
    heads_local = head_cols // HD
    hidden_local = up_weight.shape[1]
    tensor_rank = lax.axis_index("tensor")
    col_start = tensor_rank * head_cols
    head_start = tensor_rank * heads_local
    hidden_start = tensor_rank * hidden_local
    row_count = tokens.shape[0]
    bucket_count = row_count // BUCKET_SLOTS
    (
        gain_one,
        shift_one,
        gain_two,
        shift_two,
        bias_query,
        bias_value,
        bias_output,
        bias_down,
        bias_up,
        rel_table,
        gate_matrix,
        gate_offset,
        gate_scale,
    ) = split_small(small_params)
    local_bias_query = lax.dynamic_slice_in_dim(bias_query, col_start, head_cols)
    local_bias_value = lax.dynamic_slice_in_dim(bias_value, col_start, head_cols)
    local_bias_up = lax.dynamic_slice_in_dim(bias_up, hidden_start, hidden_local)
    scale_local = lax.dynamic_slice_in_dim(gate_scale, head_start, heads_local)
    table_local = lax.dynamic_slice_in_dim(rel_table.reshape(NB, H), head_start, heads_local, 1)
    allowed = jax.vmap(allowed_mask)(clip_lengths, key_mask.reshape(bucket_count, BUCKET_SLOTS))[
        :, None
    ]
    leading = (tensor_rank == 0).astype(jnp.float32)
    inputs = tokens.astype(jnp.float32)
    upstream = cotangent.astype(jnp.float32)
    query_bf = (
        jnp.dot(tokens, query_weight, preferred_element_type=jnp.float32) + local_bias_query
    ).astype(jnp.bfloat16)
    key_bf = jnp.dot(tokens, key_weight, preferred_element_type=jnp.float32).astype(jnp.bfloat16)
    value_bf = (
        jnp.dot(tokens, value_weight, preferred_element_type=jnp.float32) + local_bias_value
    ).astype(jnp.bfloat16)
    head_shape = (bucket_count, BUCKET_SLOTS, heads_local, HD)
    heads_of_query = query_bf.reshape(head_shape)
    heads_of_key = key_bf.reshape(head_shape)
    heads_of_value = value_bf.reshape(head_shape)
    head_inputs = lax.dynamic_slice_in_dim(inputs, col_start, head_cols, 1).reshape(head_shape)
    extra, pull_position = jax.vjp(
        partial(position_terms, rel_buckets=rel_buckets),
        head_inputs,
        gate_matrix,
        gate_offset,
        scale_local,
        table_local,
    )
    attention_logits = (
        jnp.einsum(
            "blhd,bmhd->bhlm", heads_of_query, heads_of_key, preferred_element_type=jnp.float32
        )
        * 0.125
    )
    scores = jnp.where(allowed, attention_logits + extra, MASK_VALUE)
    row_max = jnp.max(scores, axis=-1, keepdims=True)
    exponent = jnp.exp(scores - row_max)
    denominator = jnp.sum(exponent, axis=-1, keepdims=True)
    log_total = row_max + jnp.log(denominator)
    probs_bf = (exponent / denominator).astype(jnp.bfloat16)
    context_bf = (
        jnp.einsum("bhlm,bmhd->blhd", probs_bf, heads_of_value, preferred_element_type=jnp.float32)
        .reshape(row_count, head_cols)
        .astype(jnp.bfloat16)
    )
    attention_part = jnp.einsum(
        "nw,dw->nd", context_bf, output_weight, preferred_element_type=jnp.float32
    )
    attention = lax.psum(attention_part, "tensor") + bias_output
    normed, pull_norm_one = jax.vjp(
        layer_norm, DEEP_ALPHA * inputs + attention, gain_one, shift_one
    )
    normed_bf = normed.astype(jnp.bfloat16)
    up_pre = jnp.dot(normed_bf, up_weight, preferred_element_type=jnp.float32) + local_bias_up
    activated, pull_gelu = jax.vjp(gelu_exact, up_pre)
    activated_bf = activated.astype(jnp.bfloat16)
    down_part = jnp.einsum(
        "nf,df->nd", activated_bf, down_weight, preferred_element_type=jnp.float32
    )
    feedforward = lax.psum(down_part, "tensor") + bias_down
    output_values, pull_norm_two = jax.vjp(
        layer_norm, DEEP_ALPHA * normed + feedforward, gain_two, shift_two
    )
    block_output = output_values.astype(jnp.bfloat16)
    grad_res_two, grad_gain_two, grad_shift_two = pull_norm_two(upstream)
    grad_ffn_share = grad_res_two.astype(jnp.bfloat16)
    grad_bias_down = column_sum(grad_ffn_share)
    down_grad = jnp.einsum(
        "nd,nf->df", grad_ffn_share, activated_bf, preferred_element_type=jnp.float32
    )
    grad_activated = jnp.einsum(
        "nd,df->nf", grad_ffn_share, down_weight, preferred_element_type=jnp.float32
    )
    (grad_up_pre,) = pull_gelu(grad_activated)
    grad_up_bf = grad_up_pre.astype(jnp.bfloat16)
    grad_bias_up = column_sum(grad_up_bf)
    up_grad = jnp.einsum("nd,nf->df", normed_bf, grad_up_bf, preferred_element_type=jnp.float32)
    normed_part = jnp.einsum("nf,df->nd", grad_up_bf, up_weight, preferred_element_type=jnp.float32)
    normed_sum = lax.psum(normed_part, "tensor")
    grad_normed = normed_sum + DEEP_ALPHA * grad_res_two
    grad_res_one, grad_gain_one, grad_shift_one = pull_norm_one(grad_normed)
    grad_attention_share = grad_res_one.astype(jnp.bfloat16)
    grad_bias_output = column_sum(grad_attention_share)
    output_grad = jnp.einsum(
        "nd,nw->dw", grad_attention_share, context_bf, preferred_element_type=jnp.float32
    )
    grad_context_bf = jnp.einsum(
        "nd,dw->nw", grad_attention_share, output_weight, preferred_element_type=jnp.float32
    ).astype(jnp.bfloat16)
    grad_heads = grad_context_bf.reshape(head_shape)
    attention_probabilities = jnp.exp(scores - log_total)
    recomputed_bf = attention_probabilities.astype(jnp.bfloat16)
    grad_probs = jnp.einsum(
        "blhd,bmhd->bhlm", grad_heads, heads_of_value, preferred_element_type=jnp.float32
    )
    inner = jnp.sum(grad_probs * attention_probabilities, axis=-1, keepdims=True)
    grad_scores_bf = (attention_probabilities * (grad_probs - inner)).astype(jnp.bfloat16)
    grad_query = (
        (
            jnp.einsum(
                "bhlm,bmhd->blhd", grad_scores_bf, heads_of_key, preferred_element_type=jnp.float32
            )
            * 0.125
        )
        .astype(jnp.bfloat16)
        .reshape(row_count, head_cols)
    )
    grad_key = (
        (
            jnp.einsum(
                "bhlm,blhd->bmhd",
                grad_scores_bf,
                heads_of_query,
                preferred_element_type=jnp.float32,
            )
            * 0.125
        )
        .astype(jnp.bfloat16)
        .reshape(row_count, head_cols)
    )
    grad_value = (
        jnp.einsum("bhlm,blhd->bmhd", recomputed_bf, grad_heads, preferred_element_type=jnp.float32)
        .astype(jnp.bfloat16)
        .reshape(row_count, head_cols)
    )
    grad_head_inputs, grad_gate_matrix, grad_gate_offset, grad_scale_local, grad_table_local = (
        pull_position(grad_scores_bf.astype(jnp.float32))
    )
    query_grad = jnp.einsum("nd,nw->dw", tokens, grad_query, preferred_element_type=jnp.float32)
    key_grad = jnp.einsum("nd,nw->dw", tokens, grad_key, preferred_element_type=jnp.float32)
    value_grad = jnp.einsum("nd,nw->dw", tokens, grad_value, preferred_element_type=jnp.float32)
    input_part = (
        jnp.einsum("nw,dw->nd", grad_query, query_weight, preferred_element_type=jnp.float32)
        + jnp.einsum("nw,dw->nd", grad_key, key_weight, preferred_element_type=jnp.float32)
        + jnp.einsum("nw,dw->nd", grad_value, value_weight, preferred_element_type=jnp.float32)
    )
    own_columns = lax.dynamic_slice_in_dim(input_part, col_start, head_cols, 1)
    input_part = lax.dynamic_update_slice_in_dim(
        input_part, own_columns + grad_head_inputs.reshape(row_count, head_cols), col_start, 1
    )
    grad_inputs = lax.psum(input_part, "tensor") + DEEP_ALPHA * grad_res_one
    tokens_grad = grad_inputs.astype(jnp.bfloat16)
    table_grad = lax.dynamic_update_slice_in_dim(
        jnp.zeros((NB, H), jnp.float32), grad_table_local, head_start, 1
    ).reshape(-1)
    local_small = jnp.concatenate(
        [
            grad_gain_one * leading,
            grad_shift_one * leading,
            grad_gain_two * leading,
            grad_shift_two * leading,
            placed(MODEL_WIDTH, column_sum(grad_query), col_start),
            placed(MODEL_WIDTH, column_sum(grad_value), col_start),
            grad_bias_output * leading,
            grad_bias_down * leading,
            placed(FF, grad_bias_up, hidden_start),
            table_grad,
            grad_gate_matrix,
            grad_gate_offset,
            placed(H, grad_scale_local, head_start),
        ]
    )
    small_grad = lax.psum(local_small, ("dp", "tensor"))
    local_attention = jnp.stack([query_grad, key_grad, value_grad, output_grad])
    local_forward = jnp.stack([up_grad, down_grad])
    summed_attention, summed_forward = lax.psum((local_attention, local_forward), "dp")
    owner_rank = lax.axis_index("dp")
    owned_rows = attention_weights.shape[1]
    share_attention = lax.dynamic_slice_in_dim(
        summed_attention, owner_rank * owned_rows, owned_rows, 1
    )
    share_forward = lax.dynamic_slice_in_dim(summed_forward, owner_rank * owned_rows, owned_rows, 1)
    share_squares = jnp.sum(share_attention * share_attention) + jnp.sum(
        share_forward * share_forward
    )
    big_squares = lax.psum(share_squares, ("dp", "tensor"))
    global_norm = jnp.sqrt(big_squares + jnp.sum(small_grad * small_grad))
    factor = CLIP_LIMIT / jnp.maximum(global_norm, CLIP_LIMIT)
    attention_moment, attention_square, attention_master = adam_step(
        attention_weights,
        attention_first,
        attention_second,
        factor * share_attention,
        RATE_MATRIX,
        WEIGHT_DECAY,
    )
    feedforward_moment, feedforward_square, feedforward_master = adam_step(
        feedforward_weights,
        feedforward_first,
        feedforward_second,
        factor * share_forward,
        RATE_MATRIX,
        WEIGHT_DECAY,
    )
    small_moment, small_square, small_master = adam_step(
        small_params, small_first, small_second, factor * small_grad, RATE_SMALL, 0.0
    )
    return (
        global_norm,
        attention_moment,
        attention_square,
        attention_master,
        attention_master.astype(jnp.bfloat16),
        feedforward_moment,
        feedforward_square,
        feedforward_master,
        feedforward_master.astype(jnp.bfloat16),
        small_moment,
        small_square,
        small_master,
        block_output,
        tokens_grad,
    )


F32 = jnp.float32
BF16 = jnp.bfloat16
MESH_ID = pl.DeviceIdType.MESH
LANES = 128
SMALL_ROWS = 104
TABLE_ROW = 72
GATE_ROW = 102
OFFSET_ROW = 103
INV_SQRT2 = 0.5**0.5
INV_SQRT_2PI = 0.3989422804014327
CHUNK = 128
HALF = 256
W = MODEL_WIDTH
NT = (((1,), (1,)), ((), ()))
TN = (((0,), (0,)), ((), ()))


def mm(a, b):
    return jnp.dot(a, b, preferred_element_type=F32)


def mm_nt(a, b):
    return lax.dot_general(a, b, NT, preferred_element_type=F32)


def mm_tn(a, b):
    return lax.dot_general(a, b, TN, preferred_element_type=F32)


def exact_nt(a, b):
    return lax.dot_general(a, b, NT, precision=FULL_PRECISION, preferred_element_type=F32)


def exact_tn(a, b):
    return lax.dot_general(a, b, TN, precision=FULL_PRECISION, preferred_element_type=F32)


def exact_mm(a, b):
    return jnp.dot(a, b, precision=FULL_PRECISION, preferred_element_type=F32)


def iota(shape, axis):
    return lax.broadcasted_iota(jnp.int32, shape, axis)


def layer_scratch(owned, nz, qkv_pad, heads, head_cols, hidden):
    rows = 2 * BUCKET_SLOTS
    out_pad = -(-head_cols // LANES) * LANES
    dma = pltpu.SemaphoreType.DMA
    vm = pltpu.VMEM
    steps = 2 * nz - 1
    shapes = dict(
        tok=vm((rows, W), BF16),
        cot=vm((2, HALF, W), BF16),
        wqkv=vm((W, qkv_pad), BF16),
        wo=vm((W, out_pad), BF16),
        wup=vm((W, hidden), BF16),
        wdown=vm((W, hidden), BF16),
        q=vm((rows, head_cols), BF16),
        k=vm((rows, head_cols), BF16),
        v=vm((rows, head_cols), BF16),
        ctx=vm((rows, head_cols), BF16),
        dctx=vm((rows, head_cols), BF16),
        dqkv=vm((rows, qkv_pad), BF16),
        prob=vm((2 * heads, BUCKET_SLOTS, BUCKET_SLOTS), F32),
        gsb=vm((heads, BUCKET_SLOTS, BUCKET_SLOTS), BF16),
        pbb=vm((heads, BUCKET_SLOTS, BUCKET_SLOTS), BF16),
        dqf=vm((BUCKET_SLOTS, head_cols), F32),
        mbias=vm((2, BUCKET_SLOTS, BUCKET_SLOTS), BF16),
        band=vm((heads, LANES, 2 * BUCKET_SLOTS), F32),
        dband=vm((heads, LANES, 2 * BUCKET_SLOTS), F32),
        gate=vm((rows, LANES), F32),
        gu=vm((rows, LANES), F32),
        gw=vm((rows, LANES), F32),
        dgate=vm((rows, LANES), F32),
        dlin=vm((rows, LANES), F32),
        gmat=vm((W, LANES), F32),
        vecs=vm((16, W), F32),
        acc=vm((16, W), F32),
        nb=vm((rows, W), BF16),
        held=vm((2, HALF, W), F32),
        xh1=vm((2, HALF, W), F32),
        rstd1=vm((2, HALF, LANES), F32),
        act=vm((rows, hidden), BF16),
        gelup=vm((rows, hidden), F32),
        gffn=vm((rows, W), BF16),
        gub=vm((rows, hidden), BF16),
        gattn=vm((rows, W), BF16),
        stage=vm((2, HALF, W), BF16),
        tstage=vm((2, HALF, W), BF16),
        ownf=vm((HALF, W), F32),
        cs=vm((2, HALF, W), BF16),
        cr=vm((2, HALF, W), BF16),
        ys=vm((2, HALF, W), BF16),
        yr=vm((2, 2, HALF, W), BF16),
        xrqkv=vm((nz, owned, qkv_pad), BF16),
        xro=vm((nz, owned, out_pad), BF16),
        xrup=vm((nz, owned, hidden), BF16),
        xrdown=vm((nz, owned, hidden), BF16),
        zsqkv=vm((nz - 1, owned, qkv_pad), BF16),
        zso=vm((nz - 1, owned, out_pad), BF16),
        zsup=vm((nz - 1, owned, hidden), BF16),
        zsdown=vm((nz - 1, owned, hidden), BF16),
        zrqkv=vm((nz - 1, owned, qkv_pad), BF16),
        zro=vm((nz - 1, owned, out_pad), BF16),
        zrup=vm((nz - 1, owned, hidden), BF16),
        zrdown=vm((nz - 1, owned, hidden), BF16),
        sm=vm((4, SMALL_ROWS, LANES), F32),
        smr=vm((3, SMALL_ROWS, LANES), F32),
        smz=vm((nz, SMALL_ROWS, LANES), F32),
        sqt=vm((4, 8, LANES), F32),
        sqd=vm((2 * nz, 8, LANES), F32),
        s_in=dma((3,)),
        s_gs=dma((4, steps)),
        s_gr=dma((4, steps)),
        s_cs=dma((4, 2)),
        s_cr=dma((4, 2)),
        s_ys=dma((4, 2)),
        s_yr=dma((4, 2)),
        s_as=dma((3, 2)),
        s_ar=dma((3, 2)),
        s_ol=dma((2, 2)),
        s_os=dma((2, 2)),
        s_or=dma((2, 2)),
        s_xs=dma((4, nz)),
        s_xr=dma((4, nz)),
        s_zs=dma((4, nz)),
        s_zr=dma((4, nz)),
        s_ms=dma((3 + nz,)),
        s_mr=dma((3 + nz,)),
        s_ts=dma((4,)),
        s_tr=dma((4,)),
        s_ds=dma((2 * nz,)),
        s_dr=dma((2 * nz,)),
    )
    return shapes


def layer_kernel(names, dims, *refs):
    n_dp, owned, qkv_pad, heads, head_cols, hidden = dims
    nz = n_dp // 2
    (tok_in, cot_in, lens, keep, relb, wa, wf, small) = refs[:8]
    (bo_out, tg_out, sh_qkv, sh_o, sh_up, sh_down, small_out, norm_out) = refs[8:16]
    m = SimpleNamespace(**dict(zip(names, refs[16:], strict=True)))
    D = lax.axis_index("dp")
    T = lax.axis_index("tensor")
    z = lax.div(D, 2)
    x = lax.rem(D, 2)
    c = lax.rem(T, 2)
    yy = lax.div(T, 2)
    core_dev = (D, T + 1 - 2 * c)
    y_dev = (D, lax.rem(T + 2, 4))
    x_dev = (z * 2 + 1 - x, T)

    def z_at(k):
        return lax.rem(z + k, nz)

    def z_dev(k):
        return (z_at(k) * 2 + x, T)

    def remote(src, dst, ss, rs, dev):
        return pltpu.make_async_remote_copy(
            src_ref=src, dst_ref=dst, send_sem=ss, recv_sem=rs, device_id=dev, device_id_type=MESH_ID
        )

    def loop(n, step):
        def run(i, carry):
            step(i)
            return carry

        lax.fori_loop(0, n, run, 0)

    def block(owner):
        return pl.ds(pl.multiple_of(owner * owned, owned), owned)

    tok_copy = pltpu.make_async_copy(tok_in, m.tok, m.s_in.at[0])
    tok_copy.start()
    cot_copies = []
    for b in range(2):
        rows = pl.ds(pl.multiple_of(b * BUCKET_SLOTS + c * HALF, HALF), HALF)
        cp = pltpu.make_async_copy(cot_in.at[rows], m.cot.at[b], m.s_in.at[1 + b])
        cp.start()
        cot_copies.append(cp)
    barrier = pltpu.get_barrier_semaphore()
    for k in range(1, 4):
        pl.semaphore_signal(barrier, inc=1, device_id=(D, lax.rem(T + k, 4)), device_id_type=MESH_ID)
    for k in range(1, n_dp):
        pl.semaphore_signal(barrier, inc=1, device_id=(lax.rem(D + k, n_dp), T), device_id_type=MESH_ID)
    mine = block(D)
    qkv_own = [wa[0], wa[1], wa[2]]
    if qkv_pad > 3 * head_cols:
        qkv_own.append(jnp.zeros((owned, qkv_pad - 3 * head_cols), F32))
    m.wqkv[mine, :] = jnp.concatenate(qkv_own, axis=1).astype(BF16)
    out_pad = m.wo.shape[1]
    o_own = [wa[3]]
    if out_pad > head_cols:
        o_own.append(jnp.zeros((owned, out_pad - head_cols), F32))
    m.wo[mine, :] = jnp.concatenate(o_own, axis=1).astype(BF16)
    m.wup[mine, :] = wf[0].astype(BF16)
    m.wdown[mine, :] = wf[1].astype(BF16)
    pl.semaphore_wait(barrier, 3 + n_dp - 1)

    def gather_start(which, buf):
        own = buf.at[mine]
        sent = []
        for k in range(1, nz):
            sent.append(
                remote(own, own, m.s_gs.at[which, k], m.s_gr.at[which, nz - k], z_dev(k))
            )
        sent.append(remote(own, own, m.s_gs.at[which, 0], m.s_gr.at[which, 0], x_dev))
        for cp in sent:
            cp.start()
        gathers[which] = sent

    def gather_pass(which, buf):
        sent = gathers[which]
        for j in range(1, nz):
            part = buf.at[block(z_at(j) * 2 + x)]
            remote(part, part, m.s_gs.at[which, j], m.s_gr.at[which, j], x_dev).wait_recv()
            cp = remote(
                part, part, m.s_gs.at[which, nz - 1 + j], m.s_gr.at[which, nz - 1 + j], x_dev
            )
            cp.start()
            sent.append(cp)

    def gather_end(which, buf):
        for j in range(nz):
            part = buf.at[block(z_at(j) * 2 + 1 - x)]
            index = 0 if j == 0 else nz - 1 + j
            remote(
                part, part, m.s_gs.at[which, index], m.s_gr.at[which, index], x_dev
            ).wait_recv()

    gathers = {}
    gather_start(0, m.wqkv)

    def small_row(first, count):
        return jnp.concatenate([small[first + i : first + i + 1, :] for i in range(count)], axis=1)

    def pick(values, size):
        total = jnp.zeros((1, size), F32)
        for t in range(4):
            total = total + jnp.where(T == t, values[:, t * size : (t + 1) * size], 0.0)
        return total

    vecs = m.vecs
    vecs[...] = jnp.zeros_like(vecs)
    m.acc[...] = jnp.zeros((16, W), F32)
    for at, first in ((0, 0), (1, 6), (2, 12), (3, 18), (4, 36), (5, 42)):
        vecs[at : at + 1, :] = small_row(first, W // LANES)
    vecs[6:7, :] = pick(small_row(48, FF // LANES), hidden)
    bq = pick(small_row(24, W // LANES), head_cols)
    bv = pick(small_row(30, W // LANES), head_cols)
    bias_qkv = jnp.concatenate(
        [bq, jnp.zeros_like(bq), bv, jnp.zeros((1, qkv_pad - 3 * head_cols), F32)], axis=1
    )
    vecs[7:8, 0:qkv_pad] = bias_qkv

    lane = iota((1, LANES), 1)
    col = iota((W, LANES), 0)
    col_lane = iota((W, LANES), 1)
    gate_row = small[GATE_ROW : GATE_ROW + 1, :]
    col_in_head = lax.rem(col, HD)
    picked_u = jnp.sum(
        jnp.where(col_lane == 2 * col_in_head, gate_row, 0.0), axis=1, keepdims=True
    )
    picked_w = jnp.sum(
        jnp.where(col_lane == 2 * col_in_head + 1, gate_row, 0.0), axis=1, keepdims=True
    )
    in_group = lax.rem(col_lane, 8)
    own_head = (col_lane < 16) & (in_group < heads) & (lax.div(col, HD) == T * heads + in_group)
    m.gmat[...] = jnp.where(own_head, jnp.where(col_lane < 8, picked_u, picked_w), 0.0)
    offset_row = small[OFFSET_ROW : OFFSET_ROW + 1, :]
    offset_u = jnp.sum(jnp.where(lane == 0, offset_row, 0.0), axis=1, keepdims=True)
    offset_w = jnp.sum(jnp.where(lane == 1, offset_row, 0.0), axis=1, keepdims=True)
    scale = jnp.zeros((1, LANES), F32)
    for h in range(heads):
        one = jnp.sum(jnp.where(lane == 2 + T * heads + h, offset_row, 0.0), axis=1, keepdims=True)
        scale = scale + jnp.where(lane == h, one, 0.0)
    head_lane = lane < heads

    offsets = jnp.concatenate([relb[i : i + 1, :] for i in range(2 * BUCKET_SLOTS // LANES)], axis=1)
    table = small[TABLE_ROW : TABLE_ROW + 32, :]
    long_row = 2 * BUCKET_SLOTS
    sub8 = iota((8, long_row), 0)
    for h in range(heads):
        flat = offsets * H + (T * heads + h)
        at_row = lax.div(flat, LANES)
        at_lane = lax.rem(flat, LANES)
        hot_row = jnp.where(iota((32, long_row), 0) == at_row, 1.0, 0.0)
        spread = exact_tn(table, hot_row)
        values = jnp.sum(
            jnp.where(iota((LANES, long_row), 0) == at_lane, spread, 0.0), axis=0, keepdims=True
        )
        stack = jnp.broadcast_to(pltpu.roll(jnp.broadcast_to(values, (8, long_row)), 1, 1), (8, long_row))
        for bit in (1, 2, 4):
            stack = jnp.where(lax.rem(lax.div(sub8, bit), 2) == 1, pltpu.roll(stack, bit, 1), stack)
        size = 8
        m.band[h, 0:8, :] = stack
        while size < LANES:
            m.band[h, size : 2 * size, :] = pltpu.roll(m.band[h, 0:size, :], size, 1)
            size *= 2
    m.dband[...] = jnp.zeros(m.dband.shape, F32)

    for b in range(2):
        end = 0
        ends = []
        for i in range(CLIPS):
            end = end + lens[b, i]
            ends.append(end)
        key_at = iota((1, BUCKET_SLOTS), 1)
        key_segment = jnp.zeros((1, BUCKET_SLOTS), jnp.int32)
        for end in ends:
            key_segment = key_segment + jnp.where(key_at >= end, 1, 0)
        kept = jnp.concatenate([keep[4 * b + i : 4 * b + i + 1, :] for i in range(4)], axis=1)
        live = jnp.where((kept == 1) & (key_segment < CLIPS), key_segment, -1)

        def mask_chunk(i, b=b, ends=ends, live=live):
            query_at = iota((CHUNK, BUCKET_SLOTS), 0) + i * CHUNK
            segment = jnp.zeros((CHUNK, BUCKET_SLOTS), jnp.int32)
            for end in ends:
                segment = segment + jnp.where(query_at >= end, 1, 0)
            allowed = (segment == live) | (query_at == iota((CHUNK, BUCKET_SLOTS), 1))
            m.mbias[b, pl.ds(pl.multiple_of(i * CHUNK, CHUNK), CHUNK), :] = jnp.where(
                allowed, 0.0, MASK_VALUE
            ).astype(BF16)

        loop(BUCKET_SLOTS // CHUNK, mask_chunk)

    tok_copy.wait()
    gmat = m.gmat[...]
    part_hi = gmat.astype(BF16)
    rest = gmat - part_hi.astype(F32)
    part_mid = rest.astype(BF16)
    part_lo = (rest - part_mid.astype(F32)).astype(BF16)

    def gate_chunk(i):
        rows = pl.ds(pl.multiple_of(i * HALF, HALF), HALF)
        tokens = m.tok[rows, :]
        linear = mm(tokens, part_hi) + mm(tokens, part_mid) + mm(tokens, part_lo)
        u = jax.nn.sigmoid(linear + offset_u)
        w = jax.nn.sigmoid(pltpu.roll(linear, LANES - 8, 1) + offset_w)
        m.gu[rows, :] = u
        m.gw[rows, :] = w
        m.gate[rows, :] = u * (w * scale - 1.0) + 2.0

    loop(4, gate_chunk)

    gather_pass(0, m.wqkv)
    gather_end(0, m.wqkv)
    gather_start(1, m.wo)
    gather_start(2, m.wup)
    gather_start(3, m.wdown)

    def project(i):
        rows = pl.ds(pl.multiple_of(i * HALF, HALF), HALF)
        both = mm(m.tok[rows, :], m.wqkv[...]) + vecs[7:8, 0:qkv_pad]
        query = both[:, 0:head_cols].astype(BF16)
        m.q[rows, :] = (query.astype(F32) * 0.125).astype(BF16)
        m.k[rows, :] = both[:, head_cols : 2 * head_cols].astype(BF16)
        m.v[rows, :] = both[:, 2 * head_cols : 3 * head_cols].astype(BF16)

    loop(4, project)

    head_of = lax.div(iota((1, head_cols), 1), HD)
    head_masks = [jnp.where(head_of == h, 1.0, 0.0) for h in range(heads)]
    low_masks = [m.astype(BF16) for m in head_masks]

    def attend(b):
        keys = m.k[b * BUCKET_SLOTS : (b + 1) * BUCKET_SLOTS, :]
        values = m.v[b * BUCKET_SLOTS : (b + 1) * BUCKET_SLOTS, :]

        def chunk(i):
            local = pl.ds(pl.multiple_of(i * CHUNK, CHUNK), CHUNK)
            rows = pl.ds(pl.multiple_of(b * BUCKET_SLOTS + i * CHUNK, CHUNK), CHUNK)
            window = pl.ds(pl.multiple_of(BUCKET_SLOTS - i * CHUNK, CHUNK), BUCKET_SLOTS)
            query = m.q[rows, :]
            gates = m.gate[rows, :]
            context = jnp.zeros((CHUNK, head_cols), F32)
            for h in range(heads):
                scores = mm_nt(query * low_masks[h], keys)
                scores = scores + gates[:, h : h + 1] * m.band[h, :, window]
                scores = scores + m.mbias[b, local, :].astype(F32)
                top = jnp.max(scores, axis=1, keepdims=True)
                weight = jnp.exp(scores - top)
                total = jnp.sum(weight, axis=1, keepdims=True)
                probability = weight * (1.0 / total)
                m.prob[b * heads + h, local, :] = probability
                context = context + mm(probability.astype(BF16), values) * head_masks[h]
            m.ctx[rows, :] = context.astype(BF16)

        loop(BUCKET_SLOTS // CHUNK, chunk)

    core_sent = {}
    y_sent = {}

    def exchange(phase, b, product):
        other = b * BUCKET_SLOTS + (1 - c) * HALF
        own = b * BUCKET_SLOTS + c * HALF
        if (phase - 1, b) in core_sent:
            core_sent[(phase - 1, b)].wait_send()
            y_sent[(phase - 1, b)].wait_send()

        def send_chunk(i):
            at = pl.ds(pl.multiple_of(i * CHUNK, CHUNK), CHUNK)
            rows = pl.ds(pl.multiple_of(other + i * CHUNK, CHUNK), CHUNK)
            m.cs[b, at, :] = product(rows).astype(BF16)

        loop(HALF // CHUNK, send_chunk)
        cp = remote(
            m.cs.at[b], m.cr.at[b], m.s_cs.at[phase, b], m.s_cr.at[phase, b], core_dev
        )
        cp.start()
        core_sent[(phase, b)] = cp

        def own_chunk(i):
            at = pl.ds(pl.multiple_of(i * CHUNK, CHUNK), CHUNK)
            rows = pl.ds(pl.multiple_of(own + i * CHUNK, CHUNK), CHUNK)
            m.ownf[at, :] = product(rows)

        loop(HALF // CHUNK, own_chunk)
        cp.wait_recv()

        def add_chunk(i):
            at = pl.ds(pl.multiple_of(i * CHUNK, CHUNK), CHUNK)
            m.ys[b, at, :] = (m.ownf[at, :] + m.cr[b, at, :].astype(F32)).astype(BF16)

        loop(HALF // CHUNK, add_chunk)
        cp = remote(
            m.ys.at[b],
            m.yr.at[phase % 2, b],
            m.s_ys.at[phase, b],
            m.s_yr.at[phase, b],
            y_dev,
        )
        cp.start()
        y_sent[(phase, b)] = cp

    def arrived(phase, b, at):
        return m.ys[b, at, :].astype(F32) + m.yr[phase % 2, b, at, :].astype(F32)

    def own_rows(b, i):
        return pl.ds(pl.multiple_of(b * BUCKET_SLOTS + c * HALF + i * CHUNK, CHUNK), CHUNK)

    core_spread = {}

    def spread_start(which, buf, b):
        rows = pl.ds(pl.multiple_of(b * BUCKET_SLOTS + c * HALF, HALF), HALF)
        part = buf.at[rows]
        cp = remote(part, part, m.s_as.at[which, b], m.s_ar.at[which, b], core_dev)
        cp.start()
        core_spread[(which, b)] = cp

    def spread_end(which, b):
        core_spread[(which, b)].wait_recv()

    def row_mean(values):
        return jnp.mean(values, axis=1, keepdims=True)

    def add_row(at, values):
        m.acc[at : at + 1, 0 : values.shape[1]] += jnp.sum(values, axis=0, keepdims=True)

    def norm_one(b):
        y_sent[(0, b)].wait_recv()

        def chunk(i):
            at = pl.ds(pl.multiple_of(i * CHUNK, CHUNK), CHUNK)
            rows = own_rows(b, i)
            residual = DEEP_ALPHA * m.tok[rows, :].astype(F32) + (arrived(0, b, at) + vecs[4:5, :])
            centred = residual - row_mean(residual)
            rstd = lax.rsqrt(row_mean(centred * centred) + NORM_EPSILON)
            hat = centred * rstd
            normed = hat * vecs[0:1, :] + vecs[1:2, :]
            m.xh1[b, at, :] = hat
            m.rstd1[b, at, :] = jnp.broadcast_to(rstd, (CHUNK, LANES))
            m.held[b, at, :] = normed
            m.nb[rows, :] = normed.astype(BF16)

        loop(HALF // CHUNK, chunk)
        spread_start(0, m.nb, b)

    def feed(b):
        spread_end(0, b)

        def chunk(i):
            rows = pl.ds(pl.multiple_of(b * BUCKET_SLOTS + i * CHUNK, CHUNK), CHUNK)
            up = mm(m.nb[rows, :], m.wup[...]) + vecs[6:7, :]
            half_phi = 0.5 * (1.0 + lax.erf(up * INV_SQRT2))
            m.act[rows, :] = (up * half_phi).astype(BF16)
            m.gelup[rows, :] = half_phi + up * (jnp.exp(up * up * -0.5) * INV_SQRT_2PI)

        loop(BUCKET_SLOTS // CHUNK, chunk)

    out_copies = []

    def result_rows(which, b, stage, out):
        rows = pl.ds(pl.multiple_of(b * BUCKET_SLOTS + c * HALF, HALF), HALF)
        part = stage.at[b]
        here = pltpu.make_async_copy(part, out.at[rows], m.s_ol.at[which, b])
        there = remote(part, out.at[rows], m.s_os.at[which, b], m.s_or.at[which, b], core_dev)
        here.start()
        there.start()
        out_copies.append((here, there))

    def norm_two(b):
        y_sent[(1, b)].wait_recv()
        cot_copies[b].wait()

        def chunk(i):
            at = pl.ds(pl.multiple_of(i * CHUNK, CHUNK), CHUNK)
            rows = own_rows(b, i)
            residual = DEEP_ALPHA * m.held[b, at, :] + (arrived(1, b, at) + vecs[5:6, :])
            centred = residual - row_mean(residual)
            rstd = lax.rsqrt(row_mean(centred * centred) + NORM_EPSILON)
            hat = centred * rstd
            m.stage[b, at, :] = (hat * vecs[2:3, :] + vecs[3:4, :]).astype(BF16)
            upstream = m.cot[b, at, :].astype(F32)
            add_row(2, upstream * hat)
            add_row(3, upstream)
            scaled = upstream * vecs[2:3, :]
            grad = rstd * (scaled - row_mean(scaled) - hat * row_mean(scaled * hat))
            m.held[b, at, :] = grad
            low = grad.astype(BF16)
            m.gffn[rows, :] = low
            add_row(5, low.astype(F32))

        loop(HALF // CHUNK, chunk)
        spread_start(1, m.gffn, b)
        result_rows(0, b, m.stage, bo_out)

    def feed_back(b):
        spread_end(1, b)

        def chunk(i):
            rows = pl.ds(pl.multiple_of(b * BUCKET_SLOTS + i * CHUNK, CHUNK), CHUNK)
            grad = mm(m.gffn[rows, :], m.wdown[...]) * m.gelup[rows, :]
            low = grad.astype(BF16)
            m.gub[rows, :] = low
            add_row(6, low.astype(F32))

        loop(BUCKET_SLOTS // CHUNK, chunk)

    def norm_one_back(b):
        y_sent[(2, b)].wait_recv()

        def chunk(i):
            at = pl.ds(pl.multiple_of(i * CHUNK, CHUNK), CHUNK)
            rows = own_rows(b, i)
            upstream = arrived(2, b, at) + DEEP_ALPHA * m.held[b, at, :]
            hat = m.xh1[b, at, :]
            add_row(0, upstream * hat)
            add_row(1, upstream)
            scaled = upstream * vecs[0:1, :]
            rstd = m.rstd1[b, at, 0:1]
            grad = rstd * (scaled - row_mean(scaled) - hat * row_mean(scaled * hat))
            m.held[b, at, :] = grad
            low = grad.astype(BF16)
            m.gattn[rows, :] = low
            add_row(4, low.astype(F32))

        loop(HALF // CHUNK, chunk)
        spread_start(2, m.gattn, b)

    def attend_back(b):
        spread_end(2, b)
        keys = m.k[b * BUCKET_SLOTS : (b + 1) * BUCKET_SLOTS, :]
        values = m.v[b * BUCKET_SLOTS : (b + 1) * BUCKET_SLOTS, :]

        def chunk(i):
            local = pl.ds(pl.multiple_of(i * CHUNK, CHUNK), CHUNK)
            rows = pl.ds(pl.multiple_of(b * BUCKET_SLOTS + i * CHUNK, CHUNK), CHUNK)
            window = pl.ds(pl.multiple_of(BUCKET_SLOTS - i * CHUNK, CHUNK), BUCKET_SLOTS)
            place = pl.ds(pl.multiple_of(3 * CHUNK - i * CHUNK, CHUNK), BUCKET_SLOTS)
            grad_context = mm(m.gattn[rows, :], m.wo[:, 0:head_cols]).astype(BF16)
            m.dctx[rows, :] = grad_context
            gates = m.gate[rows, :]
            grad_query = jnp.zeros((CHUNK, head_cols), F32)
            grad_gates = jnp.zeros((CHUNK, LANES), F32)
            for h in range(heads):
                grad_probs = mm_nt(grad_context * low_masks[h], values)
                probability = m.prob[b * heads + h, local, :]
                m.pbb[h, local, :] = probability.astype(BF16)
                inner = jnp.sum(grad_probs * probability, axis=1, keepdims=True)
                low = (probability * (grad_probs - inner)).astype(BF16)
                m.gsb[h, local, :] = low
                grad_query = grad_query + mm(low, keys) * head_masks[h]
                rounded = low.astype(F32)
                one = jnp.sum(rounded * m.band[h, :, window], axis=1, keepdims=True)
                grad_gates = grad_gates + jnp.where(lane == h, one, 0.0)
                m.dband[h, :, place] += rounded * gates[:, h : h + 1]
            m.dqf[local, :] = grad_query * 0.125
            m.dgate[rows, :] = grad_gates

        loop(BUCKET_SLOTS // CHUNK, chunk)
        all_rows = slice(b * BUCKET_SLOTS, (b + 1) * BUCKET_SLOTS)
        grad_key = jnp.zeros((BUCKET_SLOTS, head_cols), F32)
        grad_value = jnp.zeros((BUCKET_SLOTS, head_cols), F32)
        for h in range(heads):
            grad_key = grad_key + mm_tn(m.gsb[h], m.q[all_rows, :]) * head_masks[h]
            grad_value = grad_value + mm_tn(m.pbb[h], m.dctx[all_rows, :]) * head_masks[h]
        pieces = [m.dqf[...], grad_key, grad_value]
        if qkv_pad > 3 * head_cols:
            pieces.append(jnp.zeros((BUCKET_SLOTS, qkv_pad - 3 * head_cols), F32))
        low = jnp.concatenate(pieces, axis=1).astype(BF16)
        m.dqkv[all_rows, :] = low
        add_row(7, low.astype(F32))

        def gate_back(i):
            rows = pl.ds(pl.multiple_of(b * BUCKET_SLOTS + i * CHUNK, CHUNK), CHUNK)
            grad = m.dgate[rows, :]
            u = m.gu[rows, :]
            w = m.gw[rows, :]
            grad_u = grad * (w * scale - 1.0) * u * (1.0 - u)
            grad_w = grad * u * scale * w * (1.0 - w)
            grad_u = jnp.where(head_lane, grad_u, 0.0)
            grad_w = jnp.where(head_lane, grad_w, 0.0)
            m.dlin[rows, :] = grad_u + pltpu.roll(grad_w, 8, 1)
            add_row(8, jnp.where(head_lane, grad * u * w, 0.0))

        loop(BUCKET_SLOTS // CHUNK, gate_back)

    def input_part(rows):
        return mm_nt(m.dqkv[rows, :], m.wqkv[...]) + exact_nt(m.dlin[rows, :], m.gmat[...])

    def token_rows(b):
        y_sent[(3, b)].wait_recv()

        def chunk(i):
            at = pl.ds(pl.multiple_of(i * CHUNK, CHUNK), CHUNK)
            total = arrived(3, b, at) + DEEP_ALPHA * m.held[b, at, :]
            m.tstage[b, at, :] = total.astype(BF16)

        loop(HALF // CHUNK, chunk)
        result_rows(1, b, m.tstage, tg_out)

    def weight_grad(which, buf, left, right, width):
        for cp in gathers.pop(which):
            cp.wait_send()

        def chunk(i):
            cols = pl.ds(pl.multiple_of(i * HALF, HALF), HALF)
            part = mm_tn(left[:, cols], right[...])
            if width < buf.shape[1]:
                part = jnp.concatenate([part, jnp.zeros((HALF, buf.shape[1] - width), F32)], axis=1)
            buf[cols, :] = part.astype(BF16)

        loop(W // HALF, chunk)

    reduces = []

    def reduce_start(which, buf, land):
        for zt in range(nz):
            cp = remote(
                buf.at[block(2 * zt + 1 - x)],
                land.at[zt],
                m.s_xs.at[which, zt],
                m.s_xr.at[which, zt],
                x_dev,
            )
            cp.start()
            reduces.append(cp)

    def reduce_pass(which, buf, land, out, arrive, share):
        for k in list(range(1, nz)) + [0]:
            zt = z_at(k)
            here = land.at[zt]
            remote(here, here, m.s_xs.at[which, zt], m.s_xr.at[which, zt], x_dev).wait_recv()
            total = buf[block(2 * zt + x), :].astype(F32) + land[zt].astype(F32)
            if k == 0:
                share[...] = total
            else:
                out[k - 1] = total.astype(BF16)
                cp = remote(
                    out.at[k - 1],
                    arrive.at[k - 1],
                    m.s_zs.at[which, k],
                    m.s_zr.at[which, k],
                    z_dev(k),
                )
                cp.start()
                reduces.append(cp)

    def reduce_end(which, arrive, share):
        total = share[...]
        for k in range(1, nz):
            here = arrive.at[k - 1]
            remote(here, here, m.s_zs.at[which, k], m.s_zr.at[which, k], z_dev(k)).wait_recv()
            total = total + arrive[k - 1].astype(F32)
        share[...] = total
        squares = total * total
        folded = jnp.zeros((owned, LANES), F32)
        for i in range(total.shape[1] // LANES):
            folded = folded + squares[:, i * LANES : (i + 1) * LANES]
        tile = jnp.zeros((8, LANES), F32)
        for i in range(owned // 8):
            tile = tile + folded[8 * i : 8 * i + 8, :]
        return tile

    attend(0)
    gather_pass(1, m.wo)
    gather_end(1, m.wo)
    out_product = lambda rows: mm_nt(m.ctx[rows, :], m.wo[:, 0:head_cols])
    exchange(0, 0, out_product)
    attend(1)
    gather_pass(2, m.wup)
    exchange(0, 1, out_product)
    gather_pass(3, m.wdown)
    norm_one(0)
    gather_end(2, m.wup)
    feed(0)
    gather_end(3, m.wdown)
    down_product = lambda rows: mm_nt(m.act[rows, :], m.wdown[...])
    exchange(1, 0, down_product)
    norm_one(1)
    feed(1)
    exchange(1, 1, down_product)
    up_product = lambda rows: mm_nt(m.gub[rows, :], m.wup[...])
    norm_two(0)
    feed_back(0)
    exchange(2, 0, up_product)
    norm_two(1)
    feed_back(1)
    exchange(2, 1, up_product)
    weight_grad(3, m.wdown, m.gffn, m.act, hidden)
    reduce_start(0, m.wdown, m.xrdown)
    weight_grad(2, m.wup, m.nb, m.gub, hidden)
    reduce_start(1, m.wup, m.xrup)
    norm_one_back(0)
    attend_back(0)
    exchange(3, 0, input_part)
    reduce_pass(0, m.wdown, m.xrdown, m.zsdown, m.zrdown, sh_down)
    norm_one_back(1)
    attend_back(1)
    exchange(3, 1, input_part)
    weight_grad(0, m.wqkv, m.tok, m.dqkv, qkv_pad)
    reduce_start(3, m.wqkv, m.xrqkv)
    reduce_pass(1, m.wup, m.xrup, m.zsup, m.zrup, sh_up)
    weight_grad(1, m.wo, m.gattn, m.ctx, head_cols)
    reduce_start(2, m.wo, m.xro)

    sm = m.sm
    acc = m.acc
    lead = jnp.where(yy == 0, 1.0, 0.0)

    def put(first, values):
        for i in range(values.shape[1] // LANES):
            sm[0, first + i : first + i + 1, :] = values[:, i * LANES : (i + 1) * LANES]

    def spot(values):
        return jnp.concatenate([jnp.where(T == t, values, 0.0) for t in range(4)], axis=1)

    for at, first in ((0, 0), (1, 6), (2, 12), (3, 18), (4, 36), (5, 42)):
        put(first, acc[at : at + 1, :] * lead)
    put(24, spot(acc[7:8, 0:head_cols]))
    put(30, spot(acc[7:8, 2 * head_cols : 3 * head_cols]))
    put(48, spot(acc[6:7, 0:hidden]))
    table_grad = jnp.zeros((32, LANES), F32)
    for h in range(heads):
        size = LANES // 2
        left = m.dband[h]
        while size >= 1:
            left = left[0:size, :] + pltpu.roll(left[size : 2 * size, :], long_row - size, 1) if size >= 8 else left
            if size < 8:
                break
            size //= 2
        for bit in (1, 2, 4):
            left = jnp.where(lax.rem(lax.div(sub8, bit), 2) == 1, pltpu.roll(left, long_row - bit, 1), left)
        diagonal = jnp.sum(left, axis=0, keepdims=True)
        diagonal = pltpu.roll(jnp.broadcast_to(diagonal, (8, long_row)), LANES - 1, 1)[0:1, :]
        flat = offsets * H + (T * heads + h)
        at_row = lax.div(flat, LANES)
        at_lane = lax.rem(flat, LANES)
        valid = iota((1, long_row), 1) < long_row - 1
        hot_row = jnp.where((iota((32, long_row), 0) == at_row) & valid, 1.0, 0.0)
        hot_lane = jnp.where(iota((LANES, long_row), 0) == at_lane, diagonal, 0.0)
        table_grad = table_grad + exact_nt(hot_row, hot_lane)
    sm[0, TABLE_ROW : TABLE_ROW + 30, :] = table_grad[0:30, :]

    lin = m.dlin[...]
    lin_hi = lin.astype(BF16)
    lin_rest = lin - lin_hi.astype(F32)
    lin_mid = lin_rest.astype(BF16)
    lin_lo = (lin_rest - lin_mid.astype(F32)).astype(BF16)
    lin_grad = mm_tn(lin_hi, m.tok[...]) + mm_tn(lin_mid, m.tok[...]) + mm_tn(lin_lo, m.tok[...])
    group = iota((16, W), 0)
    mine_here = (lax.rem(group, 8) < heads) & (
        lax.div(iota((16, W), 1), HD) == T * heads + lax.rem(group, 8)
    )
    lin_grad = jnp.where(mine_here, lin_grad[0:16, :], 0.0)
    hot = jnp.where(lax.rem(col, HD) == lax.div(col_lane, 2), 1.0, 0.0)
    folded = exact_mm(lin_grad, hot)
    by_lane = jnp.where(
        lax.rem(lane, 2) == 0,
        jnp.sum(folded[0:8, :], axis=0, keepdims=True),
        jnp.sum(folded[8:16, :], axis=0, keepdims=True),
    )
    sm[0, GATE_ROW : GATE_ROW + 1, :] = by_lane
    lin_total = jnp.sum(lin, axis=0, keepdims=True)
    total_u = jnp.sum(jnp.where(lane < 8, lin_total, 0.0), axis=1, keepdims=True)
    total_w = jnp.sum(jnp.where((lane >= 8) & (lane < 16), lin_total, 0.0), axis=1, keepdims=True)
    last = jnp.where(lane == 0, total_u, 0.0) + jnp.where(lane == 1, total_w, 0.0)
    scale_grad = acc[8:9, 0:LANES]
    for h in range(heads):
        one = jnp.sum(jnp.where(lane == h, scale_grad, 0.0), axis=1, keepdims=True)
        last = last + jnp.where(lane == 2 + T * heads + h, one, 0.0)
    sm[0, OFFSET_ROW : OFFSET_ROW + 1, :] = last

    small_sent = []

    def small_step(at, dev):
        cp = remote(sm.at[at], m.smr.at[at], m.s_ms.at[at], m.s_mr.at[at], dev)
        cp.start()
        small_sent.append(cp)
        return cp

    token_rows(0)
    small_copy = small_step(0, core_dev)
    small_copy.wait_recv()
    sm[1] = sm[0] + m.smr[0]
    small_copy = small_step(1, y_dev)
    reduce_pass(3, m.wqkv, m.xrqkv, m.zsqkv, m.zrqkv, sh_qkv)
    small_copy.wait_recv()
    sm[2] = sm[1] + m.smr[1]
    small_copy = small_step(2, x_dev)
    reduce_pass(2, m.wo, m.xro, m.zso, m.zro, sh_o)
    token_rows(1)
    small_copy.wait_recv()
    sm[3] = sm[2] + m.smr[2]
    for k in range(1, nz):
        cp = remote(
            sm.at[3], m.smz.at[z], m.s_ms.at[2 + k], m.s_mr.at[2 + k], z_dev(k)
        )
        cp.start()
        small_sent.append(cp)
    m.smz[z] = sm[3]
    squares = reduce_end(0, m.zrdown, sh_down)
    squares = squares + reduce_end(1, m.zrup, sh_up)
    squares = squares + reduce_end(2, m.zro, sh_o)
    squares = squares + reduce_end(3, m.zrqkv, sh_qkv)
    sqt = m.sqt
    sqt[T] = squares
    tail_sent = []
    for k in range(1, 4):
        cp = remote(
            sqt.at[T], sqt.at[T], m.s_ts.at[k], m.s_tr.at[k], (D, lax.rem(T + k, 4))
        )
        cp.start()
        tail_sent.append(cp)
    for k in range(1, nz):
        here = m.smz.at[z_at(nz - k)]
        remote(here, here, m.s_ms.at[2 + k], m.s_mr.at[2 + k], z_dev(k)).wait_recv()
    small_total = m.smz[0]
    for i in range(1, nz):
        small_total = small_total + m.smz[i]
    small_out[...] = small_total
    small_square = small_total * small_total
    small_tile = jnp.zeros((8, LANES), F32)
    for i in range(SMALL_ROWS // 8):
        small_tile = small_tile + small_square[8 * i : 8 * i + 8, :]
    for k in range(1, 4):
        here = sqt.at[lax.rem(T + 4 - k, 4)]
        remote(here, here, m.s_ts.at[k], m.s_tr.at[k], core_dev).wait_recv()
    sqd = m.sqd
    sqd[D] = sqt[0] + sqt[1] + sqt[2] + sqt[3]
    for k in range(1, n_dp):
        cp = remote(
            sqd.at[D], sqd.at[D], m.s_ds.at[k], m.s_dr.at[k], (lax.rem(D + k, n_dp), T)
        )
        cp.start()
        tail_sent.append(cp)
    for k in range(1, n_dp):
        here = sqd.at[lax.rem(D + n_dp - k, n_dp)]
        remote(here, here, m.s_ds.at[k], m.s_dr.at[k], core_dev).wait_recv()
    everything = small_tile
    for i in range(n_dp):
        everything = everything + sqd[i]
    sum_all = jnp.sum(jnp.sum(everything, axis=0, keepdims=True), axis=1, keepdims=True)
    norm_out[...] = jnp.broadcast_to(jnp.sqrt(sum_all), (8, LANES))

    for cp in reduces + small_sent + tail_sent:
        cp.wait_send()
    for cp in core_spread.values():
        cp.wait_send()
    for b in range(2):
        core_sent[(3, b)].wait_send()
        y_sent[(3, b)].wait_send()
    for here, there in out_copies:
        here.wait()
        there.wait()


def adam_kernel(
    head_cols,
    sh_qkv, sh_o, sh_up, sh_down, sh_small, norm,
    aw, am, av, fw, fm, fv, sw, sm, sv,
    norm_out,
    o_am, o_av, o_aw, o_ac, o_fm, o_fv, o_fw, o_fc, o_sm, o_sv, o_sw,
):
    length = norm[0:1, 0:1]
    factor = CLIP_LIMIT / jnp.maximum(length, CLIP_LIMIT)
    for i in range(4):
        if i < 3:
            grad = sh_qkv[:, i * head_cols : (i + 1) * head_cols]
        else:
            grad = sh_o[:, 0:head_cols]
        moment, square, master = adam_step(
            aw[i], am[i], av[i], factor * grad, RATE_MATRIX, WEIGHT_DECAY
        )
        o_am[i] = moment
        o_av[i] = square
        o_aw[i] = master
        o_ac[i] = master.astype(BF16)
    for i, share in enumerate((sh_up, sh_down)):
        moment, square, master = adam_step(
            fw[i], fm[i], fv[i], factor * share[...], RATE_MATRIX, WEIGHT_DECAY
        )
        o_fm[i] = moment
        o_fv[i] = square
        o_fw[i] = master
        o_fc[i] = master.astype(BF16)
    moment, square, master = adam_step(sw[...], sm[...], sv[...], factor * sh_small[...], RATE_SMALL, 0.0)
    o_sm[...] = moment
    o_sv[...] = square
    o_sw[...] = master
    norm_out[...] = jnp.broadcast_to(length, (8, LANES))


def tiles(vector):
    return jnp.pad(vector, (0, SMALL_ROWS * LANES - vector.shape[0])).reshape(SMALL_ROWS, LANES)


def fused_body(
    n_dp,
    tokens,
    cotangent,
    clip_lengths,
    key_mask,
    rel_buckets,
    attention_weights,
    attention_first,
    attention_second,
    feedforward_weights,
    feedforward_first,
    feedforward_second,
    small_params,
    small_first,
    small_second,
):
    rows = tokens.shape[0]
    owned, head_cols = attention_weights.shape[1:]
    hidden = feedforward_weights.shape[2]
    heads = head_cols // HD
    qkv_pad = -(-3 * head_cols // LANES) * LANES
    out_pad = -(-head_cols // LANES) * LANES
    nz = n_dp // 2
    small = tiles(small_params)
    offsets = jnp.pad(rel_buckets, (0, 1)).reshape(2 * BUCKET_SLOTS // LANES, LANES)
    keep = key_mask.reshape(rows // LANES, LANES)
    scratch = layer_scratch(owned, nz, qkv_pad, heads, head_cols, hidden)
    names = tuple(scratch)
    vmem = pl.BlockSpec(memory_space=pltpu.VMEM)
    smem = pl.BlockSpec(memory_space=pltpu.SMEM)
    anywhere = pl.BlockSpec(memory_space=pl.ANY)
    sds = jax.ShapeDtypeStruct
    block_rows, token_rows, sh_qkv, sh_o, sh_up, sh_down, sh_small, norm = pl.pallas_call(
        partial(layer_kernel, names, (n_dp, owned, qkv_pad, heads, head_cols, hidden)),
        out_shape=(
            sds((rows, W), BF16),
            sds((rows, W), BF16),
            sds((owned, qkv_pad), F32),
            sds((owned, out_pad), F32),
            sds((owned, hidden), F32),
            sds((owned, hidden), F32),
            sds((SMALL_ROWS, LANES), F32),
            sds((8, LANES), F32),
        ),
        in_specs=[anywhere, anywhere, smem, vmem, vmem, vmem, vmem, vmem],
        out_specs=(anywhere, anywhere, vmem, vmem, vmem, vmem, vmem, vmem),
        scratch_shapes=list(scratch.values()),
        compiler_params=pltpu.CompilerParams(
            collective_id=1, has_side_effects=True, vmem_limit_bytes=60 * 1024 * 1024
        ),
        name="layer",
    )(tokens, cotangent, clip_lengths, keep, offsets, attention_weights, feedforward_weights, small)
    like = lambda a, dtype=F32: sds(a.shape, dtype)
    results = pl.pallas_call(
        partial(adam_kernel, head_cols),
        out_shape=(
            sds((8, LANES), F32),
            like(attention_weights),
            like(attention_weights),
            like(attention_weights),
            like(attention_weights, BF16),
            like(feedforward_weights),
            like(feedforward_weights),
            like(feedforward_weights),
            like(feedforward_weights, BF16),
            sds((SMALL_ROWS, LANES), F32),
            sds((SMALL_ROWS, LANES), F32),
            sds((SMALL_ROWS, LANES), F32),
        ),
        in_specs=[vmem] * 15,
        out_specs=(vmem,) * 12,
        compiler_params=pltpu.CompilerParams(vmem_limit_bytes=32 * 1024 * 1024),
        name="adam",
    )(
        sh_qkv,
        sh_o,
        sh_up,
        sh_down,
        sh_small,
        norm,
        attention_weights,
        attention_first,
        attention_second,
        feedforward_weights,
        feedforward_first,
        feedforward_second,
        small,
        tiles(small_first),
        tiles(small_second),
    )
    length = small_params.shape[0]
    flat = lambda a: a.reshape(-1)[:length]
    return (
        results[0][0, 0],
        *results[1:9],
        flat(results[9]),
        flat(results[10]),
        flat(results[11]),
        block_rows,
        token_rows,
    )


def fused_fits(mesh, owned):
    return mesh.shape["tensor"] == 4 and mesh.shape["dp"] % 2 == 0 and owned % 16 == 0

def solution(mesh):
    in_specs = (
        P("dp", None),
        P("dp", None),
        P("dp", None),
        P("dp"),
        P(),
        P(None, "dp", "tensor"),
        P(None, "dp", "tensor"),
        P(None, "dp", "tensor"),
        P(None, "dp", "tensor"),
        P(None, "dp", "tensor"),
        P(None, "dp", "tensor"),
        P(),
        P(),
        P(),
    )
    out_specs = (
        P(),
        P(None, "dp", "tensor"),
        P(None, "dp", "tensor"),
        P(None, "dp", "tensor"),
        P(None, "dp", "tensor"),
        P(None, "dp", "tensor"),
        P(None, "dp", "tensor"),
        P(None, "dp", "tensor"),
        P(None, "dp", "tensor"),
        P(),
        P(),
        P(),
        P("dp", None),
        P("dp", None),
    )
    n_dp = mesh.shape["dp"]
    body = general_body
    if fused_fits(mesh, MODEL_WIDTH // n_dp):
        body = partial(fused_body, n_dp)
    return jax.shard_map(body, mesh=mesh, in_specs=in_specs, out_specs=out_specs, check_vma=False)
```

```python
from functools import partial
from types import SimpleNamespace

import jax
import jax.numpy as jnp
from jax import lax
from jax.experimental import pallas as pl
from jax.experimental.pallas import tpu as pltpu
from jax.sharding import PartitionSpec as P

MODEL_WIDTH = 768
H = 12
HD = 64
FF = 3072
NB = 320
BUCKET_SLOTS = 512
CLIPS = 8
STEP = 5


FULL_PRECISION = lax.Precision.HIGHEST
DEEP_ALPHA = 24.0**0.25
NORM_EPSILON = 1e-05
MASK_VALUE = -1e30
BETA_FIRST = 0.9
BETA_SECOND = 0.98
RATE_MATRIX = 0.03
RATE_SMALL = 0.5
WEIGHT_DECAY = 0.01
ADAM_EPSILON = 1e-08
CLIP_LIMIT = 0.1


def layer_norm(values, norm_gain, norm_shift):
    row_mean = jnp.mean(values, axis=-1, keepdims=True)
    centred = values - row_mean
    variance = jnp.mean(centred * centred, axis=-1, keepdims=True)
    return centred * lax.rsqrt(variance + NORM_EPSILON) * norm_gain + norm_shift


def gelu_exact(values):
    return jax.nn.gelu(values, approximate=False)


def split_small(vector):
    widths = [MODEL_WIDTH] * 8 + [FF, NB * H, HD * 2, 2, H]
    pieces = []
    offset = 0
    for extent in widths:
        pieces.append(vector[offset : offset + extent])
        offset += extent
    return pieces


def allowed_mask(lengths_row, keep_row):
    positions = jnp.arange(BUCKET_SLOTS, dtype=jnp.int32)
    clip_ends = jnp.cumsum(lengths_row)
    segment = jnp.sum((positions[:, None] >= clip_ends[None, :]).astype(jnp.int32), axis=1)
    live_keys = (keep_row == 1) & (segment < CLIPS)
    same_clip = segment[:, None] == segment[None, :]
    return same_clip & (live_keys[None, :] | (positions[:, None] == positions[None, :]))


def band_matrix(diagonals):
    head_count = diagonals.shape[0]
    length = (diagonals.shape[1] + 1) // 2
    padded = jnp.concatenate([diagonals, jnp.zeros((head_count, 1), diagonals.dtype)], axis=1)
    repeated = jnp.tile(padded, (1, length))
    folded = repeated[:, : length * (2 * length - 1)].reshape(head_count, length, 2 * length - 1)
    return folded[:, :, length - 1 :]


def position_terms(head_inputs, gate_matrix, gate_offset, scale_local, table_local, rel_buckets):
    linear = (
        jnp.einsum(
            "blhd,dk->bhlk", head_inputs, gate_matrix.reshape(HD, 2), precision=FULL_PRECISION
        )
        + gate_offset
    )
    sigmoid = jax.nn.sigmoid(linear)
    gate = sigmoid[..., 0] * (sigmoid[..., 1] * scale_local[None, :, None] - 1.0) + 2.0
    onehot = (rel_buckets[:, None] == jnp.arange(NB, dtype=jnp.int32)[None, :]).astype(jnp.float32)
    per_offset = jnp.dot(
        onehot, table_local, precision=FULL_PRECISION, preferred_element_type=jnp.float32
    )
    toeplitz = band_matrix(per_offset.T)
    return gate[..., None] * toeplitz[None]


def adam_step(weights, moment, second, gradient, step_rate, decay_rate):
    moment_new = BETA_FIRST * moment + (1.0 - BETA_FIRST) * gradient
    second_new = BETA_SECOND * second + (1.0 - BETA_SECOND) * gradient * gradient
    moment_hat = moment_new / (1.0 - BETA_FIRST**STEP)
    second_hat = second_new / (1.0 - BETA_SECOND**STEP)
    master = weights - step_rate * (
        moment_hat / (jnp.sqrt(second_hat) + ADAM_EPSILON) + decay_rate * weights
    )
    return (moment_new, second_new, master)


def placed(total_length, piece, start):
    return lax.dynamic_update_slice_in_dim(jnp.zeros((total_length,), jnp.float32), piece, start, 0)


def column_sum(values):
    return jnp.sum(values.astype(jnp.float32), axis=0)


def general_body(
    tokens,
    cotangent,
    clip_lengths,
    key_mask,
    rel_buckets,
    attention_weights,
    attention_first,
    attention_second,
    feedforward_weights,
    feedforward_first,
    feedforward_second,
    small_params,
    small_first,
    small_second,
):
    gathered_attention, gathered_forward = (
        lax.all_gather(attention_weights.astype(jnp.bfloat16), "dp", axis=1, tiled=True),
        lax.all_gather(feedforward_weights.astype(jnp.bfloat16), "dp", axis=1, tiled=True),
    )
    query_weight = gathered_attention[0]
    key_weight = gathered_attention[1]
    value_weight = gathered_attention[2]
    output_weight = gathered_attention[3]
    up_weight = gathered_forward[0]
    down_weight = gathered_forward[1]
    head_cols = query_weight.shape[1]
    heads_local = head_cols // HD
    hidden_local = up_weight.shape[1]
    tensor_rank = lax.axis_index("tensor")
    col_start = tensor_rank * head_cols
    head_start = tensor_rank * heads_local
    hidden_start = tensor_rank * hidden_local
    row_count = tokens.shape[0]
    bucket_count = row_count // BUCKET_SLOTS
    (
        gain_one,
        shift_one,
        gain_two,
        shift_two,
        bias_query,
        bias_value,
        bias_output,
        bias_down,
        bias_up,
        rel_table,
        gate_matrix,
        gate_offset,
        gate_scale,
    ) = split_small(small_params)
    local_bias_query = lax.dynamic_slice_in_dim(bias_query, col_start, head_cols)
    local_bias_value = lax.dynamic_slice_in_dim(bias_value, col_start, head_cols)
    local_bias_up = lax.dynamic_slice_in_dim(bias_up, hidden_start, hidden_local)
    scale_local = lax.dynamic_slice_in_dim(gate_scale, head_start, heads_local)
    table_local = lax.dynamic_slice_in_dim(rel_table.reshape(NB, H), head_start, heads_local, 1)
    allowed = jax.vmap(allowed_mask)(clip_lengths, key_mask.reshape(bucket_count, BUCKET_SLOTS))[
        :, None
    ]
    leading = (tensor_rank == 0).astype(jnp.float32)
    inputs = tokens.astype(jnp.float32)
    upstream = cotangent.astype(jnp.float32)
    query_bf = (
        jnp.dot(tokens, query_weight, preferred_element_type=jnp.float32) + local_bias_query
    ).astype(jnp.bfloat16)
    key_bf = jnp.dot(tokens, key_weight, preferred_element_type=jnp.float32).astype(jnp.bfloat16)
    value_bf = (
        jnp.dot(tokens, value_weight, preferred_element_type=jnp.float32) + local_bias_value
    ).astype(jnp.bfloat16)
    head_shape = (bucket_count, BUCKET_SLOTS, heads_local, HD)
    heads_of_query = query_bf.reshape(head_shape)
    heads_of_key = key_bf.reshape(head_shape)
    heads_of_value = value_bf.reshape(head_shape)
    head_inputs = lax.dynamic_slice_in_dim(inputs, col_start, head_cols, 1).reshape(head_shape)
    extra, pull_position = jax.vjp(
        partial(position_terms, rel_buckets=rel_buckets),
        head_inputs,
        gate_matrix,
        gate_offset,
        scale_local,
        table_local,
    )
    attention_logits = (
        jnp.einsum(
            "blhd,bmhd->bhlm", heads_of_query, heads_of_key, preferred_element_type=jnp.float32
        )
        * 0.125
    )
    scores = jnp.where(allowed, attention_logits + extra, MASK_VALUE)
    row_max = jnp.max(scores, axis=-1, keepdims=True)
    exponent = jnp.exp(scores - row_max)
    denominator = jnp.sum(exponent, axis=-1, keepdims=True)
    log_total = row_max + jnp.log(denominator)
    probs_bf = (exponent / denominator).astype(jnp.bfloat16)
    context_bf = (
        jnp.einsum("bhlm,bmhd->blhd", probs_bf, heads_of_value, preferred_element_type=jnp.float32)
        .reshape(row_count, head_cols)
        .astype(jnp.bfloat16)
    )
    attention_part = jnp.einsum(
        "nw,dw->nd", context_bf, output_weight, preferred_element_type=jnp.float32
    )
    attention = lax.psum(attention_part, "tensor") + bias_output
    normed, pull_norm_one = jax.vjp(
        layer_norm, DEEP_ALPHA * inputs + attention, gain_one, shift_one
    )
    normed_bf = normed.astype(jnp.bfloat16)
    up_pre = jnp.dot(normed_bf, up_weight, preferred_element_type=jnp.float32) + local_bias_up
    activated, pull_gelu = jax.vjp(gelu_exact, up_pre)
    activated_bf = activated.astype(jnp.bfloat16)
    down_part = jnp.einsum(
        "nf,df->nd", activated_bf, down_weight, preferred_element_type=jnp.float32
    )
    feedforward = lax.psum(down_part, "tensor") + bias_down
    output_values, pull_norm_two = jax.vjp(
        layer_norm, DEEP_ALPHA * normed + feedforward, gain_two, shift_two
    )
    block_output = output_values.astype(jnp.bfloat16)
    grad_res_two, grad_gain_two, grad_shift_two = pull_norm_two(upstream)
    grad_ffn_share = grad_res_two.astype(jnp.bfloat16)
    grad_bias_down = column_sum(grad_ffn_share)
    down_grad = jnp.einsum(
        "nd,nf->df", grad_ffn_share, activated_bf, preferred_element_type=jnp.float32
    )
    grad_activated = jnp.einsum(
        "nd,df->nf", grad_ffn_share, down_weight, preferred_element_type=jnp.float32
    )
    (grad_up_pre,) = pull_gelu(grad_activated)
    grad_up_bf = grad_up_pre.astype(jnp.bfloat16)
    grad_bias_up = column_sum(grad_up_bf)
    up_grad = jnp.einsum("nd,nf->df", normed_bf, grad_up_bf, preferred_element_type=jnp.float32)
    normed_part = jnp.einsum("nf,df->nd", grad_up_bf, up_weight, preferred_element_type=jnp.float32)
    normed_sum = lax.psum(normed_part, "tensor")
    grad_normed = normed_sum + DEEP_ALPHA * grad_res_two
    grad_res_one, grad_gain_one, grad_shift_one = pull_norm_one(grad_normed)
    grad_attention_share = grad_res_one.astype(jnp.bfloat16)
    grad_bias_output = column_sum(grad_attention_share)
    output_grad = jnp.einsum(
        "nd,nw->dw", grad_attention_share, context_bf, preferred_element_type=jnp.float32
    )
    grad_context_bf = jnp.einsum(
        "nd,dw->nw", grad_attention_share, output_weight, preferred_element_type=jnp.float32
    ).astype(jnp.bfloat16)
    grad_heads = grad_context_bf.reshape(head_shape)
    attention_probabilities = jnp.exp(scores - log_total)
    recomputed_bf = attention_probabilities.astype(jnp.bfloat16)
    grad_probs = jnp.einsum(
        "blhd,bmhd->bhlm", grad_heads, heads_of_value, preferred_element_type=jnp.float32
    )
    inner = jnp.sum(grad_probs * attention_probabilities, axis=-1, keepdims=True)
    grad_scores_bf = (attention_probabilities * (grad_probs - inner)).astype(jnp.bfloat16)
    grad_query = (
        (
            jnp.einsum(
                "bhlm,bmhd->blhd", grad_scores_bf, heads_of_key, preferred_element_type=jnp.float32
            )
            * 0.125
        )
        .astype(jnp.bfloat16)
        .reshape(row_count, head_cols)
    )
    grad_key = (
        (
            jnp.einsum(
                "bhlm,blhd->bmhd",
                grad_scores_bf,
                heads_of_query,
                preferred_element_type=jnp.float32,
            )
            * 0.125
        )
        .astype(jnp.bfloat16)
        .reshape(row_count, head_cols)
    )
    grad_value = (
        jnp.einsum("bhlm,blhd->bmhd", recomputed_bf, grad_heads, preferred_element_type=jnp.float32)
        .astype(jnp.bfloat16)
        .reshape(row_count, head_cols)
    )
    grad_head_inputs, grad_gate_matrix, grad_gate_offset, grad_scale_local, grad_table_local = (
        pull_position(grad_scores_bf.astype(jnp.float32))
    )
    query_grad = jnp.einsum("nd,nw->dw", tokens, grad_query, preferred_element_type=jnp.float32)
    key_grad = jnp.einsum("nd,nw->dw", tokens, grad_key, preferred_element_type=jnp.float32)
    value_grad = jnp.einsum("nd,nw->dw", tokens, grad_value, preferred_element_type=jnp.float32)
    input_part = (
        jnp.einsum("nw,dw->nd", grad_query, query_weight, preferred_element_type=jnp.float32)
        + jnp.einsum("nw,dw->nd", grad_key, key_weight, preferred_element_type=jnp.float32)
        + jnp.einsum("nw,dw->nd", grad_value, value_weight, preferred_element_type=jnp.float32)
    )
    own_columns = lax.dynamic_slice_in_dim(input_part, col_start, head_cols, 1)
    input_part = lax.dynamic_update_slice_in_dim(
        input_part, own_columns + grad_head_inputs.reshape(row_count, head_cols), col_start, 1
    )
    grad_inputs = lax.psum(input_part, "tensor") + DEEP_ALPHA * grad_res_one
    tokens_grad = grad_inputs.astype(jnp.bfloat16)
    table_grad = lax.dynamic_update_slice_in_dim(
        jnp.zeros((NB, H), jnp.float32), grad_table_local, head_start, 1
    ).reshape(-1)
    local_small = jnp.concatenate(
        [
            grad_gain_one * leading,
            grad_shift_one * leading,
            grad_gain_two * leading,
            grad_shift_two * leading,
            placed(MODEL_WIDTH, column_sum(grad_query), col_start),
            placed(MODEL_WIDTH, column_sum(grad_value), col_start),
            grad_bias_output * leading,
            grad_bias_down * leading,
            placed(FF, grad_bias_up, hidden_start),
            table_grad,
            grad_gate_matrix,
            grad_gate_offset,
            placed(H, grad_scale_local, head_start),
        ]
    )
    small_grad = lax.psum(local_small, ("dp", "tensor"))
    local_attention = jnp.stack([query_grad, key_grad, value_grad, output_grad])
    local_forward = jnp.stack([up_grad, down_grad])
    summed_attention, summed_forward = lax.psum((local_attention, local_forward), "dp")
    owner_rank = lax.axis_index("dp")
    owned_rows = attention_weights.shape[1]
    share_attention = lax.dynamic_slice_in_dim(
        summed_attention, owner_rank * owned_rows, owned_rows, 1
    )
    share_forward = lax.dynamic_slice_in_dim(summed_forward, owner_rank * owned_rows, owned_rows, 1)
    share_squares = jnp.sum(share_attention * share_attention) + jnp.sum(
        share_forward * share_forward
    )
    big_squares = lax.psum(share_squares, ("dp", "tensor"))
    global_norm = jnp.sqrt(big_squares + jnp.sum(small_grad * small_grad))
    factor = CLIP_LIMIT / jnp.maximum(global_norm, CLIP_LIMIT)
    attention_moment, attention_square, attention_master = adam_step(
        attention_weights,
        attention_first,
        attention_second,
        factor * share_attention,
        RATE_MATRIX,
        WEIGHT_DECAY,
    )
    feedforward_moment, feedforward_square, feedforward_master = adam_step(
        feedforward_weights,
        feedforward_first,
        feedforward_second,
        factor * share_forward,
        RATE_MATRIX,
        WEIGHT_DECAY,
    )
    small_moment, small_square, small_master = adam_step(
        small_params, small_first, small_second, factor * small_grad, RATE_SMALL, 0.0
    )
    return (
        global_norm,
        attention_moment,
        attention_square,
        attention_master,
        attention_master.astype(jnp.bfloat16),
        feedforward_moment,
        feedforward_square,
        feedforward_master,
        feedforward_master.astype(jnp.bfloat16),
        small_moment,
        small_square,
        small_master,
        block_output,
        tokens_grad,
    )


F32 = jnp.float32
BF16 = jnp.bfloat16
MESH_ID = pl.DeviceIdType.MESH
LANES = 128
SMALL_ROWS = 104
TABLE_ROW = 72
GATE_ROW = 102
OFFSET_ROW = 103
INV_SQRT2 = 0.5**0.5
INV_SQRT_2PI = 0.3989422804014327
CHUNK = 128
HALF = 256
W = MODEL_WIDTH
NT = (((1,), (1,)), ((), ()))
TN = (((0,), (0,)), ((), ()))


def mm(a, b):
    return jnp.dot(a, b, preferred_element_type=F32)


def mm_nt(a, b):
    return lax.dot_general(a, b, NT, preferred_element_type=F32)


def mm_tn(a, b):
    return lax.dot_general(a, b, TN, preferred_element_type=F32)


def exact_nt(a, b):
    return lax.dot_general(a, b, NT, precision=FULL_PRECISION, preferred_element_type=F32)


def exact_tn(a, b):
    return lax.dot_general(a, b, TN, precision=FULL_PRECISION, preferred_element_type=F32)


def exact_mm(a, b):
    return jnp.dot(a, b, precision=FULL_PRECISION, preferred_element_type=F32)


def iota(shape, axis):
    return lax.broadcasted_iota(jnp.int32, shape, axis)


def layer_scratch(owned, nz, qkv_pad, heads, head_cols, hidden):
    rows = 2 * BUCKET_SLOTS
    dma = pltpu.SemaphoreType.DMA
    vm = pltpu.VMEM
    shapes = dict(
        tok=vm((rows, W), BF16),
        cot=vm((2, HALF, W), BF16),
        wqkv=vm((W, qkv_pad), BF16),
        wo1=vm((W, LANES), BF16),
        wo=vm((W, head_cols), BF16),
        wot=vm((head_cols, W), BF16),
        wqkvt=vm((qkv_pad + LANES, W), BF16),
        wupt=vm((hidden, W), BF16),
        wdownt=vm((hidden, W), BF16),
        go=vm((W, LANES), BF16),
        glin=vm((W, LANES), F32),
        wup=vm((W, hidden), BF16),
        wdown=vm((W, hidden), BF16),
        q=vm((rows, head_cols), BF16),
        k=vm((rows, head_cols), BF16),
        v=vm((rows, head_cols), BF16),
        kt=vm((head_cols, rows), BF16),
        vt=vm((head_cols, rows), BF16),
        ctx=vm((rows, head_cols), BF16),
        dctx=vm((rows, head_cols), BF16),
        dqkv=vm((rows, qkv_pad + LANES), BF16),
        prob=vm((2 * heads, BUCKET_SLOTS, BUCKET_SLOTS), F32),
        gsb=vm((heads, BUCKET_SLOTS, BUCKET_SLOTS), BF16),
        dqf=vm((BUCKET_SLOTS, head_cols), F32),
        mbias=vm((2, BUCKET_SLOTS, BUCKET_SLOTS), BF16),
        band=vm((heads, LANES, 2 * BUCKET_SLOTS), F32),
        dband=vm((heads, LANES, 2 * BUCKET_SLOTS), F32),
        gate=vm((rows, LANES), F32),
        gu=vm((rows, LANES), F32),
        dgate=vm((rows, LANES), F32),
        gmat=vm((W, LANES), F32),
        vecs=vm((16, W), F32),
        acc=vm((16, W), F32),
        nb=vm((rows, W), BF16),
        held=vm((2, HALF, W), F32),
        xh1=vm((2, HALF, W), F32),
        rstd1=vm((2, HALF, LANES), F32),
        act=vm((rows, hidden), BF16),
        gelup=vm((rows, hidden), F32),
        gffn=vm((rows, W), BF16),
        gub=vm((rows, hidden), BF16),
        gattn=vm((rows, W), BF16),
        stage=vm((2, HALF, W), BF16),
        ownf=vm((HALF, W), F32),
        cs=vm((2, HALF, W), BF16),
        cr=vm((2, HALF, W), BF16),
        ys=vm((2, HALF, W), BF16),
        yr=vm((2, 2, HALF, W), BF16),
        xrqkv=vm((nz, owned, qkv_pad), BF16),
        xro=vm((nz, owned, LANES), BF16),
        xrup=vm((nz, owned, hidden), BF16),
        xrdown=vm((nz, owned, hidden), BF16),
        zsqkv=vm((nz - 1, owned, qkv_pad), BF16),
        zso=vm((nz - 1, owned, LANES), BF16),
        zsup=vm((nz - 1, owned, hidden), BF16),
        zsdown=vm((nz - 1, owned, hidden), BF16),
        zrqkv=vm((nz - 1, owned, qkv_pad), BF16),
        zro=vm((nz - 1, owned, LANES), BF16),
        zrup=vm((nz - 1, owned, hidden), BF16),
        zrdown=vm((nz - 1, owned, hidden), BF16),
        sm=vm((4, SMALL_ROWS, LANES), F32),
        smr=vm((3, SMALL_ROWS, LANES), F32),
        smz=vm((nz, SMALL_ROWS, LANES), F32),
        sqt=vm((4, 8, LANES), F32),
        sqd=vm((2 * nz, 8, LANES), F32),
        s_in=dma((3,)),
        s_gs=dma((6,)),
        s_gr=dma((6,)),
        s_ls=dma((6, 2, nz)),
        s_lr=dma((6, 2, nz)),
        s_lxs=dma((6, 2, nz)),
        s_lxr=dma((6, 2, nz)),
        s_cs=dma((4, 2, 2)),
        s_cr=dma((4, 2, 2)),
        s_ys=dma((4, 2, 2)),
        s_yr=dma((4, 2, 2)),
        s_as=dma((3, 2, 2)),
        s_ar=dma((3, 2, 2)),
        s_ol=dma((2, 2)),
        s_os=dma((2, 2)),
        s_or=dma((2, 2)),
        s_xs=dma((4, nz)),
        s_xr=dma((4, nz)),
        s_zs=dma((4, nz)),
        s_zr=dma((4, nz)),
        s_ms=dma((3 + nz,)),
        s_mr=dma((3 + nz,)),
        s_ts=dma((4,)),
        s_tr=dma((4,)),
        s_ds=dma((2 * nz,)),
        s_dr=dma((2 * nz,)),
    )
    return shapes


def layer_kernel(names, dims, *refs):
    n_dp, owned, qkv_pad, heads, head_cols, hidden = dims
    nz = n_dp // 2
    (tok_in, cot_in, lens, keep, wa, wf, small) = refs[:7]
    (bo_out, tg_out, sh_qkv, sh_o, sh_up, sh_down, small_out, norm_out) = refs[7:15]
    m = SimpleNamespace(**dict(zip(names, refs[15:], strict=True)))
    D = lax.axis_index("dp")
    T = lax.axis_index("tensor")
    z = lax.div(D, 2)
    x = lax.rem(D, 2)
    c = lax.rem(T, 2)
    yy = lax.div(T, 2)
    core_dev = (D, T + 1 - 2 * c)
    y_dev = (D, lax.rem(T + 2, 4))
    x_dev = (z * 2 + 1 - x, T)

    def z_at(k):
        return lax.rem(z + k, nz)

    z_order = sorted(range(1, nz), key=lambda k: min(k, nz - k))

    def z_dev(k):
        return (z_at(k) * 2 + x, T)

    def remote(src, dst, ss, rs, dev):
        return pltpu.make_async_remote_copy(
            src_ref=src, dst_ref=dst, send_sem=ss, recv_sem=rs, device_id=dev, device_id_type=MESH_ID
        )

    def loop(n, step):
        def run(i, carry):
            step(i)
            return carry

        lax.fori_loop(0, n, run, 0)

    def block(owner):
        return pl.ds(pl.multiple_of(owner * owned, owned), owned)

    tok_copy = pltpu.make_async_copy(tok_in, m.tok, m.s_in.at[0])
    tok_copy.start()
    cot_copies = []
    for b in range(2):
        rows = pl.ds(pl.multiple_of(b * BUCKET_SLOTS + c * HALF, HALF), HALF)
        cp = pltpu.make_async_copy(cot_in.at[rows], m.cot.at[b], m.s_in.at[1 + b])
        cp.start()
        cot_copies.append(cp)
    barrier = pltpu.get_barrier_semaphore()
    for k in range(1, 4):
        pl.semaphore_signal(barrier, inc=1, device_id=(D, lax.rem(T + k, 4)), device_id_type=MESH_ID)
    for k in range(1, n_dp):
        pl.semaphore_signal(barrier, inc=1, device_id=(lax.rem(D + k, n_dp), T), device_id_type=MESH_ID)
    mine = block(D)
    first_o = qkv_pad - 3 * head_cols
    m.wqkv[mine, :] = jnp.concatenate([wa[0], wa[1], wa[2], wa[3, :, 0:first_o]], axis=1).astype(BF16)
    m.wo1[mine, :] = wa[3, :, first_o:head_cols].astype(BF16)
    m.wup[mine, :] = wf[0].astype(BF16)
    m.wdown[mine, :] = wf[1].astype(BF16)
    pl.semaphore_wait(barrier, 3 + n_dp - 1)

    part_rows = owned // 2 if owned % 32 == 0 else owned
    pieces = [(m.wqkv, 0, owned), (m.wo1, 0, owned)]
    for buf in (m.wup, m.wdown):
        pieces.append((buf, 0, part_rows))
        pieces.append((buf, owned - part_rows, part_rows))

    def piece(which, owner):
        buf, first, count = pieces[which]
        return buf.at[pl.ds(pl.multiple_of(owner * owned + first, 16), count)]

    gathers = {}

    def launch(record, where):
        remote(*where()).start()
        record.append(where)

    def when(condition, action):
        pl.when(condition)(action)

    def from_z(way, step):
        owner_z = z - step if way == 0 else z + step
        return owner_z, (owner_z >= 0) if way == 0 else (owner_z < nz)

    def send_when(which, condition, where):
        when(condition(), lambda: remote(*where()).start())
        gathers.setdefault(which, []).append((condition, where))

    def line_send(which, way, step, hops):
        origin = step - hops

        def where():
            part = piece(which, from_z(way, origin)[0] * 2 + x)
            target = ((z + hops if way == 0 else z - hops) * 2 + x, T)
            return part, part, m.s_ls.at[which, way, step], m.s_lr.at[which, way, step], target

        def condition():
            there = (z + hops < nz) if way == 0 else (z >= hops)
            return there & from_z(way, origin)[1]

        send_when(which, condition, where)

    def line_start(which, hops):
        for hop in range(1, hops + 1):
            for way in range(2):
                line_send(which, way, hop, hop)

    def gather_x(which):
        def where():
            own = piece(which, D)
            return own, own, m.s_gs.at[which], m.s_gr.at[which], x_dev

        send_when(which, lambda: D >= 0, where)

    def line_step(which, step, hops):
        for way in range(2):

            def landed(way=way):
                part = piece(which, from_z(way, step)[0] * 2 + x)
                sems = m.s_ls.at[which, way, step], m.s_lr.at[which, way, step]
                remote(part, part, *sems, x_dev).wait_recv()

            when(from_z(way, step)[1], landed)
            if step >= hops and step + 1 < nz:
                line_send(which, way, step + 1, 1)

            def where(way=way):
                part = piece(which, from_z(way, step)[0] * 2 + x)
                return part, part, m.s_lxs.at[which, way, step], m.s_lxr.at[which, way, step], x_dev

            send_when(which, lambda way=way: from_z(way, step)[1], where)

    def line_end(which):
        part = piece(which, z * 2 + 1 - x)
        remote(part, part, m.s_gs.at[which], m.s_gr.at[which], x_dev).wait_recv()
        for step in range(1, nz):
            for way in range(2):

                def landed(way=way):
                    part = piece(which, from_z(way, step)[0] * 2 + 1 - x)
                    sems = m.s_lxs.at[which, way, step], m.s_lxr.at[which, way, step]
                    remote(part, part, *sems, x_dev).wait_recv()

                when(from_z(way, step)[1], landed)

    def sent_all(which):
        for condition, where in gathers.pop(which):
            when(condition(), lambda where=where: remote(*where()).wait_send())

    def turn(source, target):
        count = source.shape[1]
        step = HALF if count % HALF == 0 else LANES

        def chunk(i):
            at = pl.ds(pl.multiple_of(i * step, step), step)
            target[at, :] = source[:, at].T

        loop(count // step, chunk)

    line_start(0, 1)
    gather_x(0)

    def small_row(first, count):
        return jnp.concatenate([small[first + i : first + i + 1, :] for i in range(count)], axis=1)

    def pick(values, size):
        total = jnp.zeros((1, size), F32)
        for t in range(4):
            total = total + jnp.where(T == t, values[:, t * size : (t + 1) * size], 0.0)
        return total

    vecs = m.vecs
    vecs[...] = jnp.zeros_like(vecs)
    m.acc[...] = jnp.zeros((16, W), F32)
    for at, first in ((0, 0), (1, 6), (2, 12), (3, 18), (4, 36), (5, 42)):
        vecs[at : at + 1, :] = small_row(first, W // LANES)
    vecs[6:7, :] = pick(small_row(48, FF // LANES), hidden)
    bq = pick(small_row(24, W // LANES), head_cols)
    bv = pick(small_row(30, W // LANES), head_cols)
    bias_qkv = jnp.concatenate(
        [bq, jnp.zeros_like(bq), bv, jnp.zeros((1, qkv_pad - 3 * head_cols), F32)], axis=1
    )
    vecs[7:8, 0:qkv_pad] = bias_qkv

    lane = iota((1, LANES), 1)
    col = iota((W, LANES), 0)
    col_lane = iota((W, LANES), 1)
    gate_row = small[GATE_ROW : GATE_ROW + 1, :]
    col_in_head = lax.rem(col, HD)
    picked_u = jnp.sum(
        jnp.where(col_lane == 2 * col_in_head, gate_row, 0.0), axis=1, keepdims=True
    )
    picked_w = jnp.sum(
        jnp.where(col_lane == 2 * col_in_head + 1, gate_row, 0.0), axis=1, keepdims=True
    )
    in_group = lax.rem(col_lane, 8)
    own_head = (col_lane < 16) & (in_group < heads) & (lax.div(col, HD) == T * heads + in_group)
    m.gmat[...] = jnp.where(own_head, jnp.where(col_lane < 8, picked_u, picked_w), 0.0)
    offset_row = small[OFFSET_ROW : OFFSET_ROW + 1, :]
    offset_u = jnp.sum(jnp.where(lane == 0, offset_row, 0.0), axis=1, keepdims=True)
    offset_w = jnp.sum(jnp.where(lane == 1, offset_row, 0.0), axis=1, keepdims=True)
    scale = jnp.zeros((1, LANES), F32)
    for h in range(heads):
        one = jnp.sum(jnp.where(lane == 2 + T * heads + h, offset_row, 0.0), axis=1, keepdims=True)
        scale = scale + jnp.where(lane == h, one, 0.0)
    head_lane = lane < heads

    line_step(0, 1, 1)

    offsets = small_row(3 * SMALL_ROWS, 2 * BUCKET_SLOTS // LANES).astype(jnp.int32)
    table = small[TABLE_ROW : TABLE_ROW + 32, :]
    long_row = 2 * BUCKET_SLOTS
    sub8 = iota((8, long_row), 0)
    for h in range(heads):
        flat = offsets * H + (T * heads + h)
        at_row = lax.div(flat, LANES)
        at_lane = lax.rem(flat, LANES)
        hot_row = jnp.where(iota((32, long_row), 0) == at_row, 1.0, 0.0)
        spread = exact_tn(table, hot_row)
        values = jnp.sum(
            jnp.where(iota((LANES, long_row), 0) == at_lane, spread, 0.0), axis=0, keepdims=True
        )
        stack = jnp.broadcast_to(pltpu.roll(jnp.broadcast_to(values, (8, long_row)), 1, 1), (8, long_row))
        for bit in (1, 2, 4):
            stack = jnp.where(lax.rem(lax.div(sub8, bit), 2) == 1, pltpu.roll(stack, bit, 1), stack)
        size = 8
        m.band[h, 0:8, :] = stack
        while size < LANES:
            m.band[h, size : 2 * size, :] = pltpu.roll(m.band[h, 0:size, :], size, 1)
            size *= 2
    m.dband[...] = jnp.zeros(m.dband.shape, F32)

    line_step(0, 2, 1)

    for b in range(2):
        end = 0
        ends = []
        for i in range(CLIPS):
            end = end + lens[b, i]
            ends.append(end)
        key_at = iota((1, BUCKET_SLOTS), 1)
        key_segment = jnp.zeros((1, BUCKET_SLOTS), jnp.int32)
        for end in ends:
            key_segment = key_segment + jnp.where(key_at >= end, 1, 0)
        kept = jnp.concatenate([keep[4 * b + i : 4 * b + i + 1, :] for i in range(4)], axis=1)
        live = jnp.where((kept == 1) & (key_segment < CLIPS), key_segment, -1)

        def mask_chunk(i, b=b, ends=ends, live=live):
            query_at = iota((CHUNK, BUCKET_SLOTS), 0) + i * CHUNK
            segment = jnp.zeros((CHUNK, BUCKET_SLOTS), jnp.int32)
            for end in ends:
                segment = segment + jnp.where(query_at >= end, 1, 0)
            allowed = (segment == live) | (query_at == iota((CHUNK, BUCKET_SLOTS), 1))
            m.mbias[b, pl.ds(pl.multiple_of(i * CHUNK, CHUNK), CHUNK), :] = jnp.where(
                allowed, 0.0, MASK_VALUE
            ).astype(BF16)

        loop(BUCKET_SLOTS // CHUNK, mask_chunk)

    for step in range(3, nz):
        line_step(0, step, 1)
    line_start(1, 2)

    tok_copy.wait()
    gmat = m.gmat[...]
    part_hi = gmat.astype(BF16)
    rest = gmat - part_hi.astype(F32)
    part_mid = rest.astype(BF16)
    part_lo = (rest - part_mid.astype(F32)).astype(BF16)
    gate_parts = (part_hi, part_hi, part_hi, part_mid, part_mid, part_lo)
    stacked = jnp.zeros((W, LANES), F32)
    for i, part in enumerate(gate_parts):
        moved = part.astype(F32)
        stacked = stacked + (pltpu.roll(moved, 16 * i, 1) if i else moved)
    m.wqkvt[qkv_pad : qkv_pad + LANES, :] = stacked.astype(BF16).T

    def gate_chunk(i):
        rows = pl.ds(pl.multiple_of(i * HALF, HALF), HALF)
        tokens = m.tok[rows, :]
        linear = mm(tokens, part_hi) + mm(tokens, part_mid) + mm(tokens, part_lo)
        both = jax.nn.sigmoid(linear + jnp.where(lane < 8, offset_u, offset_w))
        m.gu[rows, :] = both
        m.gate[rows, :] = both * (pltpu.roll(both, LANES - 8, 1) * scale - 1.0) + 2.0

    loop(4, gate_chunk)

    line_end(0)
    gather_x(1)
    line_start(2, 2)
    gather_x(2)

    def project(i):
        rows = pl.ds(pl.multiple_of(i * HALF, HALF), HALF)
        both = mm(m.tok[rows, :], m.wqkv[...]) + vecs[7:8, 0:qkv_pad]
        query = both[:, 0:head_cols].astype(BF16)
        m.q[rows, :] = (query.astype(F32) * 0.125).astype(BF16)
        key = both[:, head_cols : 2 * head_cols].astype(BF16)
        value = both[:, 2 * head_cols : 3 * head_cols].astype(BF16)
        m.k[rows, :] = key
        m.v[rows, :] = value
        m.kt[:, rows] = key.T
        m.vt[:, rows] = value.T

    loop(4, project)

    head_of = lax.div(iota((1, head_cols), 1), HD)
    head_masks = [jnp.where(head_of == h, 1.0, 0.0) for h in range(heads)]
    low_masks = [m.astype(BF16) for m in head_masks]

    def hooked(first, count, chunk, hooks):
        def step_of(i):
            step = i + first
            chunk(step)
            for at, action in hooks.items():
                if first <= at < first + count:
                    when(step == at, action)

        loop(count, step_of)

    def attend(b, hooks):
        keys = m.kt[:, b * BUCKET_SLOTS : (b + 1) * BUCKET_SLOTS]
        values = m.v[b * BUCKET_SLOTS : (b + 1) * BUCKET_SLOTS, :]

        def chunk(i):
            local = pl.ds(pl.multiple_of(i * CHUNK, CHUNK), CHUNK)
            rows = pl.ds(pl.multiple_of(b * BUCKET_SLOTS + i * CHUNK, CHUNK), CHUNK)
            window = pl.ds(pl.multiple_of(BUCKET_SLOTS - i * CHUNK, CHUNK), BUCKET_SLOTS)
            query = m.q[rows, :]
            gates = m.gate[rows, :]
            context = jnp.zeros((CHUNK, head_cols), F32)
            for h in range(heads):
                scores = mm(query * low_masks[h], keys)
                scores = scores + gates[:, h : h + 1] * m.band[h, :, window]
                scores = scores + m.mbias[b, local, :].astype(F32)
                top = jnp.max(scores, axis=1, keepdims=True)
                weight = jnp.exp(scores - top)
                total = jnp.sum(weight, axis=1, keepdims=True)
                probability = weight * (1.0 / total)
                m.prob[b * heads + h, local, :] = probability
                context = context + mm(probability.astype(BF16), values) * head_masks[h]
            m.ctx[rows, :] = context.astype(BF16)

        hooked(0, BUCKET_SLOTS // CHUNK, chunk, hooks)

    core_sent = {}
    y_sent = {}

    def exchange(phase, b, product):
        other = b * BUCKET_SLOTS + (1 - c) * HALF
        own = b * BUCKET_SLOTS + c * HALF
        for cp in core_sent.get((phase - 1, b), []) + y_sent.get((phase - 1, b), []):
            cp.wait_send()
        for i in range(2):
            at = slice(i * CHUNK, (i + 1) * CHUNK)
            rows = pl.ds(pl.multiple_of(other + i * CHUNK, CHUNK), CHUNK)
            m.cs[b, at, :] = product(rows).astype(BF16)
            cp = remote(
                m.cs.at[b, at], m.cr.at[b, at], m.s_cs.at[phase, b, i], m.s_cr.at[phase, b, i], core_dev
            )
            cp.start()
            core_sent.setdefault((phase, b), []).append(cp)
        for i in range(2):
            at = slice(i * CHUNK, (i + 1) * CHUNK)
            rows = pl.ds(pl.multiple_of(own + i * CHUNK, CHUNK), CHUNK)
            m.ownf[at, :] = product(rows)
        for i in range(2):
            at = slice(i * CHUNK, (i + 1) * CHUNK)
            core_sent[(phase, b)][i].wait_recv()
            m.ys[b, at, :] = (m.ownf[at, :] + m.cr[b, at, :].astype(F32)).astype(BF16)
            cp = remote(
                m.ys.at[b, at],
                m.yr.at[phase % 2, b, at],
                m.s_ys.at[phase, b, i],
                m.s_yr.at[phase, b, i],
                y_dev,
            )
            cp.start()
            y_sent.setdefault((phase, b), []).append(cp)

    def arrived(phase, b, at):
        return m.ys[b, at, :].astype(F32) + m.yr[phase % 2, b, at, :].astype(F32)

    def own_rows(b, i):
        return pl.ds(pl.multiple_of(b * BUCKET_SLOTS + c * HALF + i * CHUNK, CHUNK), CHUNK)

    core_spread = {}

    def spread(which, buf, b, i):
        part = buf.at[own_rows(b, i)]
        cp = remote(part, part, m.s_as.at[which, b, i], m.s_ar.at[which, b, i], core_dev)
        cp.start()
        core_spread.setdefault((which, b), []).append(cp)

    spread_done = set()

    def spread_end(which, b, i):
        if (which, b, i) not in spread_done:
            core_spread[(which, b)][i].wait_recv()
            spread_done.add((which, b, i))

    def as_it_lands(phase, b, chunk):
        for i in range(2):
            y_sent[(phase, b)][i].wait_recv()
            chunk(i)

    def row_mean(values):
        return jnp.mean(values, axis=1, keepdims=True)

    def add_row(at, values):
        m.acc[at : at + 1, 0 : values.shape[1]] += jnp.sum(values, axis=0, keepdims=True)

    def norm_one(b):

        def chunk(i):
            at = pl.ds(pl.multiple_of(i * CHUNK, CHUNK), CHUNK)
            rows = own_rows(b, i)
            residual = DEEP_ALPHA * m.tok[rows, :].astype(F32) + (arrived(0, b, at) + vecs[4:5, :])
            centred = residual - row_mean(residual)
            rstd = lax.rsqrt(row_mean(centred * centred) + NORM_EPSILON)
            hat = centred * rstd
            normed = hat * vecs[0:1, :] + vecs[1:2, :]
            m.xh1[b, at, :] = hat
            m.rstd1[b, at, :] = jnp.broadcast_to(rstd, (CHUNK, LANES))
            m.held[b, at, :] = normed
            m.nb[rows, :] = normed.astype(BF16)
            spread(0, m.nb, b, i)

        as_it_lands(0, b, chunk)

    def own_first(which, b, chunk):
        def rows_at(step):
            i = lax.rem(step + 2 * c, 4)
            return pl.ds(pl.multiple_of(b * BUCKET_SLOTS + i * CHUNK, CHUNK), CHUNK)

        loop(2, lambda step: chunk(rows_at(step)))
        for i in range(2):
            spread_end(which, b, i)
            chunk(rows_at(2 + i))

    def feed(b):
        def chunk(rows):
            up = mm(m.nb[rows, :], m.wup[...]) + vecs[6:7, :]
            half_phi = 0.5 * (1.0 + lax.erf(up * INV_SQRT2))
            m.act[rows, :] = (up * half_phi).astype(BF16)
            m.gelup[rows, :] = half_phi + up * (jnp.exp(up * up * -0.5) * INV_SQRT_2PI)

        own_first(0, b, chunk)

    out_copies = []

    def result_rows(which, b, stage, out):
        rows = pl.ds(pl.multiple_of(b * BUCKET_SLOTS + c * HALF, HALF), HALF)
        part = stage.at[b]
        here = pltpu.make_async_copy(part, out.at[rows], m.s_ol.at[which, b])
        there = remote(part, out.at[rows], m.s_os.at[which, b], m.s_or.at[which, b], core_dev)
        here.start()
        there.start()
        out_copies.append((here, there))

    def norm_two(b):
        cot_copies[b].wait()

        def chunk(i):
            at = pl.ds(pl.multiple_of(i * CHUNK, CHUNK), CHUNK)
            rows = own_rows(b, i)
            residual = DEEP_ALPHA * m.held[b, at, :] + (arrived(1, b, at) + vecs[5:6, :])
            centred = residual - row_mean(residual)
            rstd = lax.rsqrt(row_mean(centred * centred) + NORM_EPSILON)
            hat = centred * rstd
            m.stage[b, at, :] = (hat * vecs[2:3, :] + vecs[3:4, :]).astype(BF16)
            upstream = m.cot[b, at, :].astype(F32)
            add_row(2, upstream * hat)
            add_row(3, upstream)
            scaled = upstream * vecs[2:3, :]
            grad = rstd * (scaled - row_mean(scaled) - hat * row_mean(scaled * hat))
            m.held[b, at, :] = grad
            low = grad.astype(BF16)
            m.gffn[rows, :] = low
            spread(1, m.gffn, b, i)
            add_row(5, low.astype(F32))

        as_it_lands(1, b, chunk)
        result_rows(0, b, m.stage, bo_out)

    def feed_back(b):
        def chunk(rows):
            grad = mm(m.gffn[rows, :], m.wdown[...]) * m.gelup[rows, :]
            low = grad.astype(BF16)
            m.gub[rows, :] = low
            add_row(6, low.astype(F32))

        own_first(1, b, chunk)

    def norm_one_back(b):

        def chunk(i):
            at = pl.ds(pl.multiple_of(i * CHUNK, CHUNK), CHUNK)
            rows = own_rows(b, i)
            upstream = arrived(2, b, at) + DEEP_ALPHA * m.held[b, at, :]
            hat = m.xh1[b, at, :]
            add_row(0, upstream * hat)
            add_row(1, upstream)
            scaled = upstream * vecs[0:1, :]
            rstd = m.rstd1[b, at, 0:1]
            grad = rstd * (scaled - row_mean(scaled) - hat * row_mean(scaled * hat))
            m.held[b, at, :] = grad
            low = grad.astype(BF16)
            m.gattn[rows, :] = low
            spread(2, m.gattn, b, i)
            add_row(4, low.astype(F32))

        as_it_lands(2, b, chunk)

    def attend_back(b, hooks):
        keys = m.k[b * BUCKET_SLOTS : (b + 1) * BUCKET_SLOTS, :]
        values = m.vt[:, b * BUCKET_SLOTS : (b + 1) * BUCKET_SLOTS]

        def chunk(step):
            i = lax.rem(step + 2 * c, 4)
            local = pl.ds(pl.multiple_of(i * CHUNK, CHUNK), CHUNK)
            rows = pl.ds(pl.multiple_of(b * BUCKET_SLOTS + i * CHUNK, CHUNK), CHUNK)
            window = pl.ds(pl.multiple_of(BUCKET_SLOTS - i * CHUNK, CHUNK), BUCKET_SLOTS)
            place = pl.ds(pl.multiple_of(3 * CHUNK - i * CHUNK, CHUNK), BUCKET_SLOTS)
            grad_context = mm(m.gattn[rows, :], m.wo[...]).astype(BF16)
            m.dctx[rows, :] = grad_context
            gates = m.gate[rows, :]
            grad_query = jnp.zeros((CHUNK, head_cols), F32)
            grad_gates = jnp.zeros((CHUNK, LANES), F32)
            for h in range(heads):
                grad_probs = mm(grad_context * low_masks[h], values)
                probability = m.prob[b * heads + h, local, :]
                inner = jnp.sum(grad_probs * probability, axis=1, keepdims=True)
                low = (probability * (grad_probs - inner)).astype(BF16)
                m.gsb[h, local, :] = low
                grad_query = grad_query + mm(low, keys) * head_masks[h]
                rounded = low.astype(F32)
                one = jnp.sum(rounded * m.band[h, :, window], axis=1, keepdims=True)
                grad_gates = grad_gates + jnp.where(lane == h, one, 0.0)
                m.dband[h, :, place] += rounded * gates[:, h : h + 1]
            m.dqf[local, :] = grad_query * 0.125
            m.dgate[rows, :] = grad_gates

        hooked(0, 2, chunk, hooks)
        spread_end(2, b, 0)
        spread_end(2, b, 1)
        hooked(2, 2, chunk, hooks)
        all_rows = slice(b * BUCKET_SLOTS, (b + 1) * BUCKET_SLOTS)
        grad_key = jnp.zeros((BUCKET_SLOTS, head_cols), F32)
        grad_value = jnp.zeros((BUCKET_SLOTS, head_cols), F32)
        for h in range(heads):
            grad_key = grad_key + mm_tn(m.gsb[h], m.q[all_rows, :]) * head_masks[h]
            probs = m.prob[b * heads + h].astype(BF16)
            grad_value = grad_value + mm_tn(probs, m.dctx[all_rows, :]) * head_masks[h]
        pad = jnp.zeros((BUCKET_SLOTS, qkv_pad - 3 * head_cols), F32)
        low = jnp.concatenate([m.dqf[...], grad_key, grad_value, pad], axis=1).astype(BF16)
        m.dqkv[all_rows, 0:qkv_pad] = low
        add_row(7, low.astype(F32))

        def gate_back(i):
            rows = pl.ds(pl.multiple_of(b * BUCKET_SLOTS + i * CHUNK, CHUNK), CHUNK)
            grad = m.dgate[rows, :]
            u = m.gu[rows, :]
            w = pltpu.roll(u, LANES - 8, 1)
            grad_u = jnp.where(head_lane, grad * (w * scale - 1.0) * u * (1.0 - u), 0.0)
            grad_w = jnp.where(head_lane, grad * u * scale * w * (1.0 - w), 0.0)
            add_row(8, jnp.where(head_lane, grad * u * w, 0.0))
            linear = grad_u + pltpu.roll(grad_w, 8, 1)
            add_row(9, linear)
            hi = linear.astype(BF16).astype(F32)
            mid = (linear - hi).astype(BF16).astype(F32)
            lo = (linear - hi - mid).astype(BF16).astype(F32)
            stacked = hi
            for at, part in enumerate((mid, lo, hi, mid, hi)):
                stacked = stacked + pltpu.roll(part, 16 * (at + 1), 1)
            m.dqkv[rows, qkv_pad : qkv_pad + LANES] = stacked.astype(BF16)

        loop(BUCKET_SLOTS // CHUNK, gate_back)

    def input_part(rows):
        return mm(m.dqkv[rows, :], m.wqkvt[...])

    def token_rows(b):
        for cp in out_copies[b]:
            cp.wait()

        def chunk(i):
            at = pl.ds(pl.multiple_of(i * CHUNK, CHUNK), CHUNK)
            total = arrived(3, b, at) + DEEP_ALPHA * m.held[b, at, :]
            m.stage[b, at, :] = total.astype(BF16)

        as_it_lands(3, b, chunk)
        result_rows(1, b, m.stage, tg_out)

    def weight_grad(sent, left, right, put_part, rows=slice(None)):
        for which in sent:
            sent_all(which)

        def chunk(i):
            cols = pl.ds(pl.multiple_of(i * HALF, HALF), HALF)
            put_part(cols, mm_tn(left[rows, cols], right[rows, :]))

        loop(W // HALF, chunk)

    def add_whole(buf):
        def put_part(cols, part):
            buf[cols, :] = (buf[cols, :].astype(F32) + part).astype(BF16)

        return put_part

    def put_whole(buf):
        def put_part(cols, part):
            buf[cols, :] = part.astype(BF16)

        return put_part

    def put_qkv(cols, part):
        m.wqkv[cols, 0 : 3 * head_cols] = part[:, 0 : 3 * head_cols].astype(BF16)
        m.glin[cols, :] = part[:, qkv_pad : qkv_pad + LANES]

    def put_o(cols, part):
        m.wqkv[cols, 3 * head_cols : qkv_pad] = part[:, 0:first_o].astype(BF16)
        m.go[cols, :] = part[:, first_o:head_cols].astype(BF16)

    reduces = []

    pass_order = z_order + [0]

    def reduce_start(which, buf, land):
        for k in pass_order:

            def where(k=k):
                rows = block(2 * z_at(k) + 1 - x)
                return buf.at[rows], land.at[k], m.s_xs.at[which, k], m.s_xr.at[which, k], x_dev

            launch(reduces, where)

    def reduce_block(k, which, buf, land, out, arrive, share):
        here = land.at[k]
        remote(here, here, m.s_xs.at[which, k], m.s_xr.at[which, k], x_dev).wait_recv()
        total = buf[block(2 * z_at(k) + x), :].astype(F32) + land[k].astype(F32)
        if k == 0:
            share[...] = total
        else:
            out[k - 1] = total.astype(BF16)

            def where():
                start = out.at[k - 1]
                return start, arrive.at[k - 1], m.s_zs.at[which, k], m.s_zr.at[which, k], z_dev(k)

            launch(reduces, where)

    def reduce_pass(*matrix):
        for k in pass_order:
            reduce_block(k, *matrix)

    def reduce_end(which, arrive, share):
        total = share[...]
        for k in range(1, nz):
            here = arrive.at[k - 1]
            remote(here, here, m.s_zs.at[which, k], m.s_zr.at[which, k], z_dev(k)).wait_recv()
            total = total + arrive[k - 1].astype(F32)
        share[...] = total
        squares = total * total
        folded = jnp.zeros((owned, LANES), F32)
        for i in range(total.shape[1] // LANES):
            folded = folded + squares[:, i * LANES : (i + 1) * LANES]
        tile = jnp.zeros((8, LANES), F32)
        for i in range(owned // 8):
            tile = tile + folded[8 * i : 8 * i + 8, :]
        return tile

    def pass_on(which):
        line_step(which, 1, 2)
        line_step(which, 2, 2)

    def pass_last(which):
        for step in range(3, nz):
            line_step(which, step, 2)

    line_start(3, 2)
    gather_x(3)

    def first_pass():
        pass_on(1)
        line_start(4, 2)
        gather_x(4)

    def second_pass():
        pass_last(1)
        pass_on(2)
        line_start(5, 2)
        gather_x(5)

    attend(0, {0: first_pass, 2: second_pass})
    pass_last(2)
    line_end(1)
    turn(m.wqkv, m.wqkvt)
    m.wo[...] = jnp.concatenate([m.wqkv[:, 3 * head_cols : qkv_pad], m.wo1[...]], axis=1)
    m.wot[0:first_o, :] = m.wqkvt[3 * head_cols : qkv_pad, :]
    m.wot[first_o:head_cols, :] = m.wo1[...].T
    out_product = lambda rows: mm(m.ctx[rows, :], m.wot[...])
    exchange(0, 0, out_product)
    attend(1, {0: lambda: pass_on(3), 1: lambda: pass_last(3), 2: lambda: pass_on(4), 3: lambda: pass_last(4)})
    pass_on(5)
    exchange(0, 1, out_product)
    pass_last(5)
    norm_one(0)
    line_end(2)
    line_end(3)
    feed(0)
    line_end(4)
    line_end(5)
    turn(m.wdown, m.wdownt)
    down_product = lambda rows: mm(m.act[rows, :], m.wdownt[...])
    exchange(1, 0, down_product)
    norm_one(1)
    feed(1)
    exchange(1, 1, down_product)
    turn(m.wup, m.wupt)
    up_product = lambda rows: mm(m.gub[rows, :], m.wupt[...])
    norm_two(0)
    feed_back(0)
    exchange(2, 0, up_product)
    first_rows, last_rows = slice(0, BUCKET_SLOTS), slice(BUCKET_SLOTS, 2 * BUCKET_SLOTS)
    weight_grad((), m.gffn, m.act, put_whole(m.wdownt), first_rows)
    weight_grad((2, 3), m.nb, m.gub, put_whole(m.wup), first_rows)
    norm_two(1)
    feed_back(1)
    weight_grad((), m.gffn, m.act, add_whole(m.wdownt), last_rows)
    reduce_start(0, m.wdownt, m.xrdown)
    exchange(2, 1, up_product)
    weight_grad((), m.nb, m.gub, add_whole(m.wup), last_rows)
    reduce_start(1, m.wup, m.xrup)
    down = (0, m.wdownt, m.xrdown, m.zsdown, m.zrdown, sh_down)
    up = (1, m.wup, m.xrup, m.zsup, m.zrup, sh_up)
    out = (2, m.go, m.xro, m.zso, m.zro, sh_o)
    qkv = (3, m.wqkv, m.xrqkv, m.zsqkv, m.zrqkv, sh_qkv)
    norm_one_back(0)
    blocks = lambda ks, matrix: lambda: [reduce_block(k, *matrix) for k in ks] and None
    early = [pass_order[0:1], pass_order[1:2], pass_order[2:-1]]
    attend_back(0, {1 + i: blocks(ks, down) for i, ks in enumerate(early)})
    exchange(3, 0, input_part)
    reduce_block(0, *down)
    norm_one_back(1)
    spread_end(2, 1, 0)
    spread_end(2, 1, 1)
    weight_grad((0, 1), m.gattn, m.ctx, put_o)
    reduce_start(2, m.go, m.xro)
    attend_back(1, {i: blocks(ks, up) for i, ks in zip((0, 2, 3), early)})
    weight_grad((), m.tok, m.dqkv, put_qkv)
    reduce_start(3, m.wqkv, m.xrqkv)
    reduce_block(0, *up)
    reduce_pass(*out)
    exchange(3, 1, input_part)

    sm = m.sm
    acc = m.acc
    lead = jnp.where(yy == 0, 1.0, 0.0)

    def put(first, values):
        for i in range(values.shape[1] // LANES):
            sm[0, first + i : first + i + 1, :] = values[:, i * LANES : (i + 1) * LANES]

    def spot(values):
        return jnp.concatenate([jnp.where(T == t, values, 0.0) for t in range(4)], axis=1)

    for at, first in ((0, 0), (1, 6), (2, 12), (3, 18), (4, 36), (5, 42)):
        put(first, acc[at : at + 1, :] * lead)
    put(24, spot(acc[7:8, 0:head_cols]))
    put(30, spot(acc[7:8, 2 * head_cols : 3 * head_cols]))
    put(48, spot(acc[6:7, 0:hidden]))
    table_grad = jnp.zeros((32, LANES), F32)
    for h in range(heads):
        size = LANES // 2
        left = m.dband[h]
        while size >= 1:
            left = left[0:size, :] + pltpu.roll(left[size : 2 * size, :], long_row - size, 1) if size >= 8 else left
            if size < 8:
                break
            size //= 2
        for bit in (1, 2, 4):
            left = jnp.where(lax.rem(lax.div(sub8, bit), 2) == 1, pltpu.roll(left, long_row - bit, 1), left)
        diagonal = jnp.sum(left, axis=0, keepdims=True)
        diagonal = pltpu.roll(jnp.broadcast_to(diagonal, (8, long_row)), LANES - 1, 1)[0:1, :]
        flat = offsets * H + (T * heads + h)
        at_row = lax.div(flat, LANES)
        at_lane = lax.rem(flat, LANES)
        valid = iota((1, long_row), 1) < long_row - 1
        hot_row = jnp.where((iota((32, long_row), 0) == at_row) & valid, 1.0, 0.0)
        hot_lane = jnp.where(iota((LANES, long_row), 0) == at_lane, diagonal, 0.0)
        table_grad = table_grad + exact_nt(hot_row, hot_lane)
    sm[0, TABLE_ROW : TABLE_ROW + 30, :] = table_grad[0:30, :]

    lin_grad = m.glin[...]
    lin_grad = lin_grad + pltpu.roll(lin_grad, LANES - 16, 1) + pltpu.roll(lin_grad, LANES - 32, 1)
    lin_grad = jnp.where(own_head, lin_grad, 0.0)
    grad_u = jnp.sum(jnp.where(col_lane < 8, lin_grad, 0.0), axis=1, keepdims=True)
    grad_w = jnp.sum(jnp.where(col_lane >= 8, lin_grad, 0.0), axis=1, keepdims=True)
    by_lane = jnp.where(col_lane == 2 * col_in_head, grad_u, 0.0)
    by_lane = by_lane + jnp.where(col_lane == 2 * col_in_head + 1, grad_w, 0.0)
    sm[0, GATE_ROW : GATE_ROW + 1, :] = jnp.sum(by_lane, axis=0, keepdims=True)
    lin_total = acc[9:10, 0:LANES]
    total_u = jnp.sum(jnp.where(lane < 8, lin_total, 0.0), axis=1, keepdims=True)
    total_w = jnp.sum(jnp.where((lane >= 8) & (lane < 16), lin_total, 0.0), axis=1, keepdims=True)
    last = jnp.where(lane == 0, total_u, 0.0) + jnp.where(lane == 1, total_w, 0.0)
    scale_grad = acc[8:9, 0:LANES]
    for h in range(heads):
        one = jnp.sum(jnp.where(lane == h, scale_grad, 0.0), axis=1, keepdims=True)
        last = last + jnp.where(lane == 2 + T * heads + h, one, 0.0)
    sm[0, OFFSET_ROW : OFFSET_ROW + 1, :] = last

    small_sent = []

    def small_step(at, dev):
        cp = remote(sm.at[at], m.smr.at[at], m.s_ms.at[at], m.s_mr.at[at], dev)
        cp.start()
        small_sent.append(cp)
        return cp

    small_copy = small_step(0, core_dev)
    for k in pass_order[0:1]:
        reduce_block(k, *qkv)
    small_copy.wait_recv()
    sm[1] = sm[0] + m.smr[0]
    small_copy = small_step(1, y_dev)
    for k in pass_order[1:-1]:
        reduce_block(k, *qkv)
    token_rows(0)
    small_copy.wait_recv()
    sm[2] = sm[1] + m.smr[1]
    small_copy = small_step(2, x_dev)
    reduce_block(0, *qkv)
    small_copy.wait_recv()
    sm[3] = sm[2] + m.smr[2]
    for k in range(1, nz):
        cp = remote(
            sm.at[3], m.smz.at[z], m.s_ms.at[2 + k], m.s_mr.at[2 + k], z_dev(k)
        )
        cp.start()
        small_sent.append(cp)
    m.smz[z] = sm[3]
    token_rows(1)
    squares = reduce_end(0, m.zrdown, sh_down)
    squares = squares + reduce_end(1, m.zrup, sh_up)
    squares = squares + reduce_end(2, m.zro, sh_o)
    squares = squares + reduce_end(3, m.zrqkv, sh_qkv)
    sqt = m.sqt
    sqt[T] = squares
    tail_sent = []
    for k in range(1, 4):
        cp = remote(
            sqt.at[T], sqt.at[T], m.s_ts.at[k], m.s_tr.at[k], (D, lax.rem(T + k, 4))
        )
        cp.start()
        tail_sent.append(cp)
    for k in range(1, nz):
        here = m.smz.at[z_at(nz - k)]
        remote(here, here, m.s_ms.at[2 + k], m.s_mr.at[2 + k], z_dev(k)).wait_recv()
    small_total = m.smz[0]
    for i in range(1, nz):
        small_total = small_total + m.smz[i]
    for i in range(3):
        small_out[i] = small[i * SMALL_ROWS : (i + 1) * SMALL_ROWS, :]
    small_out[3] = small_total
    small_square = small_total * small_total
    small_tile = jnp.zeros((8, LANES), F32)
    for i in range(SMALL_ROWS // 8):
        small_tile = small_tile + small_square[8 * i : 8 * i + 8, :]
    for k in range(1, 4):
        here = sqt.at[lax.rem(T + 4 - k, 4)]
        remote(here, here, m.s_ts.at[k], m.s_tr.at[k], core_dev).wait_recv()
    sqd = m.sqd
    sqd[D] = sqt[0] + sqt[1] + sqt[2] + sqt[3]
    for k in range(1, n_dp):
        cp = remote(
            sqd.at[D], sqd.at[D], m.s_ds.at[k], m.s_dr.at[k], (lax.rem(D + k, n_dp), T)
        )
        cp.start()
        tail_sent.append(cp)
    for k in range(1, n_dp):
        here = sqd.at[lax.rem(D + n_dp - k, n_dp)]
        remote(here, here, m.s_ds.at[k], m.s_dr.at[k], core_dev).wait_recv()
    everything = small_tile
    for i in range(n_dp):
        everything = everything + sqd[i]
    sum_all = jnp.sum(jnp.sum(everything, axis=0, keepdims=True), axis=1, keepdims=True)
    norm_out[...] = jnp.broadcast_to(jnp.sqrt(sum_all), (8, LANES))

    for which in list(gathers):
        sent_all(which)
    for where in reduces:
        remote(*where()).wait_send()
    for cp in small_sent + tail_sent:
        cp.wait_send()
    for sent in core_spread.values():
        for cp in sent:
            cp.wait_send()
    for b in range(2):
        for cp in core_sent[(3, b)] + y_sent[(3, b)]:
            cp.wait_send()
    for here, there in out_copies[2:]:
        here.wait()
        there.wait()


def adam_kernel(head_cols, *refs):
    ins, rest = refs[:14], refs[14:]
    block_in, token_in = ins[12:14]
    outs, rest = rest[:14], rest[14:]
    norm_out, block_out, token_out = outs[0], outs[12], outs[13]
    held, made = rest[:12], rest[12:24]
    block_held, token_held, s_in, s_out = rest[24:]
    loads = [pltpu.make_async_copy(ins[i], held[i], s_in.at[i]) for i in range(12)]
    for cp in loads:
        cp.start()
    passing = [
        pltpu.make_async_copy(block_in, block_held, s_in.at[12]),
        pltpu.make_async_copy(token_in, token_held, s_in.at[13]),
    ]
    passed = [
        pltpu.make_async_copy(block_held, block_out, s_out.at[12]),
        pltpu.make_async_copy(token_held, token_out, s_out.at[13]),
    ]
    for cp in passing:
        cp.start()
    stores = []

    def store(i):
        cp = pltpu.make_async_copy(made[i], outs[i], s_out.at[i])
        cp.start()
        stores.append(cp)

    sh_qkv, sh_o, sh_up, sh_down, sh_small, norm, aw, am, av, fw, fm, fv = held
    (o_norm, o_am, o_av, o_aw, o_ac, o_fm, o_fv, o_fw, o_fc, o_sm, o_sv, o_sw) = made
    for i in (0, 1, 2, 3, 5):
        loads[i].wait()
    length = norm[0:1, 0:1]
    factor = CLIP_LIMIT / jnp.maximum(length, CLIP_LIMIT)
    o_norm[...] = jnp.broadcast_to(length, (8, LANES))
    store(0)
    for i in (6, 7, 8):
        loads[i].wait()
    for i in range(4):
        if i < 3:
            grad = sh_qkv[:, i * head_cols : (i + 1) * head_cols]
        else:
            grad = jnp.concatenate([sh_qkv[:, 3 * head_cols :], sh_o[...]], axis=1)
        moment, square, master = adam_step(
            aw[i], am[i], av[i], factor * grad, RATE_MATRIX, WEIGHT_DECAY
        )
        o_am[i] = moment
        o_av[i] = square
        o_aw[i] = master
        o_ac[i] = master.astype(BF16)
    for i in (1, 2, 3, 4):
        store(i)
    for first, second in zip(passing, passed, strict=True):
        first.wait()
        second.start()
    for i in (9, 10, 11):
        loads[i].wait()
    for i, share in enumerate((sh_up, sh_down)):
        moment, square, master = adam_step(
            fw[i], fm[i], fv[i], factor * share[...], RATE_MATRIX, WEIGHT_DECAY
        )
        o_fm[i] = moment
        o_fv[i] = square
        o_fw[i] = master
        o_fc[i] = master.astype(BF16)
    for i in (5, 6, 7, 8):
        store(i)
    loads[4].wait()
    moment, square, master = adam_step(
        sh_small[0], sh_small[1], sh_small[2], factor * sh_small[3], RATE_SMALL, 0.0
    )
    o_sm[...] = moment
    o_sv[...] = square
    o_sw[...] = master
    for i in (9, 10, 11):
        store(i)
    for cp in stores + passed:
        cp.wait()


def tiles(vector):
    return jnp.pad(vector, (0, SMALL_ROWS * LANES - vector.shape[0]))


def fused_body(
    n_dp,
    tokens,
    cotangent,
    clip_lengths,
    key_mask,
    rel_buckets,
    attention_weights,
    attention_first,
    attention_second,
    feedforward_weights,
    feedforward_first,
    feedforward_second,
    small_params,
    small_first,
    small_second,
):
    rows = tokens.shape[0]
    owned, head_cols = attention_weights.shape[1:]
    hidden = feedforward_weights.shape[2]
    heads = head_cols // HD
    qkv_pad = -(-3 * head_cols // LANES) * LANES
    nz = n_dp // 2
    packed = jnp.concatenate(
        [
            tiles(small_params),
            tiles(small_first),
            tiles(small_second),
            jnp.pad(rel_buckets.astype(F32), (0, 1)),
        ]
    ).reshape(-1, LANES)
    keep = key_mask.reshape(rows // LANES, LANES)
    scratch = layer_scratch(owned, nz, qkv_pad, heads, head_cols, hidden)
    names = tuple(scratch)
    vmem = pl.BlockSpec(memory_space=pltpu.VMEM)
    smem = pl.BlockSpec(memory_space=pltpu.SMEM)
    anywhere = pl.BlockSpec(memory_space=pl.ANY)
    sds = jax.ShapeDtypeStruct
    block_rows, token_rows, sh_qkv, sh_o, sh_up, sh_down, sh_small, norm = pl.pallas_call(
        partial(layer_kernel, names, (n_dp, owned, qkv_pad, heads, head_cols, hidden)),
        out_shape=(
            sds((rows, W), BF16),
            sds((rows, W), BF16),
            sds((owned, qkv_pad), F32),
            sds((owned, LANES), F32),
            sds((owned, hidden), F32),
            sds((owned, hidden), F32),
            sds((4, SMALL_ROWS, LANES), F32),
            sds((8, LANES), F32),
        ),
        in_specs=[anywhere, anywhere, smem, vmem, vmem, vmem, vmem],
        out_specs=(anywhere, anywhere, vmem, vmem, vmem, vmem, vmem, vmem),
        scratch_shapes=list(scratch.values()),
        compiler_params=pltpu.CompilerParams(
            collective_id=1, has_side_effects=True, vmem_limit_bytes=62 * 1024 * 1024
        ),
        name="layer",
    )(tokens, cotangent, clip_lengths, keep, attention_weights, feedforward_weights, packed)
    like = lambda a, dtype=F32: sds(a.shape, dtype)
    small_like = sds((SMALL_ROWS, LANES), F32)
    made = (
        sds((8, LANES), F32),
        like(attention_weights),
        like(attention_weights),
        like(attention_weights),
        like(attention_weights, BF16),
        like(feedforward_weights),
        like(feedforward_weights),
        like(feedforward_weights),
        like(feedforward_weights, BF16),
        small_like,
        small_like,
        small_like,
    )
    operands = (
        sh_qkv,
        sh_o,
        sh_up,
        sh_down,
        sh_small,
        norm,
        attention_weights,
        attention_first,
        attention_second,
        feedforward_weights,
        feedforward_first,
        feedforward_second,
        block_rows,
        token_rows,
    )
    in_vmem = lambda a: pltpu.VMEM(a.shape, a.dtype)
    results = pl.pallas_call(
        partial(adam_kernel, head_cols),
        out_shape=(*made, like(tokens, BF16), like(tokens, BF16)),
        in_specs=[anywhere] * len(operands),
        out_specs=(anywhere,) * (len(made) + 2),
        scratch_shapes=[in_vmem(a) for a in operands[:12]]
        + [in_vmem(a) for a in made]
        + [in_vmem(tokens), in_vmem(tokens)]
        + [pltpu.SemaphoreType.DMA((14,)), pltpu.SemaphoreType.DMA((14,))],
        compiler_params=pltpu.CompilerParams(vmem_limit_bytes=62 * 1024 * 1024),
        name="adam",
    )(*operands)
    length = small_params.shape[0]
    flat = lambda a: a.reshape(-1)[:length]
    return (
        results[0][0, 0],
        *results[1:9],
        flat(results[9]),
        flat(results[10]),
        flat(results[11]),
        *results[12:],
    )


def fused_fits(mesh, owned):
    return mesh.shape["tensor"] == 4 and mesh.shape["dp"] % 2 == 0 and owned % 16 == 0

def solution(mesh):
    in_specs = (
        P("dp", None),
        P("dp", None),
        P("dp", None),
        P("dp"),
        P(),
        P(None, "dp", "tensor"),
        P(None, "dp", "tensor"),
        P(None, "dp", "tensor"),
        P(None, "dp", "tensor"),
        P(None, "dp", "tensor"),
        P(None, "dp", "tensor"),
        P(),
        P(),
        P(),
    )
    out_specs = (
        P(),
        P(None, "dp", "tensor"),
        P(None, "dp", "tensor"),
        P(None, "dp", "tensor"),
        P(None, "dp", "tensor"),
        P(None, "dp", "tensor"),
        P(None, "dp", "tensor"),
        P(None, "dp", "tensor"),
        P(None, "dp", "tensor"),
        P(),
        P(),
        P(),
        P("dp", None),
        P("dp", None),
    )
    n_dp = mesh.shape["dp"]
    body = general_body
    if fused_fits(mesh, MODEL_WIDTH // n_dp):
        body = partial(fused_body, n_dp)
    return jax.shard_map(body, mesh=mesh, in_specs=in_specs, out_specs=out_specs, check_vma=False)
```

```python
from functools import partial
from types import SimpleNamespace

import jax
import jax.numpy as jnp
from jax import lax
from jax.experimental import pallas as pl
from jax.experimental.pallas import tpu as pltpu
from jax.sharding import PartitionSpec as P

MODEL_WIDTH = 768
H = 12
HD = 64
FF = 3072
NB = 320
BUCKET_SLOTS = 512
CLIPS = 8
STEP = 5


FULL_PRECISION = lax.Precision.HIGHEST
DEEP_ALPHA = 24.0**0.25
NORM_EPSILON = 1e-05
MASK_VALUE = -1e30
BETA_FIRST = 0.9
BETA_SECOND = 0.98
RATE_MATRIX = 0.03
RATE_SMALL = 0.5
WEIGHT_DECAY = 0.01
ADAM_EPSILON = 1e-08
CLIP_LIMIT = 0.1


def layer_norm(values, norm_gain, norm_shift):
    row_mean = jnp.mean(values, axis=-1, keepdims=True)
    centred = values - row_mean
    variance = jnp.mean(centred * centred, axis=-1, keepdims=True)
    return centred * lax.rsqrt(variance + NORM_EPSILON) * norm_gain + norm_shift


def gelu_exact(values):
    return jax.nn.gelu(values, approximate=False)


def split_small(vector):
    widths = [MODEL_WIDTH] * 8 + [FF, NB * H, HD * 2, 2, H]
    pieces = []
    offset = 0
    for extent in widths:
        pieces.append(vector[offset : offset + extent])
        offset += extent
    return pieces


def allowed_mask(lengths_row, keep_row):
    positions = jnp.arange(BUCKET_SLOTS, dtype=jnp.int32)
    clip_ends = jnp.cumsum(lengths_row)
    segment = jnp.sum((positions[:, None] >= clip_ends[None, :]).astype(jnp.int32), axis=1)
    live_keys = (keep_row == 1) & (segment < CLIPS)
    same_clip = segment[:, None] == segment[None, :]
    return same_clip & (live_keys[None, :] | (positions[:, None] == positions[None, :]))


def band_matrix(diagonals):
    head_count = diagonals.shape[0]
    length = (diagonals.shape[1] + 1) // 2
    padded = jnp.concatenate([diagonals, jnp.zeros((head_count, 1), diagonals.dtype)], axis=1)
    repeated = jnp.tile(padded, (1, length))
    folded = repeated[:, : length * (2 * length - 1)].reshape(head_count, length, 2 * length - 1)
    return folded[:, :, length - 1 :]


def position_terms(head_inputs, gate_matrix, gate_offset, scale_local, table_local, rel_buckets):
    linear = (
        jnp.einsum(
            "blhd,dk->bhlk", head_inputs, gate_matrix.reshape(HD, 2), precision=FULL_PRECISION
        )
        + gate_offset
    )
    sigmoid = jax.nn.sigmoid(linear)
    gate = sigmoid[..., 0] * (sigmoid[..., 1] * scale_local[None, :, None] - 1.0) + 2.0
    onehot = (rel_buckets[:, None] == jnp.arange(NB, dtype=jnp.int32)[None, :]).astype(jnp.float32)
    per_offset = jnp.dot(
        onehot, table_local, precision=FULL_PRECISION, preferred_element_type=jnp.float32
    )
    toeplitz = band_matrix(per_offset.T)
    return gate[..., None] * toeplitz[None]


def adam_step(weights, moment, second, gradient, step_rate, decay_rate):
    moment_new = BETA_FIRST * moment + (1.0 - BETA_FIRST) * gradient
    second_new = BETA_SECOND * second + (1.0 - BETA_SECOND) * gradient * gradient
    moment_hat = moment_new / (1.0 - BETA_FIRST**STEP)
    second_hat = second_new / (1.0 - BETA_SECOND**STEP)
    master = weights - step_rate * (
        moment_hat / (jnp.sqrt(second_hat) + ADAM_EPSILON) + decay_rate * weights
    )
    return (moment_new, second_new, master)


def placed(total_length, piece, start):
    return lax.dynamic_update_slice_in_dim(jnp.zeros((total_length,), jnp.float32), piece, start, 0)


def column_sum(values):
    return jnp.sum(values.astype(jnp.float32), axis=0)


def general_body(
    tokens,
    cotangent,
    clip_lengths,
    key_mask,
    rel_buckets,
    attention_weights,
    attention_first,
    attention_second,
    feedforward_weights,
    feedforward_first,
    feedforward_second,
    small_params,
    small_first,
    small_second,
):
    gathered_attention, gathered_forward = (
        lax.all_gather(attention_weights.astype(jnp.bfloat16), "dp", axis=1, tiled=True),
        lax.all_gather(feedforward_weights.astype(jnp.bfloat16), "dp", axis=1, tiled=True),
    )
    query_weight = gathered_attention[0]
    key_weight = gathered_attention[1]
    value_weight = gathered_attention[2]
    output_weight = gathered_attention[3]
    up_weight = gathered_forward[0]
    down_weight = gathered_forward[1]
    head_cols = query_weight.shape[1]
    heads_local = head_cols // HD
    hidden_local = up_weight.shape[1]
    tensor_rank = lax.axis_index("tensor")
    col_start = tensor_rank * head_cols
    head_start = tensor_rank * heads_local
    hidden_start = tensor_rank * hidden_local
    row_count = tokens.shape[0]
    bucket_count = row_count // BUCKET_SLOTS
    (
        gain_one,
        shift_one,
        gain_two,
        shift_two,
        bias_query,
        bias_value,
        bias_output,
        bias_down,
        bias_up,
        rel_table,
        gate_matrix,
        gate_offset,
        gate_scale,
    ) = split_small(small_params)
    local_bias_query = lax.dynamic_slice_in_dim(bias_query, col_start, head_cols)
    local_bias_value = lax.dynamic_slice_in_dim(bias_value, col_start, head_cols)
    local_bias_up = lax.dynamic_slice_in_dim(bias_up, hidden_start, hidden_local)
    scale_local = lax.dynamic_slice_in_dim(gate_scale, head_start, heads_local)
    table_local = lax.dynamic_slice_in_dim(rel_table.reshape(NB, H), head_start, heads_local, 1)
    allowed = jax.vmap(allowed_mask)(clip_lengths, key_mask.reshape(bucket_count, BUCKET_SLOTS))[
        :, None
    ]
    leading = (tensor_rank == 0).astype(jnp.float32)
    inputs = tokens.astype(jnp.float32)
    upstream = cotangent.astype(jnp.float32)
    query_bf = (
        jnp.dot(tokens, query_weight, preferred_element_type=jnp.float32) + local_bias_query
    ).astype(jnp.bfloat16)
    key_bf = jnp.dot(tokens, key_weight, preferred_element_type=jnp.float32).astype(jnp.bfloat16)
    value_bf = (
        jnp.dot(tokens, value_weight, preferred_element_type=jnp.float32) + local_bias_value
    ).astype(jnp.bfloat16)
    head_shape = (bucket_count, BUCKET_SLOTS, heads_local, HD)
    heads_of_query = query_bf.reshape(head_shape)
    heads_of_key = key_bf.reshape(head_shape)
    heads_of_value = value_bf.reshape(head_shape)
    head_inputs = lax.dynamic_slice_in_dim(inputs, col_start, head_cols, 1).reshape(head_shape)
    extra, pull_position = jax.vjp(
        partial(position_terms, rel_buckets=rel_buckets),
        head_inputs,
        gate_matrix,
        gate_offset,
        scale_local,
        table_local,
    )
    attention_logits = (
        jnp.einsum(
            "blhd,bmhd->bhlm", heads_of_query, heads_of_key, preferred_element_type=jnp.float32
        )
        * 0.125
    )
    scores = jnp.where(allowed, attention_logits + extra, MASK_VALUE)
    row_max = jnp.max(scores, axis=-1, keepdims=True)
    exponent = jnp.exp(scores - row_max)
    denominator = jnp.sum(exponent, axis=-1, keepdims=True)
    log_total = row_max + jnp.log(denominator)
    probs_bf = (exponent / denominator).astype(jnp.bfloat16)
    context_bf = (
        jnp.einsum("bhlm,bmhd->blhd", probs_bf, heads_of_value, preferred_element_type=jnp.float32)
        .reshape(row_count, head_cols)
        .astype(jnp.bfloat16)
    )
    attention_part = jnp.einsum(
        "nw,dw->nd", context_bf, output_weight, preferred_element_type=jnp.float32
    )
    attention = lax.psum(attention_part, "tensor") + bias_output
    normed, pull_norm_one = jax.vjp(
        layer_norm, DEEP_ALPHA * inputs + attention, gain_one, shift_one
    )
    normed_bf = normed.astype(jnp.bfloat16)
    up_pre = jnp.dot(normed_bf, up_weight, preferred_element_type=jnp.float32) + local_bias_up
    activated, pull_gelu = jax.vjp(gelu_exact, up_pre)
    activated_bf = activated.astype(jnp.bfloat16)
    down_part = jnp.einsum(
        "nf,df->nd", activated_bf, down_weight, preferred_element_type=jnp.float32
    )
    feedforward = lax.psum(down_part, "tensor") + bias_down
    output_values, pull_norm_two = jax.vjp(
        layer_norm, DEEP_ALPHA * normed + feedforward, gain_two, shift_two
    )
    block_output = output_values.astype(jnp.bfloat16)
    grad_res_two, grad_gain_two, grad_shift_two = pull_norm_two(upstream)
    grad_ffn_share = grad_res_two.astype(jnp.bfloat16)
    grad_bias_down = column_sum(grad_ffn_share)
    down_grad = jnp.einsum(
        "nd,nf->df", grad_ffn_share, activated_bf, preferred_element_type=jnp.float32
    )
    grad_activated = jnp.einsum(
        "nd,df->nf", grad_ffn_share, down_weight, preferred_element_type=jnp.float32
    )
    (grad_up_pre,) = pull_gelu(grad_activated)
    grad_up_bf = grad_up_pre.astype(jnp.bfloat16)
    grad_bias_up = column_sum(grad_up_bf)
    up_grad = jnp.einsum("nd,nf->df", normed_bf, grad_up_bf, preferred_element_type=jnp.float32)
    normed_part = jnp.einsum("nf,df->nd", grad_up_bf, up_weight, preferred_element_type=jnp.float32)
    normed_sum = lax.psum(normed_part, "tensor")
    grad_normed = normed_sum + DEEP_ALPHA * grad_res_two
    grad_res_one, grad_gain_one, grad_shift_one = pull_norm_one(grad_normed)
    grad_attention_share = grad_res_one.astype(jnp.bfloat16)
    grad_bias_output = column_sum(grad_attention_share)
    output_grad = jnp.einsum(
        "nd,nw->dw", grad_attention_share, context_bf, preferred_element_type=jnp.float32
    )
    grad_context_bf = jnp.einsum(
        "nd,dw->nw", grad_attention_share, output_weight, preferred_element_type=jnp.float32
    ).astype(jnp.bfloat16)
    grad_heads = grad_context_bf.reshape(head_shape)
    attention_probabilities = jnp.exp(scores - log_total)
    recomputed_bf = attention_probabilities.astype(jnp.bfloat16)
    grad_probs = jnp.einsum(
        "blhd,bmhd->bhlm", grad_heads, heads_of_value, preferred_element_type=jnp.float32
    )
    inner = jnp.sum(grad_probs * attention_probabilities, axis=-1, keepdims=True)
    grad_scores_bf = (attention_probabilities * (grad_probs - inner)).astype(jnp.bfloat16)
    grad_query = (
        (
            jnp.einsum(
                "bhlm,bmhd->blhd", grad_scores_bf, heads_of_key, preferred_element_type=jnp.float32
            )
            * 0.125
        )
        .astype(jnp.bfloat16)
        .reshape(row_count, head_cols)
    )
    grad_key = (
        (
            jnp.einsum(
                "bhlm,blhd->bmhd",
                grad_scores_bf,
                heads_of_query,
                preferred_element_type=jnp.float32,
            )
            * 0.125
        )
        .astype(jnp.bfloat16)
        .reshape(row_count, head_cols)
    )
    grad_value = (
        jnp.einsum("bhlm,blhd->bmhd", recomputed_bf, grad_heads, preferred_element_type=jnp.float32)
        .astype(jnp.bfloat16)
        .reshape(row_count, head_cols)
    )
    grad_head_inputs, grad_gate_matrix, grad_gate_offset, grad_scale_local, grad_table_local = (
        pull_position(grad_scores_bf.astype(jnp.float32))
    )
    query_grad = jnp.einsum("nd,nw->dw", tokens, grad_query, preferred_element_type=jnp.float32)
    key_grad = jnp.einsum("nd,nw->dw", tokens, grad_key, preferred_element_type=jnp.float32)
    value_grad = jnp.einsum("nd,nw->dw", tokens, grad_value, preferred_element_type=jnp.float32)
    input_part = (
        jnp.einsum("nw,dw->nd", grad_query, query_weight, preferred_element_type=jnp.float32)
        + jnp.einsum("nw,dw->nd", grad_key, key_weight, preferred_element_type=jnp.float32)
        + jnp.einsum("nw,dw->nd", grad_value, value_weight, preferred_element_type=jnp.float32)
    )
    own_columns = lax.dynamic_slice_in_dim(input_part, col_start, head_cols, 1)
    input_part = lax.dynamic_update_slice_in_dim(
        input_part, own_columns + grad_head_inputs.reshape(row_count, head_cols), col_start, 1
    )
    grad_inputs = lax.psum(input_part, "tensor") + DEEP_ALPHA * grad_res_one
    tokens_grad = grad_inputs.astype(jnp.bfloat16)
    table_grad = lax.dynamic_update_slice_in_dim(
        jnp.zeros((NB, H), jnp.float32), grad_table_local, head_start, 1
    ).reshape(-1)
    local_small = jnp.concatenate(
        [
            grad_gain_one * leading,
            grad_shift_one * leading,
            grad_gain_two * leading,
            grad_shift_two * leading,
            placed(MODEL_WIDTH, column_sum(grad_query), col_start),
            placed(MODEL_WIDTH, column_sum(grad_value), col_start),
            grad_bias_output * leading,
            grad_bias_down * leading,
            placed(FF, grad_bias_up, hidden_start),
            table_grad,
            grad_gate_matrix,
            grad_gate_offset,
            placed(H, grad_scale_local, head_start),
        ]
    )
    small_grad = lax.psum(local_small, ("dp", "tensor"))
    local_attention = jnp.stack([query_grad, key_grad, value_grad, output_grad])
    local_forward = jnp.stack([up_grad, down_grad])
    summed_attention, summed_forward = lax.psum((local_attention, local_forward), "dp")
    owner_rank = lax.axis_index("dp")
    owned_rows = attention_weights.shape[1]
    share_attention = lax.dynamic_slice_in_dim(
        summed_attention, owner_rank * owned_rows, owned_rows, 1
    )
    share_forward = lax.dynamic_slice_in_dim(summed_forward, owner_rank * owned_rows, owned_rows, 1)
    share_squares = jnp.sum(share_attention * share_attention) + jnp.sum(
        share_forward * share_forward
    )
    big_squares = lax.psum(share_squares, ("dp", "tensor"))
    global_norm = jnp.sqrt(big_squares + jnp.sum(small_grad * small_grad))
    factor = CLIP_LIMIT / jnp.maximum(global_norm, CLIP_LIMIT)
    attention_moment, attention_square, attention_master = adam_step(
        attention_weights,
        attention_first,
        attention_second,
        factor * share_attention,
        RATE_MATRIX,
        WEIGHT_DECAY,
    )
    feedforward_moment, feedforward_square, feedforward_master = adam_step(
        feedforward_weights,
        feedforward_first,
        feedforward_second,
        factor * share_forward,
        RATE_MATRIX,
        WEIGHT_DECAY,
    )
    small_moment, small_square, small_master = adam_step(
        small_params, small_first, small_second, factor * small_grad, RATE_SMALL, 0.0
    )
    return (
        global_norm,
        attention_moment,
        attention_square,
        attention_master,
        attention_master.astype(jnp.bfloat16),
        feedforward_moment,
        feedforward_square,
        feedforward_master,
        feedforward_master.astype(jnp.bfloat16),
        small_moment,
        small_square,
        small_master,
        block_output,
        tokens_grad,
    )


F32 = jnp.float32
BF16 = jnp.bfloat16
MESH_ID = pl.DeviceIdType.MESH
LANES = 128
SMALL_ROWS = 104
QUARTER = 32
SUM_ROWS = 4 * QUARTER
TABLE_ROW = 72
GATE_ROW = 102
OFFSET_ROW = 103
INV_SQRT2 = 0.5**0.5
INV_SQRT_2PI = 0.3989422804014327
CHUNK = 128
HALF = 256
W = MODEL_WIDTH
NT = (((1,), (1,)), ((), ()))
TN = (((0,), (0,)), ((), ()))


def mm(a, b):
    return jnp.dot(a, b, preferred_element_type=F32)


def mm_nt(a, b):
    return lax.dot_general(a, b, NT, preferred_element_type=F32)


def mm_tn(a, b):
    return lax.dot_general(a, b, TN, preferred_element_type=F32)


def exact_nt(a, b):
    return lax.dot_general(a, b, NT, precision=FULL_PRECISION, preferred_element_type=F32)


def exact_tn(a, b):
    return lax.dot_general(a, b, TN, precision=FULL_PRECISION, preferred_element_type=F32)


def exact_mm(a, b):
    return jnp.dot(a, b, precision=FULL_PRECISION, preferred_element_type=F32)


def iota(shape, axis):
    return lax.broadcasted_iota(jnp.int32, shape, axis)


def layer_scratch(owned, nz, qkv_pad, heads, head_cols, hidden):
    rows = 2 * BUCKET_SLOTS
    dma = pltpu.SemaphoreType.DMA
    vm = pltpu.VMEM
    shapes = dict(
        wa=vm((4, owned, head_cols), F32),
        wf=vm((2, owned, hidden), F32),
        keep=vm((rows // LANES, LANES), jnp.int32),
        small=vm((3 * SMALL_ROWS + 2 * BUCKET_SLOTS // LANES, LANES), F32),
        shqkv=vm((owned, qkv_pad), F32),
        sho=vm((owned, LANES), F32),
        shup=vm((owned, hidden), F32),
        shdown=vm((owned, hidden), F32),
        smallout=vm((4, SMALL_ROWS, LANES), F32),
        tok=vm((rows, W), BF16),
        cot=vm((2, HALF, W), BF16),
        wqkv=vm((W, qkv_pad), BF16),
        wo1=vm((W, LANES), BF16),
        wo=vm((W, head_cols), BF16),
        wot=vm((head_cols, W), BF16),
        wqkvt=vm((qkv_pad + LANES, W), BF16),
        wupt=vm((hidden, W), BF16),
        wdownt=vm((hidden, W), BF16),
        go=vm((W, LANES), BF16),
        glin=vm((W, LANES), F32),
        wup=vm((W, hidden), BF16),
        wdown=vm((W, hidden), BF16),
        q=vm((rows, head_cols), BF16),
        k=vm((rows, head_cols), BF16),
        v=vm((rows, head_cols), BF16),
        kt=vm((head_cols, rows), BF16),
        qt=vm((head_cols, rows), BF16),
        dctxt=vm((head_cols, BUCKET_SLOTS), BF16),
        vt=vm((head_cols, rows), BF16),
        ctx=vm((rows, head_cols), BF16),
        dqkv=vm((rows, qkv_pad + LANES), BF16),
        prob=vm((2 * heads, BUCKET_SLOTS, BUCKET_SLOTS), F32),
        gsb=vm((heads * BUCKET_SLOTS, BUCKET_SLOTS), BF16),
        dqf=vm((BUCKET_SLOTS, head_cols), F32),
        mbias=vm((2, BUCKET_SLOTS, BUCKET_SLOTS), BF16),
        band=vm((heads, LANES, 2 * BUCKET_SLOTS), F32),
        dband=vm((heads, LANES, 2 * BUCKET_SLOTS), F32),
        gate=vm((rows, LANES), F32),
        gu=vm((rows, LANES), F32),
        gmat=vm((W, LANES), F32),
        vecs=vm((16, W), F32),
        acc=vm((16, W), F32),
        nb=vm((rows, W), BF16),
        held=vm((2, HALF, W), F32),
        xh1=vm((2, HALF, W), F32),
        rstd1=vm((2, HALF, LANES), F32),
        act=vm((rows, hidden), BF16),
        gelup=vm((rows, hidden), F32),
        gffn=vm((rows, W), BF16),
        gub=vm((rows, hidden), BF16),
        gattn=vm((rows, W), BF16),
        stage=vm((2, HALF, W), BF16),
        ownf=vm((HALF, W), F32),
        cs=vm((2, HALF, W), BF16),
        cr=vm((2, HALF, W), BF16),
        ys=vm((2, HALF, W), BF16),
        yr=vm((2, 2, HALF, W), BF16),
        xrqkv=vm((nz, owned, qkv_pad), BF16),
        xro=vm((nz, owned, LANES), BF16),
        xrup=vm((nz, owned, hidden), BF16),
        xrdown=vm((nz, owned, hidden), BF16),
        zsqkv=vm((nz - 1, owned, qkv_pad), BF16),
        zso=vm((nz - 1, owned, LANES), BF16),
        zsup=vm((nz - 1, owned, hidden), BF16),
        zsdown=vm((nz - 1, owned, hidden), BF16),
        zrqkv=vm((nz - 1, owned, qkv_pad), BF16),
        zro=vm((nz - 1, owned, LANES), BF16),
        zrup=vm((nz - 1, owned, hidden), BF16),
        zrdown=vm((nz - 1, owned, hidden), BF16),
        sm=vm((SUM_ROWS, LANES), F32),
        smc=vm((2, QUARTER, LANES), F32),
        smh=vm((2, QUARTER, LANES), F32),
        smy=vm((QUARTER, LANES), F32),
        smv=vm((QUARTER, LANES), F32),
        smx=vm((QUARTER, LANES), F32),
        smz=vm((nz, QUARTER, LANES), F32),
        sma=vm((SUM_ROWS, LANES), F32),
        sqt=vm((4, 8, LANES), F32),
        sqd=vm((2 * nz, 8, LANES), F32),
        s_in=dma((7,)),
        s_out=dma((5,)),
        s_gs=dma((6,)),
        s_gr=dma((6,)),
        s_ls=dma((7, 2, nz)),
        s_lr=dma((7, 2, nz)),
        s_lxs=dma((7, 2, nz)),
        s_lxr=dma((7, 2, nz)),
        s_cs=dma((4, 2, 2)),
        s_cr=dma((4, 2, 2)),
        s_ys=dma((4, 2, 2)),
        s_yr=dma((4, 2, 2)),
        s_as=dma((3, 2, 2)),
        s_ar=dma((3, 2, 2)),
        s_ol=dma((2, 2)),
        s_os=dma((2, 2)),
        s_or=dma((2, 2)),
        s_xs=dma((4, nz)),
        s_xr=dma((4, nz)),
        s_zs=dma((4, nz)),
        s_zr=dma((4, nz)),
        s_ms=dma((6 + nz,)),
        s_mr=dma((6 + nz,)),
        s_ts=dma((4,)),
        s_tr=dma((4,)),
        s_ds=dma((2 * nz,)),
        s_dr=dma((2 * nz,)),
    )
    return shapes


def layer_kernel(names, dims, *refs):
    n_dp, owned, qkv_pad, heads, head_cols, hidden = dims
    nz = n_dp // 2
    (tok_in, cot_in, lens, keep_in, wa_in, wf_in, small_in) = refs[:7]
    (bo_out, tg_out, out_qkv, out_o, out_up, out_down, out_small, norm_out) = refs[7:15]
    m = SimpleNamespace(**dict(zip(names, refs[15:], strict=True)))
    D = lax.axis_index("dp")
    T = lax.axis_index("tensor")
    z = lax.div(D, 2)
    x = lax.rem(D, 2)
    c = lax.rem(T, 2)
    yy = lax.div(T, 2)
    core_dev = (D, T + 1 - 2 * c)
    y_dev = (D, lax.rem(T + 2, 4))
    x_dev = (z * 2 + 1 - x, T)

    def z_at(k):
        total, bit = 0, 1
        while bit < nz:
            here = lax.rem(lax.div(z, bit), 2)
            total = total + bit * (1 - here if k & bit else here)
            bit *= 2
        return total

    def z_dev(k):
        return (z_at(k) * 2 + x, T)

    def remote(src, dst, ss, rs, dev):
        return pltpu.make_async_remote_copy(
            src_ref=src, dst_ref=dst, send_sem=ss, recv_sem=rs, device_id=dev, device_id_type=MESH_ID
        )

    def loop(n, step):
        def run(i, carry):
            step(i)
            return carry

        lax.fori_loop(0, n, run, 0)

    def block(owner):
        return pl.ds(pl.multiple_of(owner * owned, owned), owned)

    wa, wf, keep, small = m.wa, m.wf, m.keep, m.small
    sh_qkv, sh_o, sh_up, sh_down, small_out = m.shqkv, m.sho, m.shup, m.shdown, m.smallout
    first_loads = []
    for i, (source, target) in enumerate(((wa_in, wa), (wf_in, wf), (small_in, small), (keep_in, keep))):
        cp = pltpu.make_async_copy(source, target, m.s_in.at[3 + i])
        cp.start()
        first_loads.append(cp)
    tok_copy = pltpu.make_async_copy(tok_in, m.tok, m.s_in.at[0])
    tok_copy.start()
    cot_copies = []
    for b in range(2):
        rows = pl.ds(pl.multiple_of(b * BUCKET_SLOTS + c * HALF, HALF), HALF)
        cp = pltpu.make_async_copy(cot_in.at[rows], m.cot.at[b], m.s_in.at[1 + b])
        cp.start()
        cot_copies.append(cp)
    barrier = pltpu.get_barrier_semaphore()
    for k in range(1, 4):
        pl.semaphore_signal(barrier, inc=1, device_id=(D, lax.rem(T + k, 4)), device_id_type=MESH_ID)
    for k in range(1, n_dp):
        pl.semaphore_signal(barrier, inc=1, device_id=(lax.rem(D + k, n_dp), T), device_id_type=MESH_ID)
    for cp in first_loads:
        cp.wait()
    mine = block(D)
    first_o = qkv_pad - 3 * head_cols
    m.wqkv[mine, :] = jnp.concatenate([wa[0], wa[1], wa[2], wa[3, :, 0:first_o]], axis=1).astype(BF16)
    m.wo1[mine, :] = wa[3, :, first_o:head_cols].astype(BF16)
    m.wup[mine, :] = wf[0].astype(BF16)
    m.wdown[mine, :] = wf[1].astype(BF16)
    pl.semaphore_wait(barrier, 3 + n_dp - 1)

    part_rows = owned // 2 if owned % 32 == 0 else owned
    pieces = [(m.wqkv, 0, owned), (m.wo1, 0, owned)]
    for buf in (m.wup, m.wdown):
        pieces.append((buf, 0, part_rows))
        pieces.append((buf, owned - part_rows, part_rows))

    pieces.append(pieces[-1])
    across = len(pieces) - 1
    straight = (across - 1, across)

    def piece(which, owner_z, other_column=False):
        buf, first, count = pieces[which]
        column = 1 - x if other_column != (which == across) else x
        return buf.at[pl.ds(pl.multiple_of((owner_z * 2 + column) * owned + first, 16), count)]

    gathers = {}

    def launch(record, where):
        remote(*where()).start()
        record.append(where)

    def when(condition, action):
        pl.when(condition)(action)

    def from_z(way, step):
        owner_z = z - step if way == 0 else z + step
        return owner_z, (owner_z >= 0) if way == 0 else (owner_z < nz)

    def send_when(which, condition, where):
        when(condition(), lambda: remote(*where()).start())
        gathers.setdefault(which, []).append((condition, where))

    def line_send(which, way, step, hops):
        origin = step - hops

        def where():
            part = piece(which, from_z(way, origin)[0])
            target = ((z + hops if way == 0 else z - hops) * 2 + x, T)
            return part, part, m.s_ls.at[which, way, step], m.s_lr.at[which, way, step], target

        def condition():
            there = (z + hops < nz) if way == 0 else (z >= hops)
            return there & from_z(way, origin)[1]

        send_when(which, condition, where)

    def line_start(which, hops):
        for hop in range(1, hops + 1):
            for way in range(2):
                line_send(which, way, hop, hop)

    def gather_x(which):
        def where():
            own = piece(which, z)
            return own, own, m.s_gs.at[which], m.s_gr.at[which], x_dev

        send_when(which, lambda: D >= 0, where)

    def line_step(which, step, hops):
        for way in range(2):

            def landed(way=way):
                part = piece(which, from_z(way, step)[0])
                sems = m.s_ls.at[which, way, step], m.s_lr.at[which, way, step]
                remote(part, part, *sems, x_dev).wait_recv()

            when(from_z(way, step)[1], landed)
            if step >= hops and step + 1 < nz:
                line_send(which, way, step + 1, 1)
            if which in straight:
                continue

            def where(way=way):
                part = piece(which, from_z(way, step)[0])
                return part, part, m.s_lxs.at[which, way, step], m.s_lxr.at[which, way, step], x_dev

            send_when(which, lambda way=way: from_z(way, step)[1], where)

    def partner_landed(which):
        part = piece(which, z, True)
        remote(part, part, m.s_gs.at[which], m.s_gr.at[which], x_dev).wait_recv()

    def line_end(which):
        partner_landed(which)
        for step in range(1, nz):
            for way in range(2):

                def landed(way=way):
                    part = piece(which, from_z(way, step)[0], True)
                    sems = m.s_lxs.at[which, way, step], m.s_lxr.at[which, way, step]
                    remote(part, part, *sems, x_dev).wait_recv()

                when(from_z(way, step)[1], landed)

    def sent_all(which):
        for condition, where in gathers.pop(which):
            when(condition(), lambda where=where: remote(*where()).wait_send())

    def turn(source, target):
        count = source.shape[1]
        if count % LANES:
            target[...] = source[...].T
            return
        step = HALF if count % HALF == 0 else LANES

        def chunk(i):
            at = pl.ds(pl.multiple_of(i * step, step), step)
            target[at, :] = source[:, at].T

        loop(count // step, chunk)

    line_start(0, 1)
    gather_x(0)
    gather_x(across - 1)

    def small_row(first, count):
        return jnp.concatenate([small[first + i : first + i + 1, :] for i in range(count)], axis=1)

    def pick(values, size):
        total = jnp.zeros((1, size), F32)
        for t in range(4):
            total = total + jnp.where(T == t, values[:, t * size : (t + 1) * size], 0.0)
        return total

    vecs = m.vecs
    vecs[...] = jnp.zeros_like(vecs)
    m.acc[...] = jnp.zeros((16, W), F32)
    for at, first in ((0, 0), (1, 6), (2, 12), (3, 18), (4, 36), (5, 42)):
        vecs[at : at + 1, :] = small_row(first, W // LANES)
    vecs[6:7, :] = pick(small_row(48, FF // LANES), hidden)
    bq = pick(small_row(24, W // LANES), head_cols)
    bv = pick(small_row(30, W // LANES), head_cols)
    bias_qkv = jnp.concatenate(
        [bq, jnp.zeros_like(bq), bv, jnp.zeros((1, qkv_pad - 3 * head_cols), F32)], axis=1
    )
    vecs[7:8, 0:qkv_pad] = bias_qkv

    lane = iota((1, LANES), 1)
    col = iota((W, LANES), 0)
    col_lane = iota((W, LANES), 1)
    gate_row = small[GATE_ROW : GATE_ROW + 1, :]
    col_in_head = lax.rem(col, HD)
    picked_u = jnp.sum(
        jnp.where(col_lane == 2 * col_in_head, gate_row, 0.0), axis=1, keepdims=True
    )
    picked_w = jnp.sum(
        jnp.where(col_lane == 2 * col_in_head + 1, gate_row, 0.0), axis=1, keepdims=True
    )
    in_group = lax.rem(col_lane, 8)
    own_head = (col_lane < 16) & (in_group < heads) & (lax.div(col, HD) == T * heads + in_group)
    m.gmat[...] = jnp.where(own_head, jnp.where(col_lane < 8, picked_u, picked_w), 0.0)
    offset_row = small[OFFSET_ROW : OFFSET_ROW + 1, :]
    offset_u = jnp.sum(jnp.where(lane == 0, offset_row, 0.0), axis=1, keepdims=True)
    offset_w = jnp.sum(jnp.where(lane == 1, offset_row, 0.0), axis=1, keepdims=True)
    scale = jnp.zeros((1, LANES), F32)
    for h in range(heads):
        one = jnp.sum(jnp.where(lane == 2 + T * heads + h, offset_row, 0.0), axis=1, keepdims=True)
        scale = scale + jnp.where(lane == h, one, 0.0)
    head_lane = lane < heads

    line_step(0, 1, 1)

    offsets = small_row(3 * SMALL_ROWS, 2 * BUCKET_SLOTS // LANES).astype(jnp.int32)
    table = small[TABLE_ROW : TABLE_ROW + 32, :]
    long_row = 2 * BUCKET_SLOTS
    sub8 = iota((8, long_row), 0)
    for h in range(heads):
        flat = offsets * H + (T * heads + h)
        at_row = lax.div(flat, LANES)
        at_lane = lax.rem(flat, LANES)
        hot_row = jnp.where(iota((32, long_row), 0) == at_row, 1.0, 0.0)
        spread = exact_tn(table, hot_row)
        values = jnp.sum(
            jnp.where(iota((LANES, long_row), 0) == at_lane, spread, 0.0), axis=0, keepdims=True
        )
        stack = jnp.broadcast_to(pltpu.roll(jnp.broadcast_to(values, (8, long_row)), 1, 1), (8, long_row))
        for bit in (1, 2, 4):
            stack = jnp.where(lax.rem(lax.div(sub8, bit), 2) == 1, pltpu.roll(stack, bit, 1), stack)
        size = 8
        m.band[h, 0:8, :] = stack
        while size < LANES:
            m.band[h, size : 2 * size, :] = pltpu.roll(m.band[h, 0:size, :], size, 1)
            size *= 2
    m.dband[...] = jnp.zeros(m.dband.shape, F32)

    line_step(0, 2, 1)

    for b in range(2):
        end = 0
        ends = []
        for i in range(CLIPS):
            end = end + lens[b, i]
            ends.append(end)
        key_at = iota((1, BUCKET_SLOTS), 1)
        key_segment = jnp.zeros((1, BUCKET_SLOTS), jnp.int32)
        for end in ends:
            key_segment = key_segment + jnp.where(key_at >= end, 1, 0)
        kept = jnp.concatenate([keep[4 * b + i : 4 * b + i + 1, :] for i in range(4)], axis=1)
        live = jnp.where((kept == 1) & (key_segment < CLIPS), key_segment, -1)

        def mask_chunk(i, b=b, ends=ends, live=live):
            query_at = iota((CHUNK, BUCKET_SLOTS), 0) + i * CHUNK
            segment = jnp.zeros((CHUNK, BUCKET_SLOTS), jnp.int32)
            for end in ends:
                segment = segment + jnp.where(query_at >= end, 1, 0)
            allowed = (segment == live) | (query_at == iota((CHUNK, BUCKET_SLOTS), 1))
            m.mbias[b, pl.ds(pl.multiple_of(i * CHUNK, CHUNK), CHUNK), :] = jnp.where(
                allowed, 0.0, MASK_VALUE
            ).astype(BF16)

        loop(BUCKET_SLOTS // CHUNK, mask_chunk)

    for step in range(3, nz):
        line_step(0, step, 1)
    line_start(1, 2)

    tok_copy.wait()
    gmat = m.gmat[...]
    part_hi = gmat.astype(BF16)
    rest = gmat - part_hi.astype(F32)
    part_mid = rest.astype(BF16)
    part_lo = (rest - part_mid.astype(F32)).astype(BF16)
    gate_parts = (part_hi, part_hi, part_hi, part_mid, part_mid, part_lo)
    stacked = jnp.zeros((W, LANES), F32)
    for i, part in enumerate(gate_parts):
        moved = part.astype(F32)
        stacked = stacked + (pltpu.roll(moved, 16 * i, 1) if i else moved)
    m.wqkvt[qkv_pad : qkv_pad + LANES, :] = stacked.astype(BF16).T

    def gate_chunk(i):
        rows = pl.ds(pl.multiple_of(i * HALF, HALF), HALF)
        tokens = m.tok[rows, :]
        linear = mm(tokens, part_hi) + mm(tokens, part_mid) + mm(tokens, part_lo)
        both = jax.nn.sigmoid(linear + jnp.where(lane < 8, offset_u, offset_w))
        m.gu[rows, :] = both
        m.gate[rows, :] = both * (pltpu.roll(both, LANES - 8, 1) * scale - 1.0) + 2.0

    loop(4, gate_chunk)

    line_start(2, 2)
    line_end(0)
    gather_x(1)
    gather_x(2)

    def project(i):
        rows = pl.ds(pl.multiple_of(i * HALF, HALF), HALF)
        both = mm(m.tok[rows, :], m.wqkv[...]) + vecs[7:8, 0:qkv_pad]
        query = (both[:, 0:head_cols].astype(BF16).astype(F32) * 0.125).astype(BF16)
        m.q[rows, :] = query
        m.qt[:, rows] = query.T
        key = both[:, head_cols : 2 * head_cols].astype(BF16)
        value = both[:, 2 * head_cols : 3 * head_cols].astype(BF16)
        m.k[rows, :] = key
        m.v[rows, :] = value
        m.kt[:, rows] = key.T
        m.vt[:, rows] = value.T

    loop(4, project)

    head_of = lax.div(iota((1, head_cols), 1), HD)
    head_masks = [jnp.where(head_of == h, 1.0, 0.0) for h in range(heads)]
    low_masks = [m.astype(BF16) for m in head_masks]

    def hooked(first, count, chunk, hooks):
        def step_of(i):
            step = i + first
            chunk(step)
            for at, action in hooks.items():
                if first <= at < first + count:
                    when(step == at, action)

        loop(count, step_of)

    def by_head(stacked):
        total = stacked[0:CHUNK, :] * head_masks[0]
        for h in range(1, heads):
            total = total + stacked[h * CHUNK : (h + 1) * CHUNK, :] * head_masks[h]
        return total

    def attend(b, hooks):
        keys = m.kt[:, b * BUCKET_SLOTS : (b + 1) * BUCKET_SLOTS]
        values = m.v[b * BUCKET_SLOTS : (b + 1) * BUCKET_SLOTS, :]

        def chunk(i):
            local = pl.ds(pl.multiple_of(i * CHUNK, CHUNK), CHUNK)
            rows = pl.ds(pl.multiple_of(b * BUCKET_SLOTS + i * CHUNK, CHUNK), CHUNK)
            window = pl.ds(pl.multiple_of(BUCKET_SLOTS - i * CHUNK, CHUNK), BUCKET_SLOTS)
            query = m.q[rows, :]
            gates = m.gate[rows, :]
            all_scores = mm(jnp.concatenate([query * mask for mask in low_masks], axis=0), keys)
            all_probs = []
            for h in range(heads):
                scores = all_scores[h * CHUNK : (h + 1) * CHUNK, :]
                scores = scores + gates[:, h : h + 1] * m.band[h, :, window]
                scores = scores + m.mbias[b, local, :].astype(F32)
                top = jnp.max(scores, axis=1, keepdims=True)
                weight = jnp.exp(scores - top)
                total = jnp.sum(weight, axis=1, keepdims=True)
                probability = weight * (1.0 / total)
                m.prob[b * heads + h, local, :] = probability
                all_probs.append(probability.astype(BF16))
            m.ctx[rows, :] = by_head(mm(jnp.concatenate(all_probs, axis=0), values)).astype(BF16)

        hooked(0, BUCKET_SLOTS // CHUNK, chunk, hooks)

    core_sent = {}
    y_sent = {}

    def exchange(phase, b, product):
        other = b * BUCKET_SLOTS + (1 - c) * HALF
        own = b * BUCKET_SLOTS + c * HALF
        for cp in core_sent.get((phase - 1, b), []) + y_sent.get((phase - 1, b), []):
            cp.wait_send()
        for i in range(2):
            at = slice(i * CHUNK, (i + 1) * CHUNK)
            rows = pl.ds(pl.multiple_of(other + i * CHUNK, CHUNK), CHUNK)
            m.cs[b, at, :] = product(rows).astype(BF16)
            cp = remote(
                m.cs.at[b, at], m.cr.at[b, at], m.s_cs.at[phase, b, i], m.s_cr.at[phase, b, i], core_dev
            )
            cp.start()
            core_sent.setdefault((phase, b), []).append(cp)
        for i in range(2):
            at = slice(i * CHUNK, (i + 1) * CHUNK)
            rows = pl.ds(pl.multiple_of(own + i * CHUNK, CHUNK), CHUNK)
            m.ownf[at, :] = product(rows)
        for i in range(2):
            at = slice(i * CHUNK, (i + 1) * CHUNK)
            core_sent[(phase, b)][i].wait_recv()
            m.ys[b, at, :] = (m.ownf[at, :] + m.cr[b, at, :].astype(F32)).astype(BF16)
            cp = remote(
                m.ys.at[b, at],
                m.yr.at[phase % 2, b, at],
                m.s_ys.at[phase, b, i],
                m.s_yr.at[phase, b, i],
                y_dev,
            )
            cp.start()
            y_sent.setdefault((phase, b), []).append(cp)

    def arrived(phase, b, at):
        return m.ys[b, at, :].astype(F32) + m.yr[phase % 2, b, at, :].astype(F32)

    def own_rows(b, i):
        return pl.ds(pl.multiple_of(b * BUCKET_SLOTS + c * HALF + i * CHUNK, CHUNK), CHUNK)

    core_spread = {}

    def spread(which, buf, b, i):
        part = buf.at[own_rows(b, i)]
        cp = remote(part, part, m.s_as.at[which, b, i], m.s_ar.at[which, b, i], core_dev)
        cp.start()
        core_spread.setdefault((which, b), []).append(cp)

    spread_done = set()

    def spread_end(which, b, i):
        if (which, b, i) not in spread_done:
            core_spread[(which, b)][i].wait_recv()
            spread_done.add((which, b, i))

    def as_it_lands(phase, b, chunk):
        for i in range(2):
            y_sent[(phase, b)][i].wait_recv()
            chunk(i)

    def row_mean(values):
        return jnp.mean(values, axis=1, keepdims=True)

    def add_row(at, values):
        m.acc[at : at + 1, 0 : values.shape[1]] += jnp.sum(values, axis=0, keepdims=True)

    def norm_one(b):

        def chunk(i):
            at = pl.ds(pl.multiple_of(i * CHUNK, CHUNK), CHUNK)
            rows = own_rows(b, i)
            residual = DEEP_ALPHA * m.tok[rows, :].astype(F32) + (arrived(0, b, at) + vecs[4:5, :])
            centred = residual - row_mean(residual)
            rstd = lax.rsqrt(row_mean(centred * centred) + NORM_EPSILON)
            hat = centred * rstd
            normed = hat * vecs[0:1, :] + vecs[1:2, :]
            m.xh1[b, at, :] = hat
            m.rstd1[b, at, :] = jnp.broadcast_to(rstd, (CHUNK, LANES))
            m.held[b, at, :] = normed
            m.nb[rows, :] = normed.astype(BF16)
            spread(0, m.nb, b, i)

        as_it_lands(0, b, chunk)

    def own_first(which, b, chunk):
        def rows_at(step):
            i = lax.rem(step + 2 * c, 4)
            return pl.ds(pl.multiple_of(b * BUCKET_SLOTS + i * CHUNK, CHUNK), CHUNK)

        loop(2, lambda step: chunk(rows_at(step)))
        for i in range(2):
            spread_end(which, b, i)
            chunk(rows_at(2 + i))

    def feed(b):
        def chunk(rows):
            up = mm(m.nb[rows, :], m.wup[...]) + vecs[6:7, :]
            half_phi = 0.5 * (1.0 + lax.erf(up * INV_SQRT2))
            m.act[rows, :] = (up * half_phi).astype(BF16)
            m.gelup[rows, :] = half_phi + up * (jnp.exp(up * up * -0.5) * INV_SQRT_2PI)

        own_first(0, b, chunk)

    out_copies = []

    def result_rows(which, b, stage, out):
        rows = pl.ds(pl.multiple_of(b * BUCKET_SLOTS + c * HALF, HALF), HALF)
        part = stage.at[b]
        here = pltpu.make_async_copy(part, out.at[rows], m.s_ol.at[which, b])
        there = remote(part, out.at[rows], m.s_os.at[which, b], m.s_or.at[which, b], core_dev)
        here.start()
        there.start()
        out_copies.append((here, there))

    def norm_two(b):
        cot_copies[b].wait()

        def chunk(i):
            at = pl.ds(pl.multiple_of(i * CHUNK, CHUNK), CHUNK)
            rows = own_rows(b, i)
            residual = DEEP_ALPHA * m.held[b, at, :] + (arrived(1, b, at) + vecs[5:6, :])
            centred = residual - row_mean(residual)
            rstd = lax.rsqrt(row_mean(centred * centred) + NORM_EPSILON)
            hat = centred * rstd
            m.stage[b, at, :] = (hat * vecs[2:3, :] + vecs[3:4, :]).astype(BF16)
            upstream = m.cot[b, at, :].astype(F32)
            add_row(2, upstream * hat)
            add_row(3, upstream)
            scaled = upstream * vecs[2:3, :]
            grad = rstd * (scaled - row_mean(scaled) - hat * row_mean(scaled * hat))
            m.held[b, at, :] = grad
            low = grad.astype(BF16)
            m.gffn[rows, :] = low
            spread(1, m.gffn, b, i)
            add_row(5, low.astype(F32))

        as_it_lands(1, b, chunk)
        result_rows(0, b, m.stage, bo_out)

    def feed_back(b):
        def chunk(rows):
            grad = mm(m.gffn[rows, :], m.wdown[...]) * m.gelup[rows, :]
            low = grad.astype(BF16)
            m.gub[rows, :] = low
            add_row(6, low.astype(F32))

        own_first(1, b, chunk)

    def norm_one_back(b):

        def chunk(i):
            at = pl.ds(pl.multiple_of(i * CHUNK, CHUNK), CHUNK)
            rows = own_rows(b, i)
            upstream = arrived(2, b, at) + DEEP_ALPHA * m.held[b, at, :]
            hat = m.xh1[b, at, :]
            add_row(0, upstream * hat)
            add_row(1, upstream)
            scaled = upstream * vecs[0:1, :]
            rstd = m.rstd1[b, at, 0:1]
            grad = rstd * (scaled - row_mean(scaled) - hat * row_mean(scaled * hat))
            m.held[b, at, :] = grad
            low = grad.astype(BF16)
            m.gattn[rows, :] = low
            spread(2, m.gattn, b, i)
            add_row(4, low.astype(F32))

        as_it_lands(2, b, chunk)

    def gate_back(rows, grad):
        u = m.gu[rows, :]
        w = pltpu.roll(u, LANES - 8, 1)
        grad_u = jnp.where(head_lane, grad * (w * scale - 1.0) * u * (1.0 - u), 0.0)
        grad_w = jnp.where(head_lane, grad * u * scale * w * (1.0 - w), 0.0)
        add_row(8, jnp.where(head_lane, grad * u * w, 0.0))
        linear = grad_u + pltpu.roll(grad_w, 8, 1)
        add_row(9, linear)
        hi = linear.astype(BF16).astype(F32)
        mid = (linear - hi).astype(BF16).astype(F32)
        lo = (linear - hi - mid).astype(BF16).astype(F32)
        stacked = hi
        for at, part in enumerate((mid, lo, hi, mid, hi)):
            stacked = stacked + pltpu.roll(part, 16 * (at + 1), 1)
        m.dqkv[rows, qkv_pad : qkv_pad + LANES] = stacked.astype(BF16)

    def attend_back(b, hooks):
        keys = m.k[b * BUCKET_SLOTS : (b + 1) * BUCKET_SLOTS, :]
        values = m.vt[:, b * BUCKET_SLOTS : (b + 1) * BUCKET_SLOTS]

        def chunk(step):
            i = lax.rem(step + 2 * c, 4)
            local = pl.ds(pl.multiple_of(i * CHUNK, CHUNK), CHUNK)
            rows = pl.ds(pl.multiple_of(b * BUCKET_SLOTS + i * CHUNK, CHUNK), CHUNK)
            window = pl.ds(pl.multiple_of(BUCKET_SLOTS - i * CHUNK, CHUNK), BUCKET_SLOTS)
            place = pl.ds(pl.multiple_of(3 * CHUNK - i * CHUNK, CHUNK), BUCKET_SLOTS)
            grad_context = mm(m.gattn[rows, :], m.wo[...]).astype(BF16)
            m.dctxt[:, local] = grad_context.T
            gates = m.gate[rows, :]
            all_grads = mm(jnp.concatenate([grad_context * mask for mask in low_masks], axis=0), values)
            all_low = []
            grad_gates = jnp.zeros((CHUNK, LANES), F32)
            for h in range(heads):
                grad_probs = all_grads[h * CHUNK : (h + 1) * CHUNK, :]
                probability = m.prob[b * heads + h, local, :]
                inner = jnp.sum(grad_probs * probability, axis=1, keepdims=True)
                low = (probability * (grad_probs - inner)).astype(BF16)
                m.gsb[pl.ds(pl.multiple_of(h * BUCKET_SLOTS + i * CHUNK, CHUNK), CHUNK), :] = low
                all_low.append(low)
                rounded = low.astype(F32)
                one = jnp.sum(rounded * m.band[h, :, window], axis=1, keepdims=True)
                grad_gates = grad_gates + jnp.where(lane == h, one, 0.0)
                m.dband[h, :, place] += rounded * gates[:, h : h + 1]
            m.dqf[local, :] = by_head(mm(jnp.concatenate(all_low, axis=0), keys)) * 0.125
            gate_back(rows, grad_gates)

        hooked(0, 2, chunk, hooks)
        spread_end(2, b, 0)
        spread_end(2, b, 1)
        hooked(2, 2, chunk, hooks)
        all_rows = slice(b * BUCKET_SLOTS, (b + 1) * BUCKET_SLOTS)
        own_rows_of = lax.div(iota((head_cols, 1), 0), HD)
        row_masks = [jnp.where(own_rows_of == h, 1.0, 0.0).astype(BF16) for h in range(heads)]
        spread_out = lambda turned: jnp.concatenate([turned * mask for mask in row_masks], axis=1)
        grad_key = mm(spread_out(m.qt[:, all_rows]), m.gsb[...]).T
        probs = m.prob[b * heads : (b + 1) * heads].reshape(heads * BUCKET_SLOTS, BUCKET_SLOTS)
        grad_value = mm(spread_out(m.dctxt[...]), probs.astype(BF16)).T
        pad = jnp.zeros((BUCKET_SLOTS, qkv_pad - 3 * head_cols), F32)
        low = jnp.concatenate([m.dqf[...], grad_key, grad_value, pad], axis=1).astype(BF16)
        m.dqkv[all_rows, 0:qkv_pad] = low
        add_row(7, low.astype(F32))

    def input_part(rows):
        return mm(m.dqkv[rows, :], m.wqkvt[...])

    def token_rows(b):
        for cp in out_copies[b]:
            cp.wait()

        def chunk(i):
            at = pl.ds(pl.multiple_of(i * CHUNK, CHUNK), CHUNK)
            total = arrived(3, b, at) + DEEP_ALPHA * m.held[b, at, :]
            m.stage[b, at, :] = total.astype(BF16)

        as_it_lands(3, b, chunk)
        result_rows(1, b, m.stage, tg_out)

    def weight_grad(sent, left, right, put_part, rows=slice(None)):
        for which in sent:
            sent_all(which)

        def chunk(i):
            cols = pl.ds(pl.multiple_of(i * HALF, HALF), HALF)
            put_part(cols, mm_tn(left[rows, cols], right[rows, :]))

        loop(W // HALF, chunk)

    def add_whole(buf):
        def put_part(cols, part):
            buf[cols, :] = (buf[cols, :].astype(F32) + part).astype(BF16)

        return put_part

    def put_whole(buf):
        def put_part(cols, part):
            buf[cols, :] = part.astype(BF16)

        return put_part

    def put_qkv(cols, part):
        m.wqkv[cols, 0 : 3 * head_cols] = part[:, 0 : 3 * head_cols].astype(BF16)
        m.glin[cols, :] = part[:, qkv_pad : qkv_pad + LANES]

    def put_o(cols, part):
        m.wqkv[cols, 3 * head_cols : qkv_pad] = part[:, 0:first_o].astype(BF16)
        m.go[cols, :] = part[:, first_o:head_cols].astype(BF16)

    reduces = []

    def low_bit(k):
        return k & -k if k else nz

    bits = [1 << i for i in range(nz.bit_length() - 1)]
    slots = {}
    for k in range(nz):
        for bit in bits:
            if bit < low_bit(k):
                slots[(k, bit)] = len(slots)
    pass_order = sorted(range(nz), key=lambda k: (low_bit(k), -k))

    def add_landed(total, k, which, arrive):
        for bit in bits:
            if bit < low_bit(k):
                slot = slots[(k, bit)]
                here = arrive.at[slot]
                sems = m.s_zs.at[which, slot], m.s_zr.at[which, slot]
                remote(here, here, *sems, z_dev(bit)).wait_recv()
                total = total + arrive[slot].astype(F32)
        return total

    def reduce_start(which, buf, land, ks=None):
        for k in ks or pass_order:

            def where(k=k):
                rows = block(2 * z_at(k) + 1 - x)
                return buf.at[rows], land.at[k], m.s_xs.at[which, k], m.s_xr.at[which, k], x_dev

            launch(reduces, where)

    def reduce_block(k, which, buf, land, out, arrive, share):
        here = land.at[k]
        remote(here, here, m.s_xs.at[which, k], m.s_xr.at[which, k], x_dev).wait_recv()
        total = buf[block(2 * z_at(k) + x), :].astype(F32) + land[k].astype(F32)
        if k == 0:
            share[...] = total
        else:
            out[k - 1] = add_landed(total, k, which, arrive).astype(BF16)

            def where():
                bit = low_bit(k)
                slot = slots[(k - bit, bit)]
                sems = m.s_zs.at[which, slot], m.s_zr.at[which, slot]
                return out.at[k - 1], arrive.at[slot], *sems, z_dev(bit)

            launch(reduces, where)

    def reduce_pass(*matrix):
        for k in pass_order:
            reduce_block(k, *matrix)

    def reduce_end(which, arrive, share):
        total = add_landed(share[...], 0, which, arrive)
        share[...] = total
        squares = total * total
        folded = jnp.zeros((owned, LANES), F32)
        for i in range(total.shape[1] // LANES):
            folded = folded + squares[:, i * LANES : (i + 1) * LANES]
        tile = jnp.zeros((8, LANES), F32)
        for i in range(owned // 8):
            tile = tile + folded[8 * i : 8 * i + 8, :]
        return tile

    def pass_on(which):
        line_step(which, 1, 2)
        line_step(which, 2, 2)

    def pass_last(which):
        for step in range(3, nz):
            line_step(which, step, 2)

    line_start(3, 2)
    gather_x(3)

    def first_pass():
        pass_on(1)
        line_start(4, 2)
        gather_x(4)

    def second_pass():
        pass_last(1)
        pass_on(2)
        partner_landed(5)
        line_start(5, 2)
        line_start(6, 2)

    attend(0, {0: first_pass, 2: second_pass})
    line_end(1)
    m.wo[...] = jnp.concatenate([m.wqkv[:, 3 * head_cols : qkv_pad], m.wo1[...]], axis=1)
    turn(m.wo, m.wot)
    out_product = lambda rows: mm(m.ctx[rows, :], m.wot[...])
    exchange(0, 0, out_product)
    pass_last(2)
    attend(1, {1: lambda: pass_on(3), 3: lambda: pass_last(3)})
    exchange(0, 1, out_product)
    pass_on(4)
    pass_on(5)
    norm_one(0)
    pass_last(4)
    pass_on(6)
    line_end(2)
    line_end(3)
    feed(0)
    pass_last(5)
    pass_last(6)
    line_end(4)
    turn(m.wdown, m.wdownt)
    down_product = lambda rows: mm(m.act[rows, :], m.wdownt[...])
    exchange(1, 0, down_product)
    norm_one(1)
    feed(1)
    exchange(1, 1, down_product)
    turn(m.wup, m.wupt)
    turn(m.wqkv, m.wqkvt)
    up_product = lambda rows: mm(m.gub[rows, :], m.wupt[...])
    norm_two(0)
    feed_back(0)
    exchange(2, 0, up_product)
    first_rows, last_rows = slice(0, BUCKET_SLOTS), slice(BUCKET_SLOTS, 2 * BUCKET_SLOTS)
    weight_grad((), m.gffn, m.act, put_whole(m.wdownt), first_rows)
    weight_grad((2, 3), m.nb, m.gub, put_whole(m.wup), first_rows)
    norm_two(1)
    spread_end(1, 1, 0)
    spread_end(1, 1, 1)
    weight_grad((), m.gffn, m.act, add_whole(m.wdownt), last_rows)
    reduce_start(0, m.wdownt, m.xrdown)
    feed_back(1)
    exchange(2, 1, up_product)
    weight_grad((), m.nb, m.gub, add_whole(m.wup), last_rows)
    reduce_start(1, m.wup, m.xrup)
    down = (0, m.wdownt, m.xrdown, m.zsdown, m.zrdown, sh_down)
    up = (1, m.wup, m.xrup, m.zsup, m.zrup, sh_up)
    out = (2, m.go, m.xro, m.zso, m.zro, sh_o)
    qkv = (3, m.wqkv, m.xrqkv, m.zsqkv, m.zrqkv, sh_qkv)
    norm_one_back(0)
    blocks = lambda ks, matrix: lambda: [reduce_block(k, *matrix) for k in ks] and None
    early = [pass_order[0:1], pass_order[1:2], pass_order[2:-1]]
    attend_back(0, {2 + i: blocks(ks, down) for i, ks in enumerate(early[:2])})
    exchange(3, 0, input_part)
    blocks(early[2], down)()
    norm_one_back(1)
    spread_end(2, 1, 0)
    spread_end(2, 1, 1)
    weight_grad((0, 1), m.gattn, m.ctx, put_o)
    reduce_block(0, *down)
    downward = list(range(nz - 1, -1, -1))
    reduce_start(2, m.go, m.xro, downward)
    attend_back(1, {i: blocks(ks, up) for i, ks in enumerate(early[:2])})
    weight_grad((), m.tok, m.dqkv, put_qkv)
    first_part, last_part = downward[: nz // 2], downward[nz // 2 :]
    reduce_start(3, m.wqkv, m.xrqkv, first_part)
    blocks(early[2] + [0], up)()
    reduce_block(downward[0], *out)

    sm = m.sm
    sm[...] = jnp.zeros((SUM_ROWS, LANES), F32)
    acc = m.acc
    lead = jnp.where(yy == 0, 1.0, 0.0)

    def put(first, values):
        for i in range(values.shape[1] // LANES):
            sm[first + i : first + i + 1, :] = values[:, i * LANES : (i + 1) * LANES]

    def spot(values):
        return jnp.concatenate([jnp.where(T == t, values, 0.0) for t in range(4)], axis=1)

    for at, first in ((0, 0), (1, 6), (2, 12), (3, 18), (4, 36), (5, 42)):
        put(first, acc[at : at + 1, :] * lead)
    put(24, spot(acc[7:8, 0:head_cols]))
    put(30, spot(acc[7:8, 2 * head_cols : 3 * head_cols]))
    put(48, spot(acc[6:7, 0:hidden]))
    parts = []
    for h in range(heads):
        size = LANES // 2
        left = m.dband[h]
        while size >= 8:
            left = left[0:size, :] + pltpu.roll(left[size : 2 * size, :], long_row - size, 1)
            size //= 2
        for bit in (1, 2, 4):
            left = jnp.where(lax.rem(lax.div(sub8, bit), 2) == 1, pltpu.roll(left, long_row - bit, 1), left)
        left = pltpu.roll(left, LANES - 1, 1)
        diagonal = jnp.sum(left, axis=0, keepdims=True)
        hi = diagonal.astype(BF16).astype(F32)
        mid = (diagonal - hi).astype(BF16).astype(F32)
        parts += [hi, mid, diagonal - hi - mid]
    parts = jnp.concatenate(parts + [jnp.zeros((16 - len(parts), long_row), F32)], axis=0).astype(BF16)
    bucket_rows = -(-NB // LANES) * LANES
    valid = iota((1, long_row), 1) < long_row - 1
    hot_bucket = jnp.where((iota((bucket_rows, long_row), 0) == offsets) & valid, 1.0, 0.0).astype(BF16)
    by_bucket = mm_nt(parts, hot_bucket)
    bucket = iota((1, bucket_rows), 1)
    table_grad = jnp.zeros((32, LANES), F32)
    for h in range(heads):
        sums = by_bucket[3 * h : 3 * h + 1] + by_bucket[3 * h + 1 : 3 * h + 2] + by_bucket[3 * h + 2 : 3 * h + 3]
        flat = bucket * H + (T * heads + h)
        hot_row = jnp.where((iota((32, bucket_rows), 0) == lax.div(flat, LANES)) & (bucket < NB), 1.0, 0.0)
        hot_lane = jnp.where(iota((LANES, bucket_rows), 0) == lax.rem(flat, LANES), sums, 0.0)
        table_grad = table_grad + exact_nt(hot_row, hot_lane)
    sm[TABLE_ROW : TABLE_ROW + 30, :] = table_grad[0:30, :]

    lin_grad = m.glin[...]
    lin_grad = lin_grad + pltpu.roll(lin_grad, LANES - 16, 1) + pltpu.roll(lin_grad, LANES - 32, 1)
    lin_grad = jnp.where(own_head, lin_grad, 0.0)
    grad_u = jnp.sum(jnp.where(col_lane < 8, lin_grad, 0.0), axis=1, keepdims=True)
    grad_w = jnp.sum(jnp.where(col_lane >= 8, lin_grad, 0.0), axis=1, keepdims=True)
    by_lane = jnp.where(col_lane == 2 * col_in_head, grad_u, 0.0)
    by_lane = by_lane + jnp.where(col_lane == 2 * col_in_head + 1, grad_w, 0.0)
    sm[GATE_ROW : GATE_ROW + 1, :] = jnp.sum(by_lane, axis=0, keepdims=True)
    lin_total = acc[9:10, 0:LANES]
    total_u = jnp.sum(jnp.where(lane < 8, lin_total, 0.0), axis=1, keepdims=True)
    total_w = jnp.sum(jnp.where((lane >= 8) & (lane < 16), lin_total, 0.0), axis=1, keepdims=True)
    last = jnp.where(lane == 0, total_u, 0.0) + jnp.where(lane == 1, total_w, 0.0)
    scale_grad = acc[8:9, 0:LANES]
    for h in range(heads):
        one = jnp.sum(jnp.where(lane == h, scale_grad, 0.0), axis=1, keepdims=True)
        last = last + jnp.where(lane == 2 + T * heads + h, one, 0.0)
    sm[OFFSET_ROW : OFFSET_ROW + 1, :] = last

    small_sent = []

    def small_send(at, source, target, dev):
        cp = remote(source, target, m.s_ms.at[at], m.s_mr.at[at], dev)
        cp.start()
        small_sent.append(cp)
        return cp

    def quarter(index):
        return pl.ds(pl.multiple_of(index * QUARTER, QUARTER), QUARTER)

    to_core = [small_send(i, sm.at[quarter(2 * i + 1 - c)], m.smc.at[i], core_dev) for i in range(2)]
    for i in range(2):
        to_core[i].wait_recv()
        m.smh[i] = sm[quarter(2 * i + c), :] + m.smc[i]
    to_y = small_send(2, m.smh.at[1 - yy], m.smy, y_dev)
    for k in downward[1:]:
        reduce_block(k, *out)
    reduce_block(first_part[0], *qkv)
    to_y.wait_recv()
    m.smv[...] = m.smh[yy] + m.smy[...]
    to_x = small_send(3, m.smv, m.smx, x_dev)
    reduce_start(3, m.wqkv, m.xrqkv, last_part)
    exchange(3, 1, input_part)
    to_x.wait_recv()
    m.smz[z] = m.smv[...] + m.smx[...]
    for k in range(1, nz):
        small_send(3 + k, m.smz.at[z], m.smz.at[z], z_dev(k))
    for k in first_part[1:]:
        reduce_block(k, *qkv)
    for k in last_part[:-1]:
        reduce_block(k, *qkv)
    token_rows(0)
    reduce_block(0, *qkv)
    squares = reduce_end(0, m.zrdown, sh_down)
    squares = squares + reduce_end(1, m.zrup, sh_up)
    squares = squares + reduce_end(2, m.zro, sh_o)
    for k in range(1, nz):
        here = m.smz.at[z_at(k)]
        remote(here, here, m.s_ms.at[3 + k], m.s_mr.at[3 + k], z_dev(k)).wait_recv()
    own_quarter = m.smz[0]
    for i in range(1, nz):
        own_quarter = own_quarter + m.smz[i]
    m.sma[quarter(T), :] = own_quarter
    for k in range(1, 4):
        mine_small = m.sma.at[quarter(T)]
        small_send(2 + nz + k, mine_small, mine_small, (D, lax.rem(T + k, 4)))
    squares = squares + reduce_end(3, m.zrqkv, sh_qkv)
    last_copies = []
    for i, (source, target) in enumerate(
        ((sh_down, out_down), (sh_up, out_up), (sh_o, out_o), (sh_qkv, out_qkv))
    ):
        cp = pltpu.make_async_copy(source, target, m.s_out.at[i])
        cp.start()
        last_copies.append(cp)
    sqt = m.sqt
    sqt[T] = squares
    tail_sent = []
    for k in range(1, 4):
        cp = remote(
            sqt.at[T], sqt.at[T], m.s_ts.at[k], m.s_tr.at[k], (D, lax.rem(T + k, 4))
        )
        cp.start()
        tail_sent.append(cp)
    token_rows(1)
    for k in range(1, 4):
        here = m.sma.at[quarter(lax.rem(T + 4 - k, 4))]
        remote(here, here, m.s_ms.at[2 + nz + k], m.s_mr.at[2 + nz + k], core_dev).wait_recv()
    small_total = m.sma[0:SMALL_ROWS, :]
    for i in range(3):
        small_out[i] = small[i * SMALL_ROWS : (i + 1) * SMALL_ROWS, :]
    small_out[3] = small_total
    cp = pltpu.make_async_copy(small_out, out_small, m.s_out.at[4])
    cp.start()
    last_copies.append(cp)
    small_square = small_total * small_total
    small_tile = jnp.zeros((8, LANES), F32)
    for i in range(SMALL_ROWS // 8):
        small_tile = small_tile + small_square[8 * i : 8 * i + 8, :]
    for k in range(1, 4):
        here = sqt.at[lax.rem(T + 4 - k, 4)]
        remote(here, here, m.s_ts.at[k], m.s_tr.at[k], core_dev).wait_recv()
    sqd = m.sqd
    sqd[D] = sqt[0] + sqt[1] + sqt[2] + sqt[3]
    for k in range(1, n_dp):
        cp = remote(
            sqd.at[D], sqd.at[D], m.s_ds.at[k], m.s_dr.at[k], (lax.rem(D + k, n_dp), T)
        )
        cp.start()
        tail_sent.append(cp)
    for k in range(1, n_dp):
        here = sqd.at[lax.rem(D + n_dp - k, n_dp)]
        remote(here, here, m.s_ds.at[k], m.s_dr.at[k], core_dev).wait_recv()
    everything = small_tile
    for i in range(n_dp):
        everything = everything + sqd[i]
    sum_all = jnp.sum(jnp.sum(everything, axis=0, keepdims=True), axis=1, keepdims=True)
    norm_out[...] = jnp.broadcast_to(jnp.sqrt(sum_all), (8, LANES))

    for which in list(gathers):
        sent_all(which)
    for where in reduces:
        remote(*where()).wait_send()
    for cp in small_sent + tail_sent:
        cp.wait_send()
    for sent in core_spread.values():
        for cp in sent:
            cp.wait_send()
    for b in range(2):
        for cp in core_sent[(3, b)] + y_sent[(3, b)]:
            cp.wait_send()
    for cp in last_copies:
        cp.wait()
    for here, there in out_copies[2:]:
        here.wait()
        there.wait()


def adam_kernel(head_cols, *refs):
    ins, rest = refs[:14], refs[14:]
    block_in, token_in = ins[12:14]
    outs, rest = rest[:14], rest[14:]
    norm_out, block_out, token_out = outs[0], outs[12], outs[13]
    held, made = rest[:12], rest[12:24]
    block_held, token_held, s_in, s_out = rest[24:]
    loads = [pltpu.make_async_copy(ins[i], held[i], s_in.at[i]) for i in range(12)]
    for cp in loads:
        cp.start()
    passing = [
        pltpu.make_async_copy(block_in, block_held, s_in.at[12]),
        pltpu.make_async_copy(token_in, token_held, s_in.at[13]),
    ]
    passed = [
        pltpu.make_async_copy(block_held, block_out, s_out.at[12]),
        pltpu.make_async_copy(token_held, token_out, s_out.at[13]),
    ]
    for cp in passing:
        cp.start()
    stores = []

    def store(i):
        cp = pltpu.make_async_copy(made[i], outs[i], s_out.at[i])
        cp.start()
        stores.append(cp)

    sh_qkv, sh_o, sh_up, sh_down, sh_small, norm, aw, am, av, fw, fm, fv = held
    (o_norm, o_am, o_av, o_aw, o_ac, o_fm, o_fv, o_fw, o_fc, o_sm, o_sv, o_sw) = made
    for i in (0, 1, 2, 3, 5):
        loads[i].wait()
    length = norm[0:1, 0:1]
    factor = CLIP_LIMIT / jnp.maximum(length, CLIP_LIMIT)
    o_norm[...] = length
    store(0)
    for i in (6, 7, 8):
        loads[i].wait()
    for i in range(4):
        if i < 3:
            grad = sh_qkv[:, i * head_cols : (i + 1) * head_cols]
        else:
            grad = jnp.concatenate([sh_qkv[:, 3 * head_cols :], sh_o[...]], axis=1)
        moment, square, master = adam_step(
            aw[i], am[i], av[i], factor * grad, RATE_MATRIX, WEIGHT_DECAY
        )
        o_am[i] = moment
        o_av[i] = square
        o_aw[i] = master
        o_ac[i] = master.astype(BF16)
    for i in (1, 2, 3, 4):
        store(i)
    for first, second in zip(passing, passed, strict=True):
        first.wait()
        second.start()
    for i in (9, 10, 11):
        loads[i].wait()
    for i, share in enumerate((sh_up, sh_down)):
        moment, square, master = adam_step(
            fw[i], fm[i], fv[i], factor * share[...], RATE_MATRIX, WEIGHT_DECAY
        )
        o_fm[i] = moment
        o_fv[i] = square
        o_fw[i] = master
        o_fc[i] = master.astype(BF16)
    for i in (5, 6, 7, 8):
        store(i)
    loads[4].wait()
    moment, square, master = adam_step(
        sh_small[0], sh_small[1], sh_small[2], factor * sh_small[3], RATE_SMALL, 0.0
    )
    o_sm[...] = moment
    o_sv[...] = square
    o_sw[...] = master
    for i in (9, 10, 11):
        store(i)
    for cp in stores + passed:
        cp.wait()


def tiles(vector):
    return jnp.pad(vector, (0, SMALL_ROWS * LANES - vector.shape[0]))


def fused_body(
    n_dp,
    tokens,
    cotangent,
    clip_lengths,
    key_mask,
    rel_buckets,
    attention_weights,
    attention_first,
    attention_second,
    feedforward_weights,
    feedforward_first,
    feedforward_second,
    small_params,
    small_first,
    small_second,
):
    rows = tokens.shape[0]
    owned, head_cols = attention_weights.shape[1:]
    hidden = feedforward_weights.shape[2]
    heads = head_cols // HD
    qkv_pad = -(-3 * head_cols // LANES) * LANES
    nz = n_dp // 2
    packed = jnp.concatenate(
        [
            tiles(small_params),
            tiles(small_first),
            tiles(small_second),
            jnp.pad(rel_buckets.astype(F32), (0, 1)),
        ]
    ).reshape(-1, LANES)
    keep = key_mask.reshape(rows // LANES, LANES)
    scratch = layer_scratch(owned, nz, qkv_pad, heads, head_cols, hidden)
    names = tuple(scratch)
    vmem = pl.BlockSpec(memory_space=pltpu.VMEM)
    smem = pl.BlockSpec(memory_space=pltpu.SMEM)
    anywhere = pl.BlockSpec(memory_space=pl.ANY)
    sds = jax.ShapeDtypeStruct
    block_rows, token_rows, sh_qkv, sh_o, sh_up, sh_down, sh_small, norm = pl.pallas_call(
        partial(layer_kernel, names, (n_dp, owned, qkv_pad, heads, head_cols, hidden)),
        out_shape=(
            sds((rows, W), BF16),
            sds((rows, W), BF16),
            sds((owned, qkv_pad), F32),
            sds((owned, LANES), F32),
            sds((owned, hidden), F32),
            sds((owned, hidden), F32),
            sds((4, SMALL_ROWS, LANES), F32),
            sds((8, LANES), F32),
        ),
        in_specs=[anywhere, anywhere, smem] + [anywhere] * 4,
        out_specs=(anywhere,) * 7 + (vmem,),
        scratch_shapes=list(scratch.values()),
        compiler_params=pltpu.CompilerParams(
            collective_id=1, has_side_effects=True, vmem_limit_bytes=62 * 1024 * 1024
        ),
        name="layer",
    )(tokens, cotangent, clip_lengths, keep, attention_weights, feedforward_weights, packed)
    like = lambda a, dtype=F32: sds(a.shape, dtype)
    small_like = sds((SMALL_ROWS, LANES), F32)
    made = (
        sds((1, 1), F32),
        like(attention_weights),
        like(attention_weights),
        like(attention_weights),
        like(attention_weights, BF16),
        like(feedforward_weights),
        like(feedforward_weights),
        like(feedforward_weights),
        like(feedforward_weights, BF16),
        small_like,
        small_like,
        small_like,
    )
    operands = (
        sh_qkv,
        sh_o,
        sh_up,
        sh_down,
        sh_small,
        norm,
        attention_weights,
        attention_first,
        attention_second,
        feedforward_weights,
        feedforward_first,
        feedforward_second,
        block_rows,
        token_rows,
    )
    in_vmem = lambda a: pltpu.VMEM(a.shape, a.dtype)
    results = pl.pallas_call(
        partial(adam_kernel, head_cols),
        out_shape=(*made, like(tokens, BF16), like(tokens, BF16)),
        in_specs=[anywhere] * len(operands),
        out_specs=(anywhere,) * (len(made) + 2),
        scratch_shapes=[in_vmem(a) for a in operands[:12]]
        + [in_vmem(a) for a in made]
        + [in_vmem(tokens), in_vmem(tokens)]
        + [pltpu.SemaphoreType.DMA((14,)), pltpu.SemaphoreType.DMA((14,))],
        compiler_params=pltpu.CompilerParams(vmem_limit_bytes=62 * 1024 * 1024),
        name="adam",
    )(*operands)
    length = small_params.shape[0]
    flat = lambda a: a.reshape(-1)[:length]
    return (
        results[0].reshape(()),
        *results[1:9],
        flat(results[9]),
        flat(results[10]),
        flat(results[11]),
        *results[12:],
    )


def fused_fits(mesh, owned):
    columns = mesh.shape["dp"] // 2
    whole = mesh.shape["dp"] % 2 == 0 and columns & (columns - 1) == 0
    return mesh.shape["tensor"] == 4 and whole and owned % 16 == 0

def solution(mesh):
    in_specs = (
        P("dp", None),
        P("dp", None),
        P("dp", None),
        P("dp"),
        P(),
        P(None, "dp", "tensor"),
        P(None, "dp", "tensor"),
        P(None, "dp", "tensor"),
        P(None, "dp", "tensor"),
        P(None, "dp", "tensor"),
        P(None, "dp", "tensor"),
        P(),
        P(),
        P(),
    )
    out_specs = (
        P(),
        P(None, "dp", "tensor"),
        P(None, "dp", "tensor"),
        P(None, "dp", "tensor"),
        P(None, "dp", "tensor"),
        P(None, "dp", "tensor"),
        P(None, "dp", "tensor"),
        P(None, "dp", "tensor"),
        P(None, "dp", "tensor"),
        P(),
        P(),
        P(),
        P("dp", None),
        P("dp", None),
    )
    n_dp = mesh.shape["dp"]
    body = general_body
    if fused_fits(mesh, MODEL_WIDTH // n_dp):
        body = partial(fused_body, n_dp)
    return jax.shard_map(body, mesh=mesh, in_specs=in_specs, out_specs=out_specs, check_vma=False)
```

```python
from functools import partial
from types import SimpleNamespace

import jax
import jax.numpy as jnp
from jax import lax
from jax.experimental import pallas as pl
from jax.experimental.pallas import tpu as pltpu
from jax.sharding import PartitionSpec as P

MODEL_WIDTH = 768
H = 12
HD = 64
FF = 3072
NB = 320
BUCKET_SLOTS = 512
CLIPS = 8
STEP = 5


FULL_PRECISION = lax.Precision.HIGHEST
DEEP_ALPHA = 24.0**0.25
NORM_EPSILON = 1e-05
MASK_VALUE = -1e30
BETA_FIRST = 0.9
BETA_SECOND = 0.98
RATE_MATRIX = 0.03
RATE_SMALL = 0.5
WEIGHT_DECAY = 0.01
ADAM_EPSILON = 1e-08
CLIP_LIMIT = 0.1


def layer_norm(values, norm_gain, norm_shift):
    row_mean = jnp.mean(values, axis=-1, keepdims=True)
    centred = values - row_mean
    variance = jnp.mean(centred * centred, axis=-1, keepdims=True)
    return centred * lax.rsqrt(variance + NORM_EPSILON) * norm_gain + norm_shift


def gelu_exact(values):
    return jax.nn.gelu(values, approximate=False)


def split_small(vector):
    widths = [MODEL_WIDTH] * 8 + [FF, NB * H, HD * 2, 2, H]
    pieces = []
    offset = 0
    for extent in widths:
        pieces.append(vector[offset : offset + extent])
        offset += extent
    return pieces


def allowed_mask(lengths_row, keep_row):
    positions = jnp.arange(BUCKET_SLOTS, dtype=jnp.int32)
    clip_ends = jnp.cumsum(lengths_row)
    segment = jnp.sum((positions[:, None] >= clip_ends[None, :]).astype(jnp.int32), axis=1)
    live_keys = (keep_row == 1) & (segment < CLIPS)
    same_clip = segment[:, None] == segment[None, :]
    return same_clip & (live_keys[None, :] | (positions[:, None] == positions[None, :]))


def band_matrix(diagonals):
    head_count = diagonals.shape[0]
    length = (diagonals.shape[1] + 1) // 2
    padded = jnp.concatenate([diagonals, jnp.zeros((head_count, 1), diagonals.dtype)], axis=1)
    repeated = jnp.tile(padded, (1, length))
    folded = repeated[:, : length * (2 * length - 1)].reshape(head_count, length, 2 * length - 1)
    return folded[:, :, length - 1 :]


def position_terms(head_inputs, gate_matrix, gate_offset, scale_local, table_local, rel_buckets):
    linear = (
        jnp.einsum(
            "blhd,dk->bhlk", head_inputs, gate_matrix.reshape(HD, 2), precision=FULL_PRECISION
        )
        + gate_offset
    )
    sigmoid = jax.nn.sigmoid(linear)
    gate = sigmoid[..., 0] * (sigmoid[..., 1] * scale_local[None, :, None] - 1.0) + 2.0
    onehot = (rel_buckets[:, None] == jnp.arange(NB, dtype=jnp.int32)[None, :]).astype(jnp.float32)
    per_offset = jnp.dot(
        onehot, table_local, precision=FULL_PRECISION, preferred_element_type=jnp.float32
    )
    toeplitz = band_matrix(per_offset.T)
    return gate[..., None] * toeplitz[None]


def adam_step(weights, moment, second, gradient, step_rate, decay_rate):
    moment_new = BETA_FIRST * moment + (1.0 - BETA_FIRST) * gradient
    second_new = BETA_SECOND * second + (1.0 - BETA_SECOND) * gradient * gradient
    moment_hat = moment_new / (1.0 - BETA_FIRST**STEP)
    second_hat = second_new / (1.0 - BETA_SECOND**STEP)
    master = weights - step_rate * (
        moment_hat / (jnp.sqrt(second_hat) + ADAM_EPSILON) + decay_rate * weights
    )
    return (moment_new, second_new, master)


def placed(total_length, piece, start):
    return lax.dynamic_update_slice_in_dim(jnp.zeros((total_length,), jnp.float32), piece, start, 0)


def column_sum(values):
    return jnp.sum(values.astype(jnp.float32), axis=0)


def general_body(
    tokens,
    cotangent,
    clip_lengths,
    key_mask,
    rel_buckets,
    attention_weights,
    attention_first,
    attention_second,
    feedforward_weights,
    feedforward_first,
    feedforward_second,
    small_params,
    small_first,
    small_second,
):
    gathered_attention, gathered_forward = (
        lax.all_gather(attention_weights.astype(jnp.bfloat16), "dp", axis=1, tiled=True),
        lax.all_gather(feedforward_weights.astype(jnp.bfloat16), "dp", axis=1, tiled=True),
    )
    query_weight = gathered_attention[0]
    key_weight = gathered_attention[1]
    value_weight = gathered_attention[2]
    output_weight = gathered_attention[3]
    up_weight = gathered_forward[0]
    down_weight = gathered_forward[1]
    head_cols = query_weight.shape[1]
    heads_local = head_cols // HD
    hidden_local = up_weight.shape[1]
    tensor_rank = lax.axis_index("tensor")
    col_start = tensor_rank * head_cols
    head_start = tensor_rank * heads_local
    hidden_start = tensor_rank * hidden_local
    row_count = tokens.shape[0]
    bucket_count = row_count // BUCKET_SLOTS
    (
        gain_one,
        shift_one,
        gain_two,
        shift_two,
        bias_query,
        bias_value,
        bias_output,
        bias_down,
        bias_up,
        rel_table,
        gate_matrix,
        gate_offset,
        gate_scale,
    ) = split_small(small_params)
    local_bias_query = lax.dynamic_slice_in_dim(bias_query, col_start, head_cols)
    local_bias_value = lax.dynamic_slice_in_dim(bias_value, col_start, head_cols)
    local_bias_up = lax.dynamic_slice_in_dim(bias_up, hidden_start, hidden_local)
    scale_local = lax.dynamic_slice_in_dim(gate_scale, head_start, heads_local)
    table_local = lax.dynamic_slice_in_dim(rel_table.reshape(NB, H), head_start, heads_local, 1)
    allowed = jax.vmap(allowed_mask)(clip_lengths, key_mask.reshape(bucket_count, BUCKET_SLOTS))[
        :, None
    ]
    leading = (tensor_rank == 0).astype(jnp.float32)
    inputs = tokens.astype(jnp.float32)
    upstream = cotangent.astype(jnp.float32)
    query_bf = (
        jnp.dot(tokens, query_weight, preferred_element_type=jnp.float32) + local_bias_query
    ).astype(jnp.bfloat16)
    key_bf = jnp.dot(tokens, key_weight, preferred_element_type=jnp.float32).astype(jnp.bfloat16)
    value_bf = (
        jnp.dot(tokens, value_weight, preferred_element_type=jnp.float32) + local_bias_value
    ).astype(jnp.bfloat16)
    head_shape = (bucket_count, BUCKET_SLOTS, heads_local, HD)
    heads_of_query = query_bf.reshape(head_shape)
    heads_of_key = key_bf.reshape(head_shape)
    heads_of_value = value_bf.reshape(head_shape)
    head_inputs = lax.dynamic_slice_in_dim(inputs, col_start, head_cols, 1).reshape(head_shape)
    extra, pull_position = jax.vjp(
        partial(position_terms, rel_buckets=rel_buckets),
        head_inputs,
        gate_matrix,
        gate_offset,
        scale_local,
        table_local,
    )
    attention_logits = (
        jnp.einsum(
            "blhd,bmhd->bhlm", heads_of_query, heads_of_key, preferred_element_type=jnp.float32
        )
        * 0.125
    )
    scores = jnp.where(allowed, attention_logits + extra, MASK_VALUE)
    row_max = jnp.max(scores, axis=-1, keepdims=True)
    exponent = jnp.exp(scores - row_max)
    denominator = jnp.sum(exponent, axis=-1, keepdims=True)
    log_total = row_max + jnp.log(denominator)
    probs_bf = (exponent / denominator).astype(jnp.bfloat16)
    context_bf = (
        jnp.einsum("bhlm,bmhd->blhd", probs_bf, heads_of_value, preferred_element_type=jnp.float32)
        .reshape(row_count, head_cols)
        .astype(jnp.bfloat16)
    )
    attention_part = jnp.einsum(
        "nw,dw->nd", context_bf, output_weight, preferred_element_type=jnp.float32
    )
    attention = lax.psum(attention_part, "tensor") + bias_output
    normed, pull_norm_one = jax.vjp(
        layer_norm, DEEP_ALPHA * inputs + attention, gain_one, shift_one
    )
    normed_bf = normed.astype(jnp.bfloat16)
    up_pre = jnp.dot(normed_bf, up_weight, preferred_element_type=jnp.float32) + local_bias_up
    activated, pull_gelu = jax.vjp(gelu_exact, up_pre)
    activated_bf = activated.astype(jnp.bfloat16)
    down_part = jnp.einsum(
        "nf,df->nd", activated_bf, down_weight, preferred_element_type=jnp.float32
    )
    feedforward = lax.psum(down_part, "tensor") + bias_down
    output_values, pull_norm_two = jax.vjp(
        layer_norm, DEEP_ALPHA * normed + feedforward, gain_two, shift_two
    )
    block_output = output_values.astype(jnp.bfloat16)
    grad_res_two, grad_gain_two, grad_shift_two = pull_norm_two(upstream)
    grad_ffn_share = grad_res_two.astype(jnp.bfloat16)
    grad_bias_down = column_sum(grad_ffn_share)
    down_grad = jnp.einsum(
        "nd,nf->df", grad_ffn_share, activated_bf, preferred_element_type=jnp.float32
    )
    grad_activated = jnp.einsum(
        "nd,df->nf", grad_ffn_share, down_weight, preferred_element_type=jnp.float32
    )
    (grad_up_pre,) = pull_gelu(grad_activated)
    grad_up_bf = grad_up_pre.astype(jnp.bfloat16)
    grad_bias_up = column_sum(grad_up_bf)
    up_grad = jnp.einsum("nd,nf->df", normed_bf, grad_up_bf, preferred_element_type=jnp.float32)
    normed_part = jnp.einsum("nf,df->nd", grad_up_bf, up_weight, preferred_element_type=jnp.float32)
    normed_sum = lax.psum(normed_part, "tensor")
    grad_normed = normed_sum + DEEP_ALPHA * grad_res_two
    grad_res_one, grad_gain_one, grad_shift_one = pull_norm_one(grad_normed)
    grad_attention_share = grad_res_one.astype(jnp.bfloat16)
    grad_bias_output = column_sum(grad_attention_share)
    output_grad = jnp.einsum(
        "nd,nw->dw", grad_attention_share, context_bf, preferred_element_type=jnp.float32
    )
    grad_context_bf = jnp.einsum(
        "nd,dw->nw", grad_attention_share, output_weight, preferred_element_type=jnp.float32
    ).astype(jnp.bfloat16)
    grad_heads = grad_context_bf.reshape(head_shape)
    attention_probabilities = jnp.exp(scores - log_total)
    recomputed_bf = attention_probabilities.astype(jnp.bfloat16)
    grad_probs = jnp.einsum(
        "blhd,bmhd->bhlm", grad_heads, heads_of_value, preferred_element_type=jnp.float32
    )
    inner = jnp.sum(grad_probs * attention_probabilities, axis=-1, keepdims=True)
    grad_scores_bf = (attention_probabilities * (grad_probs - inner)).astype(jnp.bfloat16)
    grad_query = (
        (
            jnp.einsum(
                "bhlm,bmhd->blhd", grad_scores_bf, heads_of_key, preferred_element_type=jnp.float32
            )
            * 0.125
        )
        .astype(jnp.bfloat16)
        .reshape(row_count, head_cols)
    )
    grad_key = (
        (
            jnp.einsum(
                "bhlm,blhd->bmhd",
                grad_scores_bf,
                heads_of_query,
                preferred_element_type=jnp.float32,
            )
            * 0.125
        )
        .astype(jnp.bfloat16)
        .reshape(row_count, head_cols)
    )
    grad_value = (
        jnp.einsum("bhlm,blhd->bmhd", recomputed_bf, grad_heads, preferred_element_type=jnp.float32)
        .astype(jnp.bfloat16)
        .reshape(row_count, head_cols)
    )
    grad_head_inputs, grad_gate_matrix, grad_gate_offset, grad_scale_local, grad_table_local = (
        pull_position(grad_scores_bf.astype(jnp.float32))
    )
    query_grad = jnp.einsum("nd,nw->dw", tokens, grad_query, preferred_element_type=jnp.float32)
    key_grad = jnp.einsum("nd,nw->dw", tokens, grad_key, preferred_element_type=jnp.float32)
    value_grad = jnp.einsum("nd,nw->dw", tokens, grad_value, preferred_element_type=jnp.float32)
    input_part = (
        jnp.einsum("nw,dw->nd", grad_query, query_weight, preferred_element_type=jnp.float32)
        + jnp.einsum("nw,dw->nd", grad_key, key_weight, preferred_element_type=jnp.float32)
        + jnp.einsum("nw,dw->nd", grad_value, value_weight, preferred_element_type=jnp.float32)
    )
    own_columns = lax.dynamic_slice_in_dim(input_part, col_start, head_cols, 1)
    input_part = lax.dynamic_update_slice_in_dim(
        input_part, own_columns + grad_head_inputs.reshape(row_count, head_cols), col_start, 1
    )
    grad_inputs = lax.psum(input_part, "tensor") + DEEP_ALPHA * grad_res_one
    tokens_grad = grad_inputs.astype(jnp.bfloat16)
    table_grad = lax.dynamic_update_slice_in_dim(
        jnp.zeros((NB, H), jnp.float32), grad_table_local, head_start, 1
    ).reshape(-1)
    local_small = jnp.concatenate(
        [
            grad_gain_one * leading,
            grad_shift_one * leading,
            grad_gain_two * leading,
            grad_shift_two * leading,
            placed(MODEL_WIDTH, column_sum(grad_query), col_start),
            placed(MODEL_WIDTH, column_sum(grad_value), col_start),
            grad_bias_output * leading,
            grad_bias_down * leading,
            placed(FF, grad_bias_up, hidden_start),
            table_grad,
            grad_gate_matrix,
            grad_gate_offset,
            placed(H, grad_scale_local, head_start),
        ]
    )
    small_grad = lax.psum(local_small, ("dp", "tensor"))
    local_attention = jnp.stack([query_grad, key_grad, value_grad, output_grad])
    local_forward = jnp.stack([up_grad, down_grad])
    summed_attention, summed_forward = lax.psum((local_attention, local_forward), "dp")
    owner_rank = lax.axis_index("dp")
    owned_rows = attention_weights.shape[1]
    share_attention = lax.dynamic_slice_in_dim(
        summed_attention, owner_rank * owned_rows, owned_rows, 1
    )
    share_forward = lax.dynamic_slice_in_dim(summed_forward, owner_rank * owned_rows, owned_rows, 1)
    share_squares = jnp.sum(share_attention * share_attention) + jnp.sum(
        share_forward * share_forward
    )
    big_squares = lax.psum(share_squares, ("dp", "tensor"))
    global_norm = jnp.sqrt(big_squares + jnp.sum(small_grad * small_grad))
    factor = CLIP_LIMIT / jnp.maximum(global_norm, CLIP_LIMIT)
    attention_moment, attention_square, attention_master = adam_step(
        attention_weights,
        attention_first,
        attention_second,
        factor * share_attention,
        RATE_MATRIX,
        WEIGHT_DECAY,
    )
    feedforward_moment, feedforward_square, feedforward_master = adam_step(
        feedforward_weights,
        feedforward_first,
        feedforward_second,
        factor * share_forward,
        RATE_MATRIX,
        WEIGHT_DECAY,
    )
    small_moment, small_square, small_master = adam_step(
        small_params, small_first, small_second, factor * small_grad, RATE_SMALL, 0.0
    )
    return (
        global_norm,
        attention_moment,
        attention_square,
        attention_master,
        attention_master.astype(jnp.bfloat16),
        feedforward_moment,
        feedforward_square,
        feedforward_master,
        feedforward_master.astype(jnp.bfloat16),
        small_moment,
        small_square,
        small_master,
        block_output,
        tokens_grad,
    )


F32 = jnp.float32
BF16 = jnp.bfloat16
MESH_ID = pl.DeviceIdType.MESH
LANES = 128
SMALL_ROWS = 104
QUARTER = 32
SUM_ROWS = 4 * QUARTER
TABLE_ROW = 72
GATE_ROW = 102
OFFSET_ROW = 103
INV_SQRT2 = 0.5**0.5
INV_SQRT_2PI = 0.3989422804014327
CHUNK = 128
HALF = 256
W = MODEL_WIDTH
NT = (((1,), (1,)), ((), ()))
TN = (((0,), (0,)), ((), ()))


def mm(a, b):
    return jnp.dot(a, b, preferred_element_type=F32)


def mm_nt(a, b):
    return lax.dot_general(a, b, NT, preferred_element_type=F32)


def mm_tn(a, b):
    return lax.dot_general(a, b, TN, preferred_element_type=F32)


def exact_nt(a, b):
    return lax.dot_general(a, b, NT, precision=FULL_PRECISION, preferred_element_type=F32)


def exact_tn(a, b):
    return lax.dot_general(a, b, TN, precision=FULL_PRECISION, preferred_element_type=F32)


def exact_mm(a, b):
    return jnp.dot(a, b, precision=FULL_PRECISION, preferred_element_type=F32)


def iota(shape, axis):
    return lax.broadcasted_iota(jnp.int32, shape, axis)


def layer_scratch(owned, nz, qkv_pad, heads, head_cols, hidden):
    rows = 2 * BUCKET_SLOTS
    dma = pltpu.SemaphoreType.DMA
    vm = pltpu.VMEM
    shapes = dict(
        wa=vm((4, owned, head_cols), F32),
        wf=vm((2, owned, hidden), F32),
        keep=vm((rows // LANES, LANES), jnp.int32),
        small=vm((3 * SMALL_ROWS + 2 * BUCKET_SLOTS // LANES, LANES), F32),
        shqkv=vm((owned, qkv_pad), F32),
        sho=vm((owned, LANES), F32),
        shup=vm((owned, hidden), F32),
        shdown=vm((owned, hidden), F32),
        smallout=vm((4, SMALL_ROWS, LANES), F32),
        tok=vm((rows, W), BF16),
        cot=vm((2, HALF, W), BF16),
        wqkv=vm((W, qkv_pad), BF16),
        wo1=vm((W, LANES), BF16),
        wo=vm((W, head_cols), BF16),
        wot=vm((head_cols, W), BF16),
        wqkvt=vm((qkv_pad + LANES, W), BF16),
        wupt=vm((hidden, W), BF16),
        wdownt=vm((hidden, W), BF16),
        go=vm((W, LANES), BF16),
        glin=vm((W, LANES), F32),
        wup=vm((W, hidden), BF16),
        wdown=vm((W, hidden), BF16),
        q=vm((rows, head_cols), BF16),
        k=vm((rows, head_cols), BF16),
        v=vm((rows, head_cols), BF16),
        kt=vm((head_cols, rows), BF16),
        qt=vm((head_cols, rows), BF16),
        dctxt=vm((head_cols, BUCKET_SLOTS), BF16),
        vt=vm((head_cols, rows), BF16),
        ctx=vm((rows, head_cols), BF16),
        dqkv=vm((rows, qkv_pad + LANES), BF16),
        prob=vm((2 * heads, BUCKET_SLOTS, BUCKET_SLOTS), F32),
        gsb=vm((heads * BUCKET_SLOTS, BUCKET_SLOTS), BF16),
        dqf=vm((BUCKET_SLOTS, head_cols), F32),
        mbias=vm((2, BUCKET_SLOTS, BUCKET_SLOTS), BF16),
        band=vm((heads, LANES, 2 * BUCKET_SLOTS), F32),
        dband=vm((heads, LANES, 2 * BUCKET_SLOTS), F32),
        gate=vm((rows, LANES), F32),
        gu=vm((rows, LANES), F32),
        gmat=vm((W, LANES), F32),
        vecs=vm((16, W), F32),
        acc=vm((16, W), F32),
        nb=vm((rows, W), BF16),
        held=vm((2, HALF, W), F32),
        xh1=vm((2, HALF, W), F32),
        rstd1=vm((2, HALF, LANES), F32),
        act=vm((rows, hidden), BF16),
        gelup=vm((rows, hidden), F32),
        gffn=vm((rows, W), BF16),
        gub=vm((rows, hidden), BF16),
        gattn=vm((rows, W), BF16),
        stage=vm((2, HALF, W), BF16),
        ownf=vm((HALF, W), F32),
        cs=vm((2, HALF, W), BF16),
        cr=vm((2, HALF, W), BF16),
        ys=vm((2, HALF, W), BF16),
        yr=vm((2, 2, HALF, W), BF16),
        xrqkv=vm((nz, owned, qkv_pad), BF16),
        xro=vm((nz, owned, LANES), BF16),
        xrup=vm((nz, owned, hidden), BF16),
        xrdown=vm((nz, owned, hidden // 2), BF16),
        xrdownb=vm((nz, owned, hidden // 2), BF16),
        zsqkv=vm((nz - 1, owned, qkv_pad), BF16),
        zso=vm((nz - 1, owned, LANES), BF16),
        zsup=vm((nz - 1, owned, hidden), BF16),
        zsdown=vm((nz - 1, owned, hidden // 2), BF16),
        zsdownb=vm((nz - 1, owned, hidden // 2), BF16),
        zrqkv=vm((nz - 1, owned, qkv_pad), BF16),
        zro=vm((nz - 1, owned, LANES), BF16),
        zrup=vm((nz - 1, owned, hidden), BF16),
        zrdown=vm((nz - 1, owned, hidden // 2), BF16),
        zrdownb=vm((nz - 1, owned, hidden // 2), BF16),
        sm=vm((SUM_ROWS, LANES), F32),
        smc=vm((2, QUARTER, LANES), F32),
        smh=vm((2, QUARTER, LANES), F32),
        smy=vm((QUARTER, LANES), F32),
        smv=vm((QUARTER, LANES), F32),
        smx=vm((QUARTER, LANES), F32),
        smz=vm((nz, QUARTER, LANES), F32),
        sma=vm((SUM_ROWS, LANES), F32),
        sqt=vm((4, 8, LANES), F32),
        sqd=vm((2 * nz, 8, LANES), F32),
        s_in=dma((7,)),
        s_out=dma((5,)),
        s_gs=dma((6,)),
        s_gr=dma((6,)),
        s_ls=dma((7, 2, nz)),
        s_lr=dma((7, 2, nz)),
        s_lxs=dma((7, 2, nz)),
        s_lxr=dma((7, 2, nz)),
        s_cs=dma((4, 2, 2)),
        s_cr=dma((4, 2, 2)),
        s_ys=dma((4, 2, 2)),
        s_yr=dma((4, 2, 2)),
        s_as=dma((3, 2, 2)),
        s_ar=dma((3, 2, 2)),
        s_ol=dma((2, 2)),
        s_os=dma((2, 2)),
        s_or=dma((2, 2)),
        s_xs=dma((5, nz)),
        s_xr=dma((5, nz)),
        s_zs=dma((5, nz)),
        s_zr=dma((5, nz)),
        s_ms=dma((6 + nz,)),
        s_mr=dma((6 + nz,)),
        s_ts=dma((4,)),
        s_tr=dma((4,)),
        s_ds=dma((2 * nz,)),
        s_dr=dma((2 * nz,)),
    )
    return shapes


def layer_kernel(names, dims, *refs):
    n_dp, owned, qkv_pad, heads, head_cols, hidden = dims
    nz = n_dp // 2
    (tok_in, cot_in, lens, keep_in, wa_in, wf_in, small_in) = refs[:7]
    (bo_out, tg_out, out_qkv, out_o, out_up, out_down, out_small, norm_out) = refs[7:15]
    m = SimpleNamespace(**dict(zip(names, refs[15:], strict=True)))
    D = lax.axis_index("dp")
    T = lax.axis_index("tensor")
    z = lax.div(D, 2)
    x = lax.rem(D, 2)
    c = lax.rem(T, 2)
    yy = lax.div(T, 2)
    core_dev = (D, T + 1 - 2 * c)
    y_dev = (D, lax.rem(T + 2, 4))
    x_dev = (z * 2 + 1 - x, T)

    def z_at(k):
        total, bit = 0, 1
        while bit < nz:
            here = lax.rem(lax.div(z, bit), 2)
            total = total + bit * (1 - here if k & bit else here)
            bit *= 2
        return total

    def z_dev(k):
        return (z_at(k) * 2 + x, T)

    def remote(src, dst, ss, rs, dev):
        return pltpu.make_async_remote_copy(
            src_ref=src, dst_ref=dst, send_sem=ss, recv_sem=rs, device_id=dev, device_id_type=MESH_ID
        )

    def loop(n, step):
        def run(i, carry):
            step(i)
            return carry

        lax.fori_loop(0, n, run, 0)

    def block(owner):
        return pl.ds(pl.multiple_of(owner * owned, owned), owned)

    wa, wf, keep, small = m.wa, m.wf, m.keep, m.small
    sh_qkv, sh_o, sh_up, sh_down, small_out = m.shqkv, m.sho, m.shup, m.shdown, m.smallout
    first_loads = []
    for i, (source, target) in enumerate(((wa_in, wa), (wf_in, wf), (small_in, small), (keep_in, keep))):
        cp = pltpu.make_async_copy(source, target, m.s_in.at[3 + i])
        cp.start()
        first_loads.append(cp)
    tok_copy = pltpu.make_async_copy(tok_in, m.tok, m.s_in.at[0])
    tok_copy.start()
    cot_copies = []
    for b in range(2):
        rows = pl.ds(pl.multiple_of(b * BUCKET_SLOTS + c * HALF, HALF), HALF)
        cp = pltpu.make_async_copy(cot_in.at[rows], m.cot.at[b], m.s_in.at[1 + b])
        cp.start()
        cot_copies.append(cp)
    barrier = pltpu.get_barrier_semaphore()
    for k in range(1, 4):
        pl.semaphore_signal(barrier, inc=1, device_id=(D, lax.rem(T + k, 4)), device_id_type=MESH_ID)
    for k in range(1, n_dp):
        pl.semaphore_signal(barrier, inc=1, device_id=(lax.rem(D + k, n_dp), T), device_id_type=MESH_ID)
    for cp in first_loads:
        cp.wait()
    mine = block(D)
    first_o = qkv_pad - 3 * head_cols
    m.wqkv[mine, :] = jnp.concatenate([wa[0], wa[1], wa[2], wa[3, :, 0:first_o]], axis=1).astype(BF16)
    m.wo1[mine, :] = wa[3, :, first_o:head_cols].astype(BF16)
    m.wup[mine, :] = wf[0].astype(BF16)
    m.wdown[mine, :] = wf[1].astype(BF16)
    pl.semaphore_wait(barrier, 3 + n_dp - 1)

    part_rows = owned // 2 if owned % 32 == 0 else owned
    pieces = [(m.wqkv, 0, owned), (m.wo1, 0, owned)]
    for buf in (m.wup, m.wdown):
        pieces.append((buf, 0, part_rows))
        pieces.append((buf, owned - part_rows, part_rows))

    pieces.append(pieces[-1])
    across = len(pieces) - 1
    straight = (across - 1, across)

    def piece(which, owner_z, other_column=False):
        buf, first, count = pieces[which]
        column = 1 - x if other_column != (which == across) else x
        return buf.at[pl.ds(pl.multiple_of((owner_z * 2 + column) * owned + first, 16), count)]

    gathers = {}

    def launch(record, where):
        remote(*where()).start()
        record.append(where)

    def when(condition, action):
        pl.when(condition)(action)

    def from_z(way, step):
        owner_z = z - step if way == 0 else z + step
        return owner_z, (owner_z >= 0) if way == 0 else (owner_z < nz)

    def send_when(which, condition, where):
        when(condition(), lambda: remote(*where()).start())
        gathers.setdefault(which, []).append((condition, where))

    def line_send(which, way, step, hops):
        origin = step - hops

        def where():
            part = piece(which, from_z(way, origin)[0])
            target = ((z + hops if way == 0 else z - hops) * 2 + x, T)
            return part, part, m.s_ls.at[which, way, step], m.s_lr.at[which, way, step], target

        def condition():
            there = (z + hops < nz) if way == 0 else (z >= hops)
            return there & from_z(way, origin)[1]

        send_when(which, condition, where)

    def line_start(which, hops):
        for hop in range(1, hops + 1):
            for way in range(2):
                line_send(which, way, hop, hop)

    def gather_x(which):
        def where():
            own = piece(which, z)
            return own, own, m.s_gs.at[which], m.s_gr.at[which], x_dev

        send_when(which, lambda: D >= 0, where)

    def line_step(which, step, hops):
        for way in range(2):

            def landed(way=way):
                part = piece(which, from_z(way, step)[0])
                sems = m.s_ls.at[which, way, step], m.s_lr.at[which, way, step]
                remote(part, part, *sems, x_dev).wait_recv()

            when(from_z(way, step)[1], landed)
            if step >= hops and step + 1 < nz:
                line_send(which, way, step + 1, 1)
            if which in straight:
                continue

            def where(way=way):
                part = piece(which, from_z(way, step)[0])
                return part, part, m.s_lxs.at[which, way, step], m.s_lxr.at[which, way, step], x_dev

            send_when(which, lambda way=way: from_z(way, step)[1], where)

    def partner_landed(which):
        part = piece(which, z, True)
        remote(part, part, m.s_gs.at[which], m.s_gr.at[which], x_dev).wait_recv()

    def line_end(which):
        partner_landed(which)
        for step in range(1, nz):
            for way in range(2):

                def landed(way=way):
                    part = piece(which, from_z(way, step)[0], True)
                    sems = m.s_lxs.at[which, way, step], m.s_lxr.at[which, way, step]
                    remote(part, part, *sems, x_dev).wait_recv()

                when(from_z(way, step)[1], landed)

    def sent_all(which):
        for condition, where in gathers.pop(which):
            when(condition(), lambda where=where: remote(*where()).wait_send())

    def turn(source, target):
        count = source.shape[1]
        if count % LANES:
            target[...] = source[...].T
            return
        step = HALF if count % HALF == 0 else LANES

        def chunk(i):
            at = pl.ds(pl.multiple_of(i * step, step), step)
            target[at, :] = source[:, at].T

        loop(count // step, chunk)

    line_start(0, 1)
    gather_x(0)
    gather_x(across - 1)

    def small_row(first, count):
        return jnp.concatenate([small[first + i : first + i + 1, :] for i in range(count)], axis=1)

    def pick(values, size):
        total = jnp.zeros((1, size), F32)
        for t in range(4):
            total = total + jnp.where(T == t, values[:, t * size : (t + 1) * size], 0.0)
        return total

    vecs = m.vecs
    vecs[...] = jnp.zeros_like(vecs)
    m.acc[...] = jnp.zeros((16, W), F32)
    for at, first in ((0, 0), (1, 6), (2, 12), (3, 18), (4, 36), (5, 42)):
        vecs[at : at + 1, :] = small_row(first, W // LANES)
    vecs[6:7, :] = pick(small_row(48, FF // LANES), hidden)
    bq = pick(small_row(24, W // LANES), head_cols)
    bv = pick(small_row(30, W // LANES), head_cols)
    bias_qkv = jnp.concatenate(
        [bq, jnp.zeros_like(bq), bv, jnp.zeros((1, qkv_pad - 3 * head_cols), F32)], axis=1
    )
    vecs[7:8, 0:qkv_pad] = bias_qkv

    lane = iota((1, LANES), 1)
    col = iota((W, LANES), 0)
    col_lane = iota((W, LANES), 1)
    gate_row = small[GATE_ROW : GATE_ROW + 1, :]
    col_in_head = lax.rem(col, HD)
    picked_u = jnp.sum(
        jnp.where(col_lane == 2 * col_in_head, gate_row, 0.0), axis=1, keepdims=True
    )
    picked_w = jnp.sum(
        jnp.where(col_lane == 2 * col_in_head + 1, gate_row, 0.0), axis=1, keepdims=True
    )
    in_group = lax.rem(col_lane, 8)
    own_head = (col_lane < 16) & (in_group < heads) & (lax.div(col, HD) == T * heads + in_group)
    m.gmat[...] = jnp.where(own_head, jnp.where(col_lane < 8, picked_u, picked_w), 0.0)
    offset_row = small[OFFSET_ROW : OFFSET_ROW + 1, :]
    offset_u = jnp.sum(jnp.where(lane == 0, offset_row, 0.0), axis=1, keepdims=True)
    offset_w = jnp.sum(jnp.where(lane == 1, offset_row, 0.0), axis=1, keepdims=True)
    scale = jnp.zeros((1, LANES), F32)
    for h in range(heads):
        one = jnp.sum(jnp.where(lane == 2 + T * heads + h, offset_row, 0.0), axis=1, keepdims=True)
        scale = scale + jnp.where(lane == h, one, 0.0)
    head_lane = lane < heads

    line_step(0, 1, 1)

    offsets = small_row(3 * SMALL_ROWS, 2 * BUCKET_SLOTS // LANES).astype(jnp.int32)
    table = small[TABLE_ROW : TABLE_ROW + 32, :]
    long_row = 2 * BUCKET_SLOTS
    sub8 = iota((8, long_row), 0)
    for h in range(heads):
        flat = offsets * H + (T * heads + h)
        at_row = lax.div(flat, LANES)
        at_lane = lax.rem(flat, LANES)
        hot_row = jnp.where(iota((32, long_row), 0) == at_row, 1.0, 0.0)
        spread = exact_tn(table, hot_row)
        values = jnp.sum(
            jnp.where(iota((LANES, long_row), 0) == at_lane, spread, 0.0), axis=0, keepdims=True
        )
        stack = jnp.broadcast_to(pltpu.roll(jnp.broadcast_to(values, (8, long_row)), 1, 1), (8, long_row))
        for bit in (1, 2, 4):
            stack = jnp.where(lax.rem(lax.div(sub8, bit), 2) == 1, pltpu.roll(stack, bit, 1), stack)
        size = 8
        m.band[h, 0:8, :] = stack
        while size < LANES:
            m.band[h, size : 2 * size, :] = pltpu.roll(m.band[h, 0:size, :], size, 1)
            size *= 2
    m.dband[...] = jnp.zeros(m.dband.shape, F32)

    line_step(0, 2, 1)

    for b in range(2):
        end = 0
        ends = []
        for i in range(CLIPS):
            end = end + lens[b, i]
            ends.append(end)
        key_at = iota((1, BUCKET_SLOTS), 1)
        key_segment = jnp.zeros((1, BUCKET_SLOTS), jnp.int32)
        for end in ends:
            key_segment = key_segment + jnp.where(key_at >= end, 1, 0)
        kept = jnp.concatenate([keep[4 * b + i : 4 * b + i + 1, :] for i in range(4)], axis=1)
        live = jnp.where((kept == 1) & (key_segment < CLIPS), key_segment, -1)

        def mask_chunk(i, b=b, ends=ends, live=live):
            query_at = iota((CHUNK, BUCKET_SLOTS), 0) + i * CHUNK
            segment = jnp.zeros((CHUNK, BUCKET_SLOTS), jnp.int32)
            for end in ends:
                segment = segment + jnp.where(query_at >= end, 1, 0)
            allowed = (segment == live) | (query_at == iota((CHUNK, BUCKET_SLOTS), 1))
            m.mbias[b, pl.ds(pl.multiple_of(i * CHUNK, CHUNK), CHUNK), :] = jnp.where(
                allowed, 0.0, MASK_VALUE
            ).astype(BF16)

        loop(BUCKET_SLOTS // CHUNK, mask_chunk)

    for step in range(3, nz):
        line_step(0, step, 1)
    line_start(1, 2)

    tok_copy.wait()
    gmat = m.gmat[...]
    part_hi = gmat.astype(BF16)
    rest = gmat - part_hi.astype(F32)
    part_mid = rest.astype(BF16)
    part_lo = (rest - part_mid.astype(F32)).astype(BF16)
    gate_parts = (part_hi, part_hi, part_hi, part_mid, part_mid, part_lo)
    stacked = jnp.zeros((W, LANES), F32)
    for i, part in enumerate(gate_parts):
        moved = part.astype(F32)
        stacked = stacked + (pltpu.roll(moved, 16 * i, 1) if i else moved)
    m.wqkvt[qkv_pad : qkv_pad + LANES, :] = stacked.astype(BF16).T

    def gate_chunk(i):
        rows = pl.ds(pl.multiple_of(i * HALF, HALF), HALF)
        tokens = m.tok[rows, :]
        linear = mm(tokens, part_hi) + mm(tokens, part_mid) + mm(tokens, part_lo)
        both = jax.nn.sigmoid(linear + jnp.where(lane < 8, offset_u, offset_w))
        m.gu[rows, :] = both
        m.gate[rows, :] = both * (pltpu.roll(both, LANES - 8, 1) * scale - 1.0) + 2.0

    loop(4, gate_chunk)

    line_start(2, 2)
    line_end(0)
    gather_x(1)
    line_step(1, 1, 2)
    line_step(1, 2, 2)
    gather_x(2)

    def project(i):
        rows = pl.ds(pl.multiple_of(i * HALF, HALF), HALF)
        both = mm(m.tok[rows, :], m.wqkv[...]) + vecs[7:8, 0:qkv_pad]
        query = (both[:, 0:head_cols].astype(BF16).astype(F32) * 0.125).astype(BF16)
        m.q[rows, :] = query
        m.qt[:, rows] = query.T
        key = both[:, head_cols : 2 * head_cols].astype(BF16)
        value = both[:, 2 * head_cols : 3 * head_cols].astype(BF16)
        m.k[rows, :] = key
        m.v[rows, :] = value
        m.kt[:, rows] = key.T
        m.vt[:, rows] = value.T

    loop(4, project)

    head_of = lax.div(iota((1, head_cols), 1), HD)
    head_masks = [jnp.where(head_of == h, 1.0, 0.0) for h in range(heads)]
    low_masks = [m.astype(BF16) for m in head_masks]

    def hooked(first, count, chunk, hooks):
        def step_of(i):
            step = i + first
            chunk(step)
            for at, action in hooks.items():
                if first <= at < first + count:
                    when(step == at, action)

        loop(count, step_of)

    def by_head(stacked):
        total = stacked[0:CHUNK, :] * head_masks[0]
        for h in range(1, heads):
            total = total + stacked[h * CHUNK : (h + 1) * CHUNK, :] * head_masks[h]
        return total

    def attend(b, hooks):
        keys = m.kt[:, b * BUCKET_SLOTS : (b + 1) * BUCKET_SLOTS]
        values = m.v[b * BUCKET_SLOTS : (b + 1) * BUCKET_SLOTS, :]

        def chunk(i):
            local = pl.ds(pl.multiple_of(i * CHUNK, CHUNK), CHUNK)
            rows = pl.ds(pl.multiple_of(b * BUCKET_SLOTS + i * CHUNK, CHUNK), CHUNK)
            window = pl.ds(pl.multiple_of(BUCKET_SLOTS - i * CHUNK, CHUNK), BUCKET_SLOTS)
            query = m.q[rows, :]
            gates = m.gate[rows, :]
            all_scores = mm(jnp.concatenate([query * mask for mask in low_masks], axis=0), keys)
            all_probs = []
            for h in range(heads):
                scores = all_scores[h * CHUNK : (h + 1) * CHUNK, :]
                scores = scores + gates[:, h : h + 1] * m.band[h, :, window]
                scores = scores + m.mbias[b, local, :].astype(F32)
                top = jnp.max(scores, axis=1, keepdims=True)
                weight = jnp.exp(scores - top)
                total = jnp.sum(weight, axis=1, keepdims=True)
                probability = weight * (1.0 / total)
                m.prob[b * heads + h, local, :] = probability
                all_probs.append(probability.astype(BF16))
            m.ctx[rows, :] = by_head(mm(jnp.concatenate(all_probs, axis=0), values)).astype(BF16)

        hooked(0, BUCKET_SLOTS // CHUNK, chunk, hooks)

    core_sent = {}
    y_sent = {}

    def exchange(phase, b, product):
        other = b * BUCKET_SLOTS + (1 - c) * HALF
        own = b * BUCKET_SLOTS + c * HALF
        for cp in core_sent.get((phase - 1, b), []) + y_sent.get((phase - 1, b), []):
            cp.wait_send()
        for i in range(2):
            at = slice(i * CHUNK, (i + 1) * CHUNK)
            rows = pl.ds(pl.multiple_of(other + i * CHUNK, CHUNK), CHUNK)
            m.cs[b, at, :] = product(rows).astype(BF16)
            cp = remote(
                m.cs.at[b, at], m.cr.at[b, at], m.s_cs.at[phase, b, i], m.s_cr.at[phase, b, i], core_dev
            )
            cp.start()
            core_sent.setdefault((phase, b), []).append(cp)
        for i in range(2):
            at = slice(i * CHUNK, (i + 1) * CHUNK)
            rows = pl.ds(pl.multiple_of(own + i * CHUNK, CHUNK), CHUNK)
            m.ownf[at, :] = product(rows)
        for i in range(2):
            at = slice(i * CHUNK, (i + 1) * CHUNK)
            core_sent[(phase, b)][i].wait_recv()
            m.ys[b, at, :] = (m.ownf[at, :] + m.cr[b, at, :].astype(F32)).astype(BF16)
            cp = remote(
                m.ys.at[b, at],
                m.yr.at[phase % 2, b, at],
                m.s_ys.at[phase, b, i],
                m.s_yr.at[phase, b, i],
                y_dev,
            )
            cp.start()
            y_sent.setdefault((phase, b), []).append(cp)

    def arrived(phase, b, at):
        return m.ys[b, at, :].astype(F32) + m.yr[phase % 2, b, at, :].astype(F32)

    def own_rows(b, i):
        return pl.ds(pl.multiple_of(b * BUCKET_SLOTS + c * HALF + i * CHUNK, CHUNK), CHUNK)

    core_spread = {}

    def spread(which, buf, b, i):
        part = buf.at[own_rows(b, i)]
        cp = remote(part, part, m.s_as.at[which, b, i], m.s_ar.at[which, b, i], core_dev)
        cp.start()
        core_spread.setdefault((which, b), []).append(cp)

    spread_done = set()

    def spread_end(which, b, i):
        if (which, b, i) not in spread_done:
            core_spread[(which, b)][i].wait_recv()
            spread_done.add((which, b, i))

    def as_it_lands(phase, b, chunk):
        for i in range(2):
            y_sent[(phase, b)][i].wait_recv()
            chunk(i)

    def row_mean(values):
        return jnp.mean(values, axis=1, keepdims=True)

    def add_row(at, values):
        m.acc[at : at + 1, 0 : values.shape[1]] += jnp.sum(values, axis=0, keepdims=True)

    def norm_one(b):

        def chunk(i):
            at = pl.ds(pl.multiple_of(i * CHUNK, CHUNK), CHUNK)
            rows = own_rows(b, i)
            residual = DEEP_ALPHA * m.tok[rows, :].astype(F32) + (arrived(0, b, at) + vecs[4:5, :])
            centred = residual - row_mean(residual)
            rstd = lax.rsqrt(row_mean(centred * centred) + NORM_EPSILON)
            hat = centred * rstd
            normed = hat * vecs[0:1, :] + vecs[1:2, :]
            m.xh1[b, at, :] = hat
            m.rstd1[b, at, :] = jnp.broadcast_to(rstd, (CHUNK, LANES))
            m.held[b, at, :] = normed
            m.nb[rows, :] = normed.astype(BF16)
            spread(0, m.nb, b, i)

        as_it_lands(0, b, chunk)

    def own_first(which, b, chunk):
        def rows_at(step):
            i = lax.rem(step + 2 * c, 4)
            return pl.ds(pl.multiple_of(b * BUCKET_SLOTS + i * CHUNK, CHUNK), CHUNK)

        loop(2, lambda step: chunk(rows_at(step)))
        for i in range(2):
            spread_end(which, b, i)
            chunk(rows_at(2 + i))

    def feed(b):
        def chunk(rows):
            up = mm(m.nb[rows, :], m.wup[...]) + vecs[6:7, :]
            half_phi = 0.5 * (1.0 + lax.erf(up * INV_SQRT2))
            m.act[rows, :] = (up * half_phi).astype(BF16)
            m.gelup[rows, :] = half_phi + up * (jnp.exp(up * up * -0.5) * INV_SQRT_2PI)

        own_first(0, b, chunk)

    out_copies = []

    def result_rows(which, b, stage, out):
        rows = pl.ds(pl.multiple_of(b * BUCKET_SLOTS + c * HALF, HALF), HALF)
        part = stage.at[b]
        here = pltpu.make_async_copy(part, out.at[rows], m.s_ol.at[which, b])
        there = remote(part, out.at[rows], m.s_os.at[which, b], m.s_or.at[which, b], core_dev)
        here.start()
        there.start()
        out_copies.append((here, there))

    def norm_two(b):
        cot_copies[b].wait()

        def chunk(i):
            at = pl.ds(pl.multiple_of(i * CHUNK, CHUNK), CHUNK)
            rows = own_rows(b, i)
            residual = DEEP_ALPHA * m.held[b, at, :] + (arrived(1, b, at) + vecs[5:6, :])
            centred = residual - row_mean(residual)
            rstd = lax.rsqrt(row_mean(centred * centred) + NORM_EPSILON)
            hat = centred * rstd
            m.stage[b, at, :] = (hat * vecs[2:3, :] + vecs[3:4, :]).astype(BF16)
            upstream = m.cot[b, at, :].astype(F32)
            add_row(2, upstream * hat)
            add_row(3, upstream)
            scaled = upstream * vecs[2:3, :]
            grad = rstd * (scaled - row_mean(scaled) - hat * row_mean(scaled * hat))
            m.held[b, at, :] = grad
            low = grad.astype(BF16)
            m.gffn[rows, :] = low
            spread(1, m.gffn, b, i)
            add_row(5, low.astype(F32))

        as_it_lands(1, b, chunk)
        result_rows(0, b, m.stage, bo_out)

    def feed_back(b):
        def chunk(rows):
            grad = mm(m.gffn[rows, :], m.wdown[...]) * m.gelup[rows, :]
            low = grad.astype(BF16)
            m.gub[rows, :] = low
            add_row(6, low.astype(F32))

        own_first(1, b, chunk)

    def norm_one_back(b):

        def chunk(i):
            at = pl.ds(pl.multiple_of(i * CHUNK, CHUNK), CHUNK)
            rows = own_rows(b, i)
            upstream = arrived(2, b, at) + DEEP_ALPHA * m.held[b, at, :]
            hat = m.xh1[b, at, :]
            add_row(0, upstream * hat)
            add_row(1, upstream)
            scaled = upstream * vecs[0:1, :]
            rstd = m.rstd1[b, at, 0:1]
            grad = rstd * (scaled - row_mean(scaled) - hat * row_mean(scaled * hat))
            m.held[b, at, :] = grad
            low = grad.astype(BF16)
            m.gattn[rows, :] = low
            spread(2, m.gattn, b, i)
            add_row(4, low.astype(F32))

        as_it_lands(2, b, chunk)

    def gate_back(rows, grad):
        u = m.gu[rows, :]
        w = pltpu.roll(u, LANES - 8, 1)
        grad_u = jnp.where(head_lane, grad * (w * scale - 1.0) * u * (1.0 - u), 0.0)
        grad_w = jnp.where(head_lane, grad * u * scale * w * (1.0 - w), 0.0)
        add_row(8, jnp.where(head_lane, grad * u * w, 0.0))
        linear = grad_u + pltpu.roll(grad_w, 8, 1)
        add_row(9, linear)
        hi = linear.astype(BF16).astype(F32)
        mid = (linear - hi).astype(BF16).astype(F32)
        lo = (linear - hi - mid).astype(BF16).astype(F32)
        stacked = hi
        for at, part in enumerate((mid, lo, hi, mid, hi)):
            stacked = stacked + pltpu.roll(part, 16 * (at + 1), 1)
        m.dqkv[rows, qkv_pad : qkv_pad + LANES] = stacked.astype(BF16)

    def attend_back(b, hooks):
        keys = m.k[b * BUCKET_SLOTS : (b + 1) * BUCKET_SLOTS, :]
        values = m.vt[:, b * BUCKET_SLOTS : (b + 1) * BUCKET_SLOTS]

        def chunk(step):
            i = lax.rem(step + 2 * c, 4)
            local = pl.ds(pl.multiple_of(i * CHUNK, CHUNK), CHUNK)
            rows = pl.ds(pl.multiple_of(b * BUCKET_SLOTS + i * CHUNK, CHUNK), CHUNK)
            window = pl.ds(pl.multiple_of(BUCKET_SLOTS - i * CHUNK, CHUNK), BUCKET_SLOTS)
            place = pl.ds(pl.multiple_of(3 * CHUNK - i * CHUNK, CHUNK), BUCKET_SLOTS)
            grad_context = mm(m.gattn[rows, :], m.wo[...]).astype(BF16)
            m.dctxt[:, local] = grad_context.T
            gates = m.gate[rows, :]
            all_grads = mm(jnp.concatenate([grad_context * mask for mask in low_masks], axis=0), values)
            all_low = []
            grad_gates = jnp.zeros((CHUNK, LANES), F32)
            for h in range(heads):
                grad_probs = all_grads[h * CHUNK : (h + 1) * CHUNK, :]
                probability = m.prob[b * heads + h, local, :]
                inner = jnp.sum(grad_probs * probability, axis=1, keepdims=True)
                low = (probability * (grad_probs - inner)).astype(BF16)
                m.gsb[pl.ds(pl.multiple_of(h * BUCKET_SLOTS + i * CHUNK, CHUNK), CHUNK), :] = low
                all_low.append(low)
                rounded = low.astype(F32)
                one = jnp.sum(rounded * m.band[h, :, window], axis=1, keepdims=True)
                grad_gates = grad_gates + jnp.where(lane == h, one, 0.0)
                m.dband[h, :, place] += rounded * gates[:, h : h + 1]
            m.dqf[local, :] = by_head(mm(jnp.concatenate(all_low, axis=0), keys)) * 0.125
            gate_back(rows, grad_gates)

        hooked(0, 2, chunk, hooks)
        spread_end(2, b, 0)
        spread_end(2, b, 1)
        hooked(2, 2, chunk, hooks)
        all_rows = slice(b * BUCKET_SLOTS, (b + 1) * BUCKET_SLOTS)
        own_rows_of = lax.div(iota((head_cols, 1), 0), HD)
        row_masks = [jnp.where(own_rows_of == h, 1.0, 0.0).astype(BF16) for h in range(heads)]
        spread_out = lambda turned: jnp.concatenate([turned * mask for mask in row_masks], axis=1)
        grad_key = mm(spread_out(m.qt[:, all_rows]), m.gsb[...]).T
        probs = m.prob[b * heads : (b + 1) * heads].reshape(heads * BUCKET_SLOTS, BUCKET_SLOTS)
        grad_value = mm(spread_out(m.dctxt[...]), probs.astype(BF16)).T
        pad = jnp.zeros((BUCKET_SLOTS, qkv_pad - 3 * head_cols), F32)
        low = jnp.concatenate([m.dqf[...], grad_key, grad_value, pad], axis=1).astype(BF16)
        m.dqkv[all_rows, 0:qkv_pad] = low
        add_row(7, low.astype(F32))

    def input_part(rows):
        return mm(m.dqkv[rows, :], m.wqkvt[...])

    def token_rows(b):
        for cp in out_copies[b]:
            cp.wait()

        def chunk(i):
            at = pl.ds(pl.multiple_of(i * CHUNK, CHUNK), CHUNK)
            total = arrived(3, b, at) + DEEP_ALPHA * m.held[b, at, :]
            m.stage[b, at, :] = total.astype(BF16)

        as_it_lands(3, b, chunk)
        result_rows(1, b, m.stage, tg_out)

    def weight_grad(sent, left, right, put_part, rows=slice(None)):
        for which in sent:
            sent_all(which)

        def chunk(i):
            cols = pl.ds(pl.multiple_of(i * HALF, HALF), HALF)
            put_part(cols, mm_tn(left[rows, cols], right[rows, :]))

        loop(W // HALF, chunk)

    def add_whole(buf):
        def put_part(cols, part):
            buf[cols, :] = (buf[cols, :].astype(F32) + part).astype(BF16)

        return put_part

    def put_whole(buf):
        def put_part(cols, part):
            buf[cols, :] = part.astype(BF16)

        return put_part

    def put_qkv(cols, part):
        m.wqkv[cols, 0 : 3 * head_cols] = part[:, 0 : 3 * head_cols].astype(BF16)
        m.glin[cols, :] = part[:, qkv_pad : qkv_pad + LANES]

    def put_o(cols, part):
        m.wqkv[cols, 3 * head_cols : qkv_pad] = part[:, 0:first_o].astype(BF16)
        m.go[cols, :] = part[:, first_o:head_cols].astype(BF16)

    reduces = []

    def low_bit(k):
        return k & -k if k else nz

    bits = [1 << i for i in range(nz.bit_length() - 1)]
    slots = {}
    for k in range(nz):
        for bit in bits:
            if bit < low_bit(k):
                slots[(k, bit)] = len(slots)
    pass_order = sorted(range(nz), key=lambda k: (low_bit(k), -k))

    def add_landed(total, k, which, arrive):
        for bit in bits:
            if bit < low_bit(k):
                slot = slots[(k, bit)]
                here = arrive.at[slot]
                sems = m.s_zs.at[which, slot], m.s_zr.at[which, slot]
                remote(here, here, *sems, z_dev(bit)).wait_recv()
                total = total + arrive[slot].astype(F32)
        return total

    def reduce_start(which, buf, land, ks=None):
        for k in ks or pass_order:

            def where(k=k):
                rows = block(2 * z_at(k) + 1 - x)
                return buf.at[rows], land.at[k], m.s_xs.at[which, k], m.s_xr.at[which, k], x_dev

            launch(reduces, where)

    def reduce_block(k, which, buf, land, out, arrive, share):
        here = land.at[k]
        remote(here, here, m.s_xs.at[which, k], m.s_xr.at[which, k], x_dev).wait_recv()
        total = buf[block(2 * z_at(k) + x), :].astype(F32) + land[k].astype(F32)
        if k == 0:
            share[...] = total
        else:
            out[k - 1] = add_landed(total, k, which, arrive).astype(BF16)

            def where():
                bit = low_bit(k)
                slot = slots[(k - bit, bit)]
                sems = m.s_zs.at[which, slot], m.s_zr.at[which, slot]
                return out.at[k - 1], arrive.at[slot], *sems, z_dev(bit)

            launch(reduces, where)

    def reduce_pass(*matrix):
        for k in pass_order:
            reduce_block(k, *matrix)

    kept = [k for k in range(nz) if k % 2 == 0]
    x_slots = {k: i for i, k in enumerate(kept)}
    far_slots = {}
    for k in kept:
        for bit in bits[1:]:
            if bit < low_bit(k):
                far_slots[(k, bit)] = len(x_slots) + len(far_slots)

    def owner_rows(k, side):
        return block(2 * z_at(k) + (1 - x if side else x))

    def near_start(which, buf, land):
        for k in reversed(kept):
            for side in (1, 0):

                def where(k=k, side=side):
                    at = k + side
                    sems = m.s_xs.at[which, at], m.s_xr.at[which, at]
                    return buf.at[owner_rows(k + 1, side)], land.at[at], *sems, z_dev(1)

                launch(reduces, where)

    def near_total(k, side, which, buf, land):
        at = k + side
        here = land.at[at]
        remote(here, here, m.s_xs.at[which, at], m.s_xr.at[which, at], z_dev(1)).wait_recv()
        return buf[owner_rows(k, side), :].astype(F32) + land[at].astype(F32)

    def landed_slot(slot, which, arrive):
        here = arrive.at[slot]
        remote(here, here, m.s_zs.at[which, slot], m.s_zr.at[which, slot], x_dev).wait_recv()
        return arrive[slot].astype(F32)

    def near_across(k, which, buf, land, out, arrive, share):
        slot = x_slots[k]
        out[slot] = near_total(k, 1, which, buf, land).astype(BF16)

        def where():
            return out.at[slot], arrive.at[slot], m.s_zs.at[which, slot], m.s_zr.at[which, slot], x_dev

        launch(reduces, where)

    def near_far(k, which, buf, land, out, arrive, share):
        total = near_total(k, 0, which, buf, land) + landed_slot(x_slots[k], which, arrive)
        for bit in bits[1:]:
            if bit < low_bit(k):
                total = total + landed_slot(far_slots[(k, bit)], which, arrive)
        if k == 0:
            share[...] = total
            return
        bit = low_bit(k)
        slot = far_slots[(k - bit, bit)]
        out[slot] = total.astype(BF16)

        def where():
            sems = m.s_zs.at[which, slot], m.s_zr.at[which, slot]
            return out.at[slot], arrive.at[slot], *sems, z_dev(bit)

        launch(reduces, where)

    def squares_of(total):
        squares = total * total
        folded = jnp.zeros((owned, LANES), F32)
        for i in range(total.shape[1] // LANES):
            folded = folded + squares[:, i * LANES : (i + 1) * LANES]
        tile = jnp.zeros((8, LANES), F32)
        for i in range(owned // 8):
            tile = tile + folded[8 * i : 8 * i + 8, :]
        return tile

    def reduce_end(which, arrive, share):
        total = add_landed(share[...], 0, which, arrive)
        share[...] = total
        return squares_of(total)

    def pass_on(which):
        line_step(which, 1, 2)
        line_step(which, 2, 2)

    def pass_last(which):
        for step in range(3, nz):
            line_step(which, step, 2)

    line_start(3, 2)
    gather_x(3)

    pass_last(1)

    def first_pass():
        line_start(4, 2)
        gather_x(4)

    def second_pass():
        pass_on(2)
        partner_landed(5)
        line_start(5, 2)
        line_start(6, 2)

    attend(0, {0: first_pass, 2: second_pass})
    line_end(1)
    m.wo[...] = jnp.concatenate([m.wqkv[:, 3 * head_cols : qkv_pad], m.wo1[...]], axis=1)
    turn(m.wo, m.wot)
    out_product = lambda rows: mm(m.ctx[rows, :], m.wot[...])
    exchange(0, 0, out_product)
    pass_last(2)
    attend(1, {1: lambda: pass_on(3), 3: lambda: pass_last(3)})
    exchange(0, 1, out_product)
    pass_on(4)
    pass_on(5)
    norm_one(0)
    pass_last(4)
    pass_on(6)
    line_end(2)
    line_end(3)
    feed(0)
    pass_last(5)
    pass_last(6)
    line_end(4)
    turn(m.wdown, m.wdownt)
    down_product = lambda rows: mm(m.act[rows, :], m.wdownt[...])
    exchange(1, 0, down_product)
    norm_one(1)
    feed(1)
    exchange(1, 1, down_product)
    turn(m.wup, m.wupt)
    turn(m.wqkv, m.wqkvt)
    up_product = lambda rows: mm(m.gub[rows, :], m.wupt[...])
    norm_two(0)
    feed_back(0)
    exchange(2, 0, up_product)
    first_rows, last_rows = slice(0, BUCKET_SLOTS), slice(BUCKET_SLOTS, 2 * BUCKET_SLOTS)
    weight_grad((), m.gffn, m.act, put_whole(m.wdownt), first_rows)
    weight_grad((2, 3), m.nb, m.gub, put_whole(m.wup), first_rows)
    norm_two(1)
    spread_end(1, 1, 0)
    spread_end(1, 1, 1)
    weight_grad((), m.gffn, m.act, add_whole(m.wdownt), last_rows)
    half = hidden // 2
    left, right = m.wdownt.at[:, 0:half], m.wdownt.at[:, half:hidden]
    down = (0, left, m.xrdown, m.zsdown, m.zrdown, sh_down.at[:, 0:half])
    down_near = (4, right, m.xrdownb, m.zsdownb, m.zrdownb, sh_down.at[:, half:hidden])
    near_start(4, right, m.xrdownb)
    reduce_start(0, left, m.xrdown)
    feed_back(1)
    exchange(2, 1, up_product)
    weight_grad((), m.nb, m.gub, add_whole(m.wup), last_rows)
    reduce_start(1, m.wup, m.xrup)
    up = (1, m.wup, m.xrup, m.zsup, m.zrup, sh_up)
    out = (2, m.go, m.xro, m.zso, m.zro, sh_o)
    qkv = (3, m.wqkv, m.xrqkv, m.zsqkv, m.zrqkv, sh_qkv)
    norm_one_back(0)
    blocks = lambda ks, matrix: lambda: [reduce_block(k, *matrix) for k in ks] and None
    early = [pass_order[0:1], pass_order[1:2], pass_order[2:-1]]
    attend_back(
        0,
        {
            0: lambda: near_across(2, *down_near),
            1: lambda: near_across(0, *down_near),
            2: blocks(early[0], down),
            3: blocks(early[1], down),
        },
    )
    exchange(3, 0, input_part)
    blocks(early[0], up)()
    norm_one_back(1)
    spread_end(2, 1, 0)
    spread_end(2, 1, 1)
    weight_grad((0, 1), m.gattn, m.ctx, put_o)
    blocks(early[1], up)()
    downward = list(range(nz - 1, -1, -1))
    reduce_start(2, m.go, m.xro, downward)
    attend_back(
        1,
        {
            0: blocks(early[2] + [0], down),
            1: blocks(early[2], up),
            2: blocks([0], up),
            3: lambda: near_far(2, *down_near),
        },
    )
    weight_grad((), m.tok, m.dqkv, put_qkv)
    first_part, last_part = downward[:-1], downward[-1:]
    reduce_start(3, m.wqkv, m.xrqkv, first_part)
    reduce_block(downward[0], *out)

    sm = m.sm
    sm[...] = jnp.zeros((SUM_ROWS, LANES), F32)
    acc = m.acc
    lead = jnp.where(yy == 0, 1.0, 0.0)

    def put(first, values):
        for i in range(values.shape[1] // LANES):
            sm[first + i : first + i + 1, :] = values[:, i * LANES : (i + 1) * LANES]

    def spot(values):
        return jnp.concatenate([jnp.where(T == t, values, 0.0) for t in range(4)], axis=1)

    for at, first in ((0, 0), (1, 6), (2, 12), (3, 18), (4, 36), (5, 42)):
        put(first, acc[at : at + 1, :] * lead)
    put(24, spot(acc[7:8, 0:head_cols]))
    put(30, spot(acc[7:8, 2 * head_cols : 3 * head_cols]))
    put(48, spot(acc[6:7, 0:hidden]))
    parts = []
    for h in range(heads):
        size = LANES // 2
        left = m.dband[h]
        while size >= 8:
            left = left[0:size, :] + pltpu.roll(left[size : 2 * size, :], long_row - size, 1)
            size //= 2
        for bit in (1, 2, 4):
            left = jnp.where(lax.rem(lax.div(sub8, bit), 2) == 1, pltpu.roll(left, long_row - bit, 1), left)
        left = pltpu.roll(left, LANES - 1, 1)
        diagonal = jnp.sum(left, axis=0, keepdims=True)
        hi = diagonal.astype(BF16).astype(F32)
        mid = (diagonal - hi).astype(BF16).astype(F32)
        parts += [hi, mid, diagonal - hi - mid]
    parts = jnp.concatenate(parts + [jnp.zeros((16 - len(parts), long_row), F32)], axis=0).astype(BF16)
    bucket_rows = -(-NB // LANES) * LANES
    valid = iota((1, long_row), 1) < long_row - 1
    hot_bucket = jnp.where((iota((bucket_rows, long_row), 0) == offsets) & valid, 1.0, 0.0).astype(BF16)
    by_bucket = mm_nt(parts, hot_bucket)
    bucket = iota((1, bucket_rows), 1)
    table_grad = jnp.zeros((32, LANES), F32)
    for h in range(heads):
        sums = by_bucket[3 * h : 3 * h + 1] + by_bucket[3 * h + 1 : 3 * h + 2] + by_bucket[3 * h + 2 : 3 * h + 3]
        flat = bucket * H + (T * heads + h)
        hot_row = jnp.where((iota((32, bucket_rows), 0) == lax.div(flat, LANES)) & (bucket < NB), 1.0, 0.0)
        hot_lane = jnp.where(iota((LANES, bucket_rows), 0) == lax.rem(flat, LANES), sums, 0.0)
        table_grad = table_grad + exact_nt(hot_row, hot_lane)
    sm[TABLE_ROW : TABLE_ROW + 30, :] = table_grad[0:30, :]

    lin_grad = m.glin[...]
    lin_grad = lin_grad + pltpu.roll(lin_grad, LANES - 16, 1) + pltpu.roll(lin_grad, LANES - 32, 1)
    lin_grad = jnp.where(own_head, lin_grad, 0.0)
    grad_u = jnp.sum(jnp.where(col_lane < 8, lin_grad, 0.0), axis=1, keepdims=True)
    grad_w = jnp.sum(jnp.where(col_lane >= 8, lin_grad, 0.0), axis=1, keepdims=True)
    by_lane = jnp.where(col_lane == 2 * col_in_head, grad_u, 0.0)
    by_lane = by_lane + jnp.where(col_lane == 2 * col_in_head + 1, grad_w, 0.0)
    sm[GATE_ROW : GATE_ROW + 1, :] = jnp.sum(by_lane, axis=0, keepdims=True)
    lin_total = acc[9:10, 0:LANES]
    total_u = jnp.sum(jnp.where(lane < 8, lin_total, 0.0), axis=1, keepdims=True)
    total_w = jnp.sum(jnp.where((lane >= 8) & (lane < 16), lin_total, 0.0), axis=1, keepdims=True)
    last = jnp.where(lane == 0, total_u, 0.0) + jnp.where(lane == 1, total_w, 0.0)
    scale_grad = acc[8:9, 0:LANES]
    for h in range(heads):
        one = jnp.sum(jnp.where(lane == h, scale_grad, 0.0), axis=1, keepdims=True)
        last = last + jnp.where(lane == 2 + T * heads + h, one, 0.0)
    sm[OFFSET_ROW : OFFSET_ROW + 1, :] = last

    small_sent = []

    def small_send(at, source, target, dev):
        cp = remote(source, target, m.s_ms.at[at], m.s_mr.at[at], dev)
        cp.start()
        small_sent.append(cp)
        return cp

    def quarter(index):
        return pl.ds(pl.multiple_of(index * QUARTER, QUARTER), QUARTER)

    to_core = [small_send(i, sm.at[quarter(2 * i + 1 - c)], m.smc.at[i], core_dev) for i in range(2)]
    for i in range(2):
        to_core[i].wait_recv()
        m.smh[i] = sm[quarter(2 * i + c), :] + m.smc[i]
    to_y = small_send(2, m.smh.at[1 - yy], m.smy, y_dev)
    reduce_block(first_part[0], *qkv)
    exchange(3, 1, input_part)
    reduce_block(downward[1], *out)
    to_y.wait_recv()
    m.smv[...] = m.smh[yy] + m.smy[...]
    to_x = small_send(3, m.smv, m.smx, x_dev)
    reduce_start(3, m.wqkv, m.xrqkv, last_part)
    for k in downward[2:]:
        reduce_block(k, *out)
    to_x.wait_recv()
    m.smz[z] = m.smv[...] + m.smx[...]
    for k in range(1, nz):
        small_send(3 + k, m.smz.at[z], m.smz.at[z], z_dev(k))
    for k in first_part[1:]:
        reduce_block(k, *qkv)
    token_rows(0)
    reduce_block(0, *qkv)
    squares = reduce_end(0, m.zrdown, sh_down.at[:, 0:half])
    near_far(0, *down_near)
    squares = squares + squares_of(sh_down[:, half:hidden])
    squares = squares + reduce_end(1, m.zrup, sh_up)
    squares = squares + reduce_end(2, m.zro, sh_o)
    for k in range(1, nz):
        here = m.smz.at[z_at(k)]
        remote(here, here, m.s_ms.at[3 + k], m.s_mr.at[3 + k], z_dev(k)).wait_recv()
    own_quarter = m.smz[0]
    for i in range(1, nz):
        own_quarter = own_quarter + m.smz[i]
    m.sma[quarter(T), :] = own_quarter
    for k in range(1, 4):
        mine_small = m.sma.at[quarter(T)]
        small_send(2 + nz + k, mine_small, mine_small, (D, lax.rem(T + k, 4)))
    squares = squares + reduce_end(3, m.zrqkv, sh_qkv)
    last_copies = []
    for i, (source, target) in enumerate(
        ((sh_down, out_down), (sh_up, out_up), (sh_o, out_o), (sh_qkv, out_qkv))
    ):
        cp = pltpu.make_async_copy(source, target, m.s_out.at[i])
        cp.start()
        last_copies.append(cp)
    sqt = m.sqt
    sqt[T] = squares
    tail_sent = []
    for k in range(1, 4):
        cp = remote(
            sqt.at[T], sqt.at[T], m.s_ts.at[k], m.s_tr.at[k], (D, lax.rem(T + k, 4))
        )
        cp.start()
        tail_sent.append(cp)
    token_rows(1)
    for k in range(1, 4):
        here = m.sma.at[quarter(lax.rem(T + 4 - k, 4))]
        remote(here, here, m.s_ms.at[2 + nz + k], m.s_mr.at[2 + nz + k], core_dev).wait_recv()
    small_total = m.sma[0:SMALL_ROWS, :]
    for i in range(3):
        small_out[i] = small[i * SMALL_ROWS : (i + 1) * SMALL_ROWS, :]
    small_out[3] = small_total
    cp = pltpu.make_async_copy(small_out, out_small, m.s_out.at[4])
    cp.start()
    last_copies.append(cp)
    small_square = small_total * small_total
    small_tile = jnp.zeros((8, LANES), F32)
    for i in range(SMALL_ROWS // 8):
        small_tile = small_tile + small_square[8 * i : 8 * i + 8, :]
    for k in range(1, 4):
        here = sqt.at[lax.rem(T + 4 - k, 4)]
        remote(here, here, m.s_ts.at[k], m.s_tr.at[k], core_dev).wait_recv()
    sqd = m.sqd
    sqd[D] = sqt[0] + sqt[1] + sqt[2] + sqt[3]
    for k in range(1, n_dp):
        cp = remote(
            sqd.at[D], sqd.at[D], m.s_ds.at[k], m.s_dr.at[k], (lax.rem(D + k, n_dp), T)
        )
        cp.start()
        tail_sent.append(cp)
    for k in range(1, n_dp):
        here = sqd.at[lax.rem(D + n_dp - k, n_dp)]
        remote(here, here, m.s_ds.at[k], m.s_dr.at[k], core_dev).wait_recv()
    everything = small_tile
    for i in range(n_dp):
        everything = everything + sqd[i]
    sum_all = jnp.sum(jnp.sum(everything, axis=0, keepdims=True), axis=1, keepdims=True)
    norm_out[...] = jnp.broadcast_to(jnp.sqrt(sum_all), (8, LANES))

    for which in list(gathers):
        sent_all(which)
    for where in reduces:
        remote(*where()).wait_send()
    for cp in small_sent + tail_sent:
        cp.wait_send()
    for sent in core_spread.values():
        for cp in sent:
            cp.wait_send()
    for b in range(2):
        for cp in core_sent[(3, b)] + y_sent[(3, b)]:
            cp.wait_send()
    for cp in last_copies:
        cp.wait()
    for here, there in out_copies[2:]:
        here.wait()
        there.wait()


def adam_kernel(head_cols, *refs):
    ins, rest = refs[:14], refs[14:]
    block_in, token_in = ins[12:14]
    outs, rest = rest[:14], rest[14:]
    norm_out, block_out, token_out = outs[0], outs[12], outs[13]
    held, made = rest[:12], rest[12:24]
    block_held, token_held, s_in, s_out = rest[24:]
    loads = [pltpu.make_async_copy(ins[i], held[i], s_in.at[i]) for i in range(12)]
    passing = [
        pltpu.make_async_copy(block_in, block_held, s_in.at[12]),
        pltpu.make_async_copy(token_in, token_held, s_in.at[13]),
    ]
    passed = [
        pltpu.make_async_copy(block_held, block_out, s_out.at[12]),
        pltpu.make_async_copy(token_held, token_out, s_out.at[13]),
    ]
    for cp in loads + passing:
        cp.start()
    stores = []

    def store(i):
        cp = pltpu.make_async_copy(made[i], outs[i], s_out.at[i])
        cp.start()
        stores.append(cp)

    sh_qkv, sh_o, sh_up, sh_down, sh_small, norm, aw, am, av, fw, fm, fv = held
    (o_norm, o_am, o_av, o_aw, o_ac, o_fm, o_fv, o_fw, o_fc, o_sm, o_sv, o_sw) = made
    for i in (0, 1, 2, 3, 5):
        loads[i].wait()
    length = norm[0:1, 0:1]
    factor = CLIP_LIMIT / jnp.maximum(length, CLIP_LIMIT)
    o_norm[...] = length
    store(0)
    for i in (6, 7, 8):
        loads[i].wait()
    for i in range(4):
        if i < 3:
            grad = sh_qkv[:, i * head_cols : (i + 1) * head_cols]
        else:
            grad = jnp.concatenate([sh_qkv[:, 3 * head_cols :], sh_o[...]], axis=1)
        moment, square, master = adam_step(
            aw[i], am[i], av[i], factor * grad, RATE_MATRIX, WEIGHT_DECAY
        )
        o_am[i] = moment
        o_av[i] = square
        o_aw[i] = master
        o_ac[i] = master.astype(BF16)
    for i in (1, 2, 3, 4):
        store(i)
    for first, second in zip(passing, passed, strict=True):
        first.wait()
        second.start()
    for i in (9, 10, 11):
        loads[i].wait()
    for i, share in enumerate((sh_up, sh_down)):
        moment, square, master = adam_step(
            fw[i], fm[i], fv[i], factor * share[...], RATE_MATRIX, WEIGHT_DECAY
        )
        o_fm[i] = moment
        o_fv[i] = square
        o_fw[i] = master
        o_fc[i] = master.astype(BF16)
    for i in (5, 6, 7, 8):
        store(i)
    loads[4].wait()
    moment, square, master = adam_step(
        sh_small[0], sh_small[1], sh_small[2], factor * sh_small[3], RATE_SMALL, 0.0
    )
    o_sm[...] = moment
    o_sv[...] = square
    o_sw[...] = master
    for i in (9, 10, 11):
        store(i)
    for cp in stores + passed:
        cp.wait()


def fused_body(
    n_dp,
    tokens,
    cotangent,
    clip_lengths,
    key_mask,
    rel_buckets,
    attention_weights,
    attention_first,
    attention_second,
    feedforward_weights,
    feedforward_first,
    feedforward_second,
    small_params,
    small_first,
    small_second,
):
    rows = tokens.shape[0]
    owned, head_cols = attention_weights.shape[1:]
    hidden = feedforward_weights.shape[2]
    heads = head_cols // HD
    qkv_pad = -(-3 * head_cols // LANES) * LANES
    nz = n_dp // 2
    small_size = SMALL_ROWS * LANES
    total_size = 3 * small_size + 2 * BUCKET_SLOTS
    packed = jnp.zeros((total_size,), F32)
    pieces = (small_params, small_first, small_second, rel_buckets.astype(F32))
    for i, values in enumerate(pieces):
        after = total_size - i * small_size - values.shape[0]
        packed = packed + jnp.pad(values, (i * small_size, after))
    packed = packed.reshape(-1, LANES)
    keep = key_mask.reshape(rows // LANES, LANES)
    scratch = layer_scratch(owned, nz, qkv_pad, heads, head_cols, hidden)
    names = tuple(scratch)
    vmem = pl.BlockSpec(memory_space=pltpu.VMEM)
    smem = pl.BlockSpec(memory_space=pltpu.SMEM)
    anywhere = pl.BlockSpec(memory_space=pl.ANY)
    sds = jax.ShapeDtypeStruct
    block_rows, token_rows, sh_qkv, sh_o, sh_up, sh_down, sh_small, norm = pl.pallas_call(
        partial(layer_kernel, names, (n_dp, owned, qkv_pad, heads, head_cols, hidden)),
        out_shape=(
            sds((rows, W), BF16),
            sds((rows, W), BF16),
            sds((owned, qkv_pad), F32),
            sds((owned, LANES), F32),
            sds((owned, hidden), F32),
            sds((owned, hidden), F32),
            sds((4, SMALL_ROWS, LANES), F32),
            sds((8, LANES), F32),
        ),
        in_specs=[anywhere, anywhere, smem] + [anywhere] * 4,
        out_specs=(anywhere,) * 7 + (vmem,),
        scratch_shapes=list(scratch.values()),
        compiler_params=pltpu.CompilerParams(
            collective_id=1, has_side_effects=True, vmem_limit_bytes=62 * 1024 * 1024
        ),
        name="layer",
    )(tokens, cotangent, clip_lengths, keep, attention_weights, feedforward_weights, packed)
    like = lambda a, dtype=F32: sds(a.shape, dtype)
    small_like = sds((SMALL_ROWS, LANES), F32)
    made = (
        sds((1, 1), F32),
        like(attention_weights),
        like(attention_weights),
        like(attention_weights),
        like(attention_weights, BF16),
        like(feedforward_weights),
        like(feedforward_weights),
        like(feedforward_weights),
        like(feedforward_weights, BF16),
        small_like,
        small_like,
        small_like,
    )
    operands = (
        sh_qkv,
        sh_o,
        sh_up,
        sh_down,
        sh_small,
        norm,
        attention_weights,
        attention_first,
        attention_second,
        feedforward_weights,
        feedforward_first,
        feedforward_second,
        block_rows,
        token_rows,
    )
    in_vmem = lambda a: pltpu.VMEM(a.shape, a.dtype)
    results = pl.pallas_call(
        partial(adam_kernel, head_cols),
        out_shape=(*made, like(tokens, BF16), like(tokens, BF16)),
        in_specs=[anywhere] * len(operands),
        out_specs=(anywhere,) * (len(made) + 2),
        scratch_shapes=[in_vmem(a) for a in operands[:12]]
        + [in_vmem(a) for a in made]
        + [in_vmem(tokens), in_vmem(tokens)]
        + [pltpu.SemaphoreType.DMA((14,)), pltpu.SemaphoreType.DMA((14,))],
        compiler_params=pltpu.CompilerParams(vmem_limit_bytes=62 * 1024 * 1024),
        name="adam",
    )(*operands)
    length = small_params.shape[0]
    flat = lambda a: a.reshape(-1)[:length]
    return (
        results[0].reshape(()),
        *results[1:9],
        flat(results[9]),
        flat(results[10]),
        flat(results[11]),
        *results[12:],
    )


def fused_fits(mesh, owned):
    columns = mesh.shape["dp"] // 2
    whole = mesh.shape["dp"] % 2 == 0 and columns & (columns - 1) == 0
    return mesh.shape["tensor"] == 4 and whole and owned % 16 == 0

def solution(mesh):
    in_specs = (
        P("dp", None),
        P("dp", None),
        P("dp", None),
        P("dp"),
        P(),
        P(None, "dp", "tensor"),
        P(None, "dp", "tensor"),
        P(None, "dp", "tensor"),
        P(None, "dp", "tensor"),
        P(None, "dp", "tensor"),
        P(None, "dp", "tensor"),
        P(),
        P(),
        P(),
    )
    out_specs = (
        P(),
        P(None, "dp", "tensor"),
        P(None, "dp", "tensor"),
        P(None, "dp", "tensor"),
        P(None, "dp", "tensor"),
        P(None, "dp", "tensor"),
        P(None, "dp", "tensor"),
        P(None, "dp", "tensor"),
        P(None, "dp", "tensor"),
        P(),
        P(),
        P(),
        P("dp", None),
        P("dp", None),
    )
    n_dp = mesh.shape["dp"]
    body = general_body
    if fused_fits(mesh, MODEL_WIDTH // n_dp):
        body = partial(fused_body, n_dp)
    return jax.shard_map(body, mesh=mesh, in_specs=in_specs, out_specs=out_specs, check_vma=False)
```

```python
from functools import partial
from types import SimpleNamespace

import jax
import jax.numpy as jnp
from jax import lax
from jax.experimental import pallas as pl
from jax.experimental.pallas import tpu as pltpu
from jax.sharding import PartitionSpec as P

MODEL_WIDTH = 768
H = 12
HD = 64
FF = 3072
NB = 320
BUCKET_SLOTS = 512
CLIPS = 8
STEP = 5


FULL_PRECISION = lax.Precision.HIGHEST
DEEP_ALPHA = 24.0**0.25
NORM_EPSILON = 1e-05
MASK_VALUE = -1e30
BETA_FIRST = 0.9
BETA_SECOND = 0.98
RATE_MATRIX = 0.03
RATE_SMALL = 0.5
WEIGHT_DECAY = 0.01
ADAM_EPSILON = 1e-08
CLIP_LIMIT = 0.1


def layer_norm(values, norm_gain, norm_shift):
    row_mean = jnp.mean(values, axis=-1, keepdims=True)
    centred = values - row_mean
    variance = jnp.mean(centred * centred, axis=-1, keepdims=True)
    return centred * lax.rsqrt(variance + NORM_EPSILON) * norm_gain + norm_shift


def gelu_exact(values):
    return jax.nn.gelu(values, approximate=False)


def split_small(vector):
    widths = [MODEL_WIDTH] * 8 + [FF, NB * H, HD * 2, 2, H]
    pieces = []
    offset = 0
    for extent in widths:
        pieces.append(vector[offset : offset + extent])
        offset += extent
    return pieces


def allowed_mask(lengths_row, keep_row):
    positions = jnp.arange(BUCKET_SLOTS, dtype=jnp.int32)
    clip_ends = jnp.cumsum(lengths_row)
    segment = jnp.sum((positions[:, None] >= clip_ends[None, :]).astype(jnp.int32), axis=1)
    live_keys = (keep_row == 1) & (segment < CLIPS)
    same_clip = segment[:, None] == segment[None, :]
    return same_clip & (live_keys[None, :] | (positions[:, None] == positions[None, :]))


def band_matrix(diagonals):
    head_count = diagonals.shape[0]
    length = (diagonals.shape[1] + 1) // 2
    padded = jnp.concatenate([diagonals, jnp.zeros((head_count, 1), diagonals.dtype)], axis=1)
    repeated = jnp.tile(padded, (1, length))
    folded = repeated[:, : length * (2 * length - 1)].reshape(head_count, length, 2 * length - 1)
    return folded[:, :, length - 1 :]


def position_terms(head_inputs, gate_matrix, gate_offset, scale_local, table_local, rel_buckets):
    linear = (
        jnp.einsum(
            "blhd,dk->bhlk", head_inputs, gate_matrix.reshape(HD, 2), precision=FULL_PRECISION
        )
        + gate_offset
    )
    sigmoid = jax.nn.sigmoid(linear)
    gate = sigmoid[..., 0] * (sigmoid[..., 1] * scale_local[None, :, None] - 1.0) + 2.0
    onehot = (rel_buckets[:, None] == jnp.arange(NB, dtype=jnp.int32)[None, :]).astype(jnp.float32)
    per_offset = jnp.dot(
        onehot, table_local, precision=FULL_PRECISION, preferred_element_type=jnp.float32
    )
    toeplitz = band_matrix(per_offset.T)
    return gate[..., None] * toeplitz[None]


def adam_step(weights, moment, second, gradient, step_rate, decay_rate):
    moment_new = BETA_FIRST * moment + (1.0 - BETA_FIRST) * gradient
    second_new = BETA_SECOND * second + (1.0 - BETA_SECOND) * gradient * gradient
    moment_hat = moment_new / (1.0 - BETA_FIRST**STEP)
    second_hat = second_new / (1.0 - BETA_SECOND**STEP)
    master = weights - step_rate * (
        moment_hat / (jnp.sqrt(second_hat) + ADAM_EPSILON) + decay_rate * weights
    )
    return (moment_new, second_new, master)


def placed(total_length, piece, start):
    return lax.dynamic_update_slice_in_dim(jnp.zeros((total_length,), jnp.float32), piece, start, 0)


def column_sum(values):
    return jnp.sum(values.astype(jnp.float32), axis=0)


def general_body(
    tokens,
    cotangent,
    clip_lengths,
    key_mask,
    rel_buckets,
    attention_weights,
    attention_first,
    attention_second,
    feedforward_weights,
    feedforward_first,
    feedforward_second,
    small_params,
    small_first,
    small_second,
):
    gathered_attention, gathered_forward = (
        lax.all_gather(attention_weights.astype(jnp.bfloat16), "dp", axis=1, tiled=True),
        lax.all_gather(feedforward_weights.astype(jnp.bfloat16), "dp", axis=1, tiled=True),
    )
    query_weight = gathered_attention[0]
    key_weight = gathered_attention[1]
    value_weight = gathered_attention[2]
    output_weight = gathered_attention[3]
    up_weight = gathered_forward[0]
    down_weight = gathered_forward[1]
    head_cols = query_weight.shape[1]
    heads_local = head_cols // HD
    hidden_local = up_weight.shape[1]
    tensor_rank = lax.axis_index("tensor")
    col_start = tensor_rank * head_cols
    head_start = tensor_rank * heads_local
    hidden_start = tensor_rank * hidden_local
    row_count = tokens.shape[0]
    bucket_count = row_count // BUCKET_SLOTS
    (
        gain_one,
        shift_one,
        gain_two,
        shift_two,
        bias_query,
        bias_value,
        bias_output,
        bias_down,
        bias_up,
        rel_table,
        gate_matrix,
        gate_offset,
        gate_scale,
    ) = split_small(small_params)
    local_bias_query = lax.dynamic_slice_in_dim(bias_query, col_start, head_cols)
    local_bias_value = lax.dynamic_slice_in_dim(bias_value, col_start, head_cols)
    local_bias_up = lax.dynamic_slice_in_dim(bias_up, hidden_start, hidden_local)
    scale_local = lax.dynamic_slice_in_dim(gate_scale, head_start, heads_local)
    table_local = lax.dynamic_slice_in_dim(rel_table.reshape(NB, H), head_start, heads_local, 1)
    allowed = jax.vmap(allowed_mask)(clip_lengths, key_mask.reshape(bucket_count, BUCKET_SLOTS))[
        :, None
    ]
    leading = (tensor_rank == 0).astype(jnp.float32)
    inputs = tokens.astype(jnp.float32)
    upstream = cotangent.astype(jnp.float32)
    query_bf = (
        jnp.dot(tokens, query_weight, preferred_element_type=jnp.float32) + local_bias_query
    ).astype(jnp.bfloat16)
    key_bf = jnp.dot(tokens, key_weight, preferred_element_type=jnp.float32).astype(jnp.bfloat16)
    value_bf = (
        jnp.dot(tokens, value_weight, preferred_element_type=jnp.float32) + local_bias_value
    ).astype(jnp.bfloat16)
    head_shape = (bucket_count, BUCKET_SLOTS, heads_local, HD)
    heads_of_query = query_bf.reshape(head_shape)
    heads_of_key = key_bf.reshape(head_shape)
    heads_of_value = value_bf.reshape(head_shape)
    head_inputs = lax.dynamic_slice_in_dim(inputs, col_start, head_cols, 1).reshape(head_shape)
    extra, pull_position = jax.vjp(
        partial(position_terms, rel_buckets=rel_buckets),
        head_inputs,
        gate_matrix,
        gate_offset,
        scale_local,
        table_local,
    )
    attention_logits = (
        jnp.einsum(
            "blhd,bmhd->bhlm", heads_of_query, heads_of_key, preferred_element_type=jnp.float32
        )
        * 0.125
    )
    scores = jnp.where(allowed, attention_logits + extra, MASK_VALUE)
    row_max = jnp.max(scores, axis=-1, keepdims=True)
    exponent = jnp.exp(scores - row_max)
    denominator = jnp.sum(exponent, axis=-1, keepdims=True)
    log_total = row_max + jnp.log(denominator)
    probs_bf = (exponent / denominator).astype(jnp.bfloat16)
    context_bf = (
        jnp.einsum("bhlm,bmhd->blhd", probs_bf, heads_of_value, preferred_element_type=jnp.float32)
        .reshape(row_count, head_cols)
        .astype(jnp.bfloat16)
    )
    attention_part = jnp.einsum(
        "nw,dw->nd", context_bf, output_weight, preferred_element_type=jnp.float32
    )
    attention = lax.psum(attention_part, "tensor") + bias_output
    normed, pull_norm_one = jax.vjp(
        layer_norm, DEEP_ALPHA * inputs + attention, gain_one, shift_one
    )
    normed_bf = normed.astype(jnp.bfloat16)
    up_pre = jnp.dot(normed_bf, up_weight, preferred_element_type=jnp.float32) + local_bias_up
    activated, pull_gelu = jax.vjp(gelu_exact, up_pre)
    activated_bf = activated.astype(jnp.bfloat16)
    down_part = jnp.einsum(
        "nf,df->nd", activated_bf, down_weight, preferred_element_type=jnp.float32
    )
    feedforward = lax.psum(down_part, "tensor") + bias_down
    output_values, pull_norm_two = jax.vjp(
        layer_norm, DEEP_ALPHA * normed + feedforward, gain_two, shift_two
    )
    block_output = output_values.astype(jnp.bfloat16)
    grad_res_two, grad_gain_two, grad_shift_two = pull_norm_two(upstream)
    grad_ffn_share = grad_res_two.astype(jnp.bfloat16)
    grad_bias_down = column_sum(grad_ffn_share)
    down_grad = jnp.einsum(
        "nd,nf->df", grad_ffn_share, activated_bf, preferred_element_type=jnp.float32
    )
    grad_activated = jnp.einsum(
        "nd,df->nf", grad_ffn_share, down_weight, preferred_element_type=jnp.float32
    )
    (grad_up_pre,) = pull_gelu(grad_activated)
    grad_up_bf = grad_up_pre.astype(jnp.bfloat16)
    grad_bias_up = column_sum(grad_up_bf)
    up_grad = jnp.einsum("nd,nf->df", normed_bf, grad_up_bf, preferred_element_type=jnp.float32)
    normed_part = jnp.einsum("nf,df->nd", grad_up_bf, up_weight, preferred_element_type=jnp.float32)
    normed_sum = lax.psum(normed_part, "tensor")
    grad_normed = normed_sum + DEEP_ALPHA * grad_res_two
    grad_res_one, grad_gain_one, grad_shift_one = pull_norm_one(grad_normed)
    grad_attention_share = grad_res_one.astype(jnp.bfloat16)
    grad_bias_output = column_sum(grad_attention_share)
    output_grad = jnp.einsum(
        "nd,nw->dw", grad_attention_share, context_bf, preferred_element_type=jnp.float32
    )
    grad_context_bf = jnp.einsum(
        "nd,dw->nw", grad_attention_share, output_weight, preferred_element_type=jnp.float32
    ).astype(jnp.bfloat16)
    grad_heads = grad_context_bf.reshape(head_shape)
    attention_probabilities = jnp.exp(scores - log_total)
    recomputed_bf = attention_probabilities.astype(jnp.bfloat16)
    grad_probs = jnp.einsum(
        "blhd,bmhd->bhlm", grad_heads, heads_of_value, preferred_element_type=jnp.float32
    )
    inner = jnp.sum(grad_probs * attention_probabilities, axis=-1, keepdims=True)
    grad_scores_bf = (attention_probabilities * (grad_probs - inner)).astype(jnp.bfloat16)
    grad_query = (
        (
            jnp.einsum(
                "bhlm,bmhd->blhd", grad_scores_bf, heads_of_key, preferred_element_type=jnp.float32
            )
            * 0.125
        )
        .astype(jnp.bfloat16)
        .reshape(row_count, head_cols)
    )
    grad_key = (
        (
            jnp.einsum(
                "bhlm,blhd->bmhd",
                grad_scores_bf,
                heads_of_query,
                preferred_element_type=jnp.float32,
            )
            * 0.125
        )
        .astype(jnp.bfloat16)
        .reshape(row_count, head_cols)
    )
    grad_value = (
        jnp.einsum("bhlm,blhd->bmhd", recomputed_bf, grad_heads, preferred_element_type=jnp.float32)
        .astype(jnp.bfloat16)
        .reshape(row_count, head_cols)
    )
    grad_head_inputs, grad_gate_matrix, grad_gate_offset, grad_scale_local, grad_table_local = (
        pull_position(grad_scores_bf.astype(jnp.float32))
    )
    query_grad = jnp.einsum("nd,nw->dw", tokens, grad_query, preferred_element_type=jnp.float32)
    key_grad = jnp.einsum("nd,nw->dw", tokens, grad_key, preferred_element_type=jnp.float32)
    value_grad = jnp.einsum("nd,nw->dw", tokens, grad_value, preferred_element_type=jnp.float32)
    input_part = (
        jnp.einsum("nw,dw->nd", grad_query, query_weight, preferred_element_type=jnp.float32)
        + jnp.einsum("nw,dw->nd", grad_key, key_weight, preferred_element_type=jnp.float32)
        + jnp.einsum("nw,dw->nd", grad_value, value_weight, preferred_element_type=jnp.float32)
    )
    own_columns = lax.dynamic_slice_in_dim(input_part, col_start, head_cols, 1)
    input_part = lax.dynamic_update_slice_in_dim(
        input_part, own_columns + grad_head_inputs.reshape(row_count, head_cols), col_start, 1
    )
    grad_inputs = lax.psum(input_part, "tensor") + DEEP_ALPHA * grad_res_one
    tokens_grad = grad_inputs.astype(jnp.bfloat16)
    table_grad = lax.dynamic_update_slice_in_dim(
        jnp.zeros((NB, H), jnp.float32), grad_table_local, head_start, 1
    ).reshape(-1)
    local_small = jnp.concatenate(
        [
            grad_gain_one * leading,
            grad_shift_one * leading,
            grad_gain_two * leading,
            grad_shift_two * leading,
            placed(MODEL_WIDTH, column_sum(grad_query), col_start),
            placed(MODEL_WIDTH, column_sum(grad_value), col_start),
            grad_bias_output * leading,
            grad_bias_down * leading,
            placed(FF, grad_bias_up, hidden_start),
            table_grad,
            grad_gate_matrix,
            grad_gate_offset,
            placed(H, grad_scale_local, head_start),
        ]
    )
    small_grad = lax.psum(local_small, ("dp", "tensor"))
    local_attention = jnp.stack([query_grad, key_grad, value_grad, output_grad])
    local_forward = jnp.stack([up_grad, down_grad])
    summed_attention, summed_forward = lax.psum((local_attention, local_forward), "dp")
    owner_rank = lax.axis_index("dp")
    owned_rows = attention_weights.shape[1]
    share_attention = lax.dynamic_slice_in_dim(
        summed_attention, owner_rank * owned_rows, owned_rows, 1
    )
    share_forward = lax.dynamic_slice_in_dim(summed_forward, owner_rank * owned_rows, owned_rows, 1)
    share_squares = jnp.sum(share_attention * share_attention) + jnp.sum(
        share_forward * share_forward
    )
    big_squares = lax.psum(share_squares, ("dp", "tensor"))
    global_norm = jnp.sqrt(big_squares + jnp.sum(small_grad * small_grad))
    factor = CLIP_LIMIT / jnp.maximum(global_norm, CLIP_LIMIT)
    attention_moment, attention_square, attention_master = adam_step(
        attention_weights,
        attention_first,
        attention_second,
        factor * share_attention,
        RATE_MATRIX,
        WEIGHT_DECAY,
    )
    feedforward_moment, feedforward_square, feedforward_master = adam_step(
        feedforward_weights,
        feedforward_first,
        feedforward_second,
        factor * share_forward,
        RATE_MATRIX,
        WEIGHT_DECAY,
    )
    small_moment, small_square, small_master = adam_step(
        small_params, small_first, small_second, factor * small_grad, RATE_SMALL, 0.0
    )
    return (
        global_norm,
        attention_moment,
        attention_square,
        attention_master,
        attention_master.astype(jnp.bfloat16),
        feedforward_moment,
        feedforward_square,
        feedforward_master,
        feedforward_master.astype(jnp.bfloat16),
        small_moment,
        small_square,
        small_master,
        block_output,
        tokens_grad,
    )


F32 = jnp.float32
BF16 = jnp.bfloat16
MESH_ID = pl.DeviceIdType.MESH
LANES = 128
SMALL_ROWS = 104
QUARTER = 32
SUM_ROWS = 4 * QUARTER
TABLE_ROW = 72
GATE_ROW = 102
OFFSET_ROW = 103
INV_SQRT2 = 0.5**0.5
INV_SQRT_2PI = 0.3989422804014327
CHUNK = 128
HALF = 256
W = MODEL_WIDTH
NT = (((1,), (1,)), ((), ()))
TN = (((0,), (0,)), ((), ()))


def mm(a, b):
    return jnp.dot(a, b, preferred_element_type=F32)


def mm_nt(a, b):
    return lax.dot_general(a, b, NT, preferred_element_type=F32)


def mm_tn(a, b):
    return lax.dot_general(a, b, TN, preferred_element_type=F32)


def exact_nt(a, b):
    return lax.dot_general(a, b, NT, precision=FULL_PRECISION, preferred_element_type=F32)


def exact_tn(a, b):
    return lax.dot_general(a, b, TN, precision=FULL_PRECISION, preferred_element_type=F32)


def exact_mm(a, b):
    return jnp.dot(a, b, precision=FULL_PRECISION, preferred_element_type=F32)


def iota(shape, axis):
    return lax.broadcasted_iota(jnp.int32, shape, axis)


def layer_scratch(owned, nz, qkv_pad, heads, head_cols, hidden):
    rows = 2 * BUCKET_SLOTS
    dma = pltpu.SemaphoreType.DMA
    vm = pltpu.VMEM
    shapes = dict(
        wa=vm((4, owned, head_cols), F32),
        wf=vm((2, owned, hidden), F32),
        keep=vm((rows // LANES, LANES), jnp.int32),
        small=vm((3 * SMALL_ROWS + 2 * BUCKET_SLOTS // LANES, LANES), F32),
        shqkv=vm((owned, qkv_pad), F32),
        sho=vm((owned, LANES), F32),
        shup=vm((owned, hidden), F32),
        shdown=vm((owned, hidden), F32),
        smallout=vm((4, SMALL_ROWS, LANES), F32),
        tok=vm((rows, W), BF16),
        cot=vm((2, HALF, W), BF16),
        wqkv=vm((W, qkv_pad), BF16),
        wo1=vm((W, LANES), BF16),
        wo=vm((W, head_cols), BF16),
        wot=vm((head_cols, W), BF16),
        wqkvt=vm((qkv_pad + LANES, W), BF16),
        wupt=vm((hidden, W), BF16),
        wdownt=vm((hidden, W), BF16),
        go=vm((W, LANES), BF16),
        glin=vm((W, LANES), F32),
        wup=vm((W, hidden), BF16),
        wdown=vm((W, hidden), BF16),
        q=vm((rows, head_cols), BF16),
        k=vm((rows, head_cols), BF16),
        v=vm((rows, head_cols), BF16),
        kt=vm((head_cols, rows), BF16),
        qt=vm((head_cols, rows), BF16),
        dctxt=vm((head_cols, BUCKET_SLOTS), BF16),
        vt=vm((head_cols, rows), BF16),
        ctx=vm((rows, head_cols), BF16),
        dqkv=vm((rows, qkv_pad + LANES), BF16),
        prob=vm((2 * heads, BUCKET_SLOTS, BUCKET_SLOTS), F32),
        gsb=vm((heads * BUCKET_SLOTS, BUCKET_SLOTS), BF16),
        dqf=vm((BUCKET_SLOTS, head_cols), F32),
        mbias=vm((2, BUCKET_SLOTS, BUCKET_SLOTS), BF16),
        band=vm((heads, LANES, 2 * BUCKET_SLOTS), F32),
        dband=vm((heads, LANES, 2 * BUCKET_SLOTS), F32),
        gate=vm((rows, LANES), F32),
        gu=vm((rows, LANES), F32),
        gmat=vm((W, LANES), F32),
        vecs=vm((16, W), F32),
        acc=vm((16, W), F32),
        nb=vm((rows, W), BF16),
        held=vm((2, HALF, W), F32),
        xh1=vm((2, HALF, W), F32),
        rstd1=vm((2, HALF, LANES), F32),
        act=vm((rows, hidden), BF16),
        gelup=vm((rows, hidden), F32),
        gffn=vm((rows, W), BF16),
        gub=vm((rows, hidden), BF16),
        gattn=vm((rows, W), BF16),
        stage=vm((2, HALF, W), BF16),
        ownf=vm((HALF, W), F32),
        cs=vm((2, HALF, W), BF16),
        cr=vm((2, HALF, W), BF16),
        ys=vm((2, HALF, W), BF16),
        yr=vm((2, 2, HALF, W), BF16),
        xrqkv=vm((nz, owned, qkv_pad), BF16),
        xro=vm((nz, owned, LANES), BF16),
        xrup=vm((nz, owned, hidden), BF16),
        xrdown=vm((nz, owned, hidden // 2), BF16),
        xrdownb=vm((nz, owned, hidden // 2), BF16),
        zsqkv=vm((nz - 1, owned, qkv_pad), BF16),
        zso=vm((nz - 1, owned, LANES), BF16),
        zsup=vm((nz - 1, owned, hidden), BF16),
        zsdown=vm((nz - 1, owned, hidden // 2), BF16),
        zsdownb=vm((nz - 1, owned, hidden // 2), BF16),
        zrqkv=vm((nz - 1, owned, qkv_pad), BF16),
        zro=vm((nz - 1, owned, LANES), BF16),
        zrup=vm((nz - 1, owned, hidden), BF16),
        zrdown=vm((nz - 1, owned, hidden // 2), BF16),
        zrdownb=vm((nz - 1, owned, hidden // 2), BF16),
        sm=vm((SUM_ROWS, LANES), F32),
        smc=vm((2, QUARTER, LANES), F32),
        smh=vm((2, QUARTER, LANES), F32),
        smy=vm((QUARTER, LANES), F32),
        smv=vm((QUARTER, LANES), F32),
        smx=vm((QUARTER, LANES), F32),
        smz=vm((nz, QUARTER, LANES), F32),
        sma=vm((SUM_ROWS, LANES), F32),
        sqt=vm((4, 8, LANES), F32),
        sqd=vm((2 * nz, 8, LANES), F32),
        s_in=dma((7,)),
        s_out=dma((5,)),
        s_gs=dma((8,)),
        s_gr=dma((8,)),
        s_ls=dma((8, 2, nz)),
        s_lr=dma((8, 2, nz)),
        s_lxs=dma((8, 2, nz)),
        s_lxr=dma((8, 2, nz)),
        s_cs=dma((4, 2, 2)),
        s_cr=dma((4, 2, 2)),
        s_ys=dma((4, 2, 2)),
        s_yr=dma((4, 2, 2)),
        s_as=dma((3, 2, 2)),
        s_ar=dma((3, 2, 2)),
        s_ol=dma((2, 2)),
        s_os=dma((2, 2)),
        s_or=dma((2, 2)),
        s_xs=dma((5, nz)),
        s_xr=dma((5, nz)),
        s_zs=dma((5, nz)),
        s_zr=dma((5, nz)),
        s_ms=dma((6 + nz,)),
        s_mr=dma((6 + nz,)),
        s_ts=dma((4,)),
        s_tr=dma((4,)),
        s_ds=dma((2 * nz,)),
        s_dr=dma((2 * nz,)),
    )
    return shapes


def layer_kernel(names, dims, *refs):
    n_dp, owned, qkv_pad, heads, head_cols, hidden = dims
    nz = n_dp // 2
    (tok_in, cot_in, lens, keep_in, wa_in, wf_in, small_in) = refs[:7]
    (bo_out, tg_out, out_qkv, out_o, out_up, out_down, out_small, norm_out) = refs[7:15]
    m = SimpleNamespace(**dict(zip(names, refs[15:], strict=True)))
    D = lax.axis_index("dp")
    T = lax.axis_index("tensor")
    z = lax.div(D, 2)
    x = lax.rem(D, 2)
    c = lax.rem(T, 2)
    yy = lax.div(T, 2)
    core_dev = (D, T + 1 - 2 * c)
    y_dev = (D, lax.rem(T + 2, 4))
    x_dev = (z * 2 + 1 - x, T)

    def z_at(k):
        total, bit = 0, 1
        while bit < nz:
            here = lax.rem(lax.div(z, bit), 2)
            total = total + bit * (1 - here if k & bit else here)
            bit *= 2
        return total

    def z_dev(k):
        return (z_at(k) * 2 + x, T)

    def remote(src, dst, ss, rs, dev):
        return pltpu.make_async_remote_copy(
            src_ref=src, dst_ref=dst, send_sem=ss, recv_sem=rs, device_id=dev, device_id_type=MESH_ID
        )

    def loop(n, step):
        def run(i, carry):
            step(i)
            return carry

        lax.fori_loop(0, n, run, 0)

    def block(owner):
        return pl.ds(pl.multiple_of(owner * owned, owned), owned)

    wa, wf, keep, small = m.wa, m.wf, m.keep, m.small
    sh_qkv, sh_o, sh_up, sh_down, small_out = m.shqkv, m.sho, m.shup, m.shdown, m.smallout
    first_loads = []
    for i, (source, target) in enumerate(((wa_in, wa), (wf_in, wf), (small_in, small), (keep_in, keep))):
        cp = pltpu.make_async_copy(source, target, m.s_in.at[3 + i])
        cp.start()
        first_loads.append(cp)
    tok_copy = pltpu.make_async_copy(tok_in, m.tok, m.s_in.at[0])
    tok_copy.start()
    cot_copies = []
    for b in range(2):
        rows = pl.ds(pl.multiple_of(b * BUCKET_SLOTS + c * HALF, HALF), HALF)
        cp = pltpu.make_async_copy(cot_in.at[rows], m.cot.at[b], m.s_in.at[1 + b])
        cp.start()
        cot_copies.append(cp)
    barrier = pltpu.get_barrier_semaphore()
    for k in range(1, 4):
        pl.semaphore_signal(barrier, inc=1, device_id=(D, lax.rem(T + k, 4)), device_id_type=MESH_ID)
    for k in range(1, n_dp):
        pl.semaphore_signal(barrier, inc=1, device_id=(lax.rem(D + k, n_dp), T), device_id_type=MESH_ID)
    for cp in first_loads:
        cp.wait()
    mine = block(D)
    first_o = qkv_pad - 3 * head_cols
    m.wqkv[mine, :] = jnp.concatenate([wa[0], wa[1], wa[2], wa[3, :, 0:first_o]], axis=1).astype(BF16)
    m.wo1[mine, :] = wa[3, :, first_o:head_cols].astype(BF16)
    m.wup[mine, :] = wf[0].astype(BF16)
    m.wdown[mine, :] = wf[1].astype(BF16)
    pl.semaphore_wait(barrier, 3 + n_dp - 1)

    part_rows = owned // 2 if owned % 32 == 0 else owned
    halves = lambda buf: [(buf, 0, part_rows), (buf, owned - part_rows, part_rows)]
    pieces = halves(m.wqkv) + [(m.wo1, 0, owned)] + halves(m.wup) + halves(m.wdown)

    pieces.append(pieces[-1])
    across = len(pieces) - 1
    straight = (across - 1, across)

    def piece(which, owner_z, other_column=False):
        buf, first, count = pieces[which]
        column = 1 - x if other_column != (which == across) else x
        return buf.at[pl.ds(pl.multiple_of((owner_z * 2 + column) * owned + first, 16), count)]

    gathers = {}

    def launch(record, where):
        remote(*where()).start()
        record.append(where)

    def when(condition, action):
        pl.when(condition)(action)

    def from_z(way, step):
        owner_z = z - step if way == 0 else z + step
        return owner_z, (owner_z >= 0) if way == 0 else (owner_z < nz)

    def send_when(which, condition, where):
        when(condition(), lambda: remote(*where()).start())
        gathers.setdefault(which, []).append((condition, where))

    def line_send(which, way, step, hops):
        origin = step - hops

        def where():
            part = piece(which, from_z(way, origin)[0])
            target = ((z + hops if way == 0 else z - hops) * 2 + x, T)
            return part, part, m.s_ls.at[which, way, step], m.s_lr.at[which, way, step], target

        def condition():
            there = (z + hops < nz) if way == 0 else (z >= hops)
            return there & from_z(way, origin)[1]

        send_when(which, condition, where)

    def line_start(which, hops):
        for hop in range(1, hops + 1):
            for way in range(2):
                line_send(which, way, hop, hop)

    def gather_x(which):
        def where():
            own = piece(which, z)
            return own, own, m.s_gs.at[which], m.s_gr.at[which], x_dev

        send_when(which, lambda: D >= 0, where)

    def line_step(which, step, hops):
        for way in range(2):

            def landed(way=way):
                part = piece(which, from_z(way, step)[0])
                sems = m.s_ls.at[which, way, step], m.s_lr.at[which, way, step]
                remote(part, part, *sems, x_dev).wait_recv()

            when(from_z(way, step)[1], landed)
            if step >= hops and step + 1 < nz:
                line_send(which, way, step + 1, 1)
            if which in straight:
                continue

            def where(way=way):
                part = piece(which, from_z(way, step)[0])
                return part, part, m.s_lxs.at[which, way, step], m.s_lxr.at[which, way, step], x_dev

            send_when(which, lambda way=way: from_z(way, step)[1], where)

    def partner_landed(which):
        part = piece(which, z, True)
        remote(part, part, m.s_gs.at[which], m.s_gr.at[which], x_dev).wait_recv()

    def line_end(which):
        partner_landed(which)
        for step in range(1, nz):
            for way in range(2):

                def landed(way=way):
                    part = piece(which, from_z(way, step)[0], True)
                    sems = m.s_lxs.at[which, way, step], m.s_lxr.at[which, way, step]
                    remote(part, part, *sems, x_dev).wait_recv()

                when(from_z(way, step)[1], landed)

    def sent_all(which):
        for condition, where in gathers.pop(which):
            when(condition(), lambda where=where: remote(*where()).wait_send())

    def turn(source, target):
        count = source.shape[1]
        if count % LANES:
            target[...] = source[...].T
            return
        step = HALF if count % HALF == 0 else LANES

        def chunk(i):
            at = pl.ds(pl.multiple_of(i * step, step), step)
            target[at, :] = source[:, at].T

        loop(count // step, chunk)

    for which in (0, 1):
        line_start(which, 1)
    for which in (0, 1):
        gather_x(which)
    gather_x(across - 1)

    def small_row(first, count):
        return jnp.concatenate([small[first + i : first + i + 1, :] for i in range(count)], axis=1)

    def pick(values, size):
        total = jnp.zeros((1, size), F32)
        for t in range(4):
            total = total + jnp.where(T == t, values[:, t * size : (t + 1) * size], 0.0)
        return total

    vecs = m.vecs
    vecs[...] = jnp.zeros_like(vecs)
    m.acc[...] = jnp.zeros((16, W), F32)
    for at, first in ((0, 0), (1, 6), (2, 12), (3, 18), (4, 36), (5, 42)):
        vecs[at : at + 1, :] = small_row(first, W // LANES)
    vecs[6:7, :] = pick(small_row(48, FF // LANES), hidden)
    bq = pick(small_row(24, W // LANES), head_cols)
    bv = pick(small_row(30, W // LANES), head_cols)
    bias_qkv = jnp.concatenate(
        [bq, jnp.zeros_like(bq), bv, jnp.zeros((1, qkv_pad - 3 * head_cols), F32)], axis=1
    )
    vecs[7:8, 0:qkv_pad] = bias_qkv

    lane = iota((1, LANES), 1)
    col = iota((W, LANES), 0)
    col_lane = iota((W, LANES), 1)
    gate_row = small[GATE_ROW : GATE_ROW + 1, :]
    col_in_head = lax.rem(col, HD)
    picked_u = jnp.sum(
        jnp.where(col_lane == 2 * col_in_head, gate_row, 0.0), axis=1, keepdims=True
    )
    picked_w = jnp.sum(
        jnp.where(col_lane == 2 * col_in_head + 1, gate_row, 0.0), axis=1, keepdims=True
    )
    in_group = lax.rem(col_lane, 8)
    own_head = (col_lane < 16) & (in_group < heads) & (lax.div(col, HD) == T * heads + in_group)
    m.gmat[...] = jnp.where(own_head, jnp.where(col_lane < 8, picked_u, picked_w), 0.0)
    offset_row = small[OFFSET_ROW : OFFSET_ROW + 1, :]
    offset_u = jnp.sum(jnp.where(lane == 0, offset_row, 0.0), axis=1, keepdims=True)
    offset_w = jnp.sum(jnp.where(lane == 1, offset_row, 0.0), axis=1, keepdims=True)
    scale = jnp.zeros((1, LANES), F32)
    for h in range(heads):
        one = jnp.sum(jnp.where(lane == 2 + T * heads + h, offset_row, 0.0), axis=1, keepdims=True)
        scale = scale + jnp.where(lane == h, one, 0.0)
    head_lane = lane < heads

    line_step(0, 1, 1)
    line_step(1, 1, 1)

    offsets = small_row(3 * SMALL_ROWS, 2 * BUCKET_SLOTS // LANES).astype(jnp.int32)
    table = small[TABLE_ROW : TABLE_ROW + 32, :]
    long_row = 2 * BUCKET_SLOTS
    sub8 = iota((8, long_row), 0)
    for h in range(heads):
        flat = offsets * H + (T * heads + h)
        at_row = lax.div(flat, LANES)
        at_lane = lax.rem(flat, LANES)
        hot_row = jnp.where(iota((32, long_row), 0) == at_row, 1.0, 0.0)
        spread = exact_tn(table, hot_row)
        values = jnp.sum(
            jnp.where(iota((LANES, long_row), 0) == at_lane, spread, 0.0), axis=0, keepdims=True
        )
        stack = jnp.broadcast_to(pltpu.roll(jnp.broadcast_to(values, (8, long_row)), 1, 1), (8, long_row))
        for bit in (1, 2, 4):
            stack = jnp.where(lax.rem(lax.div(sub8, bit), 2) == 1, pltpu.roll(stack, bit, 1), stack)
        size = 8
        m.band[h, 0:8, :] = stack
        while size < LANES:
            m.band[h, size : 2 * size, :] = pltpu.roll(m.band[h, 0:size, :], size, 1)
            size *= 2
    m.dband[...] = jnp.zeros(m.dband.shape, F32)

    line_step(0, 2, 1)
    line_step(1, 2, 1)

    for b in range(2):
        end = 0
        ends = []
        for i in range(CLIPS):
            end = end + lens[b, i]
            ends.append(end)
        key_at = iota((1, BUCKET_SLOTS), 1)
        key_segment = jnp.zeros((1, BUCKET_SLOTS), jnp.int32)
        for end in ends:
            key_segment = key_segment + jnp.where(key_at >= end, 1, 0)
        kept = jnp.concatenate([keep[4 * b + i : 4 * b + i + 1, :] for i in range(4)], axis=1)
        live = jnp.where((kept == 1) & (key_segment < CLIPS), key_segment, -1)

        def mask_chunk(i, b=b, ends=ends, live=live):
            query_at = iota((CHUNK, BUCKET_SLOTS), 0) + i * CHUNK
            segment = jnp.zeros((CHUNK, BUCKET_SLOTS), jnp.int32)
            for end in ends:
                segment = segment + jnp.where(query_at >= end, 1, 0)
            allowed = (segment == live) | (query_at == iota((CHUNK, BUCKET_SLOTS), 1))
            m.mbias[b, pl.ds(pl.multiple_of(i * CHUNK, CHUNK), CHUNK), :] = jnp.where(
                allowed, 0.0, MASK_VALUE
            ).astype(BF16)

        loop(BUCKET_SLOTS // CHUNK, mask_chunk)

    for step in range(3, nz):
        line_step(0, step, 1)
        line_step(1, step, 1)
    line_start(2, 2)

    tok_copy.wait()
    gmat = m.gmat[...]
    part_hi = gmat.astype(BF16)
    rest = gmat - part_hi.astype(F32)
    part_mid = rest.astype(BF16)
    part_lo = (rest - part_mid.astype(F32)).astype(BF16)
    gate_parts = (part_hi, part_hi, part_hi, part_mid, part_mid, part_lo)
    stacked = jnp.zeros((W, LANES), F32)
    for i, part in enumerate(gate_parts):
        moved = part.astype(F32)
        stacked = stacked + (pltpu.roll(moved, 16 * i, 1) if i else moved)
    m.wqkvt[qkv_pad : qkv_pad + LANES, :] = stacked.astype(BF16).T

    def gate_chunk(i):
        rows = pl.ds(pl.multiple_of(i * HALF, HALF), HALF)
        tokens = m.tok[rows, :]
        linear = mm(tokens, part_hi) + mm(tokens, part_mid) + mm(tokens, part_lo)
        both = jax.nn.sigmoid(linear + jnp.where(lane < 8, offset_u, offset_w))
        m.gu[rows, :] = both
        m.gate[rows, :] = both * (pltpu.roll(both, LANES - 8, 1) * scale - 1.0) + 2.0

    loop(4, gate_chunk)

    line_start(3, 2)
    line_end(0)
    line_end(1)
    gather_x(2)
    line_step(2, 1, 2)
    line_step(2, 2, 2)
    gather_x(3)

    def project(i):
        rows = pl.ds(pl.multiple_of(i * HALF, HALF), HALF)
        both = mm(m.tok[rows, :], m.wqkv[...]) + vecs[7:8, 0:qkv_pad]
        query = (both[:, 0:head_cols].astype(BF16).astype(F32) * 0.125).astype(BF16)
        m.q[rows, :] = query
        m.qt[:, rows] = query.T
        key = both[:, head_cols : 2 * head_cols].astype(BF16)
        value = both[:, 2 * head_cols : 3 * head_cols].astype(BF16)
        m.k[rows, :] = key
        m.v[rows, :] = value
        m.kt[:, rows] = key.T
        m.vt[:, rows] = value.T

    loop(4, project)

    head_of = lax.div(iota((1, head_cols), 1), HD)
    head_masks = [jnp.where(head_of == h, 1.0, 0.0) for h in range(heads)]
    low_masks = [m.astype(BF16) for m in head_masks]

    def hooked(first, count, chunk, hooks):
        def step_of(i):
            step = i + first
            chunk(step)
            for at, action in hooks.items():
                if first <= at < first + count:
                    when(step == at, action)

        loop(count, step_of)

    def by_head(stacked):
        total = stacked[0:CHUNK, :] * head_masks[0]
        for h in range(1, heads):
            total = total + stacked[h * CHUNK : (h + 1) * CHUNK, :] * head_masks[h]
        return total

    def attend(b, hooks):
        keys = m.kt[:, b * BUCKET_SLOTS : (b + 1) * BUCKET_SLOTS]
        values = m.v[b * BUCKET_SLOTS : (b + 1) * BUCKET_SLOTS, :]

        def chunk(i):
            local = pl.ds(pl.multiple_of(i * CHUNK, CHUNK), CHUNK)
            rows = pl.ds(pl.multiple_of(b * BUCKET_SLOTS + i * CHUNK, CHUNK), CHUNK)
            window = pl.ds(pl.multiple_of(BUCKET_SLOTS - i * CHUNK, CHUNK), BUCKET_SLOTS)
            query = m.q[rows, :]
            gates = m.gate[rows, :]
            all_scores = mm(jnp.concatenate([query * mask for mask in low_masks], axis=0), keys)
            all_probs = []
            for h in range(heads):
                scores = all_scores[h * CHUNK : (h + 1) * CHUNK, :]
                scores = scores + gates[:, h : h + 1] * m.band[h, :, window]
                scores = scores + m.mbias[b, local, :].astype(F32)
                top = jnp.max(scores, axis=1, keepdims=True)
                weight = jnp.exp(scores - top)
                total = jnp.sum(weight, axis=1, keepdims=True)
                probability = weight * (1.0 / total)
                m.prob[b * heads + h, local, :] = probability
                all_probs.append(probability.astype(BF16))
            m.ctx[rows, :] = by_head(mm(jnp.concatenate(all_probs, axis=0), values)).astype(BF16)

        hooked(0, BUCKET_SLOTS // CHUNK, chunk, hooks)

    core_sent = {}
    y_sent = {}

    def exchange(phase, b, product):
        exchange_first(phase, b, product)
        exchange_last(phase, b)

    def exchange_first(phase, b, product):
        other = b * BUCKET_SLOTS + (1 - c) * HALF
        own = b * BUCKET_SLOTS + c * HALF
        for cp in core_sent.get((phase - 1, b), []) + y_sent.get((phase - 1, b), []):
            cp.wait_send()
        for i in range(2):
            at = slice(i * CHUNK, (i + 1) * CHUNK)
            rows = pl.ds(pl.multiple_of(other + i * CHUNK, CHUNK), CHUNK)
            m.cs[b, at, :] = product(rows).astype(BF16)
            cp = remote(
                m.cs.at[b, at], m.cr.at[b, at], m.s_cs.at[phase, b, i], m.s_cr.at[phase, b, i], core_dev
            )
            cp.start()
            core_sent.setdefault((phase, b), []).append(cp)
        for i in range(2):
            at = slice(i * CHUNK, (i + 1) * CHUNK)
            rows = pl.ds(pl.multiple_of(own + i * CHUNK, CHUNK), CHUNK)
            m.ownf[at, :] = product(rows)

    def exchange_last(phase, b):
        for i in range(2):
            at = slice(i * CHUNK, (i + 1) * CHUNK)
            core_sent[(phase, b)][i].wait_recv()
            m.ys[b, at, :] = (m.ownf[at, :] + m.cr[b, at, :].astype(F32)).astype(BF16)
            cp = remote(
                m.ys.at[b, at],
                m.yr.at[phase % 2, b, at],
                m.s_ys.at[phase, b, i],
                m.s_yr.at[phase, b, i],
                y_dev,
            )
            cp.start()
            y_sent.setdefault((phase, b), []).append(cp)

    def arrived(phase, b, at):
        return m.ys[b, at, :].astype(F32) + m.yr[phase % 2, b, at, :].astype(F32)

    def own_rows(b, i):
        return pl.ds(pl.multiple_of(b * BUCKET_SLOTS + c * HALF + i * CHUNK, CHUNK), CHUNK)

    core_spread = {}

    def spread(which, buf, b, i):
        part = buf.at[own_rows(b, i)]
        cp = remote(part, part, m.s_as.at[which, b, i], m.s_ar.at[which, b, i], core_dev)
        cp.start()
        core_spread.setdefault((which, b), []).append(cp)

    spread_done = set()

    def spread_end(which, b, i):
        if (which, b, i) not in spread_done:
            core_spread[(which, b)][i].wait_recv()
            spread_done.add((which, b, i))

    def as_it_lands(phase, b, chunk):
        for i in range(2):
            y_sent[(phase, b)][i].wait_recv()
            chunk(i)

    def row_mean(values):
        return jnp.mean(values, axis=1, keepdims=True)

    def add_row(at, values):
        m.acc[at : at + 1, 0 : values.shape[1]] += jnp.sum(values, axis=0, keepdims=True)

    def norm_one(b):

        def chunk(i):
            at = pl.ds(pl.multiple_of(i * CHUNK, CHUNK), CHUNK)
            rows = own_rows(b, i)
            residual = DEEP_ALPHA * m.tok[rows, :].astype(F32) + (arrived(0, b, at) + vecs[4:5, :])
            centred = residual - row_mean(residual)
            rstd = lax.rsqrt(row_mean(centred * centred) + NORM_EPSILON)
            hat = centred * rstd
            normed = hat * vecs[0:1, :] + vecs[1:2, :]
            m.xh1[b, at, :] = hat
            m.rstd1[b, at, :] = jnp.broadcast_to(rstd, (CHUNK, LANES))
            m.held[b, at, :] = normed
            m.nb[rows, :] = normed.astype(BF16)
            spread(0, m.nb, b, i)

        as_it_lands(0, b, chunk)

    def own_first(which, b, chunk):
        def rows_at(step):
            i = lax.rem(step + 2 * c, 4)
            return pl.ds(pl.multiple_of(b * BUCKET_SLOTS + i * CHUNK, CHUNK), CHUNK)

        loop(2, lambda step: chunk(rows_at(step)))
        for i in range(2):
            spread_end(which, b, i)
            chunk(rows_at(2 + i))

    def feed(b):
        def chunk(rows):
            up = mm(m.nb[rows, :], m.wup[...]) + vecs[6:7, :]
            half_phi = 0.5 * (1.0 + lax.erf(up * INV_SQRT2))
            m.act[rows, :] = (up * half_phi).astype(BF16)
            m.gelup[rows, :] = half_phi + up * (jnp.exp(up * up * -0.5) * INV_SQRT_2PI)

        own_first(0, b, chunk)

    out_copies = []

    def result_rows(which, b, stage, out):
        rows = pl.ds(pl.multiple_of(b * BUCKET_SLOTS + c * HALF, HALF), HALF)
        part = stage.at[b]
        here = pltpu.make_async_copy(part, out.at[rows], m.s_ol.at[which, b])
        there = remote(part, out.at[rows], m.s_os.at[which, b], m.s_or.at[which, b], core_dev)
        here.start()
        there.start()
        out_copies.append((here, there))

    def norm_two(b):
        cot_copies[b].wait()

        def chunk(i):
            at = pl.ds(pl.multiple_of(i * CHUNK, CHUNK), CHUNK)
            rows = own_rows(b, i)
            residual = DEEP_ALPHA * m.held[b, at, :] + (arrived(1, b, at) + vecs[5:6, :])
            centred = residual - row_mean(residual)
            rstd = lax.rsqrt(row_mean(centred * centred) + NORM_EPSILON)
            hat = centred * rstd
            m.stage[b, at, :] = (hat * vecs[2:3, :] + vecs[3:4, :]).astype(BF16)
            upstream = m.cot[b, at, :].astype(F32)
            add_row(2, upstream * hat)
            add_row(3, upstream)
            scaled = upstream * vecs[2:3, :]
            grad = rstd * (scaled - row_mean(scaled) - hat * row_mean(scaled * hat))
            m.held[b, at, :] = grad
            low = grad.astype(BF16)
            m.gffn[rows, :] = low
            spread(1, m.gffn, b, i)
            add_row(5, low.astype(F32))

        as_it_lands(1, b, chunk)
        result_rows(0, b, m.stage, bo_out)

    def feed_back(b):
        def chunk(rows):
            grad = mm(m.gffn[rows, :], m.wdown[...]) * m.gelup[rows, :]
            low = grad.astype(BF16)
            m.gub[rows, :] = low
            add_row(6, low.astype(F32))

        own_first(1, b, chunk)

    def norm_one_back(b):

        def chunk(i):
            at = pl.ds(pl.multiple_of(i * CHUNK, CHUNK), CHUNK)
            rows = own_rows(b, i)
            upstream = arrived(2, b, at) + DEEP_ALPHA * m.held[b, at, :]
            hat = m.xh1[b, at, :]
            add_row(0, upstream * hat)
            add_row(1, upstream)
            scaled = upstream * vecs[0:1, :]
            rstd = m.rstd1[b, at, 0:1]
            grad = rstd * (scaled - row_mean(scaled) - hat * row_mean(scaled * hat))
            m.held[b, at, :] = grad
            low = grad.astype(BF16)
            m.gattn[rows, :] = low
            spread(2, m.gattn, b, i)
            add_row(4, low.astype(F32))

        as_it_lands(2, b, chunk)

    def gate_back(rows, grad):
        u = m.gu[rows, :]
        w = pltpu.roll(u, LANES - 8, 1)
        grad_u = jnp.where(head_lane, grad * (w * scale - 1.0) * u * (1.0 - u), 0.0)
        grad_w = jnp.where(head_lane, grad * u * scale * w * (1.0 - w), 0.0)
        add_row(8, jnp.where(head_lane, grad * u * w, 0.0))
        linear = grad_u + pltpu.roll(grad_w, 8, 1)
        add_row(9, linear)
        hi = linear.astype(BF16).astype(F32)
        mid = (linear - hi).astype(BF16).astype(F32)
        lo = (linear - hi - mid).astype(BF16).astype(F32)
        stacked = hi
        for at, part in enumerate((mid, lo, hi, mid, hi)):
            stacked = stacked + pltpu.roll(part, 16 * (at + 1), 1)
        m.dqkv[rows, qkv_pad : qkv_pad + LANES] = stacked.astype(BF16)

    def attend_back(b, hooks):
        keys = m.k[b * BUCKET_SLOTS : (b + 1) * BUCKET_SLOTS, :]
        values = m.vt[:, b * BUCKET_SLOTS : (b + 1) * BUCKET_SLOTS]

        def chunk(step):
            i = lax.rem(step + 2 * c, 4)
            local = pl.ds(pl.multiple_of(i * CHUNK, CHUNK), CHUNK)
            rows = pl.ds(pl.multiple_of(b * BUCKET_SLOTS + i * CHUNK, CHUNK), CHUNK)
            window = pl.ds(pl.multiple_of(BUCKET_SLOTS - i * CHUNK, CHUNK), BUCKET_SLOTS)
            place = pl.ds(pl.multiple_of(3 * CHUNK - i * CHUNK, CHUNK), BUCKET_SLOTS)
            grad_context = mm(m.gattn[rows, :], m.wo[...]).astype(BF16)
            m.dctxt[:, local] = grad_context.T
            gates = m.gate[rows, :]
            all_grads = mm(jnp.concatenate([grad_context * mask for mask in low_masks], axis=0), values)
            all_low = []
            grad_gates = jnp.zeros((CHUNK, LANES), F32)
            for h in range(heads):
                grad_probs = all_grads[h * CHUNK : (h + 1) * CHUNK, :]
                probability = m.prob[b * heads + h, local, :]
                inner = jnp.sum(grad_probs * probability, axis=1, keepdims=True)
                low = (probability * (grad_probs - inner)).astype(BF16)
                m.gsb[pl.ds(pl.multiple_of(h * BUCKET_SLOTS + i * CHUNK, CHUNK), CHUNK), :] = low
                all_low.append(low)
                rounded = low.astype(F32)
                one = jnp.sum(rounded * m.band[h, :, window], axis=1, keepdims=True)
                grad_gates = grad_gates + jnp.where(lane == h, one, 0.0)
                m.dband[h, :, place] += rounded * gates[:, h : h + 1]
            m.dqf[local, :] = by_head(mm(jnp.concatenate(all_low, axis=0), keys)) * 0.125
            gate_back(rows, grad_gates)

        hooked(0, 2, chunk, hooks)
        spread_end(2, b, 0)
        spread_end(2, b, 1)
        hooked(2, 2, chunk, hooks)
        all_rows = slice(b * BUCKET_SLOTS, (b + 1) * BUCKET_SLOTS)
        own_rows_of = lax.div(iota((head_cols, 1), 0), HD)
        row_masks = [jnp.where(own_rows_of == h, 1.0, 0.0).astype(BF16) for h in range(heads)]
        spread_out = lambda turned: jnp.concatenate([turned * mask for mask in row_masks], axis=1)
        grad_key = mm(spread_out(m.qt[:, all_rows]), m.gsb[...]).T
        probs = m.prob[b * heads : (b + 1) * heads].reshape(heads * BUCKET_SLOTS, BUCKET_SLOTS)
        grad_value = mm(spread_out(m.dctxt[...]), probs.astype(BF16)).T
        pad = jnp.zeros((BUCKET_SLOTS, qkv_pad - 3 * head_cols), F32)
        low = jnp.concatenate([m.dqf[...], grad_key, grad_value, pad], axis=1).astype(BF16)
        m.dqkv[all_rows, 0:qkv_pad] = low
        add_row(7, low.astype(F32))

    def input_part(rows):
        return mm(m.dqkv[rows, :], m.wqkvt[...])

    def token_rows(b):
        for cp in out_copies[b]:
            cp.wait()

        def chunk(i):
            at = pl.ds(pl.multiple_of(i * CHUNK, CHUNK), CHUNK)
            total = arrived(3, b, at) + DEEP_ALPHA * m.held[b, at, :]
            m.stage[b, at, :] = total.astype(BF16)

        as_it_lands(3, b, chunk)
        result_rows(1, b, m.stage, tg_out)

    def weight_grad(sent, left, right, put_part, rows=slice(None)):
        for which in sent:
            sent_all(which)

        def chunk(i):
            cols = pl.ds(pl.multiple_of(i * HALF, HALF), HALF)
            put_part(cols, mm_tn(left[rows, cols], right[rows, :]))

        loop(W // HALF, chunk)

    def add_whole(buf):
        def put_part(cols, part):
            buf[cols, :] = (buf[cols, :].astype(F32) + part).astype(BF16)

        return put_part

    def put_whole(buf):
        def put_part(cols, part):
            buf[cols, :] = part.astype(BF16)

        return put_part

    def put_qkv(cols, part):
        m.wqkv[cols, 0 : 3 * head_cols] = part[:, 0 : 3 * head_cols].astype(BF16)
        m.glin[cols, :] = part[:, qkv_pad : qkv_pad + LANES]

    def put_o(cols, part):
        m.wqkv[cols, 3 * head_cols : qkv_pad] = part[:, 0:first_o].astype(BF16)
        m.go[cols, :] = part[:, first_o:head_cols].astype(BF16)

    reduces = []

    def low_bit(k):
        return k & -k if k else nz

    bits = [1 << i for i in range(nz.bit_length() - 1)]
    slots = {}
    for k in range(nz):
        for bit in bits:
            if bit < low_bit(k):
                slots[(k, bit)] = len(slots)
    pass_order = sorted(range(nz), key=lambda k: (low_bit(k), -k))

    def add_landed(total, k, which, arrive):
        for bit in bits:
            if bit < low_bit(k):
                slot = slots[(k, bit)]
                here = arrive.at[slot]
                sems = m.s_zs.at[which, slot], m.s_zr.at[which, slot]
                remote(here, here, *sems, z_dev(bit)).wait_recv()
                total = total + arrive[slot].astype(F32)
        return total

    def reduce_start(which, buf, land, ks=None):
        for k in ks or pass_order:

            def where(k=k):
                rows = block(2 * z_at(k) + 1 - x)
                return buf.at[rows], land.at[k], m.s_xs.at[which, k], m.s_xr.at[which, k], x_dev

            launch(reduces, where)

    def reduce_block(k, which, buf, land, out, arrive, share):
        here = land.at[k]
        remote(here, here, m.s_xs.at[which, k], m.s_xr.at[which, k], x_dev).wait_recv()
        total = buf[block(2 * z_at(k) + x), :].astype(F32) + land[k].astype(F32)
        if k == 0:
            share[...] = total
        else:
            out[k - 1] = add_landed(total, k, which, arrive).astype(BF16)

            def where():
                bit = low_bit(k)
                slot = slots[(k - bit, bit)]
                sems = m.s_zs.at[which, slot], m.s_zr.at[which, slot]
                return out.at[k - 1], arrive.at[slot], *sems, z_dev(bit)

            launch(reduces, where)

    def reduce_pass(*matrix):
        for k in pass_order:
            reduce_block(k, *matrix)

    kept = [k for k in range(nz) if k % 2 == 0]
    x_slots = {k: i for i, k in enumerate(kept)}
    far_slots = {}
    for k in kept:
        for bit in bits[1:]:
            if bit < low_bit(k):
                far_slots[(k, bit)] = len(x_slots) + len(far_slots)

    def owner_rows(k, side):
        return block(2 * z_at(k) + (1 - x if side else x))

    def near_start(which, buf, land):
        for k in reversed(kept):
            for side in (1, 0):

                def where(k=k, side=side):
                    at = k + side
                    sems = m.s_xs.at[which, at], m.s_xr.at[which, at]
                    return buf.at[owner_rows(k + 1, side)], land.at[at], *sems, z_dev(1)

                launch(reduces, where)

    def near_total(k, side, which, buf, land):
        at = k + side
        here = land.at[at]
        remote(here, here, m.s_xs.at[which, at], m.s_xr.at[which, at], z_dev(1)).wait_recv()
        return buf[owner_rows(k, side), :].astype(F32) + land[at].astype(F32)

    def landed_slot(slot, which, arrive):
        here = arrive.at[slot]
        remote(here, here, m.s_zs.at[which, slot], m.s_zr.at[which, slot], x_dev).wait_recv()
        return arrive[slot].astype(F32)

    def near_across(k, which, buf, land, out, arrive, share):
        slot = x_slots[k]
        out[slot] = near_total(k, 1, which, buf, land).astype(BF16)

        def where():
            return out.at[slot], arrive.at[slot], m.s_zs.at[which, slot], m.s_zr.at[which, slot], x_dev

        launch(reduces, where)

    def near_far(k, which, buf, land, out, arrive, share):
        total = near_total(k, 0, which, buf, land) + landed_slot(x_slots[k], which, arrive)
        for bit in bits[1:]:
            if bit < low_bit(k):
                total = total + landed_slot(far_slots[(k, bit)], which, arrive)
        if k == 0:
            share[...] = total
            return
        bit = low_bit(k)
        slot = far_slots[(k - bit, bit)]
        out[slot] = total.astype(BF16)

        def where():
            sems = m.s_zs.at[which, slot], m.s_zr.at[which, slot]
            return out.at[slot], arrive.at[slot], *sems, z_dev(bit)

        launch(reduces, where)

    def squares_of(total):
        squares = total * total
        folded = jnp.zeros((owned, LANES), F32)
        for i in range(total.shape[1] // LANES):
            folded = folded + squares[:, i * LANES : (i + 1) * LANES]
        tile = jnp.zeros((8, LANES), F32)
        for i in range(owned // 8):
            tile = tile + folded[8 * i : 8 * i + 8, :]
        return tile

    def reduce_end(which, arrive, share):
        total = add_landed(share[...], 0, which, arrive)
        share[...] = total
        return squares_of(total)

    def pass_on(which):
        line_step(which, 1, 2)
        line_step(which, 2, 2)

    def pass_last(which):
        for step in range(3, nz):
            line_step(which, step, 2)

    line_start(4, 2)
    gather_x(4)

    pass_last(2)

    def first_pass():
        line_start(5, 2)
        gather_x(5)

    def second_pass():
        pass_on(3)
        partner_landed(6)
        line_start(6, 2)
        line_start(7, 2)

    attend(0, {0: first_pass, 2: second_pass})
    line_end(2)
    m.wo[...] = jnp.concatenate([m.wqkv[:, 3 * head_cols : qkv_pad], m.wo1[...]], axis=1)
    turn(m.wo, m.wot)
    out_product = lambda rows: mm(m.ctx[rows, :], m.wot[...])
    exchange(0, 0, out_product)
    pass_last(3)
    attend(1, {1: lambda: pass_on(4), 3: lambda: pass_last(4)})
    exchange(0, 1, out_product)
    pass_on(5)
    pass_on(6)
    norm_one(0)
    pass_last(5)
    pass_on(7)
    line_end(3)
    line_end(4)
    feed(0)
    pass_last(6)
    pass_last(7)
    line_end(5)
    turn(m.wdown, m.wdownt)
    down_product = lambda rows: mm(m.act[rows, :], m.wdownt[...])
    exchange(1, 0, down_product)
    norm_one(1)
    feed(1)
    exchange(1, 1, down_product)
    turn(m.wup, m.wupt)
    turn(m.wqkv, m.wqkvt)
    up_product = lambda rows: mm(m.gub[rows, :], m.wupt[...])
    norm_two(0)
    feed_back(0)
    exchange(2, 0, up_product)
    first_rows, last_rows = slice(0, BUCKET_SLOTS), slice(BUCKET_SLOTS, 2 * BUCKET_SLOTS)
    weight_grad((), m.gffn, m.act, put_whole(m.wdownt), first_rows)
    weight_grad((3, 4), m.nb, m.gub, put_whole(m.wup), first_rows)
    norm_two(1)
    spread_end(1, 1, 0)
    spread_end(1, 1, 1)
    weight_grad((), m.gffn, m.act, add_whole(m.wdownt), last_rows)
    half = hidden // 2
    left, right = m.wdownt.at[:, 0:half], m.wdownt.at[:, half:hidden]
    down = (0, left, m.xrdown, m.zsdown, m.zrdown, sh_down.at[:, 0:half])
    down_near = (4, right, m.xrdownb, m.zsdownb, m.zrdownb, sh_down.at[:, half:hidden])
    near_start(4, right, m.xrdownb)
    reduce_start(0, left, m.xrdown)
    feed_back(1)
    exchange(2, 1, up_product)
    weight_grad((), m.nb, m.gub, add_whole(m.wup), last_rows)
    near_across(2, *down_near)
    odd, even = pass_order[: nz // 2], pass_order[nz // 2 :]
    reduce_start(1, m.wup, m.xrup, odd)
    up = (1, m.wup, m.xrup, m.zsup, m.zrup, sh_up)
    out = (2, m.go, m.xro, m.zso, m.zro, sh_o)
    qkv = (3, m.wqkv, m.xrqkv, m.zsqkv, m.zrqkv, sh_qkv)
    norm_one_back(0)
    blocks = lambda ks, matrix: lambda: [reduce_block(k, *matrix) for k in ks] and None
    early = [pass_order[0:1], pass_order[1:2], pass_order[2:-1]]

    def second_across():
        near_across(0, *down_near)
        reduce_start(1, m.wup, m.xrup, even)

    attend_back(
        0,
        {
            0: second_across,
            1: blocks(early[0], down),
            2: blocks(early[1], down),
            3: lambda: near_far(2, *down_near),
        },
    )
    exchange_first(3, 0, input_part)
    blocks(early[0], up)()
    norm_one_back(1)
    exchange_last(3, 0)
    spread_end(2, 1, 0)
    spread_end(2, 1, 1)
    weight_grad((0, 1, 2), m.gattn, m.ctx, put_o)
    blocks(early[1], up)()
    downward = list(range(nz - 1, -1, -1))
    reduce_start(2, m.go, m.xro, downward)
    attend_back(
        1,
        {
            0: blocks(early[2] + [0], down),
            3: blocks(early[2], up),
        },
    )
    weight_grad((), m.tok, m.dqkv, put_qkv)
    first_part, last_part = downward[:-1], downward[-1:]
    reduce_start(3, m.wqkv, m.xrqkv, first_part)
    reduce_block(0, *up)
    reduce_block(downward[0], *out)

    sm = m.sm
    sm[...] = jnp.zeros((SUM_ROWS, LANES), F32)
    acc = m.acc
    lead = jnp.where(yy == 0, 1.0, 0.0)

    def put(first, values):
        for i in range(values.shape[1] // LANES):
            sm[first + i : first + i + 1, :] = values[:, i * LANES : (i + 1) * LANES]

    def spot(values):
        return jnp.concatenate([jnp.where(T == t, values, 0.0) for t in range(4)], axis=1)

    for at, first in ((0, 0), (1, 6), (2, 12), (3, 18), (4, 36), (5, 42)):
        put(first, acc[at : at + 1, :] * lead)
    put(24, spot(acc[7:8, 0:head_cols]))
    put(30, spot(acc[7:8, 2 * head_cols : 3 * head_cols]))
    put(48, spot(acc[6:7, 0:hidden]))
    parts = []
    for h in range(heads):
        size = LANES // 2
        left = m.dband[h]
        while size >= 8:
            left = left[0:size, :] + pltpu.roll(left[size : 2 * size, :], long_row - size, 1)
            size //= 2
        for bit in (1, 2, 4):
            left = jnp.where(lax.rem(lax.div(sub8, bit), 2) == 1, pltpu.roll(left, long_row - bit, 1), left)
        left = pltpu.roll(left, LANES - 1, 1)
        diagonal = jnp.sum(left, axis=0, keepdims=True)
        hi = diagonal.astype(BF16).astype(F32)
        mid = (diagonal - hi).astype(BF16).astype(F32)
        parts += [hi, mid, diagonal - hi - mid]
    parts = jnp.concatenate(parts + [jnp.zeros((16 - len(parts), long_row), F32)], axis=0).astype(BF16)
    bucket_rows = -(-NB // LANES) * LANES
    valid = iota((1, long_row), 1) < long_row - 1
    hot_bucket = jnp.where((iota((bucket_rows, long_row), 0) == offsets) & valid, 1.0, 0.0).astype(BF16)
    by_bucket = mm_nt(parts, hot_bucket)
    bucket = iota((1, bucket_rows), 1)
    table_grad = jnp.zeros((32, LANES), F32)
    for h in range(heads):
        sums = by_bucket[3 * h : 3 * h + 1] + by_bucket[3 * h + 1 : 3 * h + 2] + by_bucket[3 * h + 2 : 3 * h + 3]
        flat = bucket * H + (T * heads + h)
        hot_row = jnp.where((iota((32, bucket_rows), 0) == lax.div(flat, LANES)) & (bucket < NB), 1.0, 0.0)
        hot_lane = jnp.where(iota((LANES, bucket_rows), 0) == lax.rem(flat, LANES), sums, 0.0)
        table_grad = table_grad + exact_nt(hot_row, hot_lane)
    sm[TABLE_ROW : TABLE_ROW + 30, :] = table_grad[0:30, :]

    lin_grad = m.glin[...]
    lin_grad = lin_grad + pltpu.roll(lin_grad, LANES - 16, 1) + pltpu.roll(lin_grad, LANES - 32, 1)
    lin_grad = jnp.where(own_head, lin_grad, 0.0)
    grad_u = jnp.sum(jnp.where(col_lane < 8, lin_grad, 0.0), axis=1, keepdims=True)
    grad_w = jnp.sum(jnp.where(col_lane >= 8, lin_grad, 0.0), axis=1, keepdims=True)
    by_lane = jnp.where(col_lane == 2 * col_in_head, grad_u, 0.0)
    by_lane = by_lane + jnp.where(col_lane == 2 * col_in_head + 1, grad_w, 0.0)
    sm[GATE_ROW : GATE_ROW + 1, :] = jnp.sum(by_lane, axis=0, keepdims=True)
    lin_total = acc[9:10, 0:LANES]
    total_u = jnp.sum(jnp.where(lane < 8, lin_total, 0.0), axis=1, keepdims=True)
    total_w = jnp.sum(jnp.where((lane >= 8) & (lane < 16), lin_total, 0.0), axis=1, keepdims=True)
    last = jnp.where(lane == 0, total_u, 0.0) + jnp.where(lane == 1, total_w, 0.0)
    scale_grad = acc[8:9, 0:LANES]
    for h in range(heads):
        one = jnp.sum(jnp.where(lane == h, scale_grad, 0.0), axis=1, keepdims=True)
        last = last + jnp.where(lane == 2 + T * heads + h, one, 0.0)
    sm[OFFSET_ROW : OFFSET_ROW + 1, :] = last

    small_sent = []

    def small_send(at, source, target, dev):
        cp = remote(source, target, m.s_ms.at[at], m.s_mr.at[at], dev)
        cp.start()
        small_sent.append(cp)
        return cp

    def quarter(index):
        return pl.ds(pl.multiple_of(index * QUARTER, QUARTER), QUARTER)

    to_core = [small_send(i, sm.at[quarter(2 * i + 1 - c)], m.smc.at[i], core_dev) for i in range(2)]
    for i in range(2):
        to_core[i].wait_recv()
        m.smh[i] = sm[quarter(2 * i + c), :] + m.smc[i]
    to_y = small_send(2, m.smh.at[1 - yy], m.smy, y_dev)
    reduce_block(first_part[0], *qkv)
    exchange(3, 1, input_part)
    reduce_block(downward[1], *out)
    to_y.wait_recv()
    m.smv[...] = m.smh[yy] + m.smy[...]
    to_x = small_send(3, m.smv, m.smx, x_dev)
    reduce_start(3, m.wqkv, m.xrqkv, last_part)
    for k in downward[2:]:
        reduce_block(k, *out)
    reduce_block(first_part[1], *qkv)
    to_x.wait_recv()
    m.smz[z] = m.smv[...] + m.smx[...]
    for k in range(1, nz):
        small_send(3 + k, m.smz.at[z], m.smz.at[z], z_dev(k))
    for k in first_part[2:]:
        reduce_block(k, *qkv)
    token_rows(0)
    reduce_block(0, *qkv)
    squares = reduce_end(0, m.zrdown, sh_down.at[:, 0:half])
    near_far(0, *down_near)
    squares = squares + squares_of(sh_down[:, half:hidden])
    squares = squares + reduce_end(1, m.zrup, sh_up)
    squares = squares + reduce_end(2, m.zro, sh_o)
    for k in range(1, nz):
        here = m.smz.at[z_at(k)]
        remote(here, here, m.s_ms.at[3 + k], m.s_mr.at[3 + k], z_dev(k)).wait_recv()
    own_quarter = m.smz[0]
    for i in range(1, nz):
        own_quarter = own_quarter + m.smz[i]
    m.sma[quarter(T), :] = own_quarter
    for k in range(1, 4):
        mine_small = m.sma.at[quarter(T)]
        small_send(2 + nz + k, mine_small, mine_small, (D, lax.rem(T + k, 4)))
    squares = squares + reduce_end(3, m.zrqkv, sh_qkv)
    last_copies = []
    for i, (source, target) in enumerate(
        ((sh_down, out_down), (sh_up, out_up), (sh_o, out_o), (sh_qkv, out_qkv))
    ):
        cp = pltpu.make_async_copy(source, target, m.s_out.at[i])
        cp.start()
        last_copies.append(cp)
    sqt = m.sqt
    sqt[T] = squares
    tail_sent = []
    for k in range(1, 4):
        cp = remote(
            sqt.at[T], sqt.at[T], m.s_ts.at[k], m.s_tr.at[k], (D, lax.rem(T + k, 4))
        )
        cp.start()
        tail_sent.append(cp)
    token_rows(1)
    for k in range(1, 4):
        here = m.sma.at[quarter(lax.rem(T + 4 - k, 4))]
        remote(here, here, m.s_ms.at[2 + nz + k], m.s_mr.at[2 + nz + k], core_dev).wait_recv()
    small_total = m.sma[0:SMALL_ROWS, :]
    for i in range(3):
        small_out[i] = small[i * SMALL_ROWS : (i + 1) * SMALL_ROWS, :]
    small_out[3] = small_total
    cp = pltpu.make_async_copy(small_out, out_small, m.s_out.at[4])
    cp.start()
    last_copies.append(cp)
    small_square = small_total * small_total
    small_tile = jnp.zeros((8, LANES), F32)
    for i in range(SMALL_ROWS // 8):
        small_tile = small_tile + small_square[8 * i : 8 * i + 8, :]
    for k in range(1, 4):
        here = sqt.at[lax.rem(T + 4 - k, 4)]
        remote(here, here, m.s_ts.at[k], m.s_tr.at[k], core_dev).wait_recv()
    sqd = m.sqd
    sqd[D] = sqt[0] + sqt[1] + sqt[2] + sqt[3]
    for k in range(1, n_dp):
        cp = remote(
            sqd.at[D], sqd.at[D], m.s_ds.at[k], m.s_dr.at[k], (lax.rem(D + k, n_dp), T)
        )
        cp.start()
        tail_sent.append(cp)
    for k in range(1, n_dp):
        here = sqd.at[lax.rem(D + n_dp - k, n_dp)]
        remote(here, here, m.s_ds.at[k], m.s_dr.at[k], core_dev).wait_recv()
    everything = small_tile
    for i in range(n_dp):
        everything = everything + sqd[i]
    sum_all = jnp.sum(jnp.sum(everything, axis=0, keepdims=True), axis=1, keepdims=True)
    norm_out[...] = jnp.broadcast_to(jnp.sqrt(sum_all), (8, LANES))

    for which in list(gathers):
        sent_all(which)
    for where in reduces:
        remote(*where()).wait_send()
    for cp in small_sent + tail_sent:
        cp.wait_send()
    for sent in core_spread.values():
        for cp in sent:
            cp.wait_send()
    for b in range(2):
        for cp in core_sent[(3, b)] + y_sent[(3, b)]:
            cp.wait_send()
    for cp in last_copies:
        cp.wait()
    for here, there in out_copies[2:]:
        here.wait()
        there.wait()


def adam_kernel(head_cols, *refs):
    ins, rest = refs[:14], refs[14:]
    block_in, token_in = ins[12:14]
    outs, rest = rest[:14], rest[14:]
    norm_out, block_out, token_out = outs[0], outs[12], outs[13]
    held, made = rest[:12], rest[12:24]
    block_held, token_held, s_in, s_out = rest[24:]
    loads = [pltpu.make_async_copy(ins[i], held[i], s_in.at[i]) for i in range(12)]
    passing = [
        pltpu.make_async_copy(block_in, block_held, s_in.at[12]),
        pltpu.make_async_copy(token_in, token_held, s_in.at[13]),
    ]
    passed = [
        pltpu.make_async_copy(block_held, block_out, s_out.at[12]),
        pltpu.make_async_copy(token_held, token_out, s_out.at[13]),
    ]
    for cp in loads + passing:
        cp.start()
    stores = []

    def store(i):
        cp = pltpu.make_async_copy(made[i], outs[i], s_out.at[i])
        cp.start()
        stores.append(cp)

    sh_qkv, sh_o, sh_up, sh_down, sh_small, norm, aw, am, av, fw, fm, fv = held
    (o_norm, o_am, o_av, o_aw, o_ac, o_fm, o_fv, o_fw, o_fc, o_sm, o_sv, o_sw) = made
    for i in (0, 1, 2, 3, 5):
        loads[i].wait()
    length = norm[0:1, 0:1]
    factor = CLIP_LIMIT / jnp.maximum(length, CLIP_LIMIT)
    o_norm[...] = length
    store(0)
    for i in (6, 7, 8):
        loads[i].wait()
    for i in range(4):
        if i < 3:
            grad = sh_qkv[:, i * head_cols : (i + 1) * head_cols]
        else:
            grad = jnp.concatenate([sh_qkv[:, 3 * head_cols :], sh_o[...]], axis=1)
        moment, square, master = adam_step(
            aw[i], am[i], av[i], factor * grad, RATE_MATRIX, WEIGHT_DECAY
        )
        o_am[i] = moment
        o_av[i] = square
        o_aw[i] = master
        o_ac[i] = master.astype(BF16)
    for i in (1, 2, 3, 4):
        store(i)
    for first, second in zip(passing, passed, strict=True):
        first.wait()
        second.start()
    for i in (9, 10, 11):
        loads[i].wait()
    for i, share in enumerate((sh_up, sh_down)):
        moment, square, master = adam_step(
            fw[i], fm[i], fv[i], factor * share[...], RATE_MATRIX, WEIGHT_DECAY
        )
        o_fm[i] = moment
        o_fv[i] = square
        o_fw[i] = master
        o_fc[i] = master.astype(BF16)
    for i in (5, 6, 7, 8):
        store(i)
    loads[4].wait()
    moment, square, master = adam_step(
        sh_small[0], sh_small[1], sh_small[2], factor * sh_small[3], RATE_SMALL, 0.0
    )
    o_sm[...] = moment
    o_sv[...] = square
    o_sw[...] = master
    for i in (9, 10, 11):
        store(i)
    for cp in stores + passed:
        cp.wait()


def fused_body(
    n_dp,
    tokens,
    cotangent,
    clip_lengths,
    key_mask,
    rel_buckets,
    attention_weights,
    attention_first,
    attention_second,
    feedforward_weights,
    feedforward_first,
    feedforward_second,
    small_params,
    small_first,
    small_second,
):
    rows = tokens.shape[0]
    owned, head_cols = attention_weights.shape[1:]
    hidden = feedforward_weights.shape[2]
    heads = head_cols // HD
    qkv_pad = -(-3 * head_cols // LANES) * LANES
    nz = n_dp // 2
    small_size = SMALL_ROWS * LANES
    total_size = 3 * small_size + 2 * BUCKET_SLOTS
    packed = jnp.zeros((total_size,), F32)
    pieces = (small_params, small_first, small_second, rel_buckets.astype(F32))
    for i, values in enumerate(pieces):
        after = total_size - i * small_size - values.shape[0]
        packed = packed + jnp.pad(values, (i * small_size, after))
    packed = packed.reshape(-1, LANES)
    keep = key_mask.reshape(rows // LANES, LANES)
    scratch = layer_scratch(owned, nz, qkv_pad, heads, head_cols, hidden)
    names = tuple(scratch)
    vmem = pl.BlockSpec(memory_space=pltpu.VMEM)
    smem = pl.BlockSpec(memory_space=pltpu.SMEM)
    anywhere = pl.BlockSpec(memory_space=pl.ANY)
    sds = jax.ShapeDtypeStruct
    block_rows, token_rows, sh_qkv, sh_o, sh_up, sh_down, sh_small, norm = pl.pallas_call(
        partial(layer_kernel, names, (n_dp, owned, qkv_pad, heads, head_cols, hidden)),
        out_shape=(
            sds((rows, W), BF16),
            sds((rows, W), BF16),
            sds((owned, qkv_pad), F32),
            sds((owned, LANES), F32),
            sds((owned, hidden), F32),
            sds((owned, hidden), F32),
            sds((4, SMALL_ROWS, LANES), F32),
            sds((8, LANES), F32),
        ),
        in_specs=[anywhere, anywhere, smem] + [anywhere] * 4,
        out_specs=(anywhere,) * 7 + (vmem,),
        scratch_shapes=list(scratch.values()),
        compiler_params=pltpu.CompilerParams(
            collective_id=1, has_side_effects=True, vmem_limit_bytes=62 * 1024 * 1024
        ),
        name="layer",
    )(tokens, cotangent, clip_lengths, keep, attention_weights, feedforward_weights, packed)
    like = lambda a, dtype=F32: sds(a.shape, dtype)
    small_like = sds((SMALL_ROWS, LANES), F32)
    made = (
        sds((1, 1), F32),
        like(attention_weights),
        like(attention_weights),
        like(attention_weights),
        like(attention_weights, BF16),
        like(feedforward_weights),
        like(feedforward_weights),
        like(feedforward_weights),
        like(feedforward_weights, BF16),
        small_like,
        small_like,
        small_like,
    )
    operands = (
        sh_qkv,
        sh_o,
        sh_up,
        sh_down,
        sh_small,
        norm,
        attention_weights,
        attention_first,
        attention_second,
        feedforward_weights,
        feedforward_first,
        feedforward_second,
        block_rows,
        token_rows,
    )
    in_vmem = lambda a: pltpu.VMEM(a.shape, a.dtype)
    results = pl.pallas_call(
        partial(adam_kernel, head_cols),
        out_shape=(*made, like(tokens, BF16), like(tokens, BF16)),
        in_specs=[anywhere] * len(operands),
        out_specs=(anywhere,) * (len(made) + 2),
        scratch_shapes=[in_vmem(a) for a in operands[:12]]
        + [in_vmem(a) for a in made]
        + [in_vmem(tokens), in_vmem(tokens)]
        + [pltpu.SemaphoreType.DMA((14,)), pltpu.SemaphoreType.DMA((14,))],
        compiler_params=pltpu.CompilerParams(vmem_limit_bytes=62 * 1024 * 1024),
        name="adam",
    )(*operands)
    length = small_params.shape[0]
    flat = lambda a: a.reshape(-1)[:length]
    return (
        results[0].reshape(()),
        *results[1:9],
        flat(results[9]),
        flat(results[10]),
        flat(results[11]),
        *results[12:],
    )


def fused_fits(mesh, owned):
    columns = mesh.shape["dp"] // 2
    whole = mesh.shape["dp"] % 2 == 0 and columns & (columns - 1) == 0
    return mesh.shape["tensor"] == 4 and whole and owned % 16 == 0

def solution(mesh):
    in_specs = (
        P("dp", None),
        P("dp", None),
        P("dp", None),
        P("dp"),
        P(),
        P(None, "dp", "tensor"),
        P(None, "dp", "tensor"),
        P(None, "dp", "tensor"),
        P(None, "dp", "tensor"),
        P(None, "dp", "tensor"),
        P(None, "dp", "tensor"),
        P(),
        P(),
        P(),
    )
    out_specs = (
        P(),
        P(None, "dp", "tensor"),
        P(None, "dp", "tensor"),
        P(None, "dp", "tensor"),
        P(None, "dp", "tensor"),
        P(None, "dp", "tensor"),
        P(None, "dp", "tensor"),
        P(None, "dp", "tensor"),
        P(None, "dp", "tensor"),
        P(),
        P(),
        P(),
        P("dp", None),
        P("dp", None),
    )
    n_dp = mesh.shape["dp"]
    body = general_body
    if fused_fits(mesh, MODEL_WIDTH // n_dp):
        body = partial(fused_body, n_dp)
    return jax.shard_map(body, mesh=mesh, in_specs=in_specs, out_specs=out_specs, check_vma=False)
```

```python
from functools import partial
from types import SimpleNamespace

import jax
import jax.numpy as jnp
from jax import lax
from jax.experimental import pallas as pl
from jax.experimental.pallas import tpu as pltpu
from jax.sharding import PartitionSpec as P

MODEL_WIDTH = 768
H = 12
HD = 64
FF = 3072
NB = 320
BUCKET_SLOTS = 512
CLIPS = 8
STEP = 5


FULL_PRECISION = lax.Precision.HIGHEST
DEEP_ALPHA = 24.0**0.25
NORM_EPSILON = 1e-05
MASK_VALUE = -1e30
BETA_FIRST = 0.9
BETA_SECOND = 0.98
RATE_MATRIX = 0.03
RATE_SMALL = 0.5
WEIGHT_DECAY = 0.01
ADAM_EPSILON = 1e-08
CLIP_LIMIT = 0.1


def layer_norm(values, norm_gain, norm_shift):
    row_mean = jnp.mean(values, axis=-1, keepdims=True)
    centred = values - row_mean
    variance = jnp.mean(centred * centred, axis=-1, keepdims=True)
    return centred * lax.rsqrt(variance + NORM_EPSILON) * norm_gain + norm_shift


def gelu_exact(values):
    return jax.nn.gelu(values, approximate=False)


def split_small(vector):
    widths = [MODEL_WIDTH] * 8 + [FF, NB * H, HD * 2, 2, H]
    pieces = []
    offset = 0
    for extent in widths:
        pieces.append(vector[offset : offset + extent])
        offset += extent
    return pieces


def allowed_mask(lengths_row, keep_row):
    positions = jnp.arange(BUCKET_SLOTS, dtype=jnp.int32)
    clip_ends = jnp.cumsum(lengths_row)
    segment = jnp.sum((positions[:, None] >= clip_ends[None, :]).astype(jnp.int32), axis=1)
    live_keys = (keep_row == 1) & (segment < CLIPS)
    same_clip = segment[:, None] == segment[None, :]
    return same_clip & (live_keys[None, :] | (positions[:, None] == positions[None, :]))


def band_matrix(diagonals):
    head_count = diagonals.shape[0]
    length = (diagonals.shape[1] + 1) // 2
    padded = jnp.concatenate([diagonals, jnp.zeros((head_count, 1), diagonals.dtype)], axis=1)
    repeated = jnp.tile(padded, (1, length))
    folded = repeated[:, : length * (2 * length - 1)].reshape(head_count, length, 2 * length - 1)
    return folded[:, :, length - 1 :]


def position_terms(head_inputs, gate_matrix, gate_offset, scale_local, table_local, rel_buckets):
    linear = (
        jnp.einsum(
            "blhd,dk->bhlk", head_inputs, gate_matrix.reshape(HD, 2), precision=FULL_PRECISION
        )
        + gate_offset
    )
    sigmoid = jax.nn.sigmoid(linear)
    gate = sigmoid[..., 0] * (sigmoid[..., 1] * scale_local[None, :, None] - 1.0) + 2.0
    onehot = (rel_buckets[:, None] == jnp.arange(NB, dtype=jnp.int32)[None, :]).astype(jnp.float32)
    per_offset = jnp.dot(
        onehot, table_local, precision=FULL_PRECISION, preferred_element_type=jnp.float32
    )
    toeplitz = band_matrix(per_offset.T)
    return gate[..., None] * toeplitz[None]


def adam_step(weights, moment, second, gradient, step_rate, decay_rate):
    moment_new = BETA_FIRST * moment + (1.0 - BETA_FIRST) * gradient
    second_new = BETA_SECOND * second + (1.0 - BETA_SECOND) * gradient * gradient
    moment_hat = moment_new / (1.0 - BETA_FIRST**STEP)
    second_hat = second_new / (1.0 - BETA_SECOND**STEP)
    master = weights - step_rate * (
        moment_hat / (jnp.sqrt(second_hat) + ADAM_EPSILON) + decay_rate * weights
    )
    return (moment_new, second_new, master)


def placed(total_length, piece, start):
    return lax.dynamic_update_slice_in_dim(jnp.zeros((total_length,), jnp.float32), piece, start, 0)


def column_sum(values):
    return jnp.sum(values.astype(jnp.float32), axis=0)


def general_body(
    tokens,
    cotangent,
    clip_lengths,
    key_mask,
    rel_buckets,
    attention_weights,
    attention_first,
    attention_second,
    feedforward_weights,
    feedforward_first,
    feedforward_second,
    small_params,
    small_first,
    small_second,
):
    gathered_attention, gathered_forward = (
        lax.all_gather(attention_weights.astype(jnp.bfloat16), "dp", axis=1, tiled=True),
        lax.all_gather(feedforward_weights.astype(jnp.bfloat16), "dp", axis=1, tiled=True),
    )
    query_weight = gathered_attention[0]
    key_weight = gathered_attention[1]
    value_weight = gathered_attention[2]
    output_weight = gathered_attention[3]
    up_weight = gathered_forward[0]
    down_weight = gathered_forward[1]
    head_cols = query_weight.shape[1]
    heads_local = head_cols // HD
    hidden_local = up_weight.shape[1]
    tensor_rank = lax.axis_index("tensor")
    col_start = tensor_rank * head_cols
    head_start = tensor_rank * heads_local
    hidden_start = tensor_rank * hidden_local
    row_count = tokens.shape[0]
    bucket_count = row_count // BUCKET_SLOTS
    (
        gain_one,
        shift_one,
        gain_two,
        shift_two,
        bias_query,
        bias_value,
        bias_output,
        bias_down,
        bias_up,
        rel_table,
        gate_matrix,
        gate_offset,
        gate_scale,
    ) = split_small(small_params)
    local_bias_query = lax.dynamic_slice_in_dim(bias_query, col_start, head_cols)
    local_bias_value = lax.dynamic_slice_in_dim(bias_value, col_start, head_cols)
    local_bias_up = lax.dynamic_slice_in_dim(bias_up, hidden_start, hidden_local)
    scale_local = lax.dynamic_slice_in_dim(gate_scale, head_start, heads_local)
    table_local = lax.dynamic_slice_in_dim(rel_table.reshape(NB, H), head_start, heads_local, 1)
    allowed = jax.vmap(allowed_mask)(clip_lengths, key_mask.reshape(bucket_count, BUCKET_SLOTS))[
        :, None
    ]
    leading = (tensor_rank == 0).astype(jnp.float32)
    inputs = tokens.astype(jnp.float32)
    upstream = cotangent.astype(jnp.float32)
    query_bf = (
        jnp.dot(tokens, query_weight, preferred_element_type=jnp.float32) + local_bias_query
    ).astype(jnp.bfloat16)
    key_bf = jnp.dot(tokens, key_weight, preferred_element_type=jnp.float32).astype(jnp.bfloat16)
    value_bf = (
        jnp.dot(tokens, value_weight, preferred_element_type=jnp.float32) + local_bias_value
    ).astype(jnp.bfloat16)
    head_shape = (bucket_count, BUCKET_SLOTS, heads_local, HD)
    heads_of_query = query_bf.reshape(head_shape)
    heads_of_key = key_bf.reshape(head_shape)
    heads_of_value = value_bf.reshape(head_shape)
    head_inputs = lax.dynamic_slice_in_dim(inputs, col_start, head_cols, 1).reshape(head_shape)
    extra, pull_position = jax.vjp(
        partial(position_terms, rel_buckets=rel_buckets),
        head_inputs,
        gate_matrix,
        gate_offset,
        scale_local,
        table_local,
    )
    attention_logits = (
        jnp.einsum(
            "blhd,bmhd->bhlm", heads_of_query, heads_of_key, preferred_element_type=jnp.float32
        )
        * 0.125
    )
    scores = jnp.where(allowed, attention_logits + extra, MASK_VALUE)
    row_max = jnp.max(scores, axis=-1, keepdims=True)
    exponent = jnp.exp(scores - row_max)
    denominator = jnp.sum(exponent, axis=-1, keepdims=True)
    log_total = row_max + jnp.log(denominator)
    probs_bf = (exponent / denominator).astype(jnp.bfloat16)
    context_bf = (
        jnp.einsum("bhlm,bmhd->blhd", probs_bf, heads_of_value, preferred_element_type=jnp.float32)
        .reshape(row_count, head_cols)
        .astype(jnp.bfloat16)
    )
    attention_part = jnp.einsum(
        "nw,dw->nd", context_bf, output_weight, preferred_element_type=jnp.float32
    )
    attention = lax.psum(attention_part, "tensor") + bias_output
    normed, pull_norm_one = jax.vjp(
        layer_norm, DEEP_ALPHA * inputs + attention, gain_one, shift_one
    )
    normed_bf = normed.astype(jnp.bfloat16)
    up_pre = jnp.dot(normed_bf, up_weight, preferred_element_type=jnp.float32) + local_bias_up
    activated, pull_gelu = jax.vjp(gelu_exact, up_pre)
    activated_bf = activated.astype(jnp.bfloat16)
    down_part = jnp.einsum(
        "nf,df->nd", activated_bf, down_weight, preferred_element_type=jnp.float32
    )
    feedforward = lax.psum(down_part, "tensor") + bias_down
    output_values, pull_norm_two = jax.vjp(
        layer_norm, DEEP_ALPHA * normed + feedforward, gain_two, shift_two
    )
    block_output = output_values.astype(jnp.bfloat16)
    grad_res_two, grad_gain_two, grad_shift_two = pull_norm_two(upstream)
    grad_ffn_share = grad_res_two.astype(jnp.bfloat16)
    grad_bias_down = column_sum(grad_ffn_share)
    down_grad = jnp.einsum(
        "nd,nf->df", grad_ffn_share, activated_bf, preferred_element_type=jnp.float32
    )
    grad_activated = jnp.einsum(
        "nd,df->nf", grad_ffn_share, down_weight, preferred_element_type=jnp.float32
    )
    (grad_up_pre,) = pull_gelu(grad_activated)
    grad_up_bf = grad_up_pre.astype(jnp.bfloat16)
    grad_bias_up = column_sum(grad_up_bf)
    up_grad = jnp.einsum("nd,nf->df", normed_bf, grad_up_bf, preferred_element_type=jnp.float32)
    normed_part = jnp.einsum("nf,df->nd", grad_up_bf, up_weight, preferred_element_type=jnp.float32)
    normed_sum = lax.psum(normed_part, "tensor")
    grad_normed = normed_sum + DEEP_ALPHA * grad_res_two
    grad_res_one, grad_gain_one, grad_shift_one = pull_norm_one(grad_normed)
    grad_attention_share = grad_res_one.astype(jnp.bfloat16)
    grad_bias_output = column_sum(grad_attention_share)
    output_grad = jnp.einsum(
        "nd,nw->dw", grad_attention_share, context_bf, preferred_element_type=jnp.float32
    )
    grad_context_bf = jnp.einsum(
        "nd,dw->nw", grad_attention_share, output_weight, preferred_element_type=jnp.float32
    ).astype(jnp.bfloat16)
    grad_heads = grad_context_bf.reshape(head_shape)
    attention_probabilities = jnp.exp(scores - log_total)
    recomputed_bf = attention_probabilities.astype(jnp.bfloat16)
    grad_probs = jnp.einsum(
        "blhd,bmhd->bhlm", grad_heads, heads_of_value, preferred_element_type=jnp.float32
    )
    inner = jnp.sum(grad_probs * attention_probabilities, axis=-1, keepdims=True)
    grad_scores_bf = (attention_probabilities * (grad_probs - inner)).astype(jnp.bfloat16)
    grad_query = (
        (
            jnp.einsum(
                "bhlm,bmhd->blhd", grad_scores_bf, heads_of_key, preferred_element_type=jnp.float32
            )
            * 0.125
        )
        .astype(jnp.bfloat16)
        .reshape(row_count, head_cols)
    )
    grad_key = (
        (
            jnp.einsum(
                "bhlm,blhd->bmhd",
                grad_scores_bf,
                heads_of_query,
                preferred_element_type=jnp.float32,
            )
            * 0.125
        )
        .astype(jnp.bfloat16)
        .reshape(row_count, head_cols)
    )
    grad_value = (
        jnp.einsum("bhlm,blhd->bmhd", recomputed_bf, grad_heads, preferred_element_type=jnp.float32)
        .astype(jnp.bfloat16)
        .reshape(row_count, head_cols)
    )
    grad_head_inputs, grad_gate_matrix, grad_gate_offset, grad_scale_local, grad_table_local = (
        pull_position(grad_scores_bf.astype(jnp.float32))
    )
    query_grad = jnp.einsum("nd,nw->dw", tokens, grad_query, preferred_element_type=jnp.float32)
    key_grad = jnp.einsum("nd,nw->dw", tokens, grad_key, preferred_element_type=jnp.float32)
    value_grad = jnp.einsum("nd,nw->dw", tokens, grad_value, preferred_element_type=jnp.float32)
    input_part = (
        jnp.einsum("nw,dw->nd", grad_query, query_weight, preferred_element_type=jnp.float32)
        + jnp.einsum("nw,dw->nd", grad_key, key_weight, preferred_element_type=jnp.float32)
        + jnp.einsum("nw,dw->nd", grad_value, value_weight, preferred_element_type=jnp.float32)
    )
    own_columns = lax.dynamic_slice_in_dim(input_part, col_start, head_cols, 1)
    input_part = lax.dynamic_update_slice_in_dim(
        input_part, own_columns + grad_head_inputs.reshape(row_count, head_cols), col_start, 1
    )
    grad_inputs = lax.psum(input_part, "tensor") + DEEP_ALPHA * grad_res_one
    tokens_grad = grad_inputs.astype(jnp.bfloat16)
    table_grad = lax.dynamic_update_slice_in_dim(
        jnp.zeros((NB, H), jnp.float32), grad_table_local, head_start, 1
    ).reshape(-1)
    local_small = jnp.concatenate(
        [
            grad_gain_one * leading,
            grad_shift_one * leading,
            grad_gain_two * leading,
            grad_shift_two * leading,
            placed(MODEL_WIDTH, column_sum(grad_query), col_start),
            placed(MODEL_WIDTH, column_sum(grad_value), col_start),
            grad_bias_output * leading,
            grad_bias_down * leading,
            placed(FF, grad_bias_up, hidden_start),
            table_grad,
            grad_gate_matrix,
            grad_gate_offset,
            placed(H, grad_scale_local, head_start),
        ]
    )
    small_grad = lax.psum(local_small, ("dp", "tensor"))
    local_attention = jnp.stack([query_grad, key_grad, value_grad, output_grad])
    local_forward = jnp.stack([up_grad, down_grad])
    summed_attention, summed_forward = lax.psum((local_attention, local_forward), "dp")
    owner_rank = lax.axis_index("dp")
    owned_rows = attention_weights.shape[1]
    share_attention = lax.dynamic_slice_in_dim(
        summed_attention, owner_rank * owned_rows, owned_rows, 1
    )
    share_forward = lax.dynamic_slice_in_dim(summed_forward, owner_rank * owned_rows, owned_rows, 1)
    share_squares = jnp.sum(share_attention * share_attention) + jnp.sum(
        share_forward * share_forward
    )
    big_squares = lax.psum(share_squares, ("dp", "tensor"))
    global_norm = jnp.sqrt(big_squares + jnp.sum(small_grad * small_grad))
    factor = CLIP_LIMIT / jnp.maximum(global_norm, CLIP_LIMIT)
    attention_moment, attention_square, attention_master = adam_step(
        attention_weights,
        attention_first,
        attention_second,
        factor * share_attention,
        RATE_MATRIX,
        WEIGHT_DECAY,
    )
    feedforward_moment, feedforward_square, feedforward_master = adam_step(
        feedforward_weights,
        feedforward_first,
        feedforward_second,
        factor * share_forward,
        RATE_MATRIX,
        WEIGHT_DECAY,
    )
    small_moment, small_square, small_master = adam_step(
        small_params, small_first, small_second, factor * small_grad, RATE_SMALL, 0.0
    )
    return (
        global_norm,
        attention_moment,
        attention_square,
        attention_master,
        attention_master.astype(jnp.bfloat16),
        feedforward_moment,
        feedforward_square,
        feedforward_master,
        feedforward_master.astype(jnp.bfloat16),
        small_moment,
        small_square,
        small_master,
        block_output,
        tokens_grad,
    )


F32 = jnp.float32
BF16 = jnp.bfloat16
MESH_ID = pl.DeviceIdType.MESH
LANES = 128
SMALL_ROWS = 104
QUARTER = 32
SUM_ROWS = 4 * QUARTER
TABLE_ROW = 72
GATE_ROW = 102
OFFSET_ROW = 103
INV_SQRT2 = 0.5**0.5
INV_SQRT_2PI = 0.3989422804014327
CHUNK = 128
HALF = 256
W = MODEL_WIDTH
NT = (((1,), (1,)), ((), ()))
TN = (((0,), (0,)), ((), ()))


def mm(a, b):
    return jnp.dot(a, b, preferred_element_type=F32)


def mm_nt(a, b):
    return lax.dot_general(a, b, NT, preferred_element_type=F32)


def mm_tn(a, b):
    return lax.dot_general(a, b, TN, preferred_element_type=F32)


def exact_nt(a, b):
    return lax.dot_general(a, b, NT, precision=FULL_PRECISION, preferred_element_type=F32)


def exact_tn(a, b):
    return lax.dot_general(a, b, TN, precision=FULL_PRECISION, preferred_element_type=F32)


def exact_mm(a, b):
    return jnp.dot(a, b, precision=FULL_PRECISION, preferred_element_type=F32)


def iota(shape, axis):
    return lax.broadcasted_iota(jnp.int32, shape, axis)


def layer_scratch(owned, nz, qkv_pad, heads, head_cols, hidden):
    rows = 2 * BUCKET_SLOTS
    dma = pltpu.SemaphoreType.DMA
    vm = pltpu.VMEM
    shapes = dict(
        wa=vm((4, owned, head_cols), F32),
        wf=vm((2, owned, hidden), F32),
        keep=vm((rows // LANES, LANES), jnp.int32),
        small=vm((3 * SMALL_ROWS + 2 * BUCKET_SLOTS // LANES, LANES), F32),
        shqkv=vm((owned, qkv_pad), F32),
        sho=vm((owned, LANES), F32),
        shup=vm((owned, hidden), F32),
        shdown=vm((owned, hidden), F32),
        smallout=vm((4, SMALL_ROWS, LANES), F32),
        tok=vm((rows, W), BF16),
        cot=vm((2, HALF, W), BF16),
        wqkv=vm((W, qkv_pad), BF16),
        wo1=vm((W, LANES), BF16),
        wo=vm((W, head_cols), BF16),
        wot=vm((head_cols, W), BF16),
        wqkvt=vm((qkv_pad + LANES, W), BF16),
        wupt=vm((hidden, W), BF16),
        wdownt=vm((hidden, W), BF16),
        go=vm((W, LANES), BF16),
        glin=vm((W, LANES), F32),
        wup=vm((W, hidden), BF16),
        wdown=vm((W, hidden), BF16),
        q=vm((rows, head_cols), BF16),
        k=vm((rows, head_cols), BF16),
        v=vm((rows, head_cols), BF16),
        kt=vm((head_cols, rows), BF16),
        qt=vm((head_cols, rows), BF16),
        dctxt=vm((head_cols, BUCKET_SLOTS), BF16),
        vt=vm((head_cols, rows), BF16),
        ctx=vm((rows, head_cols), BF16),
        dqkv=vm((rows, qkv_pad + LANES), BF16),
        prob=vm((2 * heads, BUCKET_SLOTS, BUCKET_SLOTS), F32),
        gsb=vm((heads * BUCKET_SLOTS, BUCKET_SLOTS), BF16),
        dqf=vm((BUCKET_SLOTS, head_cols), F32),
        mbias=vm((2, BUCKET_SLOTS, BUCKET_SLOTS), BF16),
        band=vm((heads, LANES, 2 * BUCKET_SLOTS), F32),
        dband=vm((heads, LANES, 2 * BUCKET_SLOTS), F32),
        gate=vm((rows, LANES), F32),
        gu=vm((rows, LANES), F32),
        gmat=vm((W, LANES), F32),
        vecs=vm((16, W), F32),
        acc=vm((16, W), F32),
        nb=vm((rows, W), BF16),
        held=vm((2, HALF, W), F32),
        xh1=vm((2, HALF, W), F32),
        rstd1=vm((2, HALF, LANES), F32),
        act=vm((rows, hidden), BF16),
        gelup=vm((rows, hidden), F32),
        gffn=vm((rows, W), BF16),
        gub=vm((rows, hidden), BF16),
        gattn=vm((rows, W), BF16),
        stage=vm((2, HALF, W), BF16),
        ownf=vm((HALF, W), F32),
        cs=vm((2, HALF, W), BF16),
        cr=vm((2, HALF, W), BF16),
        ys=vm((2, HALF, W), BF16),
        yr=vm((2, 2, HALF, W), BF16),
        xrqkv=vm((nz, owned, qkv_pad), BF16),
        xro=vm((nz, owned, LANES), BF16),
        xrup=vm((nz, owned, hidden), BF16),
        xrdown=vm((nz, owned, hidden // 2), BF16),
        xrdownb=vm((nz, owned, hidden // 2), BF16),
        zsqkv=vm((nz - 1, owned, qkv_pad), BF16),
        zso=vm((nz - 1, owned, LANES), BF16),
        zsup=vm((nz - 1, owned, hidden), BF16),
        zsdown=vm((nz - 1, owned, hidden // 2), BF16),
        zsdownb=vm((nz - 1, owned, hidden // 2), BF16),
        zrqkv=vm((nz - 1, owned, qkv_pad), BF16),
        zro=vm((nz - 1, owned, LANES), BF16),
        zrup=vm((nz - 1, owned, hidden), BF16),
        zrdown=vm((nz - 1, owned, hidden // 2), BF16),
        zrdownb=vm((nz - 1, owned, hidden // 2), BF16),
        sm=vm((SUM_ROWS, LANES), F32),
        smc=vm((2, QUARTER, LANES), F32),
        smh=vm((2, QUARTER, LANES), F32),
        smy=vm((QUARTER, LANES), F32),
        smv=vm((QUARTER, LANES), F32),
        smx=vm((QUARTER, LANES), F32),
        smz=vm((nz, QUARTER, LANES), F32),
        sma=vm((SUM_ROWS, LANES), F32),
        sqt=vm((4, 8, LANES), F32),
        sqd=vm((2 * nz, 8, LANES), F32),
        s_in=dma((7,)),
        s_out=dma((5,)),
        s_gs=dma((8,)),
        s_gr=dma((8,)),
        s_ls=dma((8, 2, nz)),
        s_lr=dma((8, 2, nz)),
        s_lxs=dma((8, 2, nz)),
        s_lxr=dma((8, 2, nz)),
        s_cs=dma((4, 2, 2)),
        s_cr=dma((4, 2, 2)),
        s_ys=dma((4, 2, 2)),
        s_yr=dma((4, 2, 2)),
        s_as=dma((3, 2, 2)),
        s_ar=dma((3, 2, 2)),
        s_ol=dma((2, 2)),
        s_os=dma((2, 2)),
        s_or=dma((2, 2)),
        s_xs=dma((5, nz)),
        s_xr=dma((5, nz)),
        s_zs=dma((5, nz)),
        s_zr=dma((5, nz)),
        s_ms=dma((6 + nz,)),
        s_mr=dma((6 + nz,)),
        s_ts=dma((4,)),
        s_tr=dma((4,)),
        s_ds=dma((2 * nz,)),
        s_dr=dma((2 * nz,)),
    )
    return shapes


def layer_kernel(names, dims, *refs):
    n_dp, owned, qkv_pad, heads, head_cols, hidden = dims
    nz = n_dp // 2
    (tok_in, cot_in, lens, keep_in, wa_in, wf_in, small_in) = refs[:7]
    (bo_out, tg_out, out_qkv, out_o, out_up, out_down, out_small, norm_out) = refs[7:15]
    m = SimpleNamespace(**dict(zip(names, refs[15:], strict=True)))
    D = lax.axis_index("dp")
    T = lax.axis_index("tensor")
    z = lax.div(D, 2)
    x = lax.rem(D, 2)
    c = lax.rem(T, 2)
    yy = lax.div(T, 2)
    core_dev = (D, T + 1 - 2 * c)
    y_dev = (D, lax.rem(T + 2, 4))
    x_dev = (z * 2 + 1 - x, T)

    def z_at(k):
        total, bit = 0, 1
        while bit < nz:
            here = lax.rem(lax.div(z, bit), 2)
            total = total + bit * (1 - here if k & bit else here)
            bit *= 2
        return total

    def z_dev(k):
        return (z_at(k) * 2 + x, T)

    def remote(src, dst, ss, rs, dev):
        return pltpu.make_async_remote_copy(
            src_ref=src, dst_ref=dst, send_sem=ss, recv_sem=rs, device_id=dev, device_id_type=MESH_ID
        )

    def loop(n, step):
        def run(i, carry):
            step(i)
            return carry

        lax.fori_loop(0, n, run, 0)

    def block(owner):
        return pl.ds(pl.multiple_of(owner * owned, owned), owned)

    wa, wf, keep, small = m.wa, m.wf, m.keep, m.small
    sh_qkv, sh_o, sh_up, sh_down, small_out = m.shqkv, m.sho, m.shup, m.shdown, m.smallout
    first_loads = []
    for i, (source, target) in enumerate(((wa_in, wa), (wf_in, wf), (small_in, small), (keep_in, keep))):
        cp = pltpu.make_async_copy(source, target, m.s_in.at[3 + i])
        cp.start()
        first_loads.append(cp)
    tok_copy = pltpu.make_async_copy(tok_in, m.tok, m.s_in.at[0])
    tok_copy.start()
    cot_copies = []
    for b in range(2):
        rows = pl.ds(pl.multiple_of(b * BUCKET_SLOTS + c * HALF, HALF), HALF)
        cp = pltpu.make_async_copy(cot_in.at[rows], m.cot.at[b], m.s_in.at[1 + b])
        cp.start()
        cot_copies.append(cp)
    barrier = pltpu.get_barrier_semaphore()
    for k in range(1, 4):
        pl.semaphore_signal(barrier, inc=1, device_id=(D, lax.rem(T + k, 4)), device_id_type=MESH_ID)
    for k in range(1, n_dp):
        pl.semaphore_signal(barrier, inc=1, device_id=(lax.rem(D + k, n_dp), T), device_id_type=MESH_ID)
    for cp in first_loads:
        cp.wait()
    mine = block(D)
    first_o = qkv_pad - 3 * head_cols
    m.wqkv[mine, :] = jnp.concatenate([wa[0], wa[1], wa[2], wa[3, :, 0:first_o]], axis=1).astype(BF16)
    m.wo1[mine, :] = wa[3, :, first_o:head_cols].astype(BF16)
    m.wup[mine, :] = wf[0].astype(BF16)
    m.wdown[mine, :] = wf[1].astype(BF16)
    pl.semaphore_wait(barrier, 3 + n_dp - 1)

    part_rows = owned // 2 if owned % 32 == 0 else owned
    halves = lambda buf: [(buf, 0, part_rows), (buf, owned - part_rows, part_rows)]
    pieces = halves(m.wqkv) + [(m.wo1, 0, owned)] + halves(m.wup) + halves(m.wdown)

    pieces.append(pieces[-1])
    across = len(pieces) - 1
    straight = (across - 1, across)

    def piece(which, owner_z, other_column=False):
        buf, first, count = pieces[which]
        column = 1 - x if other_column != (which == across) else x
        return buf.at[pl.ds(pl.multiple_of((owner_z * 2 + column) * owned + first, 16), count)]

    gathers = {}

    def launch(record, where):
        remote(*where()).start()
        record.append(where)

    def when(condition, action):
        pl.when(condition)(action)

    def from_z(way, step):
        owner_z = z - step if way == 0 else z + step
        return owner_z, (owner_z >= 0) if way == 0 else (owner_z < nz)

    def send_when(which, condition, where):
        when(condition(), lambda: remote(*where()).start())
        gathers.setdefault(which, []).append((condition, where))

    def line_send(which, way, step, hops):
        origin = step - hops

        def where():
            part = piece(which, from_z(way, origin)[0])
            target = ((z + hops if way == 0 else z - hops) * 2 + x, T)
            return part, part, m.s_ls.at[which, way, step], m.s_lr.at[which, way, step], target

        def condition():
            there = (z + hops < nz) if way == 0 else (z >= hops)
            return there & from_z(way, origin)[1]

        send_when(which, condition, where)

    def line_start(which, hops):
        for hop in range(1, hops + 1):
            for way in range(2):
                line_send(which, way, hop, hop)

    def gather_x(which):
        def where():
            own = piece(which, z)
            return own, own, m.s_gs.at[which], m.s_gr.at[which], x_dev

        send_when(which, lambda: D >= 0, where)

    def line_step(which, step, hops):
        for way in range(2):

            def landed(way=way):
                part = piece(which, from_z(way, step)[0])
                sems = m.s_ls.at[which, way, step], m.s_lr.at[which, way, step]
                remote(part, part, *sems, x_dev).wait_recv()

            when(from_z(way, step)[1], landed)
            if step >= hops and step + 1 < nz:
                line_send(which, way, step + 1, 1)
            if which in straight:
                continue

            def where(way=way):
                part = piece(which, from_z(way, step)[0])
                return part, part, m.s_lxs.at[which, way, step], m.s_lxr.at[which, way, step], x_dev

            send_when(which, lambda way=way: from_z(way, step)[1], where)

    def partner_landed(which):
        part = piece(which, z, True)
        remote(part, part, m.s_gs.at[which], m.s_gr.at[which], x_dev).wait_recv()

    def line_end(which):
        partner_landed(which)
        for step in range(1, nz):
            for way in range(2):

                def landed(way=way):
                    part = piece(which, from_z(way, step)[0], True)
                    sems = m.s_lxs.at[which, way, step], m.s_lxr.at[which, way, step]
                    remote(part, part, *sems, x_dev).wait_recv()

                when(from_z(way, step)[1], landed)

    def sent_all(which):
        for condition, where in gathers.pop(which):
            when(condition(), lambda where=where: remote(*where()).wait_send())

    def turn(source, target):
        count = source.shape[1]
        if count % LANES:
            target[...] = source[...].T
            return
        step = HALF if count % HALF == 0 else LANES

        def chunk(i):
            at = pl.ds(pl.multiple_of(i * step, step), step)
            target[at, :] = source[:, at].T

        loop(count // step, chunk)

    for which in (0, 1):
        line_start(which, 1)
    for which in (0, 1):
        gather_x(which)
    gather_x(across - 1)

    def small_row(first, count):
        return jnp.concatenate([small[first + i : first + i + 1, :] for i in range(count)], axis=1)

    def pick(values, size):
        total = jnp.zeros((1, size), F32)
        for t in range(4):
            total = total + jnp.where(T == t, values[:, t * size : (t + 1) * size], 0.0)
        return total

    vecs = m.vecs
    vecs[...] = jnp.zeros_like(vecs)
    m.acc[...] = jnp.zeros((16, W), F32)
    for at, first in ((0, 0), (1, 6), (2, 12), (3, 18), (4, 36), (5, 42)):
        vecs[at : at + 1, :] = small_row(first, W // LANES)
    vecs[6:7, :] = pick(small_row(48, FF // LANES), hidden)
    bq = pick(small_row(24, W // LANES), head_cols)
    bv = pick(small_row(30, W // LANES), head_cols)
    bias_qkv = jnp.concatenate(
        [bq, jnp.zeros_like(bq), bv, jnp.zeros((1, qkv_pad - 3 * head_cols), F32)], axis=1
    )
    vecs[7:8, 0:qkv_pad] = bias_qkv

    lane = iota((1, LANES), 1)
    col = iota((W, LANES), 0)
    col_lane = iota((W, LANES), 1)
    gate_row = small[GATE_ROW : GATE_ROW + 1, :]
    col_in_head = lax.rem(col, HD)
    picked_u = jnp.sum(
        jnp.where(col_lane == 2 * col_in_head, gate_row, 0.0), axis=1, keepdims=True
    )
    picked_w = jnp.sum(
        jnp.where(col_lane == 2 * col_in_head + 1, gate_row, 0.0), axis=1, keepdims=True
    )
    in_group = lax.rem(col_lane, 8)
    own_head = (col_lane < 16) & (in_group < heads) & (lax.div(col, HD) == T * heads + in_group)
    m.gmat[...] = jnp.where(own_head, jnp.where(col_lane < 8, picked_u, picked_w), 0.0)
    offset_row = small[OFFSET_ROW : OFFSET_ROW + 1, :]
    offset_u = jnp.sum(jnp.where(lane == 0, offset_row, 0.0), axis=1, keepdims=True)
    offset_w = jnp.sum(jnp.where(lane == 1, offset_row, 0.0), axis=1, keepdims=True)
    scale = jnp.zeros((1, LANES), F32)
    for h in range(heads):
        one = jnp.sum(jnp.where(lane == 2 + T * heads + h, offset_row, 0.0), axis=1, keepdims=True)
        scale = scale + jnp.where(lane == h, one, 0.0)
    head_lane = lane < heads

    line_step(0, 1, 1)
    line_step(1, 1, 1)

    offsets = small_row(3 * SMALL_ROWS, 2 * BUCKET_SLOTS // LANES).astype(jnp.int32)
    table = small[TABLE_ROW : TABLE_ROW + 32, :]
    long_row = 2 * BUCKET_SLOTS
    sub8 = iota((8, long_row), 0)
    for h in range(heads):
        flat = offsets * H + (T * heads + h)
        at_row = lax.div(flat, LANES)
        at_lane = lax.rem(flat, LANES)
        hot_row = jnp.where(iota((32, long_row), 0) == at_row, 1.0, 0.0)
        spread = exact_tn(table, hot_row)
        values = jnp.sum(
            jnp.where(iota((LANES, long_row), 0) == at_lane, spread, 0.0), axis=0, keepdims=True
        )
        stack = jnp.broadcast_to(pltpu.roll(jnp.broadcast_to(values, (8, long_row)), 1, 1), (8, long_row))
        for bit in (1, 2, 4):
            stack = jnp.where(lax.rem(lax.div(sub8, bit), 2) == 1, pltpu.roll(stack, bit, 1), stack)
        size = 8
        m.band[h, 0:8, :] = stack
        while size < LANES:
            m.band[h, size : 2 * size, :] = pltpu.roll(m.band[h, 0:size, :], size, 1)
            size *= 2
    m.dband[...] = jnp.zeros(m.dband.shape, F32)

    line_step(0, 2, 1)
    line_step(1, 2, 1)

    for b in range(2):
        end = 0
        ends = []
        for i in range(CLIPS):
            end = end + lens[b, i]
            ends.append(end)
        key_at = iota((1, BUCKET_SLOTS), 1)
        key_segment = jnp.zeros((1, BUCKET_SLOTS), jnp.int32)
        for end in ends:
            key_segment = key_segment + jnp.where(key_at >= end, 1, 0)
        kept = jnp.concatenate([keep[4 * b + i : 4 * b + i + 1, :] for i in range(4)], axis=1)
        live = jnp.where((kept == 1) & (key_segment < CLIPS), key_segment, -1)

        def mask_chunk(i, b=b, ends=ends, live=live):
            query_at = iota((CHUNK, BUCKET_SLOTS), 0) + i * CHUNK
            segment = jnp.zeros((CHUNK, BUCKET_SLOTS), jnp.int32)
            for end in ends:
                segment = segment + jnp.where(query_at >= end, 1, 0)
            allowed = (segment == live) | (query_at == iota((CHUNK, BUCKET_SLOTS), 1))
            m.mbias[b, pl.ds(pl.multiple_of(i * CHUNK, CHUNK), CHUNK), :] = jnp.where(
                allowed, 0.0, MASK_VALUE
            ).astype(BF16)

        loop(BUCKET_SLOTS // CHUNK, mask_chunk)

    for step in range(3, nz):
        line_step(0, step, 1)
        line_step(1, step, 1)
    line_start(2, 2)

    tok_copy.wait()
    gmat = m.gmat[...]
    part_hi = gmat.astype(BF16)
    rest = gmat - part_hi.astype(F32)
    part_mid = rest.astype(BF16)
    part_lo = (rest - part_mid.astype(F32)).astype(BF16)
    gate_parts = (part_hi, part_hi, part_hi, part_mid, part_mid, part_lo)
    stacked = jnp.zeros((W, LANES), F32)
    for i, part in enumerate(gate_parts):
        moved = part.astype(F32)
        stacked = stacked + (pltpu.roll(moved, 16 * i, 1) if i else moved)
    m.wqkvt[qkv_pad : qkv_pad + LANES, :] = stacked.astype(BF16).T

    def gate_chunk(i):
        rows = pl.ds(pl.multiple_of(i * HALF, HALF), HALF)
        tokens = m.tok[rows, :]
        linear = mm(tokens, part_hi) + mm(tokens, part_mid) + mm(tokens, part_lo)
        both = jax.nn.sigmoid(linear + jnp.where(lane < 8, offset_u, offset_w))
        m.gu[rows, :] = both
        m.gate[rows, :] = both * (pltpu.roll(both, LANES - 8, 1) * scale - 1.0) + 2.0

    loop(4, gate_chunk)

    line_start(3, 2)
    line_end(0)
    line_end(1)
    gather_x(2)
    line_step(2, 1, 2)
    line_step(2, 2, 2)
    gather_x(3)

    def project(i):
        rows = pl.ds(pl.multiple_of(i * HALF, HALF), HALF)
        both = mm(m.tok[rows, :], m.wqkv[...]) + vecs[7:8, 0:qkv_pad]
        query = (both[:, 0:head_cols].astype(BF16).astype(F32) * 0.125).astype(BF16)
        m.q[rows, :] = query
        m.qt[:, rows] = query.T
        key = both[:, head_cols : 2 * head_cols].astype(BF16)
        value = both[:, 2 * head_cols : 3 * head_cols].astype(BF16)
        m.k[rows, :] = key
        m.v[rows, :] = value
        m.kt[:, rows] = key.T
        m.vt[:, rows] = value.T

    loop(4, project)

    head_of = lax.div(iota((1, head_cols), 1), HD)
    head_masks = [jnp.where(head_of == h, 1.0, 0.0) for h in range(heads)]
    low_masks = [m.astype(BF16) for m in head_masks]

    def hooked(first, count, chunk, hooks):
        def step_of(i):
            step = i + first
            chunk(step)
            for at, action in hooks.items():
                if first <= at < first + count:
                    when(step == at, action)

        loop(count, step_of)

    def by_head(stacked):
        total = stacked[0:CHUNK, :] * head_masks[0]
        for h in range(1, heads):
            total = total + stacked[h * CHUNK : (h + 1) * CHUNK, :] * head_masks[h]
        return total

    def attend(b, hooks):
        keys = m.kt[:, b * BUCKET_SLOTS : (b + 1) * BUCKET_SLOTS]
        values = m.v[b * BUCKET_SLOTS : (b + 1) * BUCKET_SLOTS, :]

        def chunk(i):
            local = pl.ds(pl.multiple_of(i * CHUNK, CHUNK), CHUNK)
            rows = pl.ds(pl.multiple_of(b * BUCKET_SLOTS + i * CHUNK, CHUNK), CHUNK)
            window = pl.ds(pl.multiple_of(BUCKET_SLOTS - i * CHUNK, CHUNK), BUCKET_SLOTS)
            query = m.q[rows, :]
            gates = m.gate[rows, :]
            all_scores = mm(jnp.concatenate([query * mask for mask in low_masks], axis=0), keys)
            all_probs = []
            for h in range(heads):
                scores = all_scores[h * CHUNK : (h + 1) * CHUNK, :]
                scores = scores + gates[:, h : h + 1] * m.band[h, :, window]
                scores = scores + m.mbias[b, local, :].astype(F32)
                top = jnp.max(scores, axis=1, keepdims=True)
                weight = jnp.exp(scores - top)
                total = jnp.sum(weight, axis=1, keepdims=True)
                probability = weight * (1.0 / total)
                m.prob[b * heads + h, local, :] = probability
                all_probs.append(probability.astype(BF16))
            m.ctx[rows, :] = by_head(mm(jnp.concatenate(all_probs, axis=0), values)).astype(BF16)

        hooked(0, BUCKET_SLOTS // CHUNK, chunk, hooks)

    core_sent = {}
    y_sent = {}

    def exchange(phase, b, product):
        exchange_first(phase, b, product)
        exchange_last(phase, b)

    def exchange_first(phase, b, product):
        other = b * BUCKET_SLOTS + (1 - c) * HALF
        own = b * BUCKET_SLOTS + c * HALF
        for cp in core_sent.get((phase - 1, b), []) + y_sent.get((phase - 1, b), []):
            cp.wait_send()
        for i in range(2):
            at = slice(i * CHUNK, (i + 1) * CHUNK)
            rows = pl.ds(pl.multiple_of(other + i * CHUNK, CHUNK), CHUNK)
            m.cs[b, at, :] = product(rows).astype(BF16)
            cp = remote(
                m.cs.at[b, at], m.cr.at[b, at], m.s_cs.at[phase, b, i], m.s_cr.at[phase, b, i], core_dev
            )
            cp.start()
            core_sent.setdefault((phase, b), []).append(cp)
        for i in range(2):
            at = slice(i * CHUNK, (i + 1) * CHUNK)
            rows = pl.ds(pl.multiple_of(own + i * CHUNK, CHUNK), CHUNK)
            m.ownf[at, :] = product(rows)

    def exchange_last(phase, b):
        for i in range(2):
            at = slice(i * CHUNK, (i + 1) * CHUNK)
            core_sent[(phase, b)][i].wait_recv()
            m.ys[b, at, :] = (m.ownf[at, :] + m.cr[b, at, :].astype(F32)).astype(BF16)
            cp = remote(
                m.ys.at[b, at],
                m.yr.at[phase % 2, b, at],
                m.s_ys.at[phase, b, i],
                m.s_yr.at[phase, b, i],
                y_dev,
            )
            cp.start()
            y_sent.setdefault((phase, b), []).append(cp)

    def arrived(phase, b, at):
        return m.ys[b, at, :].astype(F32) + m.yr[phase % 2, b, at, :].astype(F32)

    def own_rows(b, i):
        return pl.ds(pl.multiple_of(b * BUCKET_SLOTS + c * HALF + i * CHUNK, CHUNK), CHUNK)

    core_spread = {}

    def spread(which, buf, b, i):
        part = buf.at[own_rows(b, i)]
        cp = remote(part, part, m.s_as.at[which, b, i], m.s_ar.at[which, b, i], core_dev)
        cp.start()
        core_spread.setdefault((which, b), []).append(cp)

    spread_done = set()

    def spread_end(which, b, i):
        if (which, b, i) not in spread_done:
            core_spread[(which, b)][i].wait_recv()
            spread_done.add((which, b, i))

    def as_it_lands(phase, b, chunk):
        for i in range(2):
            y_sent[(phase, b)][i].wait_recv()
            chunk(i)

    def row_mean(values):
        return jnp.mean(values, axis=1, keepdims=True)

    def add_row(at, values):
        m.acc[at : at + 1, 0 : values.shape[1]] += jnp.sum(values, axis=0, keepdims=True)

    def norm_one(b):

        def chunk(i):
            at = pl.ds(pl.multiple_of(i * CHUNK, CHUNK), CHUNK)
            rows = own_rows(b, i)
            residual = DEEP_ALPHA * m.tok[rows, :].astype(F32) + (arrived(0, b, at) + vecs[4:5, :])
            centred = residual - row_mean(residual)
            rstd = lax.rsqrt(row_mean(centred * centred) + NORM_EPSILON)
            hat = centred * rstd
            normed = hat * vecs[0:1, :] + vecs[1:2, :]
            m.nb[rows, :] = normed.astype(BF16)
            spread(0, m.nb, b, i)
            m.xh1[b, at, :] = hat
            m.rstd1[b, at, :] = jnp.broadcast_to(rstd, (CHUNK, LANES))
            m.held[b, at, :] = normed

        as_it_lands(0, b, chunk)

    def own_first(which, b, chunk):
        def rows_at(step):
            i = lax.rem(step + 2 * c, 4)
            return pl.ds(pl.multiple_of(b * BUCKET_SLOTS + i * CHUNK, CHUNK), CHUNK)

        def rest():
            for i in range(2):
                spread_end(which, b, i)
                chunk(rows_at(2 + i))

        loop(2, lambda step: chunk(rows_at(step)))
        return rest

    def feed(b):
        def chunk(rows):
            up = mm(m.nb[rows, :], m.wup[...]) + vecs[6:7, :]
            half_phi = 0.5 * (1.0 + lax.erf(up * INV_SQRT2))
            m.act[rows, :] = (up * half_phi).astype(BF16)
            m.gelup[rows, :] = half_phi + up * (jnp.exp(up * up * -0.5) * INV_SQRT_2PI)

        own_first(0, b, chunk)()

    out_copies = []

    def result_rows(which, b, stage, out):
        rows = pl.ds(pl.multiple_of(b * BUCKET_SLOTS + c * HALF, HALF), HALF)
        part = stage.at[b]
        here = pltpu.make_async_copy(part, out.at[rows], m.s_ol.at[which, b])
        there = remote(part, out.at[rows], m.s_os.at[which, b], m.s_or.at[which, b], core_dev)
        here.start()
        there.start()
        out_copies.append((here, there))

    def norm_two(b):
        cot_copies[b].wait()

        def chunk(i):
            at = pl.ds(pl.multiple_of(i * CHUNK, CHUNK), CHUNK)
            rows = own_rows(b, i)
            residual = DEEP_ALPHA * m.held[b, at, :] + (arrived(1, b, at) + vecs[5:6, :])
            centred = residual - row_mean(residual)
            rstd = lax.rsqrt(row_mean(centred * centred) + NORM_EPSILON)
            hat = centred * rstd
            upstream = m.cot[b, at, :].astype(F32)
            scaled = upstream * vecs[2:3, :]
            grad = rstd * (scaled - row_mean(scaled) - hat * row_mean(scaled * hat))
            low = grad.astype(BF16)
            m.gffn[rows, :] = low
            spread(1, m.gffn, b, i)
            m.held[b, at, :] = grad
            m.stage[b, at, :] = (hat * vecs[2:3, :] + vecs[3:4, :]).astype(BF16)
            add_row(2, upstream * hat)
            add_row(3, upstream)
            add_row(5, low.astype(F32))

        as_it_lands(1, b, chunk)
        result_rows(0, b, m.stage, bo_out)

    def feed_back(b):
        def chunk(rows):
            grad = mm(m.gffn[rows, :], m.wdown[...]) * m.gelup[rows, :]
            low = grad.astype(BF16)
            m.gub[rows, :] = low
            add_row(6, low.astype(F32))

        return own_first(1, b, chunk)

    def norm_one_back(b):

        def chunk(i):
            at = pl.ds(pl.multiple_of(i * CHUNK, CHUNK), CHUNK)
            rows = own_rows(b, i)
            upstream = arrived(2, b, at) + DEEP_ALPHA * m.held[b, at, :]
            hat = m.xh1[b, at, :]
            scaled = upstream * vecs[0:1, :]
            rstd = m.rstd1[b, at, 0:1]
            grad = rstd * (scaled - row_mean(scaled) - hat * row_mean(scaled * hat))
            low = grad.astype(BF16)
            m.gattn[rows, :] = low
            spread(2, m.gattn, b, i)
            m.held[b, at, :] = grad
            add_row(0, upstream * hat)
            add_row(1, upstream)
            add_row(4, low.astype(F32))

        as_it_lands(2, b, chunk)

    def gate_back(rows, grad):
        u = m.gu[rows, :]
        w = pltpu.roll(u, LANES - 8, 1)
        grad_u = jnp.where(head_lane, grad * (w * scale - 1.0) * u * (1.0 - u), 0.0)
        grad_w = jnp.where(head_lane, grad * u * scale * w * (1.0 - w), 0.0)
        add_row(8, jnp.where(head_lane, grad * u * w, 0.0))
        linear = grad_u + pltpu.roll(grad_w, 8, 1)
        add_row(9, linear)
        hi = linear.astype(BF16).astype(F32)
        mid = (linear - hi).astype(BF16).astype(F32)
        lo = (linear - hi - mid).astype(BF16).astype(F32)
        stacked = hi
        for at, part in enumerate((mid, lo, hi, mid, hi)):
            stacked = stacked + pltpu.roll(part, 16 * (at + 1), 1)
        m.dqkv[rows, qkv_pad : qkv_pad + LANES] = stacked.astype(BF16)

    def attend_back(b, hooks):
        keys = m.k[b * BUCKET_SLOTS : (b + 1) * BUCKET_SLOTS, :]
        values = m.vt[:, b * BUCKET_SLOTS : (b + 1) * BUCKET_SLOTS]

        def chunk(step):
            i = lax.rem(step + 2 * c, 4)
            local = pl.ds(pl.multiple_of(i * CHUNK, CHUNK), CHUNK)
            rows = pl.ds(pl.multiple_of(b * BUCKET_SLOTS + i * CHUNK, CHUNK), CHUNK)
            window = pl.ds(pl.multiple_of(BUCKET_SLOTS - i * CHUNK, CHUNK), BUCKET_SLOTS)
            place = pl.ds(pl.multiple_of(3 * CHUNK - i * CHUNK, CHUNK), BUCKET_SLOTS)
            grad_context = mm(m.gattn[rows, :], m.wo[...]).astype(BF16)
            m.dctxt[:, local] = grad_context.T
            gates = m.gate[rows, :]
            all_grads = mm(jnp.concatenate([grad_context * mask for mask in low_masks], axis=0), values)
            all_low = []
            grad_gates = jnp.zeros((CHUNK, LANES), F32)
            for h in range(heads):
                grad_probs = all_grads[h * CHUNK : (h + 1) * CHUNK, :]
                probability = m.prob[b * heads + h, local, :]
                inner = jnp.sum(grad_probs * probability, axis=1, keepdims=True)
                low = (probability * (grad_probs - inner)).astype(BF16)
                m.gsb[pl.ds(pl.multiple_of(h * BUCKET_SLOTS + i * CHUNK, CHUNK), CHUNK), :] = low
                all_low.append(low)
                rounded = low.astype(F32)
                one = jnp.sum(rounded * m.band[h, :, window], axis=1, keepdims=True)
                grad_gates = grad_gates + jnp.where(lane == h, one, 0.0)
                m.dband[h, :, place] += rounded * gates[:, h : h + 1]
            m.dqf[local, :] = by_head(mm(jnp.concatenate(all_low, axis=0), keys)) * 0.125
            gate_back(rows, grad_gates)

        hooked(0, 2, chunk, hooks)
        spread_end(2, b, 0)
        spread_end(2, b, 1)
        hooked(2, 2, chunk, hooks)
        all_rows = slice(b * BUCKET_SLOTS, (b + 1) * BUCKET_SLOTS)
        own_rows_of = lax.div(iota((head_cols, 1), 0), HD)
        row_masks = [jnp.where(own_rows_of == h, 1.0, 0.0).astype(BF16) for h in range(heads)]
        spread_out = lambda turned: jnp.concatenate([turned * mask for mask in row_masks], axis=1)
        grad_key = mm(spread_out(m.qt[:, all_rows]), m.gsb[...]).T
        probs = m.prob[b * heads : (b + 1) * heads].reshape(heads * BUCKET_SLOTS, BUCKET_SLOTS)
        grad_value = mm(spread_out(m.dctxt[...]), probs.astype(BF16)).T
        pad = jnp.zeros((BUCKET_SLOTS, qkv_pad - 3 * head_cols), F32)
        low = jnp.concatenate([m.dqf[...], grad_key, grad_value, pad], axis=1).astype(BF16)
        m.dqkv[all_rows, 0:qkv_pad] = low
        add_row(7, low.astype(F32))

    def input_part(rows):
        return mm(m.dqkv[rows, :], m.wqkvt[...])

    def token_rows(b):
        for cp in out_copies[b]:
            cp.wait()

        def chunk(i):
            at = pl.ds(pl.multiple_of(i * CHUNK, CHUNK), CHUNK)
            total = arrived(3, b, at) + DEEP_ALPHA * m.held[b, at, :]
            m.stage[b, at, :] = total.astype(BF16)

        as_it_lands(3, b, chunk)
        result_rows(1, b, m.stage, tg_out)

    def weight_grad(sent, left, right, put_part, rows=slice(None)):
        for which in sent:
            sent_all(which)

        def chunk(i):
            cols = pl.ds(pl.multiple_of(i * HALF, HALF), HALF)
            put_part(cols, mm_tn(left[rows, cols], right[rows, :]))

        loop(W // HALF, chunk)

    def add_whole(buf):
        def put_part(cols, part):
            buf[cols, :] = (buf[cols, :].astype(F32) + part).astype(BF16)

        return put_part

    def put_whole(buf):
        def put_part(cols, part):
            buf[cols, :] = part.astype(BF16)

        return put_part

    def put_qkv(cols, part):
        m.wqkv[cols, 0 : 3 * head_cols] = part[:, 0 : 3 * head_cols].astype(BF16)
        m.glin[cols, :] = part[:, qkv_pad : qkv_pad + LANES]

    def put_o(cols, part):
        m.wqkv[cols, 3 * head_cols : qkv_pad] = part[:, 0:first_o].astype(BF16)
        m.go[cols, :] = part[:, first_o:head_cols].astype(BF16)

    reduces = []

    def low_bit(k):
        return k & -k if k else nz

    bits = [1 << i for i in range(nz.bit_length() - 1)]
    slots = {}
    for k in range(nz):
        for bit in bits:
            if bit < low_bit(k):
                slots[(k, bit)] = len(slots)
    pass_order = sorted(range(nz), key=lambda k: (low_bit(k), -k))

    def add_landed(total, k, which, arrive):
        for bit in bits:
            if bit < low_bit(k):
                slot = slots[(k, bit)]
                here = arrive.at[slot]
                sems = m.s_zs.at[which, slot], m.s_zr.at[which, slot]
                remote(here, here, *sems, z_dev(bit)).wait_recv()
                total = total + arrive[slot].astype(F32)
        return total

    def reduce_start(which, buf, land, ks=None):
        for k in ks or pass_order:

            def where(k=k):
                rows = block(2 * z_at(k) + 1 - x)
                return buf.at[rows], land.at[k], m.s_xs.at[which, k], m.s_xr.at[which, k], x_dev

            launch(reduces, where)

    def reduce_block(k, which, buf, land, out, arrive, share):
        here = land.at[k]
        remote(here, here, m.s_xs.at[which, k], m.s_xr.at[which, k], x_dev).wait_recv()
        total = buf[block(2 * z_at(k) + x), :].astype(F32) + land[k].astype(F32)
        if k == 0:
            share[...] = total
        else:
            out[k - 1] = add_landed(total, k, which, arrive).astype(BF16)

            def where():
                bit = low_bit(k)
                slot = slots[(k - bit, bit)]
                sems = m.s_zs.at[which, slot], m.s_zr.at[which, slot]
                return out.at[k - 1], arrive.at[slot], *sems, z_dev(bit)

            launch(reduces, where)

    def reduce_pass(*matrix):
        for k in pass_order:
            reduce_block(k, *matrix)

    kept = [k for k in range(nz) if k % 2 == 0]
    x_slots = {k: i for i, k in enumerate(kept)}
    far_slots = {}
    for k in kept:
        for bit in bits[1:]:
            if bit < low_bit(k):
                far_slots[(k, bit)] = len(x_slots) + len(far_slots)

    def owner_rows(k, side):
        return block(2 * z_at(k) + (1 - x if side else x))

    def near_start(which, buf, land):
        for k in reversed(kept):
            for side in (1, 0):

                def where(k=k, side=side):
                    at = k + side
                    sems = m.s_xs.at[which, at], m.s_xr.at[which, at]
                    return buf.at[owner_rows(k + 1, side)], land.at[at], *sems, z_dev(1)

                launch(reduces, where)

    def near_total(k, side, which, buf, land):
        at = k + side
        here = land.at[at]
        remote(here, here, m.s_xs.at[which, at], m.s_xr.at[which, at], z_dev(1)).wait_recv()
        return buf[owner_rows(k, side), :].astype(F32) + land[at].astype(F32)

    def landed_slot(slot, which, arrive):
        here = arrive.at[slot]
        remote(here, here, m.s_zs.at[which, slot], m.s_zr.at[which, slot], x_dev).wait_recv()
        return arrive[slot].astype(F32)

    def near_across(k, which, buf, land, out, arrive, share):
        slot = x_slots[k]
        out[slot] = near_total(k, 1, which, buf, land).astype(BF16)

        def where():
            return out.at[slot], arrive.at[slot], m.s_zs.at[which, slot], m.s_zr.at[which, slot], x_dev

        launch(reduces, where)

    def near_far(k, which, buf, land, out, arrive, share):
        total = near_total(k, 0, which, buf, land) + landed_slot(x_slots[k], which, arrive)
        for bit in bits[1:]:
            if bit < low_bit(k):
                total = total + landed_slot(far_slots[(k, bit)], which, arrive)
        if k == 0:
            share[...] = total
            return
        bit = low_bit(k)
        slot = far_slots[(k - bit, bit)]
        out[slot] = total.astype(BF16)

        def where():
            sems = m.s_zs.at[which, slot], m.s_zr.at[which, slot]
            return out.at[slot], arrive.at[slot], *sems, z_dev(bit)

        launch(reduces, where)

    def squares_of(total):
        squares = total * total
        folded = jnp.zeros((owned, LANES), F32)
        for i in range(total.shape[1] // LANES):
            folded = folded + squares[:, i * LANES : (i + 1) * LANES]
        tile = jnp.zeros((8, LANES), F32)
        for i in range(owned // 8):
            tile = tile + folded[8 * i : 8 * i + 8, :]
        return tile

    def reduce_end(which, arrive, share):
        total = add_landed(share[...], 0, which, arrive)
        share[...] = total
        return squares_of(total)

    def pass_on(which):
        line_step(which, 1, 2)
        line_step(which, 2, 2)

    def pass_last(which):
        for step in range(3, nz):
            line_step(which, step, 2)

    line_start(4, 2)
    gather_x(4)

    pass_last(2)

    def first_pass():
        line_start(5, 2)
        gather_x(5)

    def second_pass():
        pass_on(3)
        partner_landed(6)
        line_start(6, 2)
        line_start(7, 2)

    attend(0, {0: first_pass, 2: second_pass})
    line_end(2)
    m.wo[...] = jnp.concatenate([m.wqkv[:, 3 * head_cols : qkv_pad], m.wo1[...]], axis=1)
    turn(m.wo, m.wot)
    out_product = lambda rows: mm(m.ctx[rows, :], m.wot[...])
    exchange(0, 0, out_product)
    pass_last(3)
    attend(1, {1: lambda: pass_on(4), 3: lambda: pass_last(4)})
    exchange(0, 1, out_product)
    pass_on(5)
    pass_on(6)
    norm_one(0)
    pass_last(5)
    pass_on(7)
    line_end(3)
    line_end(4)
    feed(0)
    pass_last(6)
    pass_last(7)
    line_end(5)
    turn(m.wdown, m.wdownt)
    down_product = lambda rows: mm(m.act[rows, :], m.wdownt[...])
    exchange(1, 0, down_product)
    norm_one(1)
    feed(1)
    exchange(1, 1, down_product)
    turn(m.wup, m.wupt)
    turn(m.wqkv, m.wqkvt)
    up_product = lambda rows: mm(m.gub[rows, :], m.wupt[...])
    norm_two(0)
    feed_back(0)()
    exchange(2, 0, up_product)
    first_rows, last_rows = slice(0, BUCKET_SLOTS), slice(BUCKET_SLOTS, 2 * BUCKET_SLOTS)
    weight_grad((), m.gffn, m.act, put_whole(m.wdownt), first_rows)
    weight_grad((3, 4), m.nb, m.gub, put_whole(m.wup), first_rows)
    norm_two(1)
    feed_rest = feed_back(1)
    spread_end(1, 1, 0)
    spread_end(1, 1, 1)
    weight_grad((), m.gffn, m.act, add_whole(m.wdownt), last_rows)
    half = hidden // 2
    left, right = m.wdownt.at[:, 0:half], m.wdownt.at[:, half:hidden]
    down = (0, left, m.xrdown, m.zsdown, m.zrdown, sh_down.at[:, 0:half])
    down_near = (4, right, m.xrdownb, m.zsdownb, m.zrdownb, sh_down.at[:, half:hidden])
    near_start(4, right, m.xrdownb)
    reduce_start(0, left, m.xrdown)
    feed_rest()
    exchange(2, 1, up_product)
    weight_grad((), m.nb, m.gub, add_whole(m.wup), last_rows)
    odd, even = pass_order[: nz // 2], pass_order[nz // 2 :]
    up = (1, m.wup, m.xrup, m.zsup, m.zrup, sh_up)
    out = (2, m.go, m.xro, m.zso, m.zro, sh_o)
    qkv = (3, m.wqkv, m.xrqkv, m.zsqkv, m.zrqkv, sh_qkv)
    norm_one_back(0)
    near_across(2, *down_near)
    reduce_start(1, m.wup, m.xrup, odd)
    blocks = lambda ks, matrix: lambda: [reduce_block(k, *matrix) for k in ks] and None
    early = [pass_order[0:1], pass_order[1:2], pass_order[2:-1]]

    def second_across():
        near_across(0, *down_near)
        reduce_start(1, m.wup, m.xrup, even)

    attend_back(
        0,
        {
            1: second_across,
            2: blocks(early[0], down),
            3: blocks(early[1], down),
        },
    )
    exchange_first(3, 0, input_part)
    near_far(2, *down_near)
    blocks(early[0], up)()
    norm_one_back(1)
    exchange_last(3, 0)
    spread_end(2, 1, 0)
    spread_end(2, 1, 1)
    weight_grad((0, 1, 2), m.gattn, m.ctx, put_o)
    blocks(early[1], up)()
    downward = list(range(nz - 1, -1, -1))
    reduce_start(2, m.go, m.xro, downward)
    attend_back(
        1,
        {
            0: blocks(early[2] + [0], down),
            3: blocks(early[2], up),
        },
    )
    weight_grad((), m.tok, m.dqkv, put_qkv)
    first_part, last_part = downward[:-1], downward[-1:]
    reduce_start(3, m.wqkv, m.xrqkv, first_part)
    reduce_block(0, *up)
    reduce_block(downward[0], *out)

    sm = m.sm
    sm[...] = jnp.zeros((SUM_ROWS, LANES), F32)
    acc = m.acc
    lead = jnp.where(yy == 0, 1.0, 0.0)

    def put(first, values):
        for i in range(values.shape[1] // LANES):
            sm[first + i : first + i + 1, :] = values[:, i * LANES : (i + 1) * LANES]

    def spot(values):
        return jnp.concatenate([jnp.where(T == t, values, 0.0) for t in range(4)], axis=1)

    for at, first in ((0, 0), (1, 6), (2, 12), (3, 18), (4, 36), (5, 42)):
        put(first, acc[at : at + 1, :] * lead)
    put(24, spot(acc[7:8, 0:head_cols]))
    put(30, spot(acc[7:8, 2 * head_cols : 3 * head_cols]))
    put(48, spot(acc[6:7, 0:hidden]))
    parts = []
    for h in range(heads):
        size = LANES // 2
        left = m.dband[h]
        while size >= 8:
            left = left[0:size, :] + pltpu.roll(left[size : 2 * size, :], long_row - size, 1)
            size //= 2
        for bit in (1, 2, 4):
            left = jnp.where(lax.rem(lax.div(sub8, bit), 2) == 1, pltpu.roll(left, long_row - bit, 1), left)
        left = pltpu.roll(left, LANES - 1, 1)
        diagonal = jnp.sum(left, axis=0, keepdims=True)
        hi = diagonal.astype(BF16).astype(F32)
        mid = (diagonal - hi).astype(BF16).astype(F32)
        parts += [hi, mid, diagonal - hi - mid]
    parts = jnp.concatenate(parts + [jnp.zeros((16 - len(parts), long_row), F32)], axis=0).astype(BF16)
    bucket_rows = -(-NB // LANES) * LANES
    valid = iota((1, long_row), 1) < long_row - 1
    hot_bucket = jnp.where((iota((bucket_rows, long_row), 0) == offsets) & valid, 1.0, 0.0).astype(BF16)
    by_bucket = mm_nt(parts, hot_bucket)
    bucket = iota((1, bucket_rows), 1)
    table_grad = jnp.zeros((32, LANES), F32)
    for h in range(heads):
        sums = by_bucket[3 * h : 3 * h + 1] + by_bucket[3 * h + 1 : 3 * h + 2] + by_bucket[3 * h + 2 : 3 * h + 3]
        flat = bucket * H + (T * heads + h)
        hot_row = jnp.where((iota((32, bucket_rows), 0) == lax.div(flat, LANES)) & (bucket < NB), 1.0, 0.0)
        hot_lane = jnp.where(iota((LANES, bucket_rows), 0) == lax.rem(flat, LANES), sums, 0.0)
        table_grad = table_grad + exact_nt(hot_row, hot_lane)
    sm[TABLE_ROW : TABLE_ROW + 30, :] = table_grad[0:30, :]

    lin_grad = m.glin[...]
    lin_grad = lin_grad + pltpu.roll(lin_grad, LANES - 16, 1) + pltpu.roll(lin_grad, LANES - 32, 1)
    lin_grad = jnp.where(own_head, lin_grad, 0.0)
    grad_u = jnp.sum(jnp.where(col_lane < 8, lin_grad, 0.0), axis=1, keepdims=True)
    grad_w = jnp.sum(jnp.where(col_lane >= 8, lin_grad, 0.0), axis=1, keepdims=True)
    by_lane = jnp.where(col_lane == 2 * col_in_head, grad_u, 0.0)
    by_lane = by_lane + jnp.where(col_lane == 2 * col_in_head + 1, grad_w, 0.0)
    sm[GATE_ROW : GATE_ROW + 1, :] = jnp.sum(by_lane, axis=0, keepdims=True)
    lin_total = acc[9:10, 0:LANES]
    total_u = jnp.sum(jnp.where(lane < 8, lin_total, 0.0), axis=1, keepdims=True)
    total_w = jnp.sum(jnp.where((lane >= 8) & (lane < 16), lin_total, 0.0), axis=1, keepdims=True)
    last = jnp.where(lane == 0, total_u, 0.0) + jnp.where(lane == 1, total_w, 0.0)
    scale_grad = acc[8:9, 0:LANES]
    for h in range(heads):
        one = jnp.sum(jnp.where(lane == h, scale_grad, 0.0), axis=1, keepdims=True)
        last = last + jnp.where(lane == 2 + T * heads + h, one, 0.0)
    sm[OFFSET_ROW : OFFSET_ROW + 1, :] = last

    small_sent = []

    def small_send(at, source, target, dev):
        cp = remote(source, target, m.s_ms.at[at], m.s_mr.at[at], dev)
        cp.start()
        small_sent.append(cp)
        return cp

    def quarter(index):
        return pl.ds(pl.multiple_of(index * QUARTER, QUARTER), QUARTER)

    to_core = [small_send(i, sm.at[quarter(2 * i + 1 - c)], m.smc.at[i], core_dev) for i in range(2)]
    for i in range(2):
        to_core[i].wait_recv()
        m.smh[i] = sm[quarter(2 * i + c), :] + m.smc[i]
    to_y = small_send(2, m.smh.at[1 - yy], m.smy, y_dev)
    reduce_block(first_part[0], *qkv)
    exchange_first(3, 1, input_part)
    reduce_block(downward[1], *out)
    exchange_last(3, 1)
    to_y.wait_recv()
    m.smv[...] = m.smh[yy] + m.smy[...]
    to_x = small_send(3, m.smv, m.smx, x_dev)
    reduce_start(3, m.wqkv, m.xrqkv, last_part)
    for k in downward[2:]:
        reduce_block(k, *out)
    reduce_block(first_part[1], *qkv)
    to_x.wait_recv()
    m.smz[z] = m.smv[...] + m.smx[...]
    for k in range(1, nz):
        small_send(3 + k, m.smz.at[z], m.smz.at[z], z_dev(k))
    for k in first_part[2:]:
        reduce_block(k, *qkv)
    token_rows(0)
    reduce_block(0, *qkv)
    squares = reduce_end(0, m.zrdown, sh_down.at[:, 0:half])
    near_far(0, *down_near)
    squares = squares + squares_of(sh_down[:, half:hidden])
    squares = squares + reduce_end(1, m.zrup, sh_up)
    squares = squares + reduce_end(2, m.zro, sh_o)
    for k in range(1, nz):
        here = m.smz.at[z_at(k)]
        remote(here, here, m.s_ms.at[3 + k], m.s_mr.at[3 + k], z_dev(k)).wait_recv()
    own_quarter = m.smz[0]
    for i in range(1, nz):
        own_quarter = own_quarter + m.smz[i]
    m.sma[quarter(T), :] = own_quarter
    for k in range(1, 4):
        mine_small = m.sma.at[quarter(T)]
        small_send(2 + nz + k, mine_small, mine_small, (D, lax.rem(T + k, 4)))
    squares = squares + reduce_end(3, m.zrqkv, sh_qkv)
    last_copies = []
    for i, (source, target) in enumerate(
        ((sh_down, out_down), (sh_up, out_up), (sh_o, out_o), (sh_qkv, out_qkv))
    ):
        cp = pltpu.make_async_copy(source, target, m.s_out.at[i])
        cp.start()
        last_copies.append(cp)
    sqt = m.sqt
    sqt[T] = squares
    tail_sent = []
    for k in range(1, 4):
        cp = remote(
            sqt.at[T], sqt.at[T], m.s_ts.at[k], m.s_tr.at[k], (D, lax.rem(T + k, 4))
        )
        cp.start()
        tail_sent.append(cp)
    token_rows(1)
    for k in range(1, 4):
        here = m.sma.at[quarter(lax.rem(T + 4 - k, 4))]
        remote(here, here, m.s_ms.at[2 + nz + k], m.s_mr.at[2 + nz + k], core_dev).wait_recv()
    small_total = m.sma[0:SMALL_ROWS, :]
    for i in range(3):
        small_out[i] = small[i * SMALL_ROWS : (i + 1) * SMALL_ROWS, :]
    small_out[3] = small_total
    cp = pltpu.make_async_copy(small_out, out_small, m.s_out.at[4])
    cp.start()
    last_copies.append(cp)
    small_square = small_total * small_total
    small_tile = jnp.zeros((8, LANES), F32)
    for i in range(SMALL_ROWS // 8):
        small_tile = small_tile + small_square[8 * i : 8 * i + 8, :]
    for k in range(1, 4):
        here = sqt.at[lax.rem(T + 4 - k, 4)]
        remote(here, here, m.s_ts.at[k], m.s_tr.at[k], core_dev).wait_recv()
    sqd = m.sqd
    sqd[D] = sqt[0] + sqt[1] + sqt[2] + sqt[3]
    for k in range(1, n_dp):
        cp = remote(
            sqd.at[D], sqd.at[D], m.s_ds.at[k], m.s_dr.at[k], (lax.rem(D + k, n_dp), T)
        )
        cp.start()
        tail_sent.append(cp)
    for k in range(1, n_dp):
        here = sqd.at[lax.rem(D + n_dp - k, n_dp)]
        remote(here, here, m.s_ds.at[k], m.s_dr.at[k], core_dev).wait_recv()
    everything = small_tile
    for i in range(n_dp):
        everything = everything + sqd[i]
    sum_all = jnp.sum(jnp.sum(everything, axis=0, keepdims=True), axis=1, keepdims=True)
    norm_out[...] = jnp.broadcast_to(jnp.sqrt(sum_all), (8, LANES))

    for which in list(gathers):
        sent_all(which)
    for where in reduces:
        remote(*where()).wait_send()
    for cp in small_sent + tail_sent:
        cp.wait_send()
    for sent in core_spread.values():
        for cp in sent:
            cp.wait_send()
    for b in range(2):
        for cp in core_sent[(3, b)] + y_sent[(3, b)]:
            cp.wait_send()
    for cp in last_copies:
        cp.wait()
    for here, there in out_copies[2:]:
        here.wait()
        there.wait()


def adam_kernel(head_cols, *refs):
    ins, rest = refs[:14], refs[14:]
    block_in, token_in = ins[12:14]
    outs, rest = rest[:14], rest[14:]
    norm_out, block_out, token_out = outs[0], outs[12], outs[13]
    held, made = rest[:12], rest[12:24]
    block_held, token_held, s_in, s_out = rest[24:]
    loads = [pltpu.make_async_copy(ins[i], held[i], s_in.at[i]) for i in range(12)]
    passing = [
        pltpu.make_async_copy(block_in, block_held, s_in.at[12]),
        pltpu.make_async_copy(token_in, token_held, s_in.at[13]),
    ]
    passed = [
        pltpu.make_async_copy(block_held, block_out, s_out.at[12]),
        pltpu.make_async_copy(token_held, token_out, s_out.at[13]),
    ]
    for cp in loads + passing:
        cp.start()
    stores = []

    def store(i):
        cp = pltpu.make_async_copy(made[i], outs[i], s_out.at[i])
        cp.start()
        stores.append(cp)

    sh_qkv, sh_o, sh_up, sh_down, sh_small, norm, aw, am, av, fw, fm, fv = held
    (o_norm, o_am, o_av, o_aw, o_ac, o_fm, o_fv, o_fw, o_fc, o_sm, o_sv, o_sw) = made
    for i in (0, 1, 2, 3, 5):
        loads[i].wait()
    length = norm[0:1, 0:1]
    factor = CLIP_LIMIT / jnp.maximum(length, CLIP_LIMIT)
    o_norm[...] = length
    store(0)
    for i in (6, 7, 8):
        loads[i].wait()
    for i in range(4):
        if i < 3:
            grad = sh_qkv[:, i * head_cols : (i + 1) * head_cols]
        else:
            grad = jnp.concatenate([sh_qkv[:, 3 * head_cols :], sh_o[...]], axis=1)
        moment, square, master = adam_step(
            aw[i], am[i], av[i], factor * grad, RATE_MATRIX, WEIGHT_DECAY
        )
        o_am[i] = moment
        o_av[i] = square
        o_aw[i] = master
        o_ac[i] = master.astype(BF16)
    for i in (1, 2, 3, 4):
        store(i)
    for first, second in zip(passing, passed, strict=True):
        first.wait()
        second.start()
    for i in (9, 10, 11):
        loads[i].wait()
    for i, share in enumerate((sh_up, sh_down)):
        moment, square, master = adam_step(
            fw[i], fm[i], fv[i], factor * share[...], RATE_MATRIX, WEIGHT_DECAY
        )
        o_fm[i] = moment
        o_fv[i] = square
        o_fw[i] = master
        o_fc[i] = master.astype(BF16)
    for i in (5, 6, 7, 8):
        store(i)
    loads[4].wait()
    moment, square, master = adam_step(
        sh_small[0], sh_small[1], sh_small[2], factor * sh_small[3], RATE_SMALL, 0.0
    )
    o_sm[...] = moment
    o_sv[...] = square
    o_sw[...] = master
    for i in (9, 10, 11):
        store(i)
    for cp in stores + passed:
        cp.wait()


def fused_body(
    n_dp,
    tokens,
    cotangent,
    clip_lengths,
    key_mask,
    rel_buckets,
    attention_weights,
    attention_first,
    attention_second,
    feedforward_weights,
    feedforward_first,
    feedforward_second,
    small_params,
    small_first,
    small_second,
):
    rows = tokens.shape[0]
    owned, head_cols = attention_weights.shape[1:]
    hidden = feedforward_weights.shape[2]
    heads = head_cols // HD
    qkv_pad = -(-3 * head_cols // LANES) * LANES
    nz = n_dp // 2
    small_size = SMALL_ROWS * LANES
    total_size = 3 * small_size + 2 * BUCKET_SLOTS
    packed = jnp.zeros((total_size,), F32)
    pieces = (small_params, small_first, small_second, rel_buckets.astype(F32))
    for i, values in enumerate(pieces):
        after = total_size - i * small_size - values.shape[0]
        packed = packed + jnp.pad(values, (i * small_size, after))
    packed = packed.reshape(-1, LANES)
    keep = key_mask.reshape(rows // LANES, LANES)
    scratch = layer_scratch(owned, nz, qkv_pad, heads, head_cols, hidden)
    names = tuple(scratch)
    vmem = pl.BlockSpec(memory_space=pltpu.VMEM)
    smem = pl.BlockSpec(memory_space=pltpu.SMEM)
    anywhere = pl.BlockSpec(memory_space=pl.ANY)
    sds = jax.ShapeDtypeStruct
    block_rows, token_rows, sh_qkv, sh_o, sh_up, sh_down, sh_small, norm = pl.pallas_call(
        partial(layer_kernel, names, (n_dp, owned, qkv_pad, heads, head_cols, hidden)),
        out_shape=(
            sds((rows, W), BF16),
            sds((rows, W), BF16),
            sds((owned, qkv_pad), F32),
            sds((owned, LANES), F32),
            sds((owned, hidden), F32),
            sds((owned, hidden), F32),
            sds((4, SMALL_ROWS, LANES), F32),
            sds((8, LANES), F32),
        ),
        in_specs=[anywhere, anywhere, smem] + [anywhere] * 4,
        out_specs=(anywhere,) * 7 + (vmem,),
        scratch_shapes=list(scratch.values()),
        compiler_params=pltpu.CompilerParams(
            collective_id=1, has_side_effects=True, vmem_limit_bytes=62 * 1024 * 1024
        ),
        name="layer",
    )(tokens, cotangent, clip_lengths, keep, attention_weights, feedforward_weights, packed)
    like = lambda a, dtype=F32: sds(a.shape, dtype)
    small_like = sds((SMALL_ROWS, LANES), F32)
    made = (
        sds((1, 1), F32),
        like(attention_weights),
        like(attention_weights),
        like(attention_weights),
        like(attention_weights, BF16),
        like(feedforward_weights),
        like(feedforward_weights),
        like(feedforward_weights),
        like(feedforward_weights, BF16),
        small_like,
        small_like,
        small_like,
    )
    operands = (
        sh_qkv,
        sh_o,
        sh_up,
        sh_down,
        sh_small,
        norm,
        attention_weights,
        attention_first,
        attention_second,
        feedforward_weights,
        feedforward_first,
        feedforward_second,
        block_rows,
        token_rows,
    )
    in_vmem = lambda a: pltpu.VMEM(a.shape, a.dtype)
    results = pl.pallas_call(
        partial(adam_kernel, head_cols),
        out_shape=(*made, like(tokens, BF16), like(tokens, BF16)),
        in_specs=[anywhere] * len(operands),
        out_specs=(anywhere,) * (len(made) + 2),
        scratch_shapes=[in_vmem(a) for a in operands[:12]]
        + [in_vmem(a) for a in made]
        + [in_vmem(tokens), in_vmem(tokens)]
        + [pltpu.SemaphoreType.DMA((14,)), pltpu.SemaphoreType.DMA((14,))],
        compiler_params=pltpu.CompilerParams(vmem_limit_bytes=62 * 1024 * 1024),
        name="adam",
    )(*operands)
    length = small_params.shape[0]
    flat = lambda a: a.reshape(-1)[:length]
    return (
        results[0].reshape(()),
        *results[1:9],
        flat(results[9]),
        flat(results[10]),
        flat(results[11]),
        *results[12:],
    )


def fused_fits(mesh, owned):
    columns = mesh.shape["dp"] // 2
    whole = mesh.shape["dp"] % 2 == 0 and columns & (columns - 1) == 0
    return mesh.shape["tensor"] == 4 and whole and owned % 16 == 0

def solution(mesh):
    in_specs = (
        P("dp", None),
        P("dp", None),
        P("dp", None),
        P("dp"),
        P(),
        P(None, "dp", "tensor"),
        P(None, "dp", "tensor"),
        P(None, "dp", "tensor"),
        P(None, "dp", "tensor"),
        P(None, "dp", "tensor"),
        P(None, "dp", "tensor"),
        P(),
        P(),
        P(),
    )
    out_specs = (
        P(),
        P(None, "dp", "tensor"),
        P(None, "dp", "tensor"),
        P(None, "dp", "tensor"),
        P(None, "dp", "tensor"),
        P(None, "dp", "tensor"),
        P(None, "dp", "tensor"),
        P(None, "dp", "tensor"),
        P(None, "dp", "tensor"),
        P(),
        P(),
        P(),
        P("dp", None),
        P("dp", None),
    )
    n_dp = mesh.shape["dp"]
    body = general_body
    if fused_fits(mesh, MODEL_WIDTH // n_dp):
        body = partial(fused_body, n_dp)
    return jax.shard_map(body, mesh=mesh, in_specs=in_specs, out_specs=out_specs, check_vma=False)
```

```python
from functools import partial
from types import SimpleNamespace

import jax
import jax.numpy as jnp
from jax import lax
from jax.experimental import pallas as pl
from jax.experimental.pallas import tpu as pltpu
from jax.sharding import PartitionSpec as P

MODEL_WIDTH = 768
H = 12
HD = 64
FF = 3072
NB = 320
BUCKET_SLOTS = 512
CLIPS = 8
STEP = 5


FULL_PRECISION = lax.Precision.HIGHEST
DEEP_ALPHA = 24.0**0.25
NORM_EPSILON = 1e-05
MASK_VALUE = -1e30
BETA_FIRST = 0.9
BETA_SECOND = 0.98
RATE_MATRIX = 0.03
RATE_SMALL = 0.5
WEIGHT_DECAY = 0.01
ADAM_EPSILON = 1e-08
CLIP_LIMIT = 0.1


def layer_norm(values, norm_gain, norm_shift):
    row_mean = jnp.mean(values, axis=-1, keepdims=True)
    centred = values - row_mean
    variance = jnp.mean(centred * centred, axis=-1, keepdims=True)
    return centred * lax.rsqrt(variance + NORM_EPSILON) * norm_gain + norm_shift


def gelu_exact(values):
    return jax.nn.gelu(values, approximate=False)


def split_small(vector):
    widths = [MODEL_WIDTH] * 8 + [FF, NB * H, HD * 2, 2, H]
    pieces = []
    offset = 0
    for extent in widths:
        pieces.append(vector[offset : offset + extent])
        offset += extent
    return pieces


def allowed_mask(lengths_row, keep_row):
    positions = jnp.arange(BUCKET_SLOTS, dtype=jnp.int32)
    clip_ends = jnp.cumsum(lengths_row)
    segment = jnp.sum((positions[:, None] >= clip_ends[None, :]).astype(jnp.int32), axis=1)
    live_keys = (keep_row == 1) & (segment < CLIPS)
    same_clip = segment[:, None] == segment[None, :]
    return same_clip & (live_keys[None, :] | (positions[:, None] == positions[None, :]))


def band_matrix(diagonals):
    head_count = diagonals.shape[0]
    length = (diagonals.shape[1] + 1) // 2
    padded = jnp.concatenate([diagonals, jnp.zeros((head_count, 1), diagonals.dtype)], axis=1)
    repeated = jnp.tile(padded, (1, length))
    folded = repeated[:, : length * (2 * length - 1)].reshape(head_count, length, 2 * length - 1)
    return folded[:, :, length - 1 :]


def position_terms(head_inputs, gate_matrix, gate_offset, scale_local, table_local, rel_buckets):
    linear = (
        jnp.einsum(
            "blhd,dk->bhlk", head_inputs, gate_matrix.reshape(HD, 2), precision=FULL_PRECISION
        )
        + gate_offset
    )
    sigmoid = jax.nn.sigmoid(linear)
    gate = sigmoid[..., 0] * (sigmoid[..., 1] * scale_local[None, :, None] - 1.0) + 2.0
    onehot = (rel_buckets[:, None] == jnp.arange(NB, dtype=jnp.int32)[None, :]).astype(jnp.float32)
    per_offset = jnp.dot(
        onehot, table_local, precision=FULL_PRECISION, preferred_element_type=jnp.float32
    )
    toeplitz = band_matrix(per_offset.T)
    return gate[..., None] * toeplitz[None]


def adam_step(weights, moment, second, gradient, step_rate, decay_rate):
    moment_new = BETA_FIRST * moment + (1.0 - BETA_FIRST) * gradient
    second_new = BETA_SECOND * second + (1.0 - BETA_SECOND) * gradient * gradient
    moment_hat = moment_new / (1.0 - BETA_FIRST**STEP)
    second_hat = second_new / (1.0 - BETA_SECOND**STEP)
    master = weights - step_rate * (
        moment_hat / (jnp.sqrt(second_hat) + ADAM_EPSILON) + decay_rate * weights
    )
    return (moment_new, second_new, master)


def placed(total_length, piece, start):
    return lax.dynamic_update_slice_in_dim(jnp.zeros((total_length,), jnp.float32), piece, start, 0)


def column_sum(values):
    return jnp.sum(values.astype(jnp.float32), axis=0)


def general_body(
    tokens,
    cotangent,
    clip_lengths,
    key_mask,
    rel_buckets,
    attention_weights,
    attention_first,
    attention_second,
    feedforward_weights,
    feedforward_first,
    feedforward_second,
    small_params,
    small_first,
    small_second,
):
    gathered_attention, gathered_forward = (
        lax.all_gather(attention_weights.astype(jnp.bfloat16), "dp", axis=1, tiled=True),
        lax.all_gather(feedforward_weights.astype(jnp.bfloat16), "dp", axis=1, tiled=True),
    )
    query_weight = gathered_attention[0]
    key_weight = gathered_attention[1]
    value_weight = gathered_attention[2]
    output_weight = gathered_attention[3]
    up_weight = gathered_forward[0]
    down_weight = gathered_forward[1]
    head_cols = query_weight.shape[1]
    heads_local = head_cols // HD
    hidden_local = up_weight.shape[1]
    tensor_rank = lax.axis_index("tensor")
    col_start = tensor_rank * head_cols
    head_start = tensor_rank * heads_local
    hidden_start = tensor_rank * hidden_local
    row_count = tokens.shape[0]
    bucket_count = row_count // BUCKET_SLOTS
    (
        gain_one,
        shift_one,
        gain_two,
        shift_two,
        bias_query,
        bias_value,
        bias_output,
        bias_down,
        bias_up,
        rel_table,
        gate_matrix,
        gate_offset,
        gate_scale,
    ) = split_small(small_params)
    local_bias_query = lax.dynamic_slice_in_dim(bias_query, col_start, head_cols)
    local_bias_value = lax.dynamic_slice_in_dim(bias_value, col_start, head_cols)
    local_bias_up = lax.dynamic_slice_in_dim(bias_up, hidden_start, hidden_local)
    scale_local = lax.dynamic_slice_in_dim(gate_scale, head_start, heads_local)
    table_local = lax.dynamic_slice_in_dim(rel_table.reshape(NB, H), head_start, heads_local, 1)
    allowed = jax.vmap(allowed_mask)(clip_lengths, key_mask.reshape(bucket_count, BUCKET_SLOTS))[
        :, None
    ]
    leading = (tensor_rank == 0).astype(jnp.float32)
    inputs = tokens.astype(jnp.float32)
    upstream = cotangent.astype(jnp.float32)
    query_bf = (
        jnp.dot(tokens, query_weight, preferred_element_type=jnp.float32) + local_bias_query
    ).astype(jnp.bfloat16)
    key_bf = jnp.dot(tokens, key_weight, preferred_element_type=jnp.float32).astype(jnp.bfloat16)
    value_bf = (
        jnp.dot(tokens, value_weight, preferred_element_type=jnp.float32) + local_bias_value
    ).astype(jnp.bfloat16)
    head_shape = (bucket_count, BUCKET_SLOTS, heads_local, HD)
    heads_of_query = query_bf.reshape(head_shape)
    heads_of_key = key_bf.reshape(head_shape)
    heads_of_value = value_bf.reshape(head_shape)
    head_inputs = lax.dynamic_slice_in_dim(inputs, col_start, head_cols, 1).reshape(head_shape)
    extra, pull_position = jax.vjp(
        partial(position_terms, rel_buckets=rel_buckets),
        head_inputs,
        gate_matrix,
        gate_offset,
        scale_local,
        table_local,
    )
    attention_logits = (
        jnp.einsum(
            "blhd,bmhd->bhlm", heads_of_query, heads_of_key, preferred_element_type=jnp.float32
        )
        * 0.125
    )
    scores = jnp.where(allowed, attention_logits + extra, MASK_VALUE)
    row_max = jnp.max(scores, axis=-1, keepdims=True)
    exponent = jnp.exp(scores - row_max)
    denominator = jnp.sum(exponent, axis=-1, keepdims=True)
    log_total = row_max + jnp.log(denominator)
    probs_bf = (exponent / denominator).astype(jnp.bfloat16)
    context_bf = (
        jnp.einsum("bhlm,bmhd->blhd", probs_bf, heads_of_value, preferred_element_type=jnp.float32)
        .reshape(row_count, head_cols)
        .astype(jnp.bfloat16)
    )
    attention_part = jnp.einsum(
        "nw,dw->nd", context_bf, output_weight, preferred_element_type=jnp.float32
    )
    attention = lax.psum(attention_part, "tensor") + bias_output
    normed, pull_norm_one = jax.vjp(
        layer_norm, DEEP_ALPHA * inputs + attention, gain_one, shift_one
    )
    normed_bf = normed.astype(jnp.bfloat16)
    up_pre = jnp.dot(normed_bf, up_weight, preferred_element_type=jnp.float32) + local_bias_up
    activated, pull_gelu = jax.vjp(gelu_exact, up_pre)
    activated_bf = activated.astype(jnp.bfloat16)
    down_part = jnp.einsum(
        "nf,df->nd", activated_bf, down_weight, preferred_element_type=jnp.float32
    )
    feedforward = lax.psum(down_part, "tensor") + bias_down
    output_values, pull_norm_two = jax.vjp(
        layer_norm, DEEP_ALPHA * normed + feedforward, gain_two, shift_two
    )
    block_output = output_values.astype(jnp.bfloat16)
    grad_res_two, grad_gain_two, grad_shift_two = pull_norm_two(upstream)
    grad_ffn_share = grad_res_two.astype(jnp.bfloat16)
    grad_bias_down = column_sum(grad_ffn_share)
    down_grad = jnp.einsum(
        "nd,nf->df", grad_ffn_share, activated_bf, preferred_element_type=jnp.float32
    )
    grad_activated = jnp.einsum(
        "nd,df->nf", grad_ffn_share, down_weight, preferred_element_type=jnp.float32
    )
    (grad_up_pre,) = pull_gelu(grad_activated)
    grad_up_bf = grad_up_pre.astype(jnp.bfloat16)
    grad_bias_up = column_sum(grad_up_bf)
    up_grad = jnp.einsum("nd,nf->df", normed_bf, grad_up_bf, preferred_element_type=jnp.float32)
    normed_part = jnp.einsum("nf,df->nd", grad_up_bf, up_weight, preferred_element_type=jnp.float32)
    normed_sum = lax.psum(normed_part, "tensor")
    grad_normed = normed_sum + DEEP_ALPHA * grad_res_two
    grad_res_one, grad_gain_one, grad_shift_one = pull_norm_one(grad_normed)
    grad_attention_share = grad_res_one.astype(jnp.bfloat16)
    grad_bias_output = column_sum(grad_attention_share)
    output_grad = jnp.einsum(
        "nd,nw->dw", grad_attention_share, context_bf, preferred_element_type=jnp.float32
    )
    grad_context_bf = jnp.einsum(
        "nd,dw->nw", grad_attention_share, output_weight, preferred_element_type=jnp.float32
    ).astype(jnp.bfloat16)
    grad_heads = grad_context_bf.reshape(head_shape)
    attention_probabilities = jnp.exp(scores - log_total)
    recomputed_bf = attention_probabilities.astype(jnp.bfloat16)
    grad_probs = jnp.einsum(
        "blhd,bmhd->bhlm", grad_heads, heads_of_value, preferred_element_type=jnp.float32
    )
    inner = jnp.sum(grad_probs * attention_probabilities, axis=-1, keepdims=True)
    grad_scores_bf = (attention_probabilities * (grad_probs - inner)).astype(jnp.bfloat16)
    grad_query = (
        (
            jnp.einsum(
                "bhlm,bmhd->blhd", grad_scores_bf, heads_of_key, preferred_element_type=jnp.float32
            )
            * 0.125
        )
        .astype(jnp.bfloat16)
        .reshape(row_count, head_cols)
    )
    grad_key = (
        (
            jnp.einsum(
                "bhlm,blhd->bmhd",
                grad_scores_bf,
                heads_of_query,
                preferred_element_type=jnp.float32,
            )
            * 0.125
        )
        .astype(jnp.bfloat16)
        .reshape(row_count, head_cols)
    )
    grad_value = (
        jnp.einsum("bhlm,blhd->bmhd", recomputed_bf, grad_heads, preferred_element_type=jnp.float32)
        .astype(jnp.bfloat16)
        .reshape(row_count, head_cols)
    )
    grad_head_inputs, grad_gate_matrix, grad_gate_offset, grad_scale_local, grad_table_local = (
        pull_position(grad_scores_bf.astype(jnp.float32))
    )
    query_grad = jnp.einsum("nd,nw->dw", tokens, grad_query, preferred_element_type=jnp.float32)
    key_grad = jnp.einsum("nd,nw->dw", tokens, grad_key, preferred_element_type=jnp.float32)
    value_grad = jnp.einsum("nd,nw->dw", tokens, grad_value, preferred_element_type=jnp.float32)
    input_part = (
        jnp.einsum("nw,dw->nd", grad_query, query_weight, preferred_element_type=jnp.float32)
        + jnp.einsum("nw,dw->nd", grad_key, key_weight, preferred_element_type=jnp.float32)
        + jnp.einsum("nw,dw->nd", grad_value, value_weight, preferred_element_type=jnp.float32)
    )
    own_columns = lax.dynamic_slice_in_dim(input_part, col_start, head_cols, 1)
    input_part = lax.dynamic_update_slice_in_dim(
        input_part, own_columns + grad_head_inputs.reshape(row_count, head_cols), col_start, 1
    )
    grad_inputs = lax.psum(input_part, "tensor") + DEEP_ALPHA * grad_res_one
    tokens_grad = grad_inputs.astype(jnp.bfloat16)
    table_grad = lax.dynamic_update_slice_in_dim(
        jnp.zeros((NB, H), jnp.float32), grad_table_local, head_start, 1
    ).reshape(-1)
    local_small = jnp.concatenate(
        [
            grad_gain_one * leading,
            grad_shift_one * leading,
            grad_gain_two * leading,
            grad_shift_two * leading,
            placed(MODEL_WIDTH, column_sum(grad_query), col_start),
            placed(MODEL_WIDTH, column_sum(grad_value), col_start),
            grad_bias_output * leading,
            grad_bias_down * leading,
            placed(FF, grad_bias_up, hidden_start),
            table_grad,
            grad_gate_matrix,
            grad_gate_offset,
            placed(H, grad_scale_local, head_start),
        ]
    )
    small_grad = lax.psum(local_small, ("dp", "tensor"))
    local_attention = jnp.stack([query_grad, key_grad, value_grad, output_grad])
    local_forward = jnp.stack([up_grad, down_grad])
    summed_attention, summed_forward = lax.psum((local_attention, local_forward), "dp")
    owner_rank = lax.axis_index("dp")
    owned_rows = attention_weights.shape[1]
    share_attention = lax.dynamic_slice_in_dim(
        summed_attention, owner_rank * owned_rows, owned_rows, 1
    )
    share_forward = lax.dynamic_slice_in_dim(summed_forward, owner_rank * owned_rows, owned_rows, 1)
    share_squares = jnp.sum(share_attention * share_attention) + jnp.sum(
        share_forward * share_forward
    )
    big_squares = lax.psum(share_squares, ("dp", "tensor"))
    global_norm = jnp.sqrt(big_squares + jnp.sum(small_grad * small_grad))
    factor = CLIP_LIMIT / jnp.maximum(global_norm, CLIP_LIMIT)
    attention_moment, attention_square, attention_master = adam_step(
        attention_weights,
        attention_first,
        attention_second,
        factor * share_attention,
        RATE_MATRIX,
        WEIGHT_DECAY,
    )
    feedforward_moment, feedforward_square, feedforward_master = adam_step(
        feedforward_weights,
        feedforward_first,
        feedforward_second,
        factor * share_forward,
        RATE_MATRIX,
        WEIGHT_DECAY,
    )
    small_moment, small_square, small_master = adam_step(
        small_params, small_first, small_second, factor * small_grad, RATE_SMALL, 0.0
    )
    return (
        global_norm,
        attention_moment,
        attention_square,
        attention_master,
        attention_master.astype(jnp.bfloat16),
        feedforward_moment,
        feedforward_square,
        feedforward_master,
        feedforward_master.astype(jnp.bfloat16),
        small_moment,
        small_square,
        small_master,
        block_output,
        tokens_grad,
    )


F32 = jnp.float32
BF16 = jnp.bfloat16
MESH_ID = pl.DeviceIdType.MESH
LANES = 128
SMALL_ROWS = 104
QUARTER = 32
SUM_ROWS = 4 * QUARTER
TABLE_ROW = 72
GATE_ROW = 102
OFFSET_ROW = 103
INV_SQRT2 = 0.5**0.5
INV_SQRT_2PI = 0.3989422804014327
CHUNK = 128
HALF = 256
W = MODEL_WIDTH
NT = (((1,), (1,)), ((), ()))
TN = (((0,), (0,)), ((), ()))


def mm(a, b):
    return jnp.dot(a, b, preferred_element_type=F32)


def mm_nt(a, b):
    return lax.dot_general(a, b, NT, preferred_element_type=F32)


def mm_tn(a, b):
    return lax.dot_general(a, b, TN, preferred_element_type=F32)


def exact_nt(a, b):
    return lax.dot_general(a, b, NT, precision=FULL_PRECISION, preferred_element_type=F32)


def exact_tn(a, b):
    return lax.dot_general(a, b, TN, precision=FULL_PRECISION, preferred_element_type=F32)


def exact_mm(a, b):
    return jnp.dot(a, b, precision=FULL_PRECISION, preferred_element_type=F32)


def iota(shape, axis):
    return lax.broadcasted_iota(jnp.int32, shape, axis)


def layer_scratch(owned, nz, qkv_pad, heads, head_cols, hidden):
    rows = 2 * BUCKET_SLOTS
    dma = pltpu.SemaphoreType.DMA
    vm = pltpu.VMEM
    shapes = dict(
        wa=vm((4, owned, head_cols), F32),
        wf=vm((2, owned, hidden), F32),
        keep=vm((rows // LANES, LANES), jnp.int32),
        small=vm((3 * SMALL_ROWS + 2 * BUCKET_SLOTS // LANES, LANES), F32),
        shqkv=vm((owned, qkv_pad), F32),
        sho=vm((owned, LANES), F32),
        shup=vm((owned, hidden), F32),
        shdown=vm((owned, hidden), F32),
        smallout=vm((4, SMALL_ROWS, LANES), F32),
        tok=vm((rows, W), BF16),
        cot=vm((2, HALF, W), BF16),
        wqkv=vm((W, qkv_pad), BF16),
        wo1=vm((W, LANES), BF16),
        wo=vm((W, head_cols), BF16),
        wot=vm((head_cols, W), BF16),
        wqkvt=vm((qkv_pad + LANES, W), BF16),
        wupt=vm((hidden, W), BF16),
        wdownt=vm((hidden, W), BF16),
        go=vm((W, LANES), BF16),
        glin=vm((W, LANES), F32),
        wup=vm((W, hidden), BF16),
        wdown=vm((W, hidden), BF16),
        q=vm((rows, head_cols), BF16),
        k=vm((rows, head_cols), BF16),
        v=vm((rows, head_cols), BF16),
        kt=vm((head_cols, rows), BF16),
        qt=vm((head_cols, rows), BF16),
        dctxt=vm((head_cols, BUCKET_SLOTS), BF16),
        vt=vm((head_cols, rows), BF16),
        ctx=vm((rows, head_cols), BF16),
        dqkv=vm((rows, qkv_pad + LANES), BF16),
        prob=vm((2 * heads, BUCKET_SLOTS, BUCKET_SLOTS), F32),
        gsb=vm((heads * BUCKET_SLOTS, BUCKET_SLOTS), BF16),
        dqf=vm((BUCKET_SLOTS, head_cols), F32),
        mbias=vm((2, BUCKET_SLOTS, BUCKET_SLOTS), BF16),
        band=vm((heads, LANES, 2 * BUCKET_SLOTS), F32),
        dband=vm((heads, LANES, 2 * BUCKET_SLOTS), F32),
        gate=vm((rows, LANES), F32),
        gu=vm((rows, LANES), F32),
        gmat=vm((W, LANES), F32),
        vecs=vm((16, W), F32),
        acc=vm((16, W), F32),
        nb=vm((rows, W), BF16),
        held=vm((2, HALF, W), F32),
        xh1=vm((2, HALF, W), F32),
        rstd1=vm((2, HALF, LANES), F32),
        act=vm((rows, hidden), BF16),
        gelup=vm((rows, hidden), F32),
        gffn=vm((rows, W), BF16),
        gub=vm((rows, hidden), BF16),
        gattn=vm((rows, W), BF16),
        stage=vm((2, HALF, W), BF16),
        ownf=vm((HALF, W), F32),
        cs=vm((2, HALF, W), BF16),
        cr=vm((2, HALF, W), BF16),
        ys=vm((2, HALF, W), BF16),
        yr=vm((2, 2, HALF, W), BF16),
        xrqkv=vm((nz, owned, qkv_pad), BF16),
        xro=vm((nz, owned, LANES), BF16),
        xrup=vm((nz, owned, hidden), BF16),
        xrdown=vm((nz, owned, hidden // 2), BF16),
        xrdownb=vm((nz, owned, hidden // 2), BF16),
        zsqkv=vm((nz - 1, owned, qkv_pad), BF16),
        zso=vm((nz - 1, owned, LANES), BF16),
        zsup=vm((nz - 1, owned, hidden), BF16),
        zsdown=vm((nz - 1, owned, hidden // 2), BF16),
        zsdownb=vm((nz - 1, owned, hidden // 2), BF16),
        zrqkv=vm((nz - 1, owned, qkv_pad), BF16),
        zro=vm((nz - 1, owned, LANES), BF16),
        zrup=vm((nz - 1, owned, hidden), BF16),
        zrdown=vm((nz - 1, owned, hidden // 2), BF16),
        zrdownb=vm((nz - 1, owned, hidden // 2), BF16),
        sm=vm((SUM_ROWS, LANES), F32),
        smc=vm((2, QUARTER, LANES), F32),
        smh=vm((2, QUARTER, LANES), F32),
        smy=vm((QUARTER, LANES), F32),
        smv=vm((QUARTER, LANES), F32),
        smx=vm((QUARTER, LANES), F32),
        smz=vm((nz, QUARTER, LANES), F32),
        sma=vm((SUM_ROWS, LANES), F32),
        sqt=vm((4, 8, LANES), F32),
        sqd=vm((2 * nz, 8, LANES), F32),
        s_in=dma((7,)),
        s_out=dma((5,)),
        s_gs=dma((8,)),
        s_gr=dma((8,)),
        s_ls=dma((8, 2, nz)),
        s_lr=dma((8, 2, nz)),
        s_lxs=dma((8, 2, nz)),
        s_lxr=dma((8, 2, nz)),
        s_cs=dma((4, 2, 2)),
        s_cr=dma((4, 2, 2)),
        s_ys=dma((4, 2, 4)),
        s_yr=dma((4, 2, 4)),
        s_as=dma((3, 2, 2)),
        s_ar=dma((3, 2, 2)),
        s_ol=dma((2, 2)),
        s_os=dma((2, 2)),
        s_or=dma((2, 2)),
        s_xs=dma((5, nz)),
        s_xr=dma((5, nz)),
        s_zs=dma((5, nz)),
        s_zr=dma((5, nz)),
        s_ms=dma((6 + nz,)),
        s_mr=dma((6 + nz,)),
        s_ts=dma((4,)),
        s_tr=dma((4,)),
        s_ds=dma((2 * nz,)),
        s_dr=dma((2 * nz,)),
    )
    return shapes


def layer_kernel(names, dims, *refs):
    n_dp, owned, qkv_pad, heads, head_cols, hidden = dims
    nz = n_dp // 2
    (tok_in, cot_in, lens, keep_in, wa_in, wf_in, small_in) = refs[:7]
    (bo_out, tg_out, out_qkv, out_o, out_up, out_down, out_small, norm_out) = refs[7:15]
    m = SimpleNamespace(**dict(zip(names, refs[15:], strict=True)))
    D = lax.axis_index("dp")
    T = lax.axis_index("tensor")
    z = lax.div(D, 2)
    x = lax.rem(D, 2)
    c = lax.rem(T, 2)
    yy = lax.div(T, 2)
    core_dev = (D, T + 1 - 2 * c)
    y_dev = (D, lax.rem(T + 2, 4))
    x_dev = (z * 2 + 1 - x, T)

    def z_at(k):
        total, bit = 0, 1
        while bit < nz:
            here = lax.rem(lax.div(z, bit), 2)
            total = total + bit * (1 - here if k & bit else here)
            bit *= 2
        return total

    def z_dev(k):
        return (z_at(k) * 2 + x, T)

    def remote(src, dst, ss, rs, dev):
        return pltpu.make_async_remote_copy(
            src_ref=src, dst_ref=dst, send_sem=ss, recv_sem=rs, device_id=dev, device_id_type=MESH_ID
        )

    def loop(n, step):
        def run(i, carry):
            step(i)
            return carry

        lax.fori_loop(0, n, run, 0)

    def block(owner):
        return pl.ds(pl.multiple_of(owner * owned, owned), owned)

    wa, wf, keep, small = m.wa, m.wf, m.keep, m.small
    sh_qkv, sh_o, sh_up, sh_down, small_out = m.shqkv, m.sho, m.shup, m.shdown, m.smallout
    first_loads = []
    for i, (source, target) in enumerate(((wa_in, wa), (wf_in, wf), (small_in, small), (keep_in, keep))):
        cp = pltpu.make_async_copy(source, target, m.s_in.at[3 + i])
        cp.start()
        first_loads.append(cp)
    tok_copy = pltpu.make_async_copy(tok_in, m.tok, m.s_in.at[0])
    tok_copy.start()
    cot_copies = []
    for b in range(2):
        rows = pl.ds(pl.multiple_of(b * BUCKET_SLOTS + c * HALF, HALF), HALF)
        cp = pltpu.make_async_copy(cot_in.at[rows], m.cot.at[b], m.s_in.at[1 + b])
        cp.start()
        cot_copies.append(cp)
    barrier = pltpu.get_barrier_semaphore()
    for k in range(1, 4):
        pl.semaphore_signal(barrier, inc=1, device_id=(D, lax.rem(T + k, 4)), device_id_type=MESH_ID)
    for k in range(1, n_dp):
        pl.semaphore_signal(barrier, inc=1, device_id=(lax.rem(D + k, n_dp), T), device_id_type=MESH_ID)
    for cp in first_loads:
        cp.wait()
    mine = block(D)
    first_o = qkv_pad - 3 * head_cols
    m.wqkv[mine, :] = jnp.concatenate([wa[0], wa[1], wa[2], wa[3, :, 0:first_o]], axis=1).astype(BF16)
    m.wo1[mine, :] = wa[3, :, first_o:head_cols].astype(BF16)
    m.wup[mine, :] = wf[0].astype(BF16)
    m.wdown[mine, :] = wf[1].astype(BF16)
    pl.semaphore_wait(barrier, 3 + n_dp - 1)

    part_rows = owned // 2 if owned % 32 == 0 else owned
    halves = lambda buf: [(buf, 0, part_rows), (buf, owned - part_rows, part_rows)]
    pieces = halves(m.wqkv) + [(m.wo1, 0, owned)] + halves(m.wup) + halves(m.wdown)

    pieces.append(pieces[-1])
    across = len(pieces) - 1
    straight = (across - 1, across)

    def piece(which, owner_z, other_column=False):
        buf, first, count = pieces[which]
        column = 1 - x if other_column != (which == across) else x
        return buf.at[pl.ds(pl.multiple_of((owner_z * 2 + column) * owned + first, 16), count)]

    gathers = {}

    def launch(record, where):
        remote(*where()).start()
        record.append(where)

    def when(condition, action):
        pl.when(condition)(action)

    def from_z(way, step):
        owner_z = z - step if way == 0 else z + step
        return owner_z, (owner_z >= 0) if way == 0 else (owner_z < nz)

    def send_when(which, condition, where):
        when(condition(), lambda: remote(*where()).start())
        gathers.setdefault(which, []).append((condition, where))

    def line_send(which, way, step, hops):
        origin = step - hops

        def where():
            part = piece(which, from_z(way, origin)[0])
            target = ((z + hops if way == 0 else z - hops) * 2 + x, T)
            return part, part, m.s_ls.at[which, way, step], m.s_lr.at[which, way, step], target

        def condition():
            there = (z + hops < nz) if way == 0 else (z >= hops)
            return there & from_z(way, origin)[1]

        send_when(which, condition, where)

    def line_start(which, hops):
        for hop in range(1, hops + 1):
            for way in range(2):
                line_send(which, way, hop, hop)

    def gather_x(which):
        def where():
            own = piece(which, z)
            return own, own, m.s_gs.at[which], m.s_gr.at[which], x_dev

        send_when(which, lambda: D >= 0, where)

    def line_step(which, step, hops):
        for way in range(2):

            def landed(way=way):
                part = piece(which, from_z(way, step)[0])
                sems = m.s_ls.at[which, way, step], m.s_lr.at[which, way, step]
                remote(part, part, *sems, x_dev).wait_recv()

            when(from_z(way, step)[1], landed)
            if step >= hops and step + 1 < nz:
                line_send(which, way, step + 1, 1)
            if which in straight:
                continue

            def where(way=way):
                part = piece(which, from_z(way, step)[0])
                return part, part, m.s_lxs.at[which, way, step], m.s_lxr.at[which, way, step], x_dev

            send_when(which, lambda way=way: from_z(way, step)[1], where)

    def partner_landed(which):
        part = piece(which, z, True)
        remote(part, part, m.s_gs.at[which], m.s_gr.at[which], x_dev).wait_recv()

    def line_end(which):
        partner_landed(which)
        for step in range(1, nz):
            for way in range(2):

                def landed(way=way):
                    part = piece(which, from_z(way, step)[0], True)
                    sems = m.s_lxs.at[which, way, step], m.s_lxr.at[which, way, step]
                    remote(part, part, *sems, x_dev).wait_recv()

                when(from_z(way, step)[1], landed)

    def sent_all(which):
        for condition, where in gathers.pop(which):
            when(condition(), lambda where=where: remote(*where()).wait_send())

    def turn(source, target):
        count = source.shape[1]
        if count % LANES:
            target[...] = source[...].T
            return
        step = HALF if count % HALF == 0 else LANES

        def chunk(i):
            at = pl.ds(pl.multiple_of(i * step, step), step)
            target[at, :] = source[:, at].T

        loop(count // step, chunk)

    for which in (0, 1):
        line_start(which, 1)
    for which in (0, 1):
        gather_x(which)
    gather_x(across - 1)

    def small_row(first, count):
        return jnp.concatenate([small[first + i : first + i + 1, :] for i in range(count)], axis=1)

    def pick(values, size):
        total = jnp.zeros((1, size), F32)
        for t in range(4):
            total = total + jnp.where(T == t, values[:, t * size : (t + 1) * size], 0.0)
        return total

    vecs = m.vecs
    vecs[...] = jnp.zeros_like(vecs)
    m.acc[...] = jnp.zeros((16, W), F32)
    for at, first in ((0, 0), (1, 6), (2, 12), (3, 18), (4, 36), (5, 42)):
        vecs[at : at + 1, :] = small_row(first, W // LANES)
    vecs[6:7, :] = pick(small_row(48, FF // LANES), hidden)
    bq = pick(small_row(24, W // LANES), head_cols)
    bv = pick(small_row(30, W // LANES), head_cols)
    bias_qkv = jnp.concatenate(
        [bq, jnp.zeros_like(bq), bv, jnp.zeros((1, qkv_pad - 3 * head_cols), F32)], axis=1
    )
    vecs[7:8, 0:qkv_pad] = bias_qkv

    lane = iota((1, LANES), 1)
    col = iota((W, LANES), 0)
    col_lane = iota((W, LANES), 1)
    gate_row = small[GATE_ROW : GATE_ROW + 1, :]
    col_in_head = lax.rem(col, HD)
    picked_u = jnp.sum(
        jnp.where(col_lane == 2 * col_in_head, gate_row, 0.0), axis=1, keepdims=True
    )
    picked_w = jnp.sum(
        jnp.where(col_lane == 2 * col_in_head + 1, gate_row, 0.0), axis=1, keepdims=True
    )
    in_group = lax.rem(col_lane, 8)
    own_head = (col_lane < 16) & (in_group < heads) & (lax.div(col, HD) == T * heads + in_group)
    m.gmat[...] = jnp.where(own_head, jnp.where(col_lane < 8, picked_u, picked_w), 0.0)
    offset_row = small[OFFSET_ROW : OFFSET_ROW + 1, :]
    offset_u = jnp.sum(jnp.where(lane == 0, offset_row, 0.0), axis=1, keepdims=True)
    offset_w = jnp.sum(jnp.where(lane == 1, offset_row, 0.0), axis=1, keepdims=True)
    scale = jnp.zeros((1, LANES), F32)
    for h in range(heads):
        one = jnp.sum(jnp.where(lane == 2 + T * heads + h, offset_row, 0.0), axis=1, keepdims=True)
        scale = scale + jnp.where(lane == h, one, 0.0)
    head_lane = lane < heads

    line_step(0, 1, 1)
    line_step(1, 1, 1)

    offsets = small_row(3 * SMALL_ROWS, 2 * BUCKET_SLOTS // LANES).astype(jnp.int32)
    table = small[TABLE_ROW : TABLE_ROW + 32, :]
    long_row = 2 * BUCKET_SLOTS
    sub8 = iota((8, long_row), 0)
    for h in range(heads):
        flat = offsets * H + (T * heads + h)
        at_row = lax.div(flat, LANES)
        at_lane = lax.rem(flat, LANES)
        hot_row = jnp.where(iota((32, long_row), 0) == at_row, 1.0, 0.0)
        spread = exact_tn(table, hot_row)
        values = jnp.sum(
            jnp.where(iota((LANES, long_row), 0) == at_lane, spread, 0.0), axis=0, keepdims=True
        )
        stack = jnp.broadcast_to(pltpu.roll(jnp.broadcast_to(values, (8, long_row)), 1, 1), (8, long_row))
        for bit in (1, 2, 4):
            stack = jnp.where(lax.rem(lax.div(sub8, bit), 2) == 1, pltpu.roll(stack, bit, 1), stack)
        size = 8
        m.band[h, 0:8, :] = stack
        while size < LANES:
            m.band[h, size : 2 * size, :] = pltpu.roll(m.band[h, 0:size, :], size, 1)
            size *= 2
    m.dband[...] = jnp.zeros(m.dband.shape, F32)

    line_step(0, 2, 1)
    line_step(1, 2, 1)

    for b in range(2):
        end = 0
        ends = []
        for i in range(CLIPS):
            end = end + lens[b, i]
            ends.append(end)
        key_at = iota((1, BUCKET_SLOTS), 1)
        key_segment = jnp.zeros((1, BUCKET_SLOTS), jnp.int32)
        for end in ends:
            key_segment = key_segment + jnp.where(key_at >= end, 1, 0)
        kept = jnp.concatenate([keep[4 * b + i : 4 * b + i + 1, :] for i in range(4)], axis=1)
        live = jnp.where((kept == 1) & (key_segment < CLIPS), key_segment, -1)

        def mask_chunk(i, b=b, ends=ends, live=live):
            query_at = iota((CHUNK, BUCKET_SLOTS), 0) + i * CHUNK
            segment = jnp.zeros((CHUNK, BUCKET_SLOTS), jnp.int32)
            for end in ends:
                segment = segment + jnp.where(query_at >= end, 1, 0)
            allowed = (segment == live) | (query_at == iota((CHUNK, BUCKET_SLOTS), 1))
            m.mbias[b, pl.ds(pl.multiple_of(i * CHUNK, CHUNK), CHUNK), :] = jnp.where(
                allowed, 0.0, MASK_VALUE
            ).astype(BF16)

        loop(BUCKET_SLOTS // CHUNK, mask_chunk)

    for step in range(3, nz):
        line_step(0, step, 1)
        line_step(1, step, 1)
    line_start(2, 2)

    tok_copy.wait()
    gmat = m.gmat[...]
    part_hi = gmat.astype(BF16)
    rest = gmat - part_hi.astype(F32)
    part_mid = rest.astype(BF16)
    part_lo = (rest - part_mid.astype(F32)).astype(BF16)
    gate_parts = (part_hi, part_hi, part_hi, part_mid, part_mid, part_lo)
    stacked = jnp.zeros((W, LANES), F32)
    for i, part in enumerate(gate_parts):
        moved = part.astype(F32)
        stacked = stacked + (pltpu.roll(moved, 16 * i, 1) if i else moved)
    m.wqkvt[qkv_pad : qkv_pad + LANES, :] = stacked.astype(BF16).T

    def gate_chunk(i):
        rows = pl.ds(pl.multiple_of(i * HALF, HALF), HALF)
        tokens = m.tok[rows, :]
        linear = mm(tokens, part_hi) + mm(tokens, part_mid) + mm(tokens, part_lo)
        both = jax.nn.sigmoid(linear + jnp.where(lane < 8, offset_u, offset_w))
        m.gu[rows, :] = both
        m.gate[rows, :] = both * (pltpu.roll(both, LANES - 8, 1) * scale - 1.0) + 2.0

    loop(4, gate_chunk)

    line_start(3, 2)
    line_end(0)
    line_end(1)
    gather_x(2)
    line_step(2, 1, 2)
    line_step(2, 2, 2)
    gather_x(3)

    def project(i):
        rows = pl.ds(pl.multiple_of(i * HALF, HALF), HALF)
        both = mm(m.tok[rows, :], m.wqkv[...]) + vecs[7:8, 0:qkv_pad]
        query = (both[:, 0:head_cols].astype(BF16).astype(F32) * 0.125).astype(BF16)
        m.q[rows, :] = query
        m.qt[:, rows] = query.T
        key = both[:, head_cols : 2 * head_cols].astype(BF16)
        value = both[:, 2 * head_cols : 3 * head_cols].astype(BF16)
        m.k[rows, :] = key
        m.v[rows, :] = value
        m.kt[:, rows] = key.T
        m.vt[:, rows] = value.T

    loop(4, project)

    head_of = lax.div(iota((1, head_cols), 1), HD)
    head_masks = [jnp.where(head_of == h, 1.0, 0.0) for h in range(heads)]
    low_masks = [m.astype(BF16) for m in head_masks]

    def hooked(first, count, chunk, hooks):
        def step_of(i):
            step = i + first
            chunk(step)
            for at, action in hooks.items():
                if first <= at < first + count:
                    when(step == at, action)

        loop(count, step_of)

    def by_head(stacked):
        total = stacked[0:CHUNK, :] * head_masks[0]
        for h in range(1, heads):
            total = total + stacked[h * CHUNK : (h + 1) * CHUNK, :] * head_masks[h]
        return total

    def attend(b, hooks):
        keys = m.kt[:, b * BUCKET_SLOTS : (b + 1) * BUCKET_SLOTS]
        values = m.v[b * BUCKET_SLOTS : (b + 1) * BUCKET_SLOTS, :]

        def chunk(i):
            local = pl.ds(pl.multiple_of(i * CHUNK, CHUNK), CHUNK)
            rows = pl.ds(pl.multiple_of(b * BUCKET_SLOTS + i * CHUNK, CHUNK), CHUNK)
            window = pl.ds(pl.multiple_of(BUCKET_SLOTS - i * CHUNK, CHUNK), BUCKET_SLOTS)
            query = m.q[rows, :]
            gates = m.gate[rows, :]
            all_scores = mm(jnp.concatenate([query * mask for mask in low_masks], axis=0), keys)
            all_probs = []
            for h in range(heads):
                scores = all_scores[h * CHUNK : (h + 1) * CHUNK, :]
                scores = scores + gates[:, h : h + 1] * m.band[h, :, window]
                scores = scores + m.mbias[b, local, :].astype(F32)
                top = jnp.max(scores, axis=1, keepdims=True)
                weight = jnp.exp(scores - top)
                total = jnp.sum(weight, axis=1, keepdims=True)
                probability = weight * (1.0 / total)
                m.prob[b * heads + h, local, :] = probability
                all_probs.append(probability.astype(BF16))
            m.ctx[rows, :] = by_head(mm(jnp.concatenate(all_probs, axis=0), values)).astype(BF16)

        hooked(0, BUCKET_SLOTS // CHUNK, chunk, hooks)

    core_sent = {}
    y_sent = {}

    def exchange(phase, b, product):
        exchange_first(phase, b, product)
        exchange_last(phase, b)

    def exchange_first(phase, b, product):
        other = b * BUCKET_SLOTS + (1 - c) * HALF
        own = b * BUCKET_SLOTS + c * HALF
        for cp in core_sent.get((phase - 1, b), []) + y_sent.get((phase - 1, b), []):
            cp.wait_send()
        for i in range(2):
            at = slice(i * CHUNK, (i + 1) * CHUNK)
            rows = pl.ds(pl.multiple_of(other + i * CHUNK, CHUNK), CHUNK)
            m.cs[b, at, :] = product(rows).astype(BF16)
            cp = remote(
                m.cs.at[b, at], m.cr.at[b, at], m.s_cs.at[phase, b, i], m.s_cr.at[phase, b, i], core_dev
            )
            cp.start()
            core_sent.setdefault((phase, b), []).append(cp)
        for i in range(2):
            at = slice(i * CHUNK, (i + 1) * CHUNK)
            rows = pl.ds(pl.multiple_of(own + i * CHUNK, CHUNK), CHUNK)
            m.ownf[at, :] = product(rows)

    def exchange_last(phase, b):
        half = CHUNK // 2
        for i in range(4):
            at = slice(i * half, (i + 1) * half)
            if i % 2 == 0:
                core_sent[(phase, b)][i // 2].wait_recv()
            m.ys[b, at, :] = (m.ownf[at, :] + m.cr[b, at, :].astype(F32)).astype(BF16)
            cp = remote(
                m.ys.at[b, at],
                m.yr.at[phase % 2, b, at],
                m.s_ys.at[phase, b, i],
                m.s_yr.at[phase, b, i],
                y_dev,
            )
            cp.start()
            y_sent.setdefault((phase, b), []).append(cp)

    def arrived(phase, b, at):
        return m.ys[b, at, :].astype(F32) + m.yr[phase % 2, b, at, :].astype(F32)

    def own_rows(b, i):
        return pl.ds(pl.multiple_of(b * BUCKET_SLOTS + c * HALF + i * CHUNK, CHUNK), CHUNK)

    core_spread = {}

    def spread(which, buf, b, i):
        part = buf.at[own_rows(b, i)]
        cp = remote(part, part, m.s_as.at[which, b, i], m.s_ar.at[which, b, i], core_dev)
        cp.start()
        core_spread.setdefault((which, b), []).append(cp)

    spread_done = set()

    def spread_end(which, b, i):
        if (which, b, i) not in spread_done:
            core_spread[(which, b)][i].wait_recv()
            spread_done.add((which, b, i))

    def as_it_lands(phase, b, chunk):
        for i in range(2):
            for cp in y_sent[(phase, b)][2 * i : 2 * i + 2]:
                cp.wait_recv()
            chunk(i)

    def row_mean(values):
        return jnp.mean(values, axis=1, keepdims=True)

    def add_row(at, values):
        m.acc[at : at + 1, 0 : values.shape[1]] += jnp.sum(values, axis=0, keepdims=True)

    def norm_one(b):

        def chunk(i):
            at = pl.ds(pl.multiple_of(i * CHUNK, CHUNK), CHUNK)
            rows = own_rows(b, i)
            residual = DEEP_ALPHA * m.tok[rows, :].astype(F32) + (arrived(0, b, at) + vecs[4:5, :])
            centred = residual - row_mean(residual)
            rstd = lax.rsqrt(row_mean(centred * centred) + NORM_EPSILON)
            hat = centred * rstd
            normed = hat * vecs[0:1, :] + vecs[1:2, :]
            m.nb[rows, :] = normed.astype(BF16)
            spread(0, m.nb, b, i)
            m.xh1[b, at, :] = hat
            m.rstd1[b, at, :] = jnp.broadcast_to(rstd, (CHUNK, LANES))
            m.held[b, at, :] = normed

        as_it_lands(0, b, chunk)

    def own_first(which, b, chunk):
        def rows_at(step):
            i = lax.rem(step + 2 * c, 4)
            return pl.ds(pl.multiple_of(b * BUCKET_SLOTS + i * CHUNK, CHUNK), CHUNK)

        def rest():
            for i in range(2):
                spread_end(which, b, i)
                chunk(rows_at(2 + i))

        loop(2, lambda step: chunk(rows_at(step)))
        return rest

    def feed(b):
        def chunk(rows):
            up = mm(m.nb[rows, :], m.wup[...]) + vecs[6:7, :]
            half_phi = 0.5 * (1.0 + lax.erf(up * INV_SQRT2))
            m.act[rows, :] = (up * half_phi).astype(BF16)
            m.gelup[rows, :] = half_phi + up * (jnp.exp(up * up * -0.5) * INV_SQRT_2PI)

        own_first(0, b, chunk)()

    out_copies = []

    def result_rows(which, b, stage, out):
        rows = pl.ds(pl.multiple_of(b * BUCKET_SLOTS + c * HALF, HALF), HALF)
        part = stage.at[b]
        here = pltpu.make_async_copy(part, out.at[rows], m.s_ol.at[which, b])
        there = remote(part, out.at[rows], m.s_os.at[which, b], m.s_or.at[which, b], core_dev)
        here.start()
        there.start()
        out_copies.append((here, there))

    def norm_two(b):
        cot_copies[b].wait()

        def chunk(i):
            at = pl.ds(pl.multiple_of(i * CHUNK, CHUNK), CHUNK)
            rows = own_rows(b, i)
            residual = DEEP_ALPHA * m.held[b, at, :] + (arrived(1, b, at) + vecs[5:6, :])
            centred = residual - row_mean(residual)
            rstd = lax.rsqrt(row_mean(centred * centred) + NORM_EPSILON)
            hat = centred * rstd
            upstream = m.cot[b, at, :].astype(F32)
            scaled = upstream * vecs[2:3, :]
            grad = rstd * (scaled - row_mean(scaled) - hat * row_mean(scaled * hat))
            low = grad.astype(BF16)
            m.gffn[rows, :] = low
            spread(1, m.gffn, b, i)
            m.held[b, at, :] = grad
            m.stage[b, at, :] = (hat * vecs[2:3, :] + vecs[3:4, :]).astype(BF16)
            add_row(2, upstream * hat)
            add_row(3, upstream)
            add_row(5, low.astype(F32))

        as_it_lands(1, b, chunk)
        result_rows(0, b, m.stage, bo_out)

    def feed_back(b):
        def chunk(rows):
            grad = mm(m.gffn[rows, :], m.wdown[...]) * m.gelup[rows, :]
            low = grad.astype(BF16)
            m.gub[rows, :] = low
            add_row(6, low.astype(F32))

        return own_first(1, b, chunk)

    def norm_one_back(b):

        def chunk(i):
            at = pl.ds(pl.multiple_of(i * CHUNK, CHUNK), CHUNK)
            rows = own_rows(b, i)
            upstream = arrived(2, b, at) + DEEP_ALPHA * m.held[b, at, :]
            hat = m.xh1[b, at, :]
            scaled = upstream * vecs[0:1, :]
            rstd = m.rstd1[b, at, 0:1]
            grad = rstd * (scaled - row_mean(scaled) - hat * row_mean(scaled * hat))
            low = grad.astype(BF16)
            m.gattn[rows, :] = low
            spread(2, m.gattn, b, i)
            m.held[b, at, :] = grad
            add_row(0, upstream * hat)
            add_row(1, upstream)
            add_row(4, low.astype(F32))

        as_it_lands(2, b, chunk)

    def gate_back(rows, grad):
        u = m.gu[rows, :]
        w = pltpu.roll(u, LANES - 8, 1)
        grad_u = jnp.where(head_lane, grad * (w * scale - 1.0) * u * (1.0 - u), 0.0)
        grad_w = jnp.where(head_lane, grad * u * scale * w * (1.0 - w), 0.0)
        add_row(8, jnp.where(head_lane, grad * u * w, 0.0))
        linear = grad_u + pltpu.roll(grad_w, 8, 1)
        add_row(9, linear)
        hi = linear.astype(BF16).astype(F32)
        mid = (linear - hi).astype(BF16).astype(F32)
        lo = (linear - hi - mid).astype(BF16).astype(F32)
        stacked = hi
        for at, part in enumerate((mid, lo, hi, mid, hi)):
            stacked = stacked + pltpu.roll(part, 16 * (at + 1), 1)
        m.dqkv[rows, qkv_pad : qkv_pad + LANES] = stacked.astype(BF16)

    def attend_back(b, hooks):
        keys = m.k[b * BUCKET_SLOTS : (b + 1) * BUCKET_SLOTS, :]
        values = m.vt[:, b * BUCKET_SLOTS : (b + 1) * BUCKET_SLOTS]

        def chunk(step):
            i = lax.rem(step + 2 * c, 4)
            local = pl.ds(pl.multiple_of(i * CHUNK, CHUNK), CHUNK)
            rows = pl.ds(pl.multiple_of(b * BUCKET_SLOTS + i * CHUNK, CHUNK), CHUNK)
            window = pl.ds(pl.multiple_of(BUCKET_SLOTS - i * CHUNK, CHUNK), BUCKET_SLOTS)
            place = pl.ds(pl.multiple_of(3 * CHUNK - i * CHUNK, CHUNK), BUCKET_SLOTS)
            grad_context = mm(m.gattn[rows, :], m.wo[...]).astype(BF16)
            m.dctxt[:, local] = grad_context.T
            gates = m.gate[rows, :]
            all_grads = mm(jnp.concatenate([grad_context * mask for mask in low_masks], axis=0), values)
            all_low = []
            grad_gates = jnp.zeros((CHUNK, LANES), F32)
            for h in range(heads):
                grad_probs = all_grads[h * CHUNK : (h + 1) * CHUNK, :]
                probability = m.prob[b * heads + h, local, :]
                inner = jnp.sum(grad_probs * probability, axis=1, keepdims=True)
                low = (probability * (grad_probs - inner)).astype(BF16)
                m.gsb[pl.ds(pl.multiple_of(h * BUCKET_SLOTS + i * CHUNK, CHUNK), CHUNK), :] = low
                all_low.append(low)
                rounded = low.astype(F32)
                one = jnp.sum(rounded * m.band[h, :, window], axis=1, keepdims=True)
                grad_gates = grad_gates + jnp.where(lane == h, one, 0.0)
                m.dband[h, :, place] += rounded * gates[:, h : h + 1]
            m.dqf[local, :] = by_head(mm(jnp.concatenate(all_low, axis=0), keys)) * 0.125
            gate_back(rows, grad_gates)

        hooked(0, 2, chunk, hooks)
        spread_end(2, b, 0)
        spread_end(2, b, 1)
        hooked(2, 2, chunk, hooks)
        all_rows = slice(b * BUCKET_SLOTS, (b + 1) * BUCKET_SLOTS)
        own_rows_of = lax.div(iota((head_cols, 1), 0), HD)
        row_masks = [jnp.where(own_rows_of == h, 1.0, 0.0).astype(BF16) for h in range(heads)]
        spread_out = lambda turned: jnp.concatenate([turned * mask for mask in row_masks], axis=1)
        grad_key = mm(spread_out(m.qt[:, all_rows]), m.gsb[...]).T
        probs = m.prob[b * heads : (b + 1) * heads].reshape(heads * BUCKET_SLOTS, BUCKET_SLOTS)
        grad_value = mm(spread_out(m.dctxt[...]), probs.astype(BF16)).T
        pad = jnp.zeros((BUCKET_SLOTS, qkv_pad - 3 * head_cols), F32)
        low = jnp.concatenate([m.dqf[...], grad_key, grad_value, pad], axis=1).astype(BF16)
        m.dqkv[all_rows, 0:qkv_pad] = low
        add_row(7, low.astype(F32))

    def input_part(rows):
        return mm(m.dqkv[rows, :], m.wqkvt[...])

    def token_rows(b):
        for cp in out_copies[b]:
            cp.wait()

        def chunk(i):
            at = pl.ds(pl.multiple_of(i * CHUNK, CHUNK), CHUNK)
            total = arrived(3, b, at) + DEEP_ALPHA * m.held[b, at, :]
            m.stage[b, at, :] = total.astype(BF16)

        as_it_lands(3, b, chunk)
        result_rows(1, b, m.stage, tg_out)

    def weight_grad(sent, left, right, put_part, rows=slice(None)):
        for which in sent:
            sent_all(which)

        def chunk(i):
            cols = pl.ds(pl.multiple_of(i * HALF, HALF), HALF)
            put_part(cols, mm_tn(left[rows, cols], right[rows, :]))

        loop(W // HALF, chunk)

    def add_whole(buf):
        def put_part(cols, part):
            buf[cols, :] = (buf[cols, :].astype(F32) + part).astype(BF16)

        return put_part

    def put_whole(buf):
        def put_part(cols, part):
            buf[cols, :] = part.astype(BF16)

        return put_part

    def put_qkv(cols, part):
        m.wqkv[cols, 0 : 3 * head_cols] = part[:, 0 : 3 * head_cols].astype(BF16)
        m.glin[cols, :] = part[:, qkv_pad : qkv_pad + LANES]

    def put_o(cols, part):
        m.wqkv[cols, 3 * head_cols : qkv_pad] = part[:, 0:first_o].astype(BF16)
        m.go[cols, :] = part[:, first_o:head_cols].astype(BF16)

    reduces = []

    def low_bit(k):
        return k & -k if k else nz

    bits = [1 << i for i in range(nz.bit_length() - 1)]
    slots = {}
    for k in range(nz):
        for bit in bits:
            if bit < low_bit(k):
                slots[(k, bit)] = len(slots)
    pass_order = sorted(range(nz), key=lambda k: (low_bit(k), -k))

    def add_landed(total, k, which, arrive):
        for bit in bits:
            if bit < low_bit(k):
                slot = slots[(k, bit)]
                here = arrive.at[slot]
                sems = m.s_zs.at[which, slot], m.s_zr.at[which, slot]
                remote(here, here, *sems, z_dev(bit)).wait_recv()
                total = total + arrive[slot].astype(F32)
        return total

    def reduce_start(which, buf, land, ks=None):
        for k in ks or pass_order:

            def where(k=k):
                rows = block(2 * z_at(k) + 1 - x)
                return buf.at[rows], land.at[k], m.s_xs.at[which, k], m.s_xr.at[which, k], x_dev

            launch(reduces, where)

    def reduce_block(k, which, buf, land, out, arrive, share):
        here = land.at[k]
        remote(here, here, m.s_xs.at[which, k], m.s_xr.at[which, k], x_dev).wait_recv()
        total = buf[block(2 * z_at(k) + x), :].astype(F32) + land[k].astype(F32)
        if k == 0:
            share[...] = total
        else:
            out[k - 1] = add_landed(total, k, which, arrive).astype(BF16)

            def where():
                bit = low_bit(k)
                slot = slots[(k - bit, bit)]
                sems = m.s_zs.at[which, slot], m.s_zr.at[which, slot]
                return out.at[k - 1], arrive.at[slot], *sems, z_dev(bit)

            launch(reduces, where)

    def reduce_pass(*matrix):
        for k in pass_order:
            reduce_block(k, *matrix)

    kept = [k for k in range(nz) if k % 2 == 0]
    x_slots = {k: i for i, k in enumerate(kept)}
    far_slots = {}
    for k in kept:
        for bit in bits[1:]:
            if bit < low_bit(k):
                far_slots[(k, bit)] = len(x_slots) + len(far_slots)

    def owner_rows(k, side):
        return block(2 * z_at(k) + (1 - x if side else x))

    def near_start(which, buf, land):
        for k in reversed(kept):
            for side in (1, 0):

                def where(k=k, side=side):
                    at = k + side
                    sems = m.s_xs.at[which, at], m.s_xr.at[which, at]
                    return buf.at[owner_rows(k + 1, side)], land.at[at], *sems, z_dev(1)

                launch(reduces, where)

    def near_total(k, side, which, buf, land):
        at = k + side
        here = land.at[at]
        remote(here, here, m.s_xs.at[which, at], m.s_xr.at[which, at], z_dev(1)).wait_recv()
        return buf[owner_rows(k, side), :].astype(F32) + land[at].astype(F32)

    def landed_slot(slot, which, arrive):
        here = arrive.at[slot]
        remote(here, here, m.s_zs.at[which, slot], m.s_zr.at[which, slot], x_dev).wait_recv()
        return arrive[slot].astype(F32)

    def near_across(k, which, buf, land, out, arrive, share):
        slot = x_slots[k]
        out[slot] = near_total(k, 1, which, buf, land).astype(BF16)

        def where():
            return out.at[slot], arrive.at[slot], m.s_zs.at[which, slot], m.s_zr.at[which, slot], x_dev

        launch(reduces, where)

    def near_far(k, which, buf, land, out, arrive, share):
        total = near_total(k, 0, which, buf, land) + landed_slot(x_slots[k], which, arrive)
        for bit in bits[1:]:
            if bit < low_bit(k):
                total = total + landed_slot(far_slots[(k, bit)], which, arrive)
        if k == 0:
            share[...] = total
            return
        bit = low_bit(k)
        slot = far_slots[(k - bit, bit)]
        out[slot] = total.astype(BF16)

        def where():
            sems = m.s_zs.at[which, slot], m.s_zr.at[which, slot]
            return out.at[slot], arrive.at[slot], *sems, z_dev(bit)

        launch(reduces, where)

    def squares_of(total):
        squares = total * total
        folded = jnp.zeros((owned, LANES), F32)
        for i in range(total.shape[1] // LANES):
            folded = folded + squares[:, i * LANES : (i + 1) * LANES]
        tile = jnp.zeros((8, LANES), F32)
        for i in range(owned // 8):
            tile = tile + folded[8 * i : 8 * i + 8, :]
        return tile

    def reduce_end(which, arrive, share):
        total = add_landed(share[...], 0, which, arrive)
        share[...] = total
        return squares_of(total)

    def pass_on(which):
        line_step(which, 1, 2)
        line_step(which, 2, 2)

    def pass_last(which):
        for step in range(3, nz):
            line_step(which, step, 2)

    line_start(4, 2)
    gather_x(4)

    pass_last(2)

    def first_pass():
        line_start(5, 2)
        gather_x(5)

    def second_pass():
        pass_on(3)
        partner_landed(6)
        line_start(6, 2)
        line_start(7, 2)

    attend(0, {0: first_pass, 2: second_pass})
    line_end(2)
    m.wo[...] = jnp.concatenate([m.wqkv[:, 3 * head_cols : qkv_pad], m.wo1[...]], axis=1)
    turn(m.wo, m.wot)
    out_product = lambda rows: mm(m.ctx[rows, :], m.wot[...])
    exchange(0, 0, out_product)
    pass_last(3)
    attend(1, {1: lambda: pass_on(4), 3: lambda: pass_last(4)})
    exchange(0, 1, out_product)
    pass_on(5)
    pass_on(6)
    norm_one(0)
    pass_last(5)
    pass_on(7)
    line_end(3)
    line_end(4)
    feed(0)
    pass_last(6)
    pass_last(7)
    line_end(5)
    turn(m.wdown, m.wdownt)
    down_product = lambda rows: mm(m.act[rows, :], m.wdownt[...])
    exchange(1, 0, down_product)
    norm_one(1)
    feed(1)
    exchange(1, 1, down_product)
    turn(m.wup, m.wupt)
    turn(m.wqkv, m.wqkvt)
    up_product = lambda rows: mm(m.gub[rows, :], m.wupt[...])
    norm_two(0)
    feed_back(0)()
    exchange(2, 0, up_product)
    first_rows, last_rows = slice(0, BUCKET_SLOTS), slice(BUCKET_SLOTS, 2 * BUCKET_SLOTS)
    weight_grad((), m.gffn, m.act, put_whole(m.wdownt), first_rows)
    weight_grad((3, 4), m.nb, m.gub, put_whole(m.wup), first_rows)
    norm_two(1)
    feed_rest = feed_back(1)
    spread_end(1, 1, 0)
    spread_end(1, 1, 1)
    weight_grad((), m.gffn, m.act, add_whole(m.wdownt), last_rows)
    half = hidden // 2
    left, right = m.wdownt.at[:, 0:half], m.wdownt.at[:, half:hidden]
    down = (0, left, m.xrdown, m.zsdown, m.zrdown, sh_down.at[:, 0:half])
    down_near = (4, right, m.xrdownb, m.zsdownb, m.zrdownb, sh_down.at[:, half:hidden])
    near_start(4, right, m.xrdownb)
    reduce_start(0, left, m.xrdown)
    feed_rest()
    exchange(2, 1, up_product)
    weight_grad((), m.nb, m.gub, add_whole(m.wup), last_rows)
    odd, even = pass_order[: nz // 2], pass_order[nz // 2 :]
    up = (1, m.wup, m.xrup, m.zsup, m.zrup, sh_up)
    out = (2, m.go, m.xro, m.zso, m.zro, sh_o)
    qkv = (3, m.wqkv, m.xrqkv, m.zsqkv, m.zrqkv, sh_qkv)
    norm_one_back(0)
    near_across(2, *down_near)
    reduce_start(1, m.wup, m.xrup, odd)
    blocks = lambda ks, matrix: lambda: [reduce_block(k, *matrix) for k in ks] and None
    early = [pass_order[0:1], pass_order[1:2], pass_order[2:-1]]

    def second_across():
        near_across(0, *down_near)
        reduce_start(1, m.wup, m.xrup, even)

    attend_back(
        0,
        {
            1: second_across,
            2: blocks(early[0], down),
            3: blocks(early[1], down),
        },
    )
    exchange_first(3, 0, input_part)
    near_far(2, *down_near)
    blocks(early[0], up)()
    norm_one_back(1)
    exchange_last(3, 0)
    spread_end(2, 1, 0)
    spread_end(2, 1, 1)
    weight_grad((0, 1, 2), m.gattn, m.ctx, put_o)
    blocks(early[1], up)()
    downward = list(range(nz - 1, -1, -1))
    reduce_start(2, m.go, m.xro, downward)
    attend_back(
        1,
        {
            0: blocks(early[2] + [0], down),
            3: blocks(early[2], up),
        },
    )
    weight_grad((), m.tok, m.dqkv, put_qkv)
    first_part, last_part = downward[:-1], downward[-1:]
    reduce_start(3, m.wqkv, m.xrqkv, first_part)
    reduce_block(0, *up)
    reduce_block(downward[0], *out)

    sm = m.sm
    sm[...] = jnp.zeros((SUM_ROWS, LANES), F32)
    acc = m.acc
    lead = jnp.where(yy == 0, 1.0, 0.0)

    def put(first, values):
        for i in range(values.shape[1] // LANES):
            sm[first + i : first + i + 1, :] = values[:, i * LANES : (i + 1) * LANES]

    def spot(values):
        return jnp.concatenate([jnp.where(T == t, values, 0.0) for t in range(4)], axis=1)

    for at, first in ((0, 0), (1, 6), (2, 12), (3, 18), (4, 36), (5, 42)):
        put(first, acc[at : at + 1, :] * lead)
    put(24, spot(acc[7:8, 0:head_cols]))
    put(30, spot(acc[7:8, 2 * head_cols : 3 * head_cols]))
    put(48, spot(acc[6:7, 0:hidden]))
    parts = []
    for h in range(heads):
        size = LANES // 2
        left = m.dband[h]
        while size >= 8:
            left = left[0:size, :] + pltpu.roll(left[size : 2 * size, :], long_row - size, 1)
            size //= 2
        for bit in (1, 2, 4):
            left = jnp.where(lax.rem(lax.div(sub8, bit), 2) == 1, pltpu.roll(left, long_row - bit, 1), left)
        left = pltpu.roll(left, LANES - 1, 1)
        diagonal = jnp.sum(left, axis=0, keepdims=True)
        hi = diagonal.astype(BF16).astype(F32)
        mid = (diagonal - hi).astype(BF16).astype(F32)
        parts += [hi, mid, diagonal - hi - mid]
    parts = jnp.concatenate(parts + [jnp.zeros((16 - len(parts), long_row), F32)], axis=0).astype(BF16)
    bucket_rows = -(-NB // LANES) * LANES
    valid = iota((1, long_row), 1) < long_row - 1
    hot_bucket = jnp.where((iota((bucket_rows, long_row), 0) == offsets) & valid, 1.0, 0.0).astype(BF16)
    by_bucket = mm_nt(parts, hot_bucket)
    bucket = iota((1, bucket_rows), 1)
    table_grad = jnp.zeros((32, LANES), F32)
    for h in range(heads):
        sums = by_bucket[3 * h : 3 * h + 1] + by_bucket[3 * h + 1 : 3 * h + 2] + by_bucket[3 * h + 2 : 3 * h + 3]
        flat = bucket * H + (T * heads + h)
        hot_row = jnp.where((iota((32, bucket_rows), 0) == lax.div(flat, LANES)) & (bucket < NB), 1.0, 0.0)
        hot_lane = jnp.where(iota((LANES, bucket_rows), 0) == lax.rem(flat, LANES), sums, 0.0)
        table_grad = table_grad + exact_nt(hot_row, hot_lane)
    sm[TABLE_ROW : TABLE_ROW + 30, :] = table_grad[0:30, :]

    lin_grad = m.glin[...]
    lin_grad = lin_grad + pltpu.roll(lin_grad, LANES - 16, 1) + pltpu.roll(lin_grad, LANES - 32, 1)
    lin_grad = jnp.where(own_head, lin_grad, 0.0)
    grad_u = jnp.sum(jnp.where(col_lane < 8, lin_grad, 0.0), axis=1, keepdims=True)
    grad_w = jnp.sum(jnp.where(col_lane >= 8, lin_grad, 0.0), axis=1, keepdims=True)
    by_lane = jnp.where(col_lane == 2 * col_in_head, grad_u, 0.0)
    by_lane = by_lane + jnp.where(col_lane == 2 * col_in_head + 1, grad_w, 0.0)
    sm[GATE_ROW : GATE_ROW + 1, :] = jnp.sum(by_lane, axis=0, keepdims=True)
    lin_total = acc[9:10, 0:LANES]
    total_u = jnp.sum(jnp.where(lane < 8, lin_total, 0.0), axis=1, keepdims=True)
    total_w = jnp.sum(jnp.where((lane >= 8) & (lane < 16), lin_total, 0.0), axis=1, keepdims=True)
    last = jnp.where(lane == 0, total_u, 0.0) + jnp.where(lane == 1, total_w, 0.0)
    scale_grad = acc[8:9, 0:LANES]
    for h in range(heads):
        one = jnp.sum(jnp.where(lane == h, scale_grad, 0.0), axis=1, keepdims=True)
        last = last + jnp.where(lane == 2 + T * heads + h, one, 0.0)
    sm[OFFSET_ROW : OFFSET_ROW + 1, :] = last

    small_sent = []

    def small_send(at, source, target, dev):
        cp = remote(source, target, m.s_ms.at[at], m.s_mr.at[at], dev)
        cp.start()
        small_sent.append(cp)
        return cp

    def quarter(index):
        return pl.ds(pl.multiple_of(index * QUARTER, QUARTER), QUARTER)

    to_core = [small_send(i, sm.at[quarter(2 * i + 1 - c)], m.smc.at[i], core_dev) for i in range(2)]
    for i in range(2):
        to_core[i].wait_recv()
        m.smh[i] = sm[quarter(2 * i + c), :] + m.smc[i]
    to_y = small_send(2, m.smh.at[1 - yy], m.smy, y_dev)
    reduce_block(first_part[0], *qkv)
    exchange_first(3, 1, input_part)
    reduce_block(downward[1], *out)
    exchange_last(3, 1)
    to_y.wait_recv()
    m.smv[...] = m.smh[yy] + m.smy[...]
    to_x = small_send(3, m.smv, m.smx, x_dev)
    reduce_start(3, m.wqkv, m.xrqkv, last_part)
    for k in downward[2:]:
        reduce_block(k, *out)
    reduce_block(first_part[1], *qkv)
    to_x.wait_recv()
    m.smz[z] = m.smv[...] + m.smx[...]
    for k in range(1, nz):
        small_send(3 + k, m.smz.at[z], m.smz.at[z], z_dev(k))
    for k in first_part[2:]:
        reduce_block(k, *qkv)
    token_rows(0)
    reduce_block(0, *qkv)
    squares = reduce_end(0, m.zrdown, sh_down.at[:, 0:half])
    near_far(0, *down_near)
    squares = squares + squares_of(sh_down[:, half:hidden])
    squares = squares + reduce_end(1, m.zrup, sh_up)
    squares = squares + reduce_end(2, m.zro, sh_o)
    for k in range(1, nz):
        here = m.smz.at[z_at(k)]
        remote(here, here, m.s_ms.at[3 + k], m.s_mr.at[3 + k], z_dev(k)).wait_recv()
    own_quarter = m.smz[0]
    for i in range(1, nz):
        own_quarter = own_quarter + m.smz[i]
    m.sma[quarter(T), :] = own_quarter
    for k in range(1, 4):
        mine_small = m.sma.at[quarter(T)]
        small_send(2 + nz + k, mine_small, mine_small, (D, lax.rem(T + k, 4)))
    squares = squares + reduce_end(3, m.zrqkv, sh_qkv)
    last_copies = []
    for i, (source, target) in enumerate(
        ((sh_down, out_down), (sh_up, out_up), (sh_o, out_o), (sh_qkv, out_qkv))
    ):
        cp = pltpu.make_async_copy(source, target, m.s_out.at[i])
        cp.start()
        last_copies.append(cp)
    sqt = m.sqt
    sqt[T] = squares
    tail_sent = []
    for k in range(1, 4):
        cp = remote(
            sqt.at[T], sqt.at[T], m.s_ts.at[k], m.s_tr.at[k], (D, lax.rem(T + k, 4))
        )
        cp.start()
        tail_sent.append(cp)
    token_rows(1)
    for k in range(1, 4):
        here = m.sma.at[quarter(lax.rem(T + 4 - k, 4))]
        remote(here, here, m.s_ms.at[2 + nz + k], m.s_mr.at[2 + nz + k], core_dev).wait_recv()
    small_total = m.sma[0:SMALL_ROWS, :]
    for i in range(3):
        small_out[i] = small[i * SMALL_ROWS : (i + 1) * SMALL_ROWS, :]
    small_out[3] = small_total
    cp = pltpu.make_async_copy(small_out, out_small, m.s_out.at[4])
    cp.start()
    last_copies.append(cp)
    small_square = small_total * small_total
    small_tile = jnp.zeros((8, LANES), F32)
    for i in range(SMALL_ROWS // 8):
        small_tile = small_tile + small_square[8 * i : 8 * i + 8, :]
    for k in range(1, 4):
        here = sqt.at[lax.rem(T + 4 - k, 4)]
        remote(here, here, m.s_ts.at[k], m.s_tr.at[k], core_dev).wait_recv()
    sqd = m.sqd
    sqd[D] = sqt[0] + sqt[1] + sqt[2] + sqt[3]
    for k in range(1, n_dp):
        cp = remote(
            sqd.at[D], sqd.at[D], m.s_ds.at[k], m.s_dr.at[k], (lax.rem(D + k, n_dp), T)
        )
        cp.start()
        tail_sent.append(cp)
    for k in range(1, n_dp):
        here = sqd.at[lax.rem(D + n_dp - k, n_dp)]
        remote(here, here, m.s_ds.at[k], m.s_dr.at[k], core_dev).wait_recv()
    everything = small_tile
    for i in range(n_dp):
        everything = everything + sqd[i]
    sum_all = jnp.sum(jnp.sum(everything, axis=0, keepdims=True), axis=1, keepdims=True)
    norm_out[...] = jnp.broadcast_to(jnp.sqrt(sum_all), (8, LANES))

    for which in list(gathers):
        sent_all(which)
    for where in reduces:
        remote(*where()).wait_send()
    for cp in small_sent + tail_sent:
        cp.wait_send()
    for sent in core_spread.values():
        for cp in sent:
            cp.wait_send()
    for b in range(2):
        for cp in core_sent[(3, b)] + y_sent[(3, b)]:
            cp.wait_send()
    for cp in last_copies:
        cp.wait()
    for here, there in out_copies[2:]:
        here.wait()
        there.wait()


def adam_kernel(head_cols, *refs):
    ins, rest = refs[:14], refs[14:]
    block_in, token_in = ins[12:14]
    outs, rest = rest[:14], rest[14:]
    norm_out, block_out, token_out = outs[0], outs[12], outs[13]
    held, made = rest[:12], rest[12:24]
    block_held, token_held, s_in, s_out = rest[24:]
    loads = [pltpu.make_async_copy(ins[i], held[i], s_in.at[i]) for i in range(12)]
    passing = [
        pltpu.make_async_copy(block_in, block_held, s_in.at[12]),
        pltpu.make_async_copy(token_in, token_held, s_in.at[13]),
    ]
    passed = [
        pltpu.make_async_copy(block_held, block_out, s_out.at[12]),
        pltpu.make_async_copy(token_held, token_out, s_out.at[13]),
    ]
    for cp in loads + passing:
        cp.start()
    stores = []

    def store(i):
        cp = pltpu.make_async_copy(made[i], outs[i], s_out.at[i])
        cp.start()
        stores.append(cp)

    sh_qkv, sh_o, sh_up, sh_down, sh_small, norm, aw, am, av, fw, fm, fv = held
    (o_norm, o_am, o_av, o_aw, o_ac, o_fm, o_fv, o_fw, o_fc, o_sm, o_sv, o_sw) = made
    for i in (0, 1, 2, 3, 5):
        loads[i].wait()
    length = norm[0:1, 0:1]
    factor = CLIP_LIMIT / jnp.maximum(length, CLIP_LIMIT)
    o_norm[...] = length
    store(0)
    for i in (6, 7, 8):
        loads[i].wait()
    for i in range(4):
        if i < 3:
            grad = sh_qkv[:, i * head_cols : (i + 1) * head_cols]
        else:
            grad = jnp.concatenate([sh_qkv[:, 3 * head_cols :], sh_o[...]], axis=1)
        moment, square, master = adam_step(
            aw[i], am[i], av[i], factor * grad, RATE_MATRIX, WEIGHT_DECAY
        )
        o_am[i] = moment
        o_av[i] = square
        o_aw[i] = master
        o_ac[i] = master.astype(BF16)
    for i in (1, 2, 3, 4):
        store(i)
    for first, second in zip(passing, passed, strict=True):
        first.wait()
        second.start()
    for i in (9, 10, 11):
        loads[i].wait()
    for i, share in enumerate((sh_up, sh_down)):
        moment, square, master = adam_step(
            fw[i], fm[i], fv[i], factor * share[...], RATE_MATRIX, WEIGHT_DECAY
        )
        o_fm[i] = moment
        o_fv[i] = square
        o_fw[i] = master
        o_fc[i] = master.astype(BF16)
    for i in (5, 6, 7, 8):
        store(i)
    loads[4].wait()
    moment, square, master = adam_step(
        sh_small[0], sh_small[1], sh_small[2], factor * sh_small[3], RATE_SMALL, 0.0
    )
    o_sm[...] = moment
    o_sv[...] = square
    o_sw[...] = master
    for i in (9, 10, 11):
        store(i)
    for cp in stores + passed:
        cp.wait()


def fused_body(
    n_dp,
    tokens,
    cotangent,
    clip_lengths,
    key_mask,
    rel_buckets,
    attention_weights,
    attention_first,
    attention_second,
    feedforward_weights,
    feedforward_first,
    feedforward_second,
    small_params,
    small_first,
    small_second,
):
    rows = tokens.shape[0]
    owned, head_cols = attention_weights.shape[1:]
    hidden = feedforward_weights.shape[2]
    heads = head_cols // HD
    qkv_pad = -(-3 * head_cols // LANES) * LANES
    nz = n_dp // 2
    small_size = SMALL_ROWS * LANES
    total_size = 3 * small_size + 2 * BUCKET_SLOTS
    packed = jnp.zeros((total_size,), F32)
    pieces = (small_params, small_first, small_second, rel_buckets.astype(F32))
    for i, values in enumerate(pieces):
        after = total_size - i * small_size - values.shape[0]
        packed = packed + jnp.pad(values, (i * small_size, after))
    packed = packed.reshape(-1, LANES)
    keep = key_mask.reshape(rows // LANES, LANES)
    scratch = layer_scratch(owned, nz, qkv_pad, heads, head_cols, hidden)
    names = tuple(scratch)
    vmem = pl.BlockSpec(memory_space=pltpu.VMEM)
    smem = pl.BlockSpec(memory_space=pltpu.SMEM)
    anywhere = pl.BlockSpec(memory_space=pl.ANY)
    sds = jax.ShapeDtypeStruct
    block_rows, token_rows, sh_qkv, sh_o, sh_up, sh_down, sh_small, norm = pl.pallas_call(
        partial(layer_kernel, names, (n_dp, owned, qkv_pad, heads, head_cols, hidden)),
        out_shape=(
            sds((rows, W), BF16),
            sds((rows, W), BF16),
            sds((owned, qkv_pad), F32),
            sds((owned, LANES), F32),
            sds((owned, hidden), F32),
            sds((owned, hidden), F32),
            sds((4, SMALL_ROWS, LANES), F32),
            sds((8, LANES), F32),
        ),
        in_specs=[anywhere, anywhere, smem] + [anywhere] * 4,
        out_specs=(anywhere,) * 7 + (vmem,),
        scratch_shapes=list(scratch.values()),
        compiler_params=pltpu.CompilerParams(
            collective_id=1, has_side_effects=True, vmem_limit_bytes=62 * 1024 * 1024
        ),
        name="layer",
    )(tokens, cotangent, clip_lengths, keep, attention_weights, feedforward_weights, packed)
    like = lambda a, dtype=F32: sds(a.shape, dtype)
    small_like = sds((SMALL_ROWS, LANES), F32)
    made = (
        sds((1, 1), F32),
        like(attention_weights),
        like(attention_weights),
        like(attention_weights),
        like(attention_weights, BF16),
        like(feedforward_weights),
        like(feedforward_weights),
        like(feedforward_weights),
        like(feedforward_weights, BF16),
        small_like,
        small_like,
        small_like,
    )
    operands = (
        sh_qkv,
        sh_o,
        sh_up,
        sh_down,
        sh_small,
        norm,
        attention_weights,
        attention_first,
        attention_second,
        feedforward_weights,
        feedforward_first,
        feedforward_second,
        block_rows,
        token_rows,
    )
    in_vmem = lambda a: pltpu.VMEM(a.shape, a.dtype)
    results = pl.pallas_call(
        partial(adam_kernel, head_cols),
        out_shape=(*made, like(tokens, BF16), like(tokens, BF16)),
        in_specs=[anywhere] * len(operands),
        out_specs=(anywhere,) * (len(made) + 2),
        scratch_shapes=[in_vmem(a) for a in operands[:12]]
        + [in_vmem(a) for a in made]
        + [in_vmem(tokens), in_vmem(tokens)]
        + [pltpu.SemaphoreType.DMA((14,)), pltpu.SemaphoreType.DMA((14,))],
        compiler_params=pltpu.CompilerParams(vmem_limit_bytes=62 * 1024 * 1024),
        name="adam",
    )(*operands)
    length = small_params.shape[0]
    flat = lambda a: a.reshape(-1)[:length]
    return (
        results[0].reshape(()),
        *results[1:9],
        flat(results[9]),
        flat(results[10]),
        flat(results[11]),
        *results[12:],
    )


def fused_fits(mesh, owned):
    columns = mesh.shape["dp"] // 2
    whole = mesh.shape["dp"] % 2 == 0 and columns & (columns - 1) == 0
    return mesh.shape["tensor"] == 4 and whole and owned % 16 == 0

def solution(mesh):
    in_specs = (
        P("dp", None),
        P("dp", None),
        P("dp", None),
        P("dp"),
        P(),
        P(None, "dp", "tensor"),
        P(None, "dp", "tensor"),
        P(None, "dp", "tensor"),
        P(None, "dp", "tensor"),
        P(None, "dp", "tensor"),
        P(None, "dp", "tensor"),
        P(),
        P(),
        P(),
    )
    out_specs = (
        P(),
        P(None, "dp", "tensor"),
        P(None, "dp", "tensor"),
        P(None, "dp", "tensor"),
        P(None, "dp", "tensor"),
        P(None, "dp", "tensor"),
        P(None, "dp", "tensor"),
        P(None, "dp", "tensor"),
        P(None, "dp", "tensor"),
        P(),
        P(),
        P(),
        P("dp", None),
        P("dp", None),
    )
    n_dp = mesh.shape["dp"]
    body = general_body
    if fused_fits(mesh, MODEL_WIDTH // n_dp):
        body = partial(fused_body, n_dp)
    return jax.shard_map(body, mesh=mesh, in_specs=in_specs, out_specs=out_specs, check_vma=False)
```
